32 devices in a mesh: dp: 4 (over y, x), head: 4 (over z), width: 2 (over core).
Axes of the slice: x: 2, y: 2, z: 4, core: 2. Of those that a mesh axis runs over, the one named last changes fastest.
Arguments:
- hidden: bfloat16 [16384, 1024], P(('dp', 'head'), 'width'), may hold values from -6 to 6
- lengths: int32 [4], P('dp'), may hold values from 1024 to 4096, as said below
- cotangent: bfloat16 [16384, 1024], P(('dp', 'head'), 'width'), may hold values from -6 to 6
- norm_gain: bfloat16 [1024], P('width'), may hold values from 0.5 to 1.5
- in_zx: bfloat16 [1024, 32, 128], P('width', 'head'), may hold values from -0.1875 to 0.1875
- in_bcdt: bfloat16 [1024, 288], P('width'), may hold values from -0.1875 to 0.1875
- conv_x: bfloat16 [4, 2048], P(None, 'head'), may hold values from -3 to 3
- conv_bc: bfloat16 [4, 256], replicated, may hold values from -3 to 3
- dt_bias: float32 [32], P('head'), may hold values from -7 to -1
- a_log: float32 [32], P('head'), may hold values from -1 to 1.5
- d_skip: float32 [32], P('head'), may hold values from 0.5 to 1.5
- gnorm_gain: bfloat16 [2048], P('head'), may hold values from 0.5 to 1.5
- out_w: bfloat16 [2048, 1024], P('head', 'width'), may hold values from -0.125 to 0.125
Outputs:
- out_hidden: bfloat16 [16384, 1024], P(('dp', 'head'), 'width')
- grad_hidden: bfloat16 [16384, 1024], P(('dp', 'head'), 'width')
- grad_norm_gain: float32 [1024], P('width')
- grad_in_zx: float32 [1024, 32, 128], P('width', 'head')
- grad_in_bcdt: float32 [1024, 288], P('width')
- grad_conv_x: float32 [4, 2048], P(None, 'head')
- grad_conv_bc: float32 [4, 256], replicated
- grad_dt_bias: float32 [32], P('head')
- grad_a_log: float32 [32], P('head')
- grad_d_skip: float32 [32], P('head')
- grad_gnorm_gain: float32 [2048], P('head')
- grad_out_w: float32 [2048, 1024], P('head', 'width')
The draws below stay inside these ranges and needn't reach their ends.
Inputs may be any that keep to these rules, and one draw needn't show every extreme that they name: `lengths`: the valid prefix of each sequence; some sequence is full and some has exactly 1024 valid tokens.
All inputs are finite; a program needn't handle non-finite values.
Results may differ from the reference program's by a relative error of at most 0.0084.
Values may be sent and summed in bfloat16 or wider, within the bound.
A program may use at most 256 MiB of HBM per device.

```python
import jax
import jax.numpy as jnp
from jax import lax

D = 1024
HEADS = 32
HEADDIM = 64
STATE = 128
KCONV = 4
SCAN_BLOCK = 256
LEN = 4096
INNER = 2048
SEQS = 4
TOKENS = 16384


def draw_lengths(key, part):
    first_key, second_key = jax.random.split(jax.random.fold_in(key, 11))
    values = jax.random.randint(first_key, (SEQS,), LEN // 4, LEN + 1)
    order = jax.random.permutation(second_key, SEQS)
    values = jnp.where(order == 0, LEN, values)
    values = jnp.where(order == 1, LEN // 4, values)
    return values.astype(jnp.int32)


def level_of(key, extent, cuts, low, largest):
    gain, own = 1.0, jax.random.fold_in(key, 6)
    for dim, parts in cuts:
        steps = jnp.exp(jax.random.uniform(jax.random.fold_in(own, dim), (parts,), jnp.float32, low / len(cuts), largest / len(cuts)))
        gain = gain * jnp.repeat(steps, extent[dim] // parts).reshape([-1 if axis == dim else 1 for axis in range(len(extent))])
    return gain


def noise(key, shape, scale, most, shards=(), held_as=jnp.bfloat16):
    factor_of = level_of(key, shape, shards, -0.22, 0.18) if shards else 1.0
    drawn = jax.random.normal(key, shape, jnp.float32) * scale * factor_of
    return jnp.minimum(jnp.maximum(drawn, -most), most).astype(held_as)


def setup_inputs(seed: int = 0) -> dict:
    key_of = jax.random.split(jax.random.key(seed), 14)
    hidden = noise(key_of[0], (TOKENS, D), 1.0, 6.0, ((0, 16), (1, 2)))
    lengths = draw_lengths(jax.random.fold_in(key_of[13], 71), 0)
    cotangent = noise(key_of[2], (TOKENS, D), 1.0, 6.0, ((0, 16), (1, 2)))
    norm_gain = jnp.clip(1.0 + 0.1 * jax.random.normal(key_of[3], (D,), jnp.float32), 0.5, 1.5).astype(jnp.bfloat16)
    in_zx = noise(key_of[4], (D, HEADS, 2 * HEADDIM), D ** -0.5, 0.1875, ((0, 2), (1, 4)))
    in_bcdt = noise(key_of[5], (D, 2 * STATE + HEADS), D ** -0.5, 0.1875, ((0, 2),))
    conv_x = noise(key_of[6], (KCONV, INNER), KCONV ** -0.5, 3.0, ((1, 4),))
    conv_bc = noise(key_of[7], (KCONV, 2 * STATE), KCONV ** -0.5, 3.0)
    dt_bias = jnp.clip(-7.0 + 6.0 * jax.random.uniform(key_of[8], (HEADS,), jnp.float32) ** level_of(key_of[8], (HEADS,), ((0, 4),), -0.2, 0.2), -7.0, -1.0)
    a_log = jnp.clip(-1.0 + 2.5 * jax.random.uniform(key_of[9], (HEADS,), jnp.float32) ** level_of(key_of[9], (HEADS,), ((0, 4),), -0.2, 0.2), -1.0, 1.5)
    d_skip = jnp.clip(0.5 + 1.0 * jax.random.uniform(key_of[10], (HEADS,), jnp.float32) ** level_of(key_of[10], (HEADS,), ((0, 4),), -0.2, 0.2), 0.5, 1.5)
    gnorm_gain = jnp.clip(1.0 + 0.1 * jax.random.normal(key_of[11], (INNER,), jnp.float32), 0.5, 1.5).astype(jnp.bfloat16)
    out_w = noise(key_of[12], (INNER, D), INNER ** -0.5, 0.125, ((0, 4), (1, 2)))
    return dict(hidden=hidden, lengths=lengths, cotangent=cotangent, norm_gain=norm_gain, in_zx=in_zx, in_bcdt=in_bcdt, conv_x=conv_x, conv_bc=conv_bc, dt_bias=dt_bias, a_log=a_log, d_skip=d_skip, gnorm_gain=gnorm_gain, out_w=out_w)


EPS = 1e-05
HIGH = lax.Precision.HIGHEST

@jax.custom_vjp
def low(v):
    return lax.optimization_barrier(v.astype(jnp.bfloat16)).astype(jnp.float32)

@jax.custom_vjp
def low_back(v):
    return v

def low_keep(v):
    return (low(v), None)

def low_pass(kept, grad):
    return (grad,)

def back_keep(v):
    return (v, None)

def back_low(kept, grad):
    return (low(grad),)
low.defvjp(low_keep, low_pass)
low_back.defvjp(back_keep, back_low)

def conv_causal(values, kernel):
    taps = kernel.shape[0]
    padded = jnp.pad(values, ((taps - 1, 0), (0, 0)))
    total = jnp.zeros_like(values)
    for offset in range(taps):
        total = total + kernel[offset] * padded[offset:offset + values.shape[0]]
    return total

def block_scan(inputs, steps, rates, bmat, cmat, block):
    length, heads, hsize = inputs.shape
    count = length // block
    in_blocks = inputs.reshape(count, block, heads, hsize)
    step_blocks = steps.reshape(count, block, heads)
    b_blocks = bmat.reshape(count, block, bmat.shape[1])
    c_blocks = cmat.reshape(count, block, cmat.shape[1])
    places = jnp.arange(block)
    lower = (places[:, None] >= places[None, :])[:, :, None]

    def advance(state, pieces):
        x_part, dt_part, b_part, c_part = pieces
        cums = jnp.cumsum(dt_part * rates, axis=0)
        spread = cums[:, None, :] - cums[None, :, :]
        decay = jnp.where(lower, jnp.exp(jnp.where(lower, spread, 0.0)), 0.0)
        scores = jnp.dot(c_part, b_part.T, precision=HIGH)
        weights = scores[:, :, None] * decay * dt_part[None, :, :]
        inside = jnp.einsum('ijh,jhp->ihp', weights, x_part, precision=HIGH)
        carried = jnp.einsum('in,hpn->ihp', c_part, state, precision=HIGH) * jnp.exp(cums)[:, :, None]
        tails = jnp.exp(cums[-1][None, :] - cums) * dt_part
        state = jnp.exp(cums[-1])[:, None, None] * state + jnp.einsum('jh,jhp,jn->hpn', tails, x_part, b_part, precision=HIGH)
        return (state, inside + carried)
    start_state = jnp.zeros((heads, hsize, bmat.shape[1]), jnp.float32)
    _, result = lax.scan(jax.checkpoint(advance), start_state, (in_blocks, step_blocks, b_blocks, c_blocks))
    return result.reshape(length, heads, hsize)

def mixer(zx, bc_raw, dt_raw, kernel_x, kernel_bc, bias_dt, log_rate, skip):
    length, heads, double = zx.shape
    hsize = double // 2
    gate = zx[:, :, :hsize]
    x_raw = zx[:, :, hsize:].reshape(length, heads * hsize)
    xs_conv = jax.nn.silu(conv_causal(x_raw, kernel_x)).reshape(length, heads, hsize)
    bc_conv = jax.nn.silu(conv_causal(bc_raw, kernel_bc))
    half = bc_conv.shape[1] // 2
    steps = jax.nn.softplus(dt_raw + bias_dt)
    rates = -jnp.exp(log_rate)
    result = block_scan(xs_conv, steps, rates, bc_conv[:, :half], bc_conv[:, half:], SCAN_BLOCK) + skip[:, None] * xs_conv
    return (result * jax.nn.silu(gate)).reshape(length, heads * hsize)

def block_forward(base, mask, norm_gain, in_zx, in_bcdt, conv_x, conv_bc, dt_bias, a_log, d_skip, gnorm_gain, out_w):
    scale = lax.rsqrt(lax.optimization_barrier(jnp.mean(base * base, axis=1, keepdims=True)) + EPS)
    normed = low(base * scale * norm_gain)
    zx = low_back(jnp.dot(normed, in_zx.reshape(D, HEADS * 2 * HEADDIM), precision=HIGH)).reshape(LEN, HEADS, 2 * HEADDIM)
    bcdt = low_back(jnp.dot(normed, in_bcdt, precision=HIGH))
    gated = mixer(zx, bcdt[:, :2 * STATE], bcdt[:, 2 * STATE:], conv_x, conv_bc, dt_bias, a_log, d_skip)
    scale_out = lax.rsqrt(lax.optimization_barrier(jnp.mean(gated * gated, axis=1, keepdims=True)) + EPS)
    mixed = low(gated * scale_out * gnorm_gain)
    branch = jnp.dot(mixed, out_w, precision=HIGH)
    return base + mask[:, None] * branch

def reference(hidden, lengths, cotangent, norm_gain, in_zx, in_bcdt, conv_x, conv_bc, dt_bias, a_log, d_skip, gnorm_gain, out_w):
    weights = tuple((w.astype(jnp.float32) for w in (norm_gain, in_zx, in_bcdt, conv_x, conv_bc, dt_bias, a_log, d_skip, gnorm_gain, out_w)))
    positions = jnp.arange(LEN)

    def one_sequence(totals, item):
        rows, grad_rows, limit = item
        mask = (positions < limit).astype(jnp.float32)

        def apply(base, *params):
            return block_forward(base, mask, *params)
        result, pull = jax.vjp(apply, rows.astype(jnp.float32), *weights)
        grads = pull(grad_rows.astype(jnp.float32))
        totals = tuple((t + g for t, g in zip(totals, grads[1:])))
        return (totals, (result.astype(jnp.bfloat16), grads[0].astype(jnp.bfloat16)))
    start_totals = tuple((jnp.zeros(w.shape, jnp.float32) for w in weights))
    totals, (outputs, grad_inputs) = lax.scan(one_sequence, start_totals, (hidden.reshape(SEQS, LEN, D), cotangent.reshape(SEQS, LEN, D), lengths))
    return (outputs.reshape(TOKENS, D), grad_inputs.reshape(TOKENS, D), totals[0], totals[1], totals[2], totals[3], totals[4], totals[5], totals[6], totals[7], totals[8], totals[9])
```

```python
import functools

import jax
import jax.numpy as jnp
import numpy as np
from jax import lax
from jax.experimental import pallas as pl
from jax.experimental.pallas import tpu as pltpu
from jax.sharding import PartitionSpec as P

D = 1024
HEADS = 32
HEADDIM = 64
STATE = 128
SCAN_BLOCK = 256
LEN = 4096
INNER = 2048
SEQS = 4


EPS = 1e-05
HIGH = lax.Precision.HIGHEST


def conv_causal(values, kernel):
    taps = kernel.shape[0]
    padded = jnp.pad(values, ((taps - 1, 0), (0, 0)))
    total = jnp.zeros_like(values)
    for offset in range(taps):
        total = total + kernel[offset] * padded[offset : offset + values.shape[0]]
    return total


def block_scan(inputs, steps, rates, bmat, cmat, block):
    length, heads, hsize = inputs.shape
    count = length // block
    in_blocks = inputs.reshape(count, block, heads, hsize)
    step_blocks = steps.reshape(count, block, heads)
    b_blocks = bmat.reshape(count, block, bmat.shape[1])
    c_blocks = cmat.reshape(count, block, cmat.shape[1])
    places = jnp.arange(block)
    lower = (places[:, None] >= places[None, :])[:, :, None]

    def advance(state, pieces):
        x_part, dt_part, b_part, c_part = pieces
        cums = jnp.cumsum(dt_part * rates, axis=0)
        spread = cums[:, None, :] - cums[None, :, :]
        decay = jnp.where(lower, jnp.exp(jnp.where(lower, spread, 0.0)), 0.0)
        scores = jnp.dot(c_part, b_part.T, precision=HIGH)
        weights = scores[:, :, None] * decay * dt_part[None, :, :]
        inside = jnp.einsum("ijh,jhp->ihp", weights, x_part, precision=HIGH)
        carried = (
            jnp.einsum("in,hpn->ihp", c_part, state, precision=HIGH) * jnp.exp(cums)[:, :, None]
        )
        tails = jnp.exp(cums[-1][None, :] - cums) * dt_part
        state = jnp.exp(cums[-1])[:, None, None] * state + jnp.einsum(
            "jh,jhp,jn->hpn", tails, x_part, b_part, precision=HIGH
        )
        return (state, inside + carried)

    start_state = jnp.zeros((heads, hsize, bmat.shape[1]), jnp.float32)
    _, result = lax.scan(
        jax.checkpoint(advance), start_state, (in_blocks, step_blocks, b_blocks, c_blocks)
    )
    return result.reshape(length, heads, hsize)


def mixer(zx, bc_raw, dt_raw, kernel_x, kernel_bc, bias_dt, log_rate, skip):
    length, heads, double = zx.shape
    hsize = double // 2
    gate = zx[:, :, :hsize]
    x_raw = zx[:, :, hsize:].reshape(length, heads * hsize)
    xs_conv = jax.nn.silu(conv_causal(x_raw, kernel_x)).reshape(length, heads, hsize)
    bc_conv = jax.nn.silu(conv_causal(bc_raw, kernel_bc))
    half = bc_conv.shape[1] // 2
    steps = jax.nn.softplus(dt_raw + bias_dt)
    rates = -jnp.exp(log_rate)
    result = (
        block_scan(xs_conv, steps, rates, bc_conv[:, :half], bc_conv[:, half:], SCAN_BLOCK)
        + skip[:, None] * xs_conv
    )
    return (result * jax.nn.silu(gate)).reshape(length, heads * hsize)


def per_device(
    hidden,
    lengths,
    cotangent,
    norm_gain,
    in_zx,
    in_bcdt,
    conv_x,
    conv_bc,
    dt_bias,
    a_log,
    d_skip,
    gnorm_gain,
    out_w,
):
    slice_rows, half_width = hidden.shape
    local_heads = in_zx.shape[1]
    head_count = lax.axis_size("head")
    head_index = lax.axis_index("head")
    total_rows = slice_rows * head_count
    seq_local = lengths.shape[0]
    inner_local = local_heads * HEADDIM
    row_ids = head_index * slice_rows + jnp.arange(slice_rows, dtype=jnp.int32)
    owner = (row_ids // LEN)[:, None] == jnp.arange(seq_local, dtype=jnp.int32)[None, :]
    limits = jnp.sum(jnp.where(owner, lengths[None, :], 0), axis=1)
    keeper = (row_ids % LEN < limits).astype(jnp.float32)[:, None]
    source = hidden.astype(jnp.float32)
    squares = lax.psum(jnp.sum(source * source, axis=1), "width")
    scale = lax.rsqrt(squares / D + EPS)[:, None]
    gain_in = norm_gain.astype(jnp.float32)
    normed = (source * scale * gain_in).astype(jnp.bfloat16)
    gathered = lax.all_gather(normed, "head", axis=0, tiled=True)
    w_zx = in_zx.reshape(half_width, local_heads * 2 * HEADDIM)
    zx_part = jnp.dot(gathered, w_zx, preferred_element_type=jnp.float32)
    bcdt_part = jnp.dot(gathered, in_bcdt, preferred_element_type=jnp.float32)
    zx_full, bcdt_full = lax.psum((zx_part, bcdt_part), "width")
    zx_seq = zx_full.reshape(seq_local, LEN, local_heads, 2 * HEADDIM)
    bc_seq = bcdt_full[:, : 2 * STATE].reshape(seq_local, LEN, 2 * STATE)
    dt_seq = lax.dynamic_slice_in_dim(
        bcdt_full, 2 * STATE + head_index * local_heads, local_heads, 1
    ).reshape(seq_local, LEN, local_heads)

    def local_mix(zx_in, bc_in, dt_in, kernel_x, kernel_bc, bias_in, log_in, skip_in):
        per_sequence = jax.vmap(mixer, in_axes=(0, 0, 0, None, None, None, None, None))
        return per_sequence(
            zx_in, bc_in, dt_in, kernel_x, kernel_bc, bias_in, log_in, skip_in
        ).reshape(total_rows, inner_local)

    gated, mix_pull = jax.vjp(
        local_mix,
        zx_seq,
        bc_seq,
        dt_seq,
        conv_x.astype(jnp.float32),
        conv_bc.astype(jnp.float32),
        dt_bias,
        a_log,
        d_skip,
    )
    total_sq = lax.psum(jnp.sum(gated * gated, axis=1), "head")
    scale_out = lax.rsqrt(total_sq / INNER + EPS)[:, None]
    gain_out = gnorm_gain.astype(jnp.float32)
    mixed = (gated * scale_out * gain_out).astype(jnp.bfloat16)
    picked = mixed
    branch = lax.psum_scatter(
        jnp.dot(picked, out_w, preferred_element_type=jnp.float32),
        "head",
        scatter_dimension=0,
        tiled=True,
    )
    out_hidden = (source + keeper * branch).astype(jnp.bfloat16)
    grad_out = cotangent.astype(jnp.float32)
    masked = (grad_out * keeper).astype(jnp.bfloat16)
    piece = lax.all_gather(masked, "head", axis=0, tiled=True)
    picked = mixed
    acc_weight = jnp.einsum("tc,td->cd", picked, piece, preferred_element_type=jnp.float32)
    product = jnp.einsum("td,cd->tc", piece, out_w, preferred_element_type=jnp.float32)
    grad_mixed = lax.psum(product, "width")
    gain_out_grad = jnp.sum(grad_mixed * gated * scale_out, axis=0)
    inner_total = lax.psum(jnp.sum(grad_mixed * gain_out * gated, axis=1), "head")
    cubed = scale_out * scale_out * scale_out
    grad_gated = scale_out * gain_out * grad_mixed - gated * cubed / INNER * inner_total[:, None]
    (
        grad_zx_seq,
        grad_bc_seq,
        grad_dt_seq,
        kernel_x_grad,
        kernel_bc_grad,
        bias_grad,
        rate_grad,
        skip_grad,
    ) = mix_pull(grad_gated)
    grad_zx = grad_zx_seq.reshape(total_rows, local_heads * 2 * HEADDIM).astype(jnp.bfloat16)
    dt_columns = jnp.zeros((total_rows, HEADS), jnp.float32)
    dt_columns = lax.dynamic_update_slice_in_dim(
        dt_columns, grad_dt_seq.reshape(total_rows, local_heads), head_index * local_heads, 1
    )
    grad_bcdt_head = jnp.concatenate(
        [grad_bc_seq.reshape(total_rows, 2 * STATE), dt_columns], axis=1
    )
    weight_zx = jnp.einsum(
        "td,tc->dc", gathered, grad_zx, preferred_element_type=jnp.float32
    ).reshape(half_width, local_heads, 2 * HEADDIM)
    normed_part = jnp.einsum("tc,dc->td", grad_zx, w_zx, preferred_element_type=jnp.float32)
    grad_normed, bcdt_summed = (
        lax.psum_scatter(normed_part, "head", scatter_dimension=0, tiled=True),
        lax.psum_scatter(grad_bcdt_head, "head", scatter_dimension=0, tiled=True),
    )
    bcdt_low = bcdt_summed.astype(jnp.bfloat16)
    grad_normed = grad_normed + jnp.einsum(
        "tk,dk->td", bcdt_low, in_bcdt, preferred_element_type=jnp.float32
    )
    weight_bcdt = jnp.einsum("td,tk->dk", normed, bcdt_low, preferred_element_type=jnp.float32)
    gain_in_grad = jnp.sum(grad_normed * source * scale, axis=0)
    across = lax.psum(jnp.sum(grad_normed * gain_in * source, axis=1), "width")
    scale_cubed = scale * scale * scale
    grad_hidden = (
        grad_out + scale * gain_in * grad_normed - source * scale_cubed / D * across[:, None]
    ).astype(jnp.bfloat16)
    summed_dp = lax.psum(
        (weight_zx, acc_weight, kernel_x_grad, bias_grad, rate_grad, skip_grad, gain_out_grad), "dp"
    )
    summed_all = lax.psum((weight_bcdt, gain_in_grad, kernel_bc_grad), ("dp", "head"))
    return (
        out_hidden,
        grad_hidden,
        summed_all[1],
        summed_dp[0],
        summed_all[0],
        summed_dp[2],
        summed_all[2],
        summed_dp[3],
        summed_dp[4],
        summed_dp[5],
        summed_dp[6],
        summed_dp[1],
    )


BF = jnp.bfloat16
F32 = jnp.float32
Q = 128
HALO = 16
NEG = -1e30
VMEM = 60 * 1024 * 1024


def dot(a, b, prec=None):
    return lax.dot_general(a, b, (((1,), (0,)), ((), ())), precision=prec, preferred_element_type=F32)


def dot_t(a, b, prec=None):
    return lax.dot_general(a, b, (((1,), (1,)), ((), ())), precision=prec, preferred_element_type=F32)


def t_dot(a, b, prec=None):
    return lax.dot_general(a, b, (((0,), (0,)), ((), ())), precision=prec, preferred_element_type=F32)


def split2(v, axis=1):
    hi = v.astype(BF)
    lo = (v - hi.astype(F32)).astype(BF)
    return jnp.concatenate([hi, lo], axis=axis)


def dot_split(v, m):
    hi = v.astype(BF)
    lo = (v - hi.astype(F32)).astype(BF)
    return dot(hi, m) + dot(lo, m)


def split_dot(m, v):
    hi = v.astype(BF)
    lo = (v - hi.astype(F32)).astype(BF)
    return dot(m, hi) + dot(m, lo)


def sigmoid(v):
    return 1.0 / (1.0 + jnp.exp(-v))


def tri(kind):
    row = lax.broadcasted_iota(jnp.int32, (Q, Q), 0)
    col = lax.broadcasted_iota(jnp.int32, (Q, Q), 1)
    return {"ge": row >= col, "le": row <= col, "gt": row > col}[kind]


def entry_kernel(
    hm, ho, hh, gain, wbc, wdt, cbc, bias, rate,
    xn_o, r_o, raw_o, rawh_o, u_o, b_o, c_o, dt_o, sig_o, cl_o, clt_o, ctot_o,
    dt2_o, e12_o, tl2_o, dttl2_o, ec2_o, edt2_o, buf,
):
    rows = hm.shape[0]
    state = b_o.shape[1]
    blocks = rows // Q
    lower = tri("ge").astype(F32)

    def norm(left, right):
        h = jnp.concatenate([left, right], axis=1).astype(F32)
        r = lax.rsqrt(jnp.mean(h * h, axis=1, keepdims=True) + EPS)
        return (h * r * gain[...]).astype(BF), r

    half = hm.shape[1]
    xnh, _ = norm(hh[:, :half], hh[:, half:])
    xn_o[rows:, :] = xnh
    buf[0:HALO, :] = dot_t(xnh, wbc[...])
    rawh_o[...] = buf[0:HALO, :]

    def first(i, carry):
        here = pl.ds(pl.multiple_of(i * Q, Q), Q)
        xn, r = norm(hm[here, :], ho[here, :])
        xn_o[here, :] = xn
        r_o[here, :] = r
        raw = dot_t(xn, wbc[...])
        raw_o[here, :] = raw
        buf[pl.ds(pl.multiple_of(HALO + i * Q, HALO), Q), :] = raw
        steps = dot_t(xn, wdt[...]) + bias[...]
        dt = jax.nn.softplus(steps)
        dt_o[here, :] = dt
        sig_o[here, :] = sigmoid(steps)
        da = dt * rate[...]
        cl_o[here, :] = dot(lower, da, HIGH)
        clt_o[:, here] = lax.dot_general(
            da, lower, (((0,), (1,)), ((), ())), precision=HIGH, preferred_element_type=F32
        )
        return carry

    lax.fori_loop(0, blocks, first, 0)

    def second(i, carry):
        here = pl.ds(pl.multiple_of(i * Q, Q), Q)
        win = buf[pl.ds(pl.multiple_of(i * Q, Q), Q + HALO), :]
        u = jnp.zeros((Q, win.shape[1]), F32)
        for k in range(4):
            u = u + cbc[k : k + 1, :] * win[HALO - 3 + k : HALO - 3 + k + Q, :]
        u_o[here, :] = u
        v = u * sigmoid(u)
        b_o[here, :] = v[:, :state].astype(BF)
        c_o[here, :] = v[:, state:].astype(BF)
        return carry

    lax.fori_loop(0, blocks, second, 0)
    tots = [cl_o[i * Q + Q - 1 : i * Q + Q, :] for i in range(blocks)]
    ctot = functools.reduce(lambda x, y: x + y, tots)
    ctot_o[...] = ctot
    off = jnp.zeros_like(ctot)
    for i in range(blocks):
        here = slice(i * Q, i * Q + Q)
        cl = cl_o[here, :]
        dt = dt_o[here, :]
        tail = jnp.exp(tots[i] - cl)
        dt2_o[here, :] = split2(dt)
        e12_o[here, :] = split2(jnp.exp(cl))
        tl2_o[here, :] = split2(tail)
        dttl2_o[here, :] = split2(dt * tail)
        ec2_o[here, :] = split2(jnp.exp(cl + off))
        edt2_o[here, :] = split2(dt * jnp.exp(ctot - cl - off))
        off = off + tots[i]


def project_kernel(
    xn, wz, wx, cw, dt2, edt2, ex, b, z_o, xr_o, xrh_o, u_o, xs_o, xdt_o, s_o, buf
):
    rows = z_o.shape[0]
    z_o[...] = dot_t(xn[0:rows, :], wz[...])
    xr = dot_t(xn[...], wx[...])
    buf[HALO:, :] = xr[0:rows, :]
    buf[0:HALO, :] = xr[rows:, :]
    xrh_o[...] = xr[rows:, :]
    s_o[...] = jnp.zeros_like(s_o)

    def step(i, carry):
        here = pl.ds(pl.multiple_of(i * Q, Q), Q)
        win = buf[pl.ds(pl.multiple_of(i * Q, Q), Q + HALO), :]
        u = jnp.zeros((Q, win.shape[1]), F32)
        for k in range(4):
            u = u + cw[k : k + 1, :] * win[HALO - 3 + k : HALO - 3 + k + Q, :]
        xr_o[here, :] = win[HALO:, :]
        u_o[here, :] = u
        xs = u * sigmoid(u)
        xs_o[here, :] = xs
        xdt_o[here, :] = (xs * dot(dt2[here, :], ex[...])).astype(BF)
        s_o[...] += t_dot((xs * dot(edt2[here, :], ex[...])).astype(BF), b[here, :])
        return carry

    lax.fori_loop(0, rows // Q, step, 0)


def decay(cl, clt, h, mask):
    return jnp.exp(jnp.where(mask, cl[:, h : h + 1] - clt[h : h + 1, :], NEG))


def lane_masks():
    lane = lax.broadcasted_iota(jnp.int32, (1, Q), 1)
    low = (lane < HEADDIM).astype(F32)
    return low.astype(BF), (1.0 - low).astype(BF)


def inside_kernel(xdt, b, c, cl, clt, y_o):
    mask = tri("ge")
    low, high = lane_masks()
    g = dot_t(c[...], b[...])
    clv, cltv = cl[...], clt[...]
    for p in range(xdt.shape[1] // Q):
        here = slice(p * Q, p * Q + Q)
        ws = [(g * decay(clv, cltv, h, mask)).astype(BF) for h in (2 * p, 2 * p + 1)]
        x = xdt[:, here]
        y_o[:, here] = dot(
            jnp.concatenate(ws, axis=1), jnp.concatenate([x * low, x * high], axis=0)
        )


def carry_kernel(
    y_in, xs, z, dyn, b, c, clt, e12, dttl2, s_in, dsk, gain, ex, ext,
    ys_o, gg_o, sum_o, st_o, s,
):
    @pl.when(pl.program_id(0) == 0)
    def _():
        s[...] = s_in[...]

    et2 = split2(jnp.broadcast_to(jnp.exp(clt[:, Q - 1 : Q]), (clt.shape[0], Q)), axis=0)
    square = jnp.zeros((Q, Q), F32)
    inner = jnp.zeros((Q, Q), F32)
    for p in range(xs.shape[1] // Q):
        here = slice(p * Q, p * Q + Q)
        sb = s[here, :].astype(BF)
        st_o[0, here, :] = sb
        x = xs[:, here]
        e1 = dot(e12[...], ex[:, here])
        y = y_in[:, here] + e1 * dot_t(c[...], sb) + dsk[:, here] * x
        ys_o[:, here] = y
        xt = (x * dot(dttl2[...], ex[:, here])).astype(BF)
        s[here, :] = dot(ext[here, :], et2) * s[here, :] + t_dot(xt, b[...])
        zz = z[:, here]
        gz = y * (zz * sigmoid(zz))
        gg = gz * gain[:, here]
        gg_o[:, here] = gg.astype(BF)
        square = square + gz * gz
        inner = inner + gg * dyn[:, here]
    lane = lax.broadcasted_iota(jnp.int32, (Q, 2), 1)
    sum_o[...] = jnp.where(
        lane == 0,
        jnp.sum(square, axis=1, keepdims=True),
        jnp.sum(inner, axis=1, keepdims=True),
    )


def gate_kernel(
    dyn, ys, z, xs, scal, gain, ec2, ex, c,
    dys_o, dz_o, yn_o, ds_o, gn_o, sk_o,
):
    @pl.when(pl.program_id(0) == 0)
    def _():
        ds_o[...] = jnp.zeros_like(ds_o)
        gn_o[...] = jnp.zeros_like(gn_o)
        sk_o[...] = jnp.zeros_like(sk_o)

    r2 = scal[:, 0:1]
    pull = scal[:, 1:2]
    for p in range(xs.shape[1] // Q):
        here = slice(p * Q, p * Q + Q)
        gn = gain[:, here]
        zz = z[:, here]
        sz = sigmoid(zz)
        silu = zz * sz
        y = ys[:, here]
        gz = y * silu
        dy_n = dyn[:, here]
        gr = gz * r2
        yn_o[:, here] = (gr * gn).astype(BF)
        gn_o[:, here] += jnp.sum(dy_n * gr, axis=0, keepdims=True)
        dgz = r2 * gn * dy_n - gz * pull
        dys = dgz * silu
        dys_o[:, here] = dys
        dz_o[:, here] = (dgz * y * (sz + silu * (1.0 - sz))).astype(BF)
        sk_o[:, here] += jnp.sum(dys * xs[:, here], axis=0, keepdims=True)
        ds_o[here, :] += t_dot((dys * dot(ec2[...], ex[:, here])).astype(BF), c[...])


def inside_back_kernel(xdt, dys, b, c, cl, clt, dx_o, db_o, dc_o, da_o, kt):
    mask = tri("ge")
    low, high = lane_masks()
    g = dot_t(c[...], b[...])
    clv, cltv = cl[...], clt[...]
    heads = clt.shape[0]
    lane = lax.broadcasted_iota(jnp.int32, (Q, heads), 1)
    dg = jnp.zeros((Q, Q), F32)
    rsum = jnp.zeros((Q, heads), F32)
    for p in range(heads // 2):
        here = slice(p * Q, p * Q + Q)
        x = xdt[:, here]
        dy = dys[:, here].astype(BF)
        pp = dot_t(dy, jnp.concatenate([x * low, x * high], axis=0))
        ws = []
        for j in range(2):
            h = 2 * p + j
            ell = decay(clv, cltv, h, mask)
            ws.append((g * ell).astype(BF))
            pe = pp[:, j * Q : j * Q + Q] * ell
            dg = dg + pe
            m = pe * g
            rsum = jnp.where(lane == h, jnp.sum(m, axis=1, keepdims=True), rsum)
            kt[h : h + 1, :] = jnp.sum(m, axis=0, keepdims=True)
        dx_o[:, here] = t_dot(
            jnp.concatenate(ws, axis=0), jnp.concatenate([dy * low, dy * high], axis=0)
        )
    dgb = dg.astype(BF)
    dc_o[...] = dot(dgb, b[...])
    db_o[...] = t_dot(dgb, c[...])
    upper = tri("le").astype(F32)
    da_o[...] = dot(upper, rsum, HIGH) - dot_t(upper, kt[...], HIGH)


def back_kernel(
    dxi, dys, u, xr, xrh, st, b, c, dbi, dci, dai, dt, sig, clt,
    dt2, e12, tl2, ubc, braw, brawh, cw, cbc, rate, dsk, dz, ds_in, ex, er, ext,
    all_o, gcx_o, gcb_o, ga_o, gbias_o, ds, du_next, db_next,
):
    step = pl.program_id(0)
    blocks = pl.num_programs(0)
    rows = all_o.shape[0] - HALO
    channels = dys.shape[1]
    heads = dt.shape[1]
    state = b.shape[1]

    @pl.when(step == 0)
    def _():
        ds[...] = ds_in[...]
        du_next[...] = jnp.zeros_like(du_next)
        db_next[...] = jnp.zeros_like(db_next)
        gcx_o[...] = jnp.zeros_like(gcx_o)
        gcb_o[...] = jnp.zeros_like(gcb_o)
        ga_o[...] = jnp.zeros_like(ga_o)
        gbias_o[...] = jnp.zeros_like(gbias_o)
        all_o[rows:, :] = jnp.zeros((HALO, all_o.shape[1]), BF)

    where = pl.ds(pl.multiple_of((blocks - 1 - step) * Q, Q), Q)
    last = step == blocks - 1
    et2 = split2(jnp.broadcast_to(jnp.exp(clt[:, Q - 1 : Q]), (heads, Q)), axis=0)
    ones = jnp.ones((8, Q), BF)

    def conv_back(d, nxt, taps, raw, rawh, grad_o, first, here):
        win = jnp.concatenate([d, nxt[:, here]], axis=0)
        back = jnp.zeros_like(d)
        sums = []
        for k in range(4):
            part = win[3 - k : 3 - k + Q, :]
            back = back + taps[k : k + 1, here] * part
            sums.append(jnp.sum(raw * part, axis=0, keepdims=True))
        grad_o[:, here] += jnp.concatenate(sums, axis=0)
        all_o[where, first] = back.astype(BF)
        nxt[:, here] = d[0:8, :]

        @pl.when(last)
        def _():
            win_h = jnp.concatenate([jnp.zeros((HALO, d.shape[1]), F32), d[0:8, :]], axis=0)
            back_h = jnp.zeros((HALO, d.shape[1]), F32)
            sums_h = []
            for k in range(4):
                part = win_h[3 - k : 3 - k + HALO, :]
                back_h = back_h + taps[k : k + 1, here] * part
                sums_h.append(jnp.sum(rawh * part, axis=0, keepdims=True))
            grad_o[:, here] += jnp.concatenate(sums_h, axis=0)
            all_o[rows:, first] = back_h.astype(BF)

    rsum = jnp.zeros((Q, heads), F32)
    gsum = jnp.zeros((Q, heads), F32)
    ddt = jnp.zeros((Q, heads), F32)
    vrow = jnp.zeros((8, heads), F32)
    dbs = dbi[...]
    dcs = dci[...]
    for p in range(channels // Q):
        here = slice(p * Q, p * Q + Q)
        ehere = er[here, :]
        sb = st[0, here, :]
        dsv = ds[here, :]
        dsb = dsv.astype(BF)
        dy = dys[:, here]
        dye = dy * dot(e12[...], ex[:, here])
        dyb = dye.astype(BF)
        rsum = rsum + dot_split(dye * dot_t(c[...], sb), ehere)
        dcs = dcs + dot(dyb, sb)
        bds = dot_t(b[...], dsb)
        tail = dot(tl2[...], ex[:, here])
        dtx = dot(dt2[...], ex[:, here])
        uu = u[:, here]
        su = sigmoid(uu)
        xs = uu * su
        xt = xs * dtx * tail
        gsum = gsum + dot_split(xt * bds, ehere)
        dbs = dbs + dot(xt.astype(BF), dsb)
        dxdt = dxi[:, here] + tail * bds
        ddt = ddt + dot_split(dxdt * xs, ehere)
        etr = dot(ext[here, :], et2)
        eds = etr * dsv
        vrow = vrow + dot_split(split_dot_t(ones, eds * sb.astype(F32)), ehere)
        ds[here, :] = eds + t_dot(dyb, c[...])
        du = (dxdt * dtx + dsk[:, here] * dy) * (su + xs * (1.0 - su))
        first = slice(channels + p * Q, channels + p * Q + Q)
        conv_back(du, du_next, cw, xr[:, here], xrh[:, here], gcx_o, first, here)
    all_o[where, 0:channels] = dz[...]
    da = (
        dai[...]
        + split_dot(tri("le").astype(BF), rsum)
        + split_dot(tri("gt").astype(BF), gsum)
        + vrow[0:1, :]
    )
    draw = (rate[...] * da + ddt) * sig[...]
    all_o[where, 2 * channels + 2 * state :] = draw.astype(BF)
    ga_o[...] += jnp.sum(da * dt[...], axis=0, keepdims=True)
    gbias_o[...] += jnp.sum(draw, axis=0, keepdims=True)
    for j, d in enumerate((dbs, dcs)):
        here = slice(j * state, j * state + state)
        v = ubc[:, here]
        sv = sigmoid(v)
        first = slice(2 * channels + j * state, 2 * channels + j * state + state)
        conv_back(
            d * (sv + v * sv * (1.0 - sv)), db_next, cbc, braw[:, here], brawh[:, here],
            gcb_o, first, here,
        )


def split_dot_t(m, v):
    hi = v.astype(BF)
    lo = (v - hi.astype(F32)).astype(BF)
    return dot_t(m, hi) + dot_t(m, lo)


def shape(dims, dtype=F32):
    return jax.ShapeDtypeStruct(dims, dtype)


def whole(array):
    rank = len(array.shape)
    return pl.BlockSpec(array.shape, lambda *_: (0,) * rank)


def params():
    return pltpu.CompilerParams(vmem_limit_bytes=VMEM)


def sequence_device(
    hidden, lengths, cotangent, norm_gain, in_zx, in_bcdt, conv_x, conv_bc,
    dt_bias, a_log, d_skip, gnorm_gain, out_w,
):
    rows, half = hidden.shape
    own_heads = in_zx.shape[1]
    nz = lax.axis_size("head")
    ndp = lax.axis_size("dp")
    zi = lax.axis_index("head")
    di = lax.axis_index("dp")
    wi = lax.axis_index("width")
    per = ndp
    heads = nz * per
    channels = heads * HEADDIM
    model = 2 * half
    blocks = rows // Q
    all_columns = 2 * channels + 2 * STATE + heads

    def swap(v):
        return lax.ppermute(v, "width", [(0, 1), (1, 0)])

    def turn(v, s):
        return lax.ppermute(v, "head", [(i, (i + s) % nz) for i in range(nz)])

    def shift(v, s):
        return lax.ppermute(v, "head", [(i, i + s) for i in range(nz) if 0 <= i + s < nz])

    def cross(v, m):
        return lax.ppermute(v, "dp", [(i, i ^ m) for i in range(ndp)])

    def pick(v, index):
        return lax.dynamic_index_in_dim(v, index, 0, keepdims=False)

    zx_t = jnp.transpose(in_zx, (1, 2, 0))
    out_h = out_w.reshape(own_heads, HEADDIM, half)

    def own_group(v):
        mine = jnp.stack([pick(v, per * wi + (di ^ m)) for m in range(per)])
        other = jnp.stack([pick(v, per * (1 - wi) + (di ^ m)) for m in range(per)])
        return jnp.concatenate([mine, swap(other)], axis=2)

    def gather(own):
        slots = [own[m] for m in range(per)]
        for s in range(1, nz):
            got = turn(own[0], s)
            slots += [got] + [cross(got, m) for m in range(1, per)]
        return slots

    hidden_o = swap(hidden)
    zx_slots = gather(own_group(zx_t))
    wz = jnp.concatenate([v[:HEADDIM] for v in zx_slots], axis=0)
    wx = jnp.concatenate([v[HEADDIM:] for v in zx_slots], axis=0)
    wout = jnp.concatenate(gather(own_group(out_h)), axis=0)
    bcdt_t = jnp.transpose(in_bcdt)
    bcdt_t = jnp.concatenate([bcdt_t, swap(bcdt_t)], axis=1)
    wbc = bcdt_t[: 2 * STATE]
    slot = jnp.arange(heads)
    slot_head = ((zi - slot // per) % nz) * own_heads + wi * per + ((slot % per) ^ di)
    pick_heads = (slot_head[:, None] == jnp.arange(HEADS)[None, :]).astype(F32)
    wdt = jnp.dot(
        pick_heads.astype(BF), bcdt_t[2 * STATE :], preferred_element_type=F32
    ).astype(BF)

    table = jnp.concatenate(
        [
            dt_bias[:, None],
            a_log[:, None],
            d_skip[:, None],
            jnp.transpose(conv_x.astype(F32).reshape(4, own_heads, HEADDIM), (1, 0, 2)).reshape(
                own_heads, 4 * HEADDIM
            ),
            gnorm_gain.astype(F32).reshape(own_heads, HEADDIM),
        ],
        axis=1,
    )
    table = jnp.stack([pick(table, per * wi + (di ^ m)) for m in range(per)])
    table = jnp.concatenate([table] + [turn(table, s) for s in range(1, nz)], axis=0)
    bias = table[:, 0][None]
    rate = -jnp.exp(table[:, 1])[None]
    skip = jnp.repeat(table[:, 2], HEADDIM)[None]
    taps = jnp.transpose(
        table[:, 3 : 3 + 4 * HEADDIM].reshape(heads, 4, HEADDIM), (1, 0, 2)
    ).reshape(4, channels)
    gain_out = table[:, 3 + 4 * HEADDIM :].reshape(1, channels)
    taps_bc = conv_bc.astype(F32)
    gain_in = jnp.concatenate([norm_gain, swap(norm_gain)])[None].astype(F32)

    onehot = np.kron(np.eye(heads), np.ones((1, HEADDIM)))
    ex = jnp.asarray(np.concatenate([onehot, onehot], axis=0), BF)
    er = jnp.asarray(onehot.T, BF)
    ext = jnp.asarray(np.concatenate([onehot.T, onehot.T], axis=1), BF)

    cot_o = swap(cotangent)
    edge = jnp.concatenate([hidden[rows - HALO :], hidden_o[rows - HALO :]], axis=1)
    edge = shift(edge, 1)
    ext_rows = rows + HALO
    narrow = shape((rows, 2 * heads), BF)
    (
        xn, r, braw, brawh, ubc, bs, cs, dt, sig, cl, clt, ctot,
        dt2, e12, tl2, dttl2, ec2, edt2,
    ) = pl.pallas_call(
        entry_kernel,
        out_shape=[
            shape((ext_rows, model), BF), shape((rows, 1)), shape((rows, 2 * STATE)),
            shape((HALO, 2 * STATE)), shape((rows, 2 * STATE)), shape((rows, STATE), BF),
            shape((rows, STATE), BF), shape((rows, heads)), shape((rows, heads)),
            shape((rows, heads)), shape((heads, rows)), shape((1, heads)),
            narrow, narrow, narrow, narrow, narrow, narrow,
        ],
        scratch_shapes=[pltpu.VMEM((ext_rows, 2 * STATE), F32)],
        compiler_params=params(),
        name="entry",
    )(hidden, hidden_o, edge, gain_in, wbc, wdt, taps_bc, bias, rate)

    def realign(v, k, group):
        return jnp.roll(v, k * group, axis=0)

    totals = ctot.reshape(heads, 1)
    after = {k: realign(shift(totals, -k), -k, per) for k in range(1, nz - 1)}
    before = {k: realign(shift(totals, k), k, per) for k in range(1, nz - 1)}

    def pass_on(local, sign, between):
        total = jnp.zeros_like(local)
        for k in range(1, nz):
            faded = jnp.zeros_like(totals)
            for j in range(1, k):
                faded = faded + between[j]
            scale = jnp.repeat(jnp.exp(faded), HEADDIM, axis=0)
            got = shift((local * scale).astype(BF), sign * k)
            total = total + realign(got, sign * k, per * HEADDIM).astype(F32)
        return total

    full = shape((rows, channels))
    pair = lambda p: (0, p)
    z, xr, xrh, u, xs, xdt, s_local = pl.pallas_call(
        project_kernel,
        grid=(channels // Q,),
        in_specs=[
            whole(xn), pl.BlockSpec((Q, model), lambda p: (p, 0)),
            pl.BlockSpec((Q, model), lambda p: (p, 0)), pl.BlockSpec((4, Q), pair), whole(dt2),
            whole(edt2), pl.BlockSpec((2 * heads, Q), pair), whole(bs),
        ],
        out_specs=[
            pl.BlockSpec((rows, Q), pair), pl.BlockSpec((rows, Q), pair),
            pl.BlockSpec((HALO, Q), pair), pl.BlockSpec((rows, Q), pair),
            pl.BlockSpec((rows, Q), pair), pl.BlockSpec((rows, Q), pair),
            pl.BlockSpec((Q, STATE), lambda p: (p, 0)),
        ],
        out_shape=[
            full, full, shape((HALO, channels)), full, full, shape((rows, channels), BF),
            shape((channels, STATE)),
        ],
        scratch_shapes=[pltpu.VMEM((ext_rows, Q), F32)],
        compiler_params=params(),
        name="project",
    )(xn, wz, wx, taps, dt2, edt2, ex, bs)
    state_in = pass_on(s_local, 1, after)

    tokens = lambda i: (i, 0)
    wide = pl.BlockSpec((Q, channels), tokens)
    bspec = pl.BlockSpec((Q, STATE), tokens)
    hspec = pl.BlockSpec((Q, heads), tokens)
    h2spec = pl.BlockSpec((Q, 2 * heads), tokens)
    tspec = pl.BlockSpec((heads, Q), lambda i: (0, i))
    y_in = pl.pallas_call(
        inside_kernel,
        grid=(blocks,),
        in_specs=[wide, bspec, bspec, hspec, tspec],
        out_specs=wide,
        out_shape=full,
        compiler_params=params(),
        name="inside",
    )(xdt, bs, cs, cl, clt)

    position = zi * rows + jnp.arange(rows, dtype=jnp.int32)
    keeper = (position < lengths[0])[:, None]
    grads = jnp.concatenate([cotangent, cot_o], axis=1)
    masked = jnp.where(keeper, grads, jnp.zeros_like(grads))
    dyn = dot_t(masked, wout)
    ys, gg, sums, states = pl.pallas_call(
        carry_kernel,
        grid=(blocks,),
        in_specs=[
            wide, wide, wide, wide, bspec, bspec, tspec, h2spec, h2spec, whole(state_in),
            whole(skip), whole(gain_out), whole(ex), whole(ext),
        ],
        out_specs=[
            wide, wide, pl.BlockSpec((Q, 2), tokens),
            pl.BlockSpec((1, channels, STATE), lambda i: (i, 0, 0)),
        ],
        out_shape=[
            full, shape((rows, channels), BF), shape((rows, 2)),
            shape((blocks, channels, STATE), BF),
        ],
        scratch_shapes=[pltpu.VMEM((channels, STATE), F32)],
        compiler_params=params(),
        name="carry",
    )(y_in, xs, z, dyn, bs, cs, clt, e12, dttl2, state_in, skip, gain_out, ex, ext)
    sums = sums + swap(sums)
    branch = dot(gg, wout)
    branch_o = swap(branch[:, half:].astype(BF))
    r2 = lax.rsqrt(sums[:, 0:1] / (2 * channels) + EPS)
    pull = sums[:, 1:2] * (r2 * r2 * r2) / (2 * channels)
    out_hidden = (
        hidden.astype(F32)
        + jnp.where(keeper, (branch[:, :half] + branch_o.astype(F32)) * r2, 0.0)
    ).astype(BF)

    acc = lambda i: (0, 0)
    dys, dz, yn, ds_local, g_gain, g_skip = pl.pallas_call(
        gate_kernel,
        grid=(blocks,),
        in_specs=[
            wide, wide, wide, wide, pl.BlockSpec((Q, 2), tokens), whole(gain_out), h2spec,
            whole(ex), bspec,
        ],
        out_specs=[
            wide, wide, wide, pl.BlockSpec((channels, STATE), acc),
            pl.BlockSpec((1, channels), acc), pl.BlockSpec((1, channels), acc),
        ],
        out_shape=[
            full, shape((rows, channels), BF), shape((rows, channels), BF),
            shape((channels, STATE)), shape((1, channels)), shape((1, channels)),
        ],
        compiler_params=params(),
        name="gate",
    )(dyn, ys, z, xs, jnp.concatenate([r2, pull], axis=1), gain_out, ec2, ex, cs)
    ds_in = pass_on(ds_local, -1, before)

    def reduce_slots(v):
        mine = v[:, 0].astype(F32)
        for m in range(1, per):
            mine = mine + cross(v[:, m], m).astype(F32)
        low = mine.astype(BF)
        total = mine[0]
        for s in range(1, nz):
            total = total + turn(low[s], -s).astype(F32)
        total = total.astype(BF)
        return jnp.stack([total] + [cross(total, m) for m in range(1, per)])

    def to_owner(v):
        v = jnp.stack([pick(v, di ^ m) for m in range(per)])
        mine, other = v[:, :, :half], swap(v[:, :, half:])
        low_w = jnp.where(wi == 0, mine, other)
        high_w = jnp.where(wi == 0, other, mine)
        return jnp.concatenate([low_w, high_w], axis=0)

    g_out = t_dot(yn, masked).astype(BF).reshape(nz, per, HEADDIM, model)
    g_out = to_owner(reduce_slots(g_out))

    dxi, dbi, dci, dai = pl.pallas_call(
        inside_back_kernel,
        grid=(blocks,),
        in_specs=[wide, wide, bspec, bspec, hspec, tspec],
        out_specs=[wide, bspec, bspec, hspec],
        out_shape=[full, shape((rows, STATE)), shape((rows, STATE)), shape((rows, heads))],
        scratch_shapes=[pltpu.VMEM((heads, Q), F32)],
        compiler_params=params(),
        name="inside_back",
    )(xdt, dys, bs, cs, cl, clt)
    rev = lambda i: (blocks - 1 - i, 0)
    rwide = pl.BlockSpec((Q, channels), rev)
    rb = pl.BlockSpec((Q, STATE), rev)
    rh = pl.BlockSpec((Q, heads), rev)
    rh2 = pl.BlockSpec((Q, 2 * heads), rev)
    rbc = pl.BlockSpec((Q, 2 * STATE), rev)
    everything, g_taps, g_taps_bc, g_rate, g_bias = pl.pallas_call(
        back_kernel,
        grid=(blocks,),
        in_specs=[
            rwide, rwide, rwide, rwide, whole(xrh),
            pl.BlockSpec((1, channels, STATE), lambda i: (blocks - 1 - i, 0, 0)),
            rb, rb, rb, rb, rh, rh, rh, pl.BlockSpec((heads, Q), lambda i: (0, blocks - 1 - i)),
            rh2, rh2, rh2, rbc, rbc, whole(brawh), whole(taps), whole(taps_bc), whole(rate),
            whole(skip), rwide, whole(ds_in), whole(ex), whole(er), whole(ext),
        ],
        out_specs=[
            pl.BlockSpec((ext_rows, all_columns), acc), pl.BlockSpec((4, channels), acc),
            pl.BlockSpec((4, 2 * STATE), acc), pl.BlockSpec((1, heads), acc),
            pl.BlockSpec((1, heads), acc),
        ],
        out_shape=[
            shape((ext_rows, all_columns), BF), shape((4, channels)), shape((4, 2 * STATE)),
            shape((1, heads)), shape((1, heads)),
        ],
        scratch_shapes=[
            pltpu.VMEM((channels, STATE), F32), pltpu.VMEM((8, channels), F32),
            pltpu.VMEM((8, 2 * STATE), F32),
        ],
        compiler_params=params(),
        name="back",
    )(
        dxi, dys, u, xr, xrh, states, bs, cs, dbi, dci, dai, dt, sig, clt, dt2, e12, tl2, ubc,
        braw, brawh, taps, taps_bc, rate, skip, dz, ds_in, ex, er, ext,
    )

    grad_all = t_dot(everything, xn)
    g_z = grad_all[:channels].astype(BF).reshape(nz, per, HEADDIM, model)
    g_x = grad_all[channels : 2 * channels].astype(BF).reshape(nz, per, HEADDIM, model)
    g_zx = to_owner(reduce_slots(jnp.concatenate([g_z, g_x], axis=2)))
    g_bcdt = jnp.concatenate(
        [
            grad_all[2 * channels : 2 * channels + 2 * STATE],
            jnp.dot(pick_heads.T, grad_all[2 * channels + 2 * STATE :], precision=HIGH),
        ],
        axis=0,
    )
    g_bcdt = g_bcdt[:, :half] + swap(g_bcdt[:, half:].astype(BF)).astype(F32)
    quarter = g_bcdt.reshape(per, -1, half)
    share = pick(quarter, di)
    for m in range(1, per):
        share = share + cross(pick(quarter, di ^ m).astype(BF), m).astype(F32)
    low_share = share.astype(BF)
    for s in range(1, nz):
        share = share + turn(low_share, s).astype(F32)
    share = share.astype(BF)
    parts = jnp.stack([share] + [cross(share, m) for m in range(1, per)])
    parts = jnp.stack([pick(parts, di ^ m) for m in range(per)])
    grad_in_bcdt = jnp.transpose(parts.reshape(-1, half).astype(F32))

    weights_all = jnp.concatenate([wz, wx, wbc, wdt], axis=0)
    dxn = dot(everything, weights_all)
    dxn = dxn[:, :half] + swap(dxn[:, half:].astype(BF)).astype(F32)
    late = shift(dxn[rows:], -1)
    dxn = jnp.concatenate([dxn[: rows - HALO], dxn[rows - HALO : rows] + late], axis=0)
    source = hidden.astype(F32)
    gain_half = gain_in[:, :half]
    across = jnp.sum(dxn * gain_half * source, axis=1, keepdims=True)
    across = across + swap(across)
    grad_hidden = (
        cotangent.astype(F32)
        + r * gain_half * dxn
        - source * (r * r * r) / model * across
    ).astype(BF)
    g_norm = jnp.sum(dxn * source * r, axis=0)

    table = jnp.concatenate(
        [
            g_bias.reshape(heads, 1),
            (g_rate * rate).reshape(heads, 1),
            jnp.sum(g_skip.reshape(heads, HEADDIM), axis=1, keepdims=True),
            jnp.transpose(g_taps.reshape(4, heads, HEADDIM), (1, 0, 2)).reshape(heads, 4 * HEADDIM),
            g_gain.reshape(heads, HEADDIM),
        ],
        axis=1,
    )
    table = jnp.dot(pick_heads.T, table, precision=HIGH)
    side = (jnp.arange(2) == wi).astype(F32)[:, None] * g_norm[None]
    small = jnp.concatenate([table.reshape(-1), g_taps_bc.reshape(-1), side.reshape(-1)])
    small = lax.psum(small, ("dp", "head", "width"))
    size = table.size
    table = lax.dynamic_slice_in_dim(
        small[:size].reshape(HEADS, -1), zi * own_heads, own_heads, 0
    )
    g_taps_bc = small[size : size + 8 * STATE].reshape(4, 2 * STATE)
    g_norm = pick(small[size + 8 * STATE :].reshape(2, half), wi)
    return (
        out_hidden,
        grad_hidden,
        g_norm,
        jnp.transpose(g_zx, (2, 0, 1)).astype(F32),
        grad_in_bcdt,
        jnp.transpose(
            table[:, 3 : 3 + 4 * HEADDIM].reshape(own_heads, 4, HEADDIM), (1, 0, 2)
        ).reshape(4, own_heads * HEADDIM),
        g_taps_bc,
        table[:, 0],
        table[:, 1],
        table[:, 2],
        table[:, 3 + 4 * HEADDIM :].reshape(-1),
        g_out.reshape(own_heads * HEADDIM, half).astype(F32),
    )


def fits(mesh):
    ndp, nz, nw = mesh.shape["dp"], mesh.shape["head"], mesh.shape["width"]
    return (
        nw == 2
        and ndp in (2, 4, 8)
        and HEADS == nz * nw * ndp
        and LEN % (nz * Q) == 0
        and SEQS == ndp
        and HEADS // nw * HEADDIM % Q == 0
    )


def solution(mesh):
    placed = (
        P(("dp", "head"), "width"),
        P("dp"),
        P(("dp", "head"), "width"),
        P("width"),
        P("width", "head", None),
        P("width", None),
        P(None, "head"),
        P(),
        P("head"),
        P("head"),
        P("head"),
        P("head"),
        P("head", "width"),
    )
    return jax.shard_map(
        sequence_device if fits(mesh) else per_device,
        mesh=mesh,
        in_specs=placed,
        out_specs=(
            P(("dp", "head"), "width"),
            P(("dp", "head"), "width"),
            P("width"),
            P("width", "head", None),
            P("width", None),
            P(None, "head"),
            P(),
            P("head"),
            P("head"),
            P("head"),
            P("head"),
            P("head", "width"),
        ),
        check_vma=False,
    )
```

```python
import functools

import jax
import jax.numpy as jnp
import numpy as np
from jax import lax
from jax.experimental import pallas as pl
from jax.experimental.pallas import tpu as pltpu
from jax.sharding import PartitionSpec as P

D = 1024
HEADS = 32
HEADDIM = 64
STATE = 128
SCAN_BLOCK = 256
LEN = 4096
INNER = 2048
SEQS = 4


EPS = 1e-05
HIGH = lax.Precision.HIGHEST


def conv_causal(values, kernel):
    taps = kernel.shape[0]
    padded = jnp.pad(values, ((taps - 1, 0), (0, 0)))
    total = jnp.zeros_like(values)
    for offset in range(taps):
        total = total + kernel[offset] * padded[offset : offset + values.shape[0]]
    return total


def block_scan(inputs, steps, rates, bmat, cmat, block):
    length, heads, hsize = inputs.shape
    count = length // block
    in_blocks = inputs.reshape(count, block, heads, hsize)
    step_blocks = steps.reshape(count, block, heads)
    b_blocks = bmat.reshape(count, block, bmat.shape[1])
    c_blocks = cmat.reshape(count, block, cmat.shape[1])
    places = jnp.arange(block)
    lower = (places[:, None] >= places[None, :])[:, :, None]

    def advance(state, pieces):
        x_part, dt_part, b_part, c_part = pieces
        cums = jnp.cumsum(dt_part * rates, axis=0)
        spread = cums[:, None, :] - cums[None, :, :]
        decay = jnp.where(lower, jnp.exp(jnp.where(lower, spread, 0.0)), 0.0)
        scores = jnp.dot(c_part, b_part.T, precision=HIGH)
        weights = scores[:, :, None] * decay * dt_part[None, :, :]
        inside = jnp.einsum("ijh,jhp->ihp", weights, x_part, precision=HIGH)
        carried = (
            jnp.einsum("in,hpn->ihp", c_part, state, precision=HIGH) * jnp.exp(cums)[:, :, None]
        )
        tails = jnp.exp(cums[-1][None, :] - cums) * dt_part
        state = jnp.exp(cums[-1])[:, None, None] * state + jnp.einsum(
            "jh,jhp,jn->hpn", tails, x_part, b_part, precision=HIGH
        )
        return (state, inside + carried)

    start_state = jnp.zeros((heads, hsize, bmat.shape[1]), jnp.float32)
    _, result = lax.scan(
        jax.checkpoint(advance), start_state, (in_blocks, step_blocks, b_blocks, c_blocks)
    )
    return result.reshape(length, heads, hsize)


def mixer(zx, bc_raw, dt_raw, kernel_x, kernel_bc, bias_dt, log_rate, skip):
    length, heads, double = zx.shape
    hsize = double // 2
    gate = zx[:, :, :hsize]
    x_raw = zx[:, :, hsize:].reshape(length, heads * hsize)
    xs_conv = jax.nn.silu(conv_causal(x_raw, kernel_x)).reshape(length, heads, hsize)
    bc_conv = jax.nn.silu(conv_causal(bc_raw, kernel_bc))
    half = bc_conv.shape[1] // 2
    steps = jax.nn.softplus(dt_raw + bias_dt)
    rates = -jnp.exp(log_rate)
    result = (
        block_scan(xs_conv, steps, rates, bc_conv[:, :half], bc_conv[:, half:], SCAN_BLOCK)
        + skip[:, None] * xs_conv
    )
    return (result * jax.nn.silu(gate)).reshape(length, heads * hsize)


def per_device(
    hidden,
    lengths,
    cotangent,
    norm_gain,
    in_zx,
    in_bcdt,
    conv_x,
    conv_bc,
    dt_bias,
    a_log,
    d_skip,
    gnorm_gain,
    out_w,
):
    slice_rows, half_width = hidden.shape
    local_heads = in_zx.shape[1]
    head_count = lax.axis_size("head")
    head_index = lax.axis_index("head")
    total_rows = slice_rows * head_count
    seq_local = lengths.shape[0]
    inner_local = local_heads * HEADDIM
    row_ids = head_index * slice_rows + jnp.arange(slice_rows, dtype=jnp.int32)
    owner = (row_ids // LEN)[:, None] == jnp.arange(seq_local, dtype=jnp.int32)[None, :]
    limits = jnp.sum(jnp.where(owner, lengths[None, :], 0), axis=1)
    keeper = (row_ids % LEN < limits).astype(jnp.float32)[:, None]
    source = hidden.astype(jnp.float32)
    squares = lax.psum(jnp.sum(source * source, axis=1), "width")
    scale = lax.rsqrt(squares / D + EPS)[:, None]
    gain_in = norm_gain.astype(jnp.float32)
    normed = (source * scale * gain_in).astype(jnp.bfloat16)
    gathered = lax.all_gather(normed, "head", axis=0, tiled=True)
    w_zx = in_zx.reshape(half_width, local_heads * 2 * HEADDIM)
    zx_part = jnp.dot(gathered, w_zx, preferred_element_type=jnp.float32)
    bcdt_part = jnp.dot(gathered, in_bcdt, preferred_element_type=jnp.float32)
    zx_full, bcdt_full = lax.psum((zx_part, bcdt_part), "width")
    zx_seq = zx_full.reshape(seq_local, LEN, local_heads, 2 * HEADDIM)
    bc_seq = bcdt_full[:, : 2 * STATE].reshape(seq_local, LEN, 2 * STATE)
    dt_seq = lax.dynamic_slice_in_dim(
        bcdt_full, 2 * STATE + head_index * local_heads, local_heads, 1
    ).reshape(seq_local, LEN, local_heads)

    def local_mix(zx_in, bc_in, dt_in, kernel_x, kernel_bc, bias_in, log_in, skip_in):
        per_sequence = jax.vmap(mixer, in_axes=(0, 0, 0, None, None, None, None, None))
        return per_sequence(
            zx_in, bc_in, dt_in, kernel_x, kernel_bc, bias_in, log_in, skip_in
        ).reshape(total_rows, inner_local)

    gated, mix_pull = jax.vjp(
        local_mix,
        zx_seq,
        bc_seq,
        dt_seq,
        conv_x.astype(jnp.float32),
        conv_bc.astype(jnp.float32),
        dt_bias,
        a_log,
        d_skip,
    )
    total_sq = lax.psum(jnp.sum(gated * gated, axis=1), "head")
    scale_out = lax.rsqrt(total_sq / INNER + EPS)[:, None]
    gain_out = gnorm_gain.astype(jnp.float32)
    mixed = (gated * scale_out * gain_out).astype(jnp.bfloat16)
    picked = mixed
    branch = lax.psum_scatter(
        jnp.dot(picked, out_w, preferred_element_type=jnp.float32),
        "head",
        scatter_dimension=0,
        tiled=True,
    )
    out_hidden = (source + keeper * branch).astype(jnp.bfloat16)
    grad_out = cotangent.astype(jnp.float32)
    masked = (grad_out * keeper).astype(jnp.bfloat16)
    piece = lax.all_gather(masked, "head", axis=0, tiled=True)
    picked = mixed
    acc_weight = jnp.einsum("tc,td->cd", picked, piece, preferred_element_type=jnp.float32)
    product = jnp.einsum("td,cd->tc", piece, out_w, preferred_element_type=jnp.float32)
    grad_mixed = lax.psum(product, "width")
    gain_out_grad = jnp.sum(grad_mixed * gated * scale_out, axis=0)
    inner_total = lax.psum(jnp.sum(grad_mixed * gain_out * gated, axis=1), "head")
    cubed = scale_out * scale_out * scale_out
    grad_gated = scale_out * gain_out * grad_mixed - gated * cubed / INNER * inner_total[:, None]
    (
        grad_zx_seq,
        grad_bc_seq,
        grad_dt_seq,
        kernel_x_grad,
        kernel_bc_grad,
        bias_grad,
        rate_grad,
        skip_grad,
    ) = mix_pull(grad_gated)
    grad_zx = grad_zx_seq.reshape(total_rows, local_heads * 2 * HEADDIM).astype(jnp.bfloat16)
    dt_columns = jnp.zeros((total_rows, HEADS), jnp.float32)
    dt_columns = lax.dynamic_update_slice_in_dim(
        dt_columns, grad_dt_seq.reshape(total_rows, local_heads), head_index * local_heads, 1
    )
    grad_bcdt_head = jnp.concatenate(
        [grad_bc_seq.reshape(total_rows, 2 * STATE), dt_columns], axis=1
    )
    weight_zx = jnp.einsum(
        "td,tc->dc", gathered, grad_zx, preferred_element_type=jnp.float32
    ).reshape(half_width, local_heads, 2 * HEADDIM)
    normed_part = jnp.einsum("tc,dc->td", grad_zx, w_zx, preferred_element_type=jnp.float32)
    grad_normed, bcdt_summed = (
        lax.psum_scatter(normed_part, "head", scatter_dimension=0, tiled=True),
        lax.psum_scatter(grad_bcdt_head, "head", scatter_dimension=0, tiled=True),
    )
    bcdt_low = bcdt_summed.astype(jnp.bfloat16)
    grad_normed = grad_normed + jnp.einsum(
        "tk,dk->td", bcdt_low, in_bcdt, preferred_element_type=jnp.float32
    )
    weight_bcdt = jnp.einsum("td,tk->dk", normed, bcdt_low, preferred_element_type=jnp.float32)
    gain_in_grad = jnp.sum(grad_normed * source * scale, axis=0)
    across = lax.psum(jnp.sum(grad_normed * gain_in * source, axis=1), "width")
    scale_cubed = scale * scale * scale
    grad_hidden = (
        grad_out + scale * gain_in * grad_normed - source * scale_cubed / D * across[:, None]
    ).astype(jnp.bfloat16)
    summed_dp = lax.psum(
        (weight_zx, acc_weight, kernel_x_grad, bias_grad, rate_grad, skip_grad, gain_out_grad), "dp"
    )
    summed_all = lax.psum((weight_bcdt, gain_in_grad, kernel_bc_grad), ("dp", "head"))
    return (
        out_hidden,
        grad_hidden,
        summed_all[1],
        summed_dp[0],
        summed_all[0],
        summed_dp[2],
        summed_all[2],
        summed_dp[3],
        summed_dp[4],
        summed_dp[5],
        summed_dp[6],
        summed_dp[1],
    )


BF = jnp.bfloat16
F32 = jnp.float32
Q = 128
HALO = 16
NEG = -1e30
VMEM = 60 * 1024 * 1024


def dot(a, b, prec=None):
    return lax.dot_general(a, b, (((1,), (0,)), ((), ())), precision=prec, preferred_element_type=F32)


def dot_t(a, b, prec=None):
    return lax.dot_general(a, b, (((1,), (1,)), ((), ())), precision=prec, preferred_element_type=F32)


def t_dot(a, b, prec=None):
    return lax.dot_general(a, b, (((0,), (0,)), ((), ())), precision=prec, preferred_element_type=F32)


def split2(v, axis=1):
    hi = v.astype(BF)
    lo = (v - hi.astype(F32)).astype(BF)
    return jnp.concatenate([hi, lo], axis=axis)


def dot_split(v, m):
    hi = v.astype(BF)
    lo = (v - hi.astype(F32)).astype(BF)
    return dot(hi, m) + dot(lo, m)


def split_dot(m, v):
    hi = v.astype(BF)
    lo = (v - hi.astype(F32)).astype(BF)
    return dot(m, hi) + dot(m, lo)


def sigmoid(v):
    return 1.0 / (1.0 + jnp.exp(-v))


def tri(kind):
    row = lax.broadcasted_iota(jnp.int32, (Q, Q), 0)
    col = lax.broadcasted_iota(jnp.int32, (Q, Q), 1)
    return {"ge": row >= col, "le": row <= col, "gt": row > col}[kind]


def entry_kernel(
    hm, ho, hh, gain, wbc, wdt, cbc, bias, rate,
    xn_o, xnh_o, r_o, raw_o, rawh_o, u_o, b_o, c_o, dt_o, sig_o, cl_o, clt_o, tot_o,
    dt2_o, e12_o, tl2_o, dttl2_o, ec2_o, edt2_o, buf,
):
    rows = hm.shape[0]
    state = b_o.shape[1]
    blocks = rows // Q
    lower = tri("ge").astype(F32)

    def norm(left, right):
        h = jnp.concatenate([left, right], axis=1).astype(F32)
        r = lax.rsqrt(jnp.mean(h * h, axis=1, keepdims=True) + EPS)
        return (h * r * gain[...]).astype(BF), r

    half = hm.shape[1]
    xnh, _ = norm(hh[:, :half], hh[:, half:])
    xnh_o[...] = xnh
    buf[0:HALO, :] = dot_t(xnh, wbc[...])
    rawh_o[...] = buf[0:HALO, :]

    def first(i, carry):
        here = pl.ds(pl.multiple_of(i * Q, Q), Q)
        xn, r = norm(hm[here, :], ho[here, :])
        xn_o[here, :] = xn
        r_o[here, :] = r
        raw = dot_t(xn, wbc[...])
        raw_o[here, :] = raw
        buf[pl.ds(pl.multiple_of(HALO + i * Q, HALO), Q), :] = raw
        steps = dot_t(xn, wdt[...]) + bias[...]
        dt = jax.nn.softplus(steps)
        dt_o[here, :] = dt
        sig_o[here, :] = sigmoid(steps)
        da = dt * rate[...]
        cl_o[here, :] = dot(lower, da, HIGH)
        clt_o[:, here] = lax.dot_general(
            da, lower, (((0,), (1,)), ((), ())), precision=HIGH, preferred_element_type=F32
        )
        return carry

    lax.fori_loop(0, blocks, first, 0, unroll=2)

    def second(i, carry):
        here = pl.ds(pl.multiple_of(i * Q, Q), Q)
        win = buf[pl.ds(pl.multiple_of(i * Q, Q), Q + HALO), :]
        u = jnp.zeros((Q, win.shape[1]), F32)
        for k in range(4):
            u = u + cbc[k : k + 1, :] * win[HALO - 3 + k : HALO - 3 + k + Q, :]
        u_o[here, :] = u
        v = u * sigmoid(u)
        b_o[here, :] = v[:, :state].astype(BF)
        c_o[here, :] = v[:, state:].astype(BF)
        return carry

    lax.fori_loop(0, blocks, second, 0, unroll=2)
    tots = [cl_o[i * Q + Q - 1 : i * Q + Q, :] for i in range(blocks)]
    ctot = functools.reduce(lambda x, y: x + y, tots)
    heads = clt_o.shape[0]
    column = functools.reduce(
        lambda x, y: x + y, [clt_o[:, i * Q + Q - 1 : i * Q + Q] for i in range(blocks)]
    )
    hi = column.astype(BF)
    mid = (column - hi.astype(F32)).astype(BF)
    low = (column - hi.astype(F32) - mid.astype(F32)).astype(BF)
    lane = lax.broadcasted_iota(jnp.int32, (heads, tot_o.shape[1]), 1)
    tot_o[...] = jnp.where(
        lane == 0,
        hi.astype(F32),
        jnp.where(lane == 1, mid.astype(F32), jnp.where(lane == 2, low.astype(F32), 0.0)),
    ).astype(BF)
    off = jnp.zeros_like(ctot)
    for i in range(blocks):
        here = slice(i * Q, i * Q + Q)
        cl = cl_o[here, :]
        dt = dt_o[here, :]
        tail = jnp.exp(tots[i] - cl)
        dt2_o[here, :] = split2(dt)
        e12_o[here, :] = split2(jnp.exp(cl))
        tl2_o[here, :] = split2(tail)
        dttl2_o[here, :] = split2(dt * tail)
        ec2_o[here, :] = split2(jnp.exp(cl + off))
        edt2_o[here, :] = split2(dt * jnp.exp(ctot - cl - off))
        off = off + tots[i]


def decay(cl, clt, h, mask):
    return jnp.exp(jnp.where(mask, cl[:, h : h + 1] - clt[h : h + 1, :], NEG))


def lane_masks():
    lane = lax.broadcasted_iota(jnp.int32, (1, Q), 1)
    low = (lane < HEADDIM).astype(F32)
    return low.astype(BF), (1.0 - low).astype(BF)


def project_kernel(s, per, *refs):
    xn, xnh, pieces, cw, dt2, edt2, ex, b, rest = take(refs, 0, 0, per, 0, 0, 0, 0, 0)
    wz_o, wx_o, z_o, xr_o, xrh_o, u_o, xs_o, xdt_o, s_o, buf, acc = rest
    rows = z_o.shape[0]
    gc = per * HEADDIM
    cols = slice(s * gc, s * gc + gc)
    wx = jnp.concatenate([v[HEADDIM:, :] for v in pieces], axis=0)
    wz = jnp.concatenate([v[:HEADDIM, :] for v in pieces], axis=0)

    @pl.when(pl.program_id(0) == 0)
    def _():
        wz_o[...] = wz
        wx_o[...] = wx
        xh = dot_t(xnh[...], wx)
        buf[0:HALO, :] = xh
        xrh_o[...] = xh
        acc[...] = jnp.zeros_like(acc)

    @pl.when(pl.program_id(0) > 0)
    def _():
        buf[0:HALO, :] = buf[rows : rows + HALO, :]

    buf[HALO:, :] = dot_t(xn[...], wx)
    z_o[...] = dot_t(xn[...], wz)
    for i in range(rows // Q):
        here = slice(i * Q, i * Q + Q)
        win = buf[i * Q : i * Q + Q + HALO, :]
        u = jnp.zeros((Q, gc), F32)
        for k in range(4):
            u = u + cw[k : k + 1, cols] * win[HALO - 3 + k : HALO - 3 + k + Q, :]
        xr_o[here, :] = win[HALO:, :]
        u_o[here, :] = u
        xs = u * sigmoid(u)
        xs_o[here, :] = xs
        xdt_o[here, :] = (xs * dot(dt2[here, :], ex[:, cols])).astype(BF)
        acc[...] += t_dot((xs * dot(edt2[here, :], ex[:, cols])).astype(BF), b[here, :])

    @pl.when(pl.program_id(0) == pl.num_programs(0) - 1)
    def _():
        s_o[...] = acc[...].astype(BF)


def inside_kernel(s, per, xdt, b, c, cl, clt, y_o):
    mask = tri("ge")
    low, high = lane_masks()
    for i in range(xdt.shape[0] // Q):
        rows = slice(i * Q, i * Q + Q)
        g = dot_t(c[rows, :], b[rows, :])
        clv, cltv = cl[rows, :], clt[:, rows]
        for p in range(xdt.shape[1] // Q):
            here = slice(p * Q, p * Q + Q)
            h = s * per + 2 * p
            ws = [(g * decay(clv, cltv, j, mask)).astype(BF) for j in (h, h + 1)]
            x = xdt[rows, here]
            y_o[rows, here] = dot(
                jnp.concatenate(ws, axis=1), jnp.concatenate([x * low, x * high], axis=0)
            )


def head_scale(clt, first, per, state):
    return jnp.concatenate(
        [
            jnp.broadcast_to(jnp.exp(clt[h : h + 1, Q - 1 : Q]), (HEADDIM, state))
            for h in range(first, first + per)
        ],
        axis=0,
    )


def from_messages(messages, sign, groups, per, state, store):
    nz = len(messages) + 1
    gc = per * HEADDIM
    top = nz * gc
    totals = [
        sum(m[top:, i : i + 1].astype(F32) for i in range(3)) for m in messages
    ]
    for at, j in enumerate(groups):
        total = jnp.zeros((gc, state), F32)
        faded = jnp.zeros((per, 1), F32)
        for k in range(1, nz):
            there = (j - sign * k) % nz
            scale = jnp.exp(faded)
            scale = jnp.concatenate(
                [jnp.broadcast_to(scale[h : h + 1, :], (HEADDIM, state)) for h in range(per)],
                axis=0,
            )
            total = total + scale * messages[k - 1][there * gc : there * gc + gc, :].astype(F32)
            faded = faded + totals[k - 1][there * per : there * per + per, :]
        store[at * gc : at * gc + gc, :] = total


def carry_kernel(groups, per, *refs):
    n = len(groups)
    y_in, xs, z, dyn, b, c, clt, e12, dttl2, messages, dsk, gain, ex, rest = take(
        refs, n, n, n, 0, 0, 0, 0, 0, 0, n - 1, 0, 0, 0
    )
    ys_o, st_o, rest = take(rest, n, n)
    gg_o, sum_o, s = rest
    gc = per * HEADDIM

    @pl.when(pl.program_id(0) == 0)
    def _():
        from_messages(messages, 1, groups, per, s.shape[1], s)

    square = jnp.zeros((Q, gc), F32)
    inner = jnp.zeros((Q, gc), F32)
    for j in groups:
        here = slice(j * gc, j * gc + gc)
        sv = s[here, :]
        sb = sv.astype(BF)
        st_o[j][0] = sb
        x = xs[j][...]
        e1 = dot(e12[...], ex[:, here])
        y = y_in[j][...] + e1 * dot_t(c[...], sb) + dsk[:, here] * x
        ys_o[j][...] = y
        xt = (x * dot(dttl2[...], ex[:, here])).astype(BF)
        s[here, :] = head_scale(clt, j * per, per, sv.shape[1]) * sv + t_dot(xt, b[...])
        zz = z[j][...]
        gz = y * (zz * sigmoid(zz))
        gg = gz * gain[:, here]
        gg_o[:, here] = gg.astype(BF)
        square = square + gz * gz
        inner = inner + gg * dyn[:, here]
    lane = lax.broadcasted_iota(jnp.int32, (Q, 2), 1)
    sum_o[...] = jnp.where(
        lane == 0,
        jnp.sum(square, axis=1, keepdims=True),
        jnp.sum(inner, axis=1, keepdims=True),
    )


def gate_kernel(groups, per, *refs):
    n = len(groups)
    ys, z, xs, dyn, sums, sums2, gain, ec2, ex, c, rest = take(refs, n, n, n, *[0] * 7)
    hidden, branch, branch2, limit, rest = take(rest, 0, 0, 0, 0)
    dys_o, rest = take(rest, n)
    dz_o, yn_o, ds_o, gn_o, sk_o, out_o, acc = rest
    gc = per * HEADDIM

    @pl.when(pl.program_id(0) == 0)
    def _():
        acc[...] = jnp.zeros_like(acc)
        gn_o[...] = jnp.zeros_like(gn_o)
        sk_o[...] = jnp.zeros_like(sk_o)

    count = n * gc * 2
    both = sums[...] + sums2[...]
    r2 = lax.rsqrt(both[:, 0:1] / count + EPS)
    pull = both[:, 1:2] * (r2 * r2 * r2) / count
    row = lax.broadcasted_iota(jnp.int32, (Q, 1), 0) + pl.program_id(0) * Q
    keep = jnp.where(row < limit[0, 0], r2, 0.0)
    out_o[...] = (
        hidden[...].astype(F32) + keep * (branch[...] + branch2[...].astype(F32))
    ).astype(BF)
    for j in groups:
        here = slice(j * gc, j * gc + gc)
        gn = gain[:, here]
        zz = z[j][...]
        sz = sigmoid(zz)
        silu = zz * sz
        y = ys[j][...]
        gz = y * silu
        dy_n = dyn[:, here]
        gr = gz * r2
        yn_o[:, here] = (gr * gn).astype(BF)
        gn_o[:, here] += jnp.sum(dy_n * gr, axis=0, keepdims=True)
        dgz = r2 * gn * dy_n - gz * pull
        dys = dgz * silu
        dys_o[j][...] = dys
        dz_o[:, here] = (dgz * y * (sz + silu * (1.0 - sz))).astype(BF)
        sk_o[:, here] += jnp.sum(dys * xs[j][...], axis=0, keepdims=True)
        acc[here, :] += t_dot((dys * dot(ec2[...], ex[:, here])).astype(BF), c[...])

    @pl.when(pl.program_id(0) == pl.num_programs(0) - 1)
    def _():
        ds_o[...] = acc[...].astype(BF)


def inside_back_kernel(groups, per, *refs):
    n = len(groups)
    xdt, dys, b, c, cl, clt, rest = take(refs, n, n, 0, 0, 0, 0)
    dx_o, rest = take(rest, n)
    db_o, dc_o, da_o, kt = rest
    mask = tri("ge")
    low, high = lane_masks()
    g = dot_t(c[...], b[...])
    clv, cltv = cl[...], clt[...]
    heads = clt.shape[0]
    lane = lax.broadcasted_iota(jnp.int32, (Q, heads), 1)
    dg = jnp.zeros((Q, Q), F32)
    rsum = jnp.zeros((Q, heads), F32)
    for s in groups:
        for p in range(per // 2):
            here = slice(p * Q, p * Q + Q)
            x = xdt[s][:, here]
            dy = dys[s][:, here].astype(BF)
            pp = dot_t(dy, jnp.concatenate([x * low, x * high], axis=0))
            ws = []
            for j in range(2):
                h = s * per + 2 * p + j
                ell = decay(clv, cltv, h, mask)
                ws.append((g * ell).astype(BF))
                pe = pp[:, j * Q : j * Q + Q] * ell
                dg = dg + pe
                m = pe * g
                rsum = jnp.where(lane == h, jnp.sum(m, axis=1, keepdims=True), rsum)
                kt[h : h + 1, :] = jnp.sum(m, axis=0, keepdims=True)
            dx_o[s][:, here] = t_dot(
                jnp.concatenate(ws, axis=0), jnp.concatenate([dy * low, dy * high], axis=0)
            )
    dgb = dg.astype(BF)
    dc_o[...] = dot(dgb, b[...])
    db_o[...] = t_dot(dgb, c[...])
    upper = tri("le").astype(F32)
    da_o[...] = dot(upper, rsum, HIGH) - dot_t(upper, kt[...], HIGH)


def conv_back(d, nxt, taps, raw, rawh, grad_o, out_o, outh_o, last):
    win = jnp.concatenate([d, nxt[...]], axis=0)
    back = jnp.zeros_like(d)
    sums = []
    for k in range(4):
        part = win[3 - k : 3 - k + Q, :]
        back = back + taps[k : k + 1, :] * part
        sums.append(jnp.sum(raw * part, axis=0, keepdims=True))
    grad_o[...] += jnp.concatenate(sums, axis=0)
    out_o[...] = back.astype(BF)
    nxt[...] = d[0:8, :]

    @pl.when(last)
    def _():
        win_h = jnp.concatenate([jnp.zeros((HALO, d.shape[1]), F32), d[0:8, :]], axis=0)
        back_h = jnp.zeros((HALO, d.shape[1]), F32)
        sums_h = []
        for k in range(4):
            part = win_h[3 - k : 3 - k + HALO, :]
            back_h = back_h + taps[k : k + 1, :] * part
            sums_h.append(jnp.sum(rawh[...] * part, axis=0, keepdims=True))
        grad_o[...] += jnp.concatenate(sums_h, axis=0)
        outh_o[...] = back_h.astype(BF)


def back_kernel(groups, per, final, *refs):
    n = len(groups)
    dxi, dys, u, xr, xrh, st, rest = take(refs, n, n, n, n, n, n)
    (b, c, dbi, dci, dai, dti, dt, sig, clt, dt2, e12, tl2), rest = rest[:12], rest[12:]
    (ubc, braw, brawh, cw, cbc, rate, dsk, ex, er), rest = rest[:9], rest[9:]
    nz = dt.shape[1] // per
    messages, _, dx_o, dxh_o, gcx_o, rest = take(rest, nz - 1, 0, n, n, n)
    db_o, dc_o, dt_o, ga_o, gbias_o, bc_o, bch_o, gcb_o, ds, vs = rest[:10]
    du_next, rest = take(rest[10:], n)
    (db_next,) = rest
    step = pl.program_id(0)
    blocks = pl.num_programs(0)
    heads = dt.shape[1]
    state = b.shape[1]
    gc = per * HEADDIM

    @pl.when(step == 0)
    def _():
        from_messages(messages, -1, groups, per, state, ds)
        for i in range(n):
            du_next[i][...] = jnp.zeros_like(du_next[i])
            gcx_o[i][...] = jnp.zeros_like(gcx_o[i])
        vs[...] = jnp.zeros_like(vs)
        db_next[...] = jnp.zeros_like(db_next)
        gcb_o[...] = jnp.zeros_like(gcb_o)
        ga_o[...] = jnp.zeros_like(ga_o)
        gbias_o[...] = jnp.zeros_like(gbias_o)

    last = step == blocks - 1
    rsum = jnp.zeros((Q, heads), F32)
    gsum = jnp.zeros((Q, heads), F32)
    ddt = jnp.zeros((Q, heads), F32)
    dbs = dbi[...]
    dcs = dci[...]
    for i, s in enumerate(groups):
        here = slice(s * gc, s * gc + gc)
        mine = slice(i * gc, i * gc + gc)
        ehere = er[here, :]
        sb = st[i][0]
        dsv = ds[mine, :]
        dsb = dsv.astype(BF)
        dy = dys[i][...]
        dye = dy * dot(e12[...], ex[:, here])
        dyb = dye.astype(BF)
        rsum = rsum + dot((dye * dot_t(c[...], sb)).astype(BF), ehere)
        dcs = dcs + dot(dyb, sb)
        bds = dot_t(b[...], dsb)
        tail = dot(tl2[...], ex[:, here])
        dtx = dot(dt2[...], ex[:, here])
        uu = u[i][...]
        su = sigmoid(uu)
        xs = uu * su
        xt = xs * dtx * tail
        gsum = gsum + dot((xt * bds).astype(BF), ehere)
        dbs = dbs + dot(xt.astype(BF), dsb)
        dxdt = dxi[i][...] + tail * bds
        ddt = ddt + dot((dxdt * xs).astype(BF), ehere)
        eds = head_scale(clt, s * per, per, state) * dsv
        ev = eds * sb.astype(F32)
        for j in range(per):
            h = s * per + j
            vs[h : h + 1, :] = jnp.sum(
                ev[j * HEADDIM : (j + 1) * HEADDIM, :], axis=0, keepdims=True
            )
        ds[mine, :] = eds + t_dot(dyb, c[...])
        du = (dxdt * dtx + dsk[:, here] * dy) * (su + xs * (1.0 - su))
        conv_back(
            du, du_next[i], cw.at[:, here], xr[i][...], xrh[i], gcx_o[i], dx_o[i], dxh_o[i], last
        )
    col = lax.broadcasted_iota(jnp.int32, (1, heads), 1)
    mine = functools.reduce(
        jnp.logical_or, [(col >= s * per) & (col < s * per + per) for s in groups]
    )
    vrow = dot_t(jnp.ones((8, state), F32), vs[...], HIGH)
    da = (
        dai[...]
        + split_dot(tri("le").astype(BF), rsum)
        + split_dot(tri("gt").astype(BF), gsum)
        + vrow[0:1, :]
    )
    da = jnp.where(mine, da, 0.0)
    draw = (rate[...] * da + ddt) * sig[...]
    dt_o[...] = (dti[...] + draw).astype(dt_o.dtype)
    ga_o[...] += jnp.sum(da * dt[...], axis=0, keepdims=True)
    gbias_o[...] += jnp.sum(draw, axis=0, keepdims=True)
    db_o[...] = dbs
    dc_o[...] = dcs
    if final:
        d = jnp.concatenate([dbs, dcs], axis=1)
        v = ubc[...]
        sv = sigmoid(v)
        conv_back(
            d * (sv + v * sv * (1.0 - sv)), db_next, cbc, braw[...], brawh, gcb_o, bc_o, bch_o, last
        )


def sum_products_kernel(n, *refs):
    a, w, rest = take(refs, n, n)
    left_o, right_o = rest
    total = dot(a[0][...], w[0][...])
    for i in range(1, n):
        total = total + dot(a[i][...], w[i][...])
    half = left_o.shape[1]
    left_o[...] = total[:, :half]
    right_o[...] = total[:, half:].astype(BF)


def pull_kernel(per, nz, *refs):
    cot, cot2, limit, own, others, rest = take(refs, 0, 0, 0, per, per)
    w_o, mask_o, dyn_o = rest
    rows = cot.shape[0]
    half = cot.shape[1]

    @pl.when(pl.program_id(0) == 0)
    def _():
        for m in range(per):
            w_o[m * HEADDIM : (m + 1) * HEADDIM, :] = own[m][...]
            for s in range(1, nz):
                at = (s * per + m) * HEADDIM
                w_o[at : at + HEADDIM, :] = others[m][(s - 1) * HEADDIM : s * HEADDIM, :]

    row = lax.broadcasted_iota(jnp.int32, (rows, 1), 0) + pl.program_id(0) * rows
    keep = row < limit[0, 0]
    for i, v in enumerate((cot, cot2)):
        mask_o[:, i * half : i * half + half] = jnp.where(keep, v[...].astype(F32), 0.0).astype(BF)
    dyn_o[...] = dot_t(mask_o[...], w_o[...])


def early_grad_kernel(per, yn, masked, dz, xn, *outs):
    g_out = t_dot(yn[...], masked[...]).astype(BF)
    g_z = t_dot(dz[...], xn[...]).astype(BF)
    for m in range(per):
        here = slice(m * HEADDIM, (m + 1) * HEADDIM)
        outs[m][0, :HEADDIM, :] = g_out[here, :]
        outs[m][0, HEADDIM:, :] = g_z[here, :]


def late_grad_kernel(n, per, final, *refs):
    dx, dxh, xn, xnh, rest = take(refs, n, n, 0, 0)
    if final:
        dbc, dbch, ddt, spread, rest = take(rest, 0, 0, 0, 0)
        outs, rest = take(rest, per)
        gbc, gdt = rest
        bc_rows = gbc.shape[0] // per
        dt_rows = gdt.shape[0] // per
        gbc[...] = t_dot(dbc[...], xn[...]) + t_dot(dbch[...], xnh[...])
        gdt[...] = split_dot(spread[...], t_dot(ddt[...], xn[...]))
    else:
        outs, rest = take(rest, per)
    for i in range(n):
        g = (t_dot(dx[i][...], xn[...]) + t_dot(dxh[i][...], xnh[...])).astype(BF)
        for m in range(per):
            outs[m][i * HEADDIM : (i + 1) * HEADDIM, :] = g[m * HEADDIM : (m + 1) * HEADDIM, :]
    if final:
        me = lax.axis_index("dp")
        for m in range(per):
            at = jnp.bitwise_xor(me, m)
            v = gbc[pl.ds(pl.multiple_of(at * bc_rows, bc_rows), bc_rows), :]
            w = gdt[pl.ds(pl.multiple_of(at * dt_rows, dt_rows), dt_rows), :]
            w = jnp.concatenate([w, jnp.zeros((HALO - dt_rows, w.shape[1]), F32)], axis=0)
            outs[m][n * HEADDIM : n * HEADDIM + bc_rows, :] = v.astype(BF)
            outs[m][n * HEADDIM + bc_rows :, :] = w.astype(BF)


def shape(dims, dtype=F32):
    return jax.ShapeDtypeStruct(dims, dtype)


def whole(array):
    rank = len(array.shape)
    return pl.BlockSpec(array.shape, lambda *_: (0,) * rank)


def params():
    return pltpu.CompilerParams(vmem_limit_bytes=VMEM)


def cost(us):
    return pl.CostEstimate(flops=int(us * 1.0e8), bytes_accessed=int(us * 1.0e3), transcendentals=0)


def take(refs, *counts):
    out, at = [], 0
    for n in counts:
        out.append(refs[at] if n == 0 else refs[at : at + n])
        at += max(n, 1)
    return out + [refs[at:]]


def sequence_device(
    hidden, lengths, cotangent, norm_gain, in_zx, in_bcdt, conv_x, conv_bc,
    dt_bias, a_log, d_skip, gnorm_gain, out_w,
):
    rows, half = hidden.shape
    own_heads = in_zx.shape[1]
    nz = lax.axis_size("head")
    ndp = lax.axis_size("dp")
    zi = lax.axis_index("head")
    di = lax.axis_index("dp")
    wi = lax.axis_index("width")
    per = ndp
    heads = nz * per
    channels = heads * HEADDIM
    model = 2 * half
    blocks = rows // Q

    def swap(v):
        return lax.ppermute(v, "width", [(0, 1), (1, 0)])

    def turn(v, s):
        return lax.ppermute(v, "head", [(i, (i + s) % nz) for i in range(nz)])

    def shift(v, s):
        return lax.ppermute(v, "head", [(i, i + s) for i in range(nz) if 0 <= i + s < nz])

    def cross(v, m):
        return lax.ppermute(v, "dp", [(i, i ^ m) for i in range(ndp)])

    def pick(v, index):
        return lax.dynamic_index_in_dim(v, index, 0, keepdims=False)

    gc = per * HEADDIM
    groups = tuple(range(nz))

    zx_t = jnp.transpose(in_zx, (1, 2, 0))
    out_h = out_w.reshape(own_heads, HEADDIM, half)

    def slot_of(v, w, m):
        return pick(v, per * w + (di ^ m))

    def join(v, m):
        return jnp.concatenate([slot_of(v, wi, m), swap(slot_of(v, 1 - wi, m))], axis=-1)

    def join_rest(v):
        mine = jnp.stack([slot_of(v, wi, m) for m in range(1, per)])
        other = jnp.stack([slot_of(v, 1 - wi, m) for m in range(1, per)])
        both = jnp.concatenate([mine, swap(other)], axis=-1)
        return [both[m] for m in range(per - 1)]

    def after_that(v, w):
        return v + (w[(0,) * w.ndim] * 0).astype(v.dtype)

    own_first = join(zx_t, 0)
    zx_rest = zx_t
    along = [turn(own_first, s) for s in range(1, nz)]
    hidden_o = swap(hidden)
    pieces = [[own_first] + join_rest(zx_rest)]
    for got in along:
        pieces.append([got] + [cross(got, m) for m in range(1, per)])
    bcdt_t = jnp.concatenate([jnp.transpose(in_bcdt), norm_gain[None]], axis=0)
    bcdt_t = jnp.concatenate([bcdt_t, swap(bcdt_t)], axis=1)
    gain_in = bcdt_t[2 * STATE + HEADS :].astype(F32)
    wbc = bcdt_t[: 2 * STATE]
    slot = jnp.arange(heads)
    slot_head = ((zi - slot // per) % nz) * own_heads + wi * per + ((slot % per) ^ di)
    pick_heads = (slot_head[:, None] == jnp.arange(HEADS)[None, :]).astype(F32)
    wdt = jnp.dot(
        pick_heads.astype(BF), bcdt_t[2 * STATE : 2 * STATE + HEADS], preferred_element_type=F32
    ).astype(BF)

    table = jnp.concatenate(
        [
            dt_bias[:, None],
            a_log[:, None],
            d_skip[:, None],
            jnp.transpose(conv_x.astype(F32).reshape(4, own_heads, HEADDIM), (1, 0, 2)).reshape(
                own_heads, 4 * HEADDIM
            ),
            gnorm_gain.astype(F32).reshape(own_heads, HEADDIM),
        ],
        axis=1,
    )
    table = jnp.stack([slot_of(table, wi, m) for m in range(per)])
    table = jnp.concatenate([table] + [turn(table, s) for s in range(1, nz)], axis=0)
    bias = table[:, 0][None]
    rate = -jnp.exp(table[:, 1])[None]
    skip = jnp.repeat(table[:, 2], HEADDIM)[None]
    taps = jnp.transpose(
        table[:, 3 : 3 + 4 * HEADDIM].reshape(heads, 4, HEADDIM), (1, 0, 2)
    ).reshape(4, channels)
    gain_out = table[:, 3 + 4 * HEADDIM :].reshape(1, channels)
    taps_bc = conv_bc.astype(F32)

    onehot = np.kron(np.eye(heads), np.ones((1, HEADDIM)))
    ex = jnp.asarray(np.concatenate([onehot, onehot], axis=0), BF)
    er = jnp.asarray(onehot.T, BF)

    edge = jnp.concatenate([hidden[rows - HALO :], hidden_o[rows - HALO :]], axis=1)
    edge = shift(edge, 1)
    ext_rows = rows + HALO
    narrow = shape((rows, 2 * heads), BF)
    (
        xn, xnh, r, braw, brawh, ubc, bs, cs, dt, sig, cl, clt, totals,
        dt2, e12, tl2, dttl2, ec2, edt2,
    ) = pl.pallas_call(
        entry_kernel,
        out_shape=[
            shape((rows, model), BF), shape((HALO, model), BF), shape((rows, 1)),
            shape((rows, 2 * STATE)),
            shape((HALO, 2 * STATE)), shape((rows, 2 * STATE)), shape((rows, STATE), BF),
            shape((rows, STATE), BF), shape((rows, heads)), shape((rows, heads)),
            shape((rows, heads)), shape((heads, rows)), shape((heads, STATE), BF),
            narrow, narrow, narrow, narrow, narrow, narrow,
        ],
        scratch_shapes=[pltpu.VMEM((ext_rows, 2 * STATE), F32)],
        compiler_params=params(),
        cost_estimate=cost(12),
        name="entry",
    )(hidden, hidden_o, edge, gain_in, wbc, wdt, taps_bc, bias, rate)

    def send_states(local, sign):
        message = jnp.concatenate([*local, totals], axis=0)
        return [shift(message, sign * k) for k in range(1, nz)]

    cut = rows // 2 if rows // 2 % Q == 0 else rows
    part = shape((rows, gc))
    full = shape((rows, channels))
    step = lambda i: (i, 0)
    fix = lambda i: (0, 0)
    gspec = pl.BlockSpec((cut, gc), step)
    wz, wx, z, xr, xrh, u, xs, xdt, s_local, y_in = ([] for _ in range(10))
    for s in groups:
        out = pl.pallas_call(
            functools.partial(project_kernel, s, per),
            grid=(rows // cut,),
            in_specs=[
                pl.BlockSpec((cut, model), step),
                pl.BlockSpec((HALO, model), fix),
                *[whole(v) for v in pieces[s]], whole(taps), pl.BlockSpec((cut, 2 * heads), step),
                pl.BlockSpec((cut, 2 * heads), step), whole(ex), pl.BlockSpec((cut, STATE), step),
            ],
            out_specs=[
                pl.BlockSpec((gc, model), fix), pl.BlockSpec((gc, model), fix), gspec, gspec,
                pl.BlockSpec((HALO, gc), fix), gspec, gspec, gspec, pl.BlockSpec((gc, STATE), fix),
            ],
            out_shape=[
                shape((gc, model), BF), shape((gc, model), BF), part, part, shape((HALO, gc)),
                part, part, shape((rows, gc), BF), shape((gc, STATE), BF),
            ],
            scratch_shapes=[pltpu.VMEM((cut + HALO, gc), F32), pltpu.VMEM((gc, STATE), F32)],
            compiler_params=params(),
            cost_estimate=cost(5),
            name="project",
        )(xn, xnh, *pieces[s], taps, dt2, edt2, ex, bs)
        for keep, v in zip((wz, wx, z, xr, xrh, u, xs, xdt, s_local), out):
            keep.append(v)
        y_in.append(
            pl.pallas_call(
                functools.partial(inside_kernel, s, per),
                grid=(rows // cut,),
                in_specs=[
                    gspec, pl.BlockSpec((cut, STATE), step), pl.BlockSpec((cut, STATE), step),
                    pl.BlockSpec((cut, heads), step), pl.BlockSpec((heads, cut), lambda i: (0, i)),
                ],
                out_specs=gspec,
                out_shape=part,
                compiler_params=params(),
                cost_estimate=cost(3),
                name="inside",
            )(xdt[s], bs, cs, cl, clt)
        )
    messages = send_states(s_local, 1)

    out_first = after_that(join(out_h, 0), pieces[-1][-1])
    out_own = [out_first] + join_rest(out_h)
    out_along = jnp.concatenate([turn(out_first, s) for s in range(1, nz)], axis=0)
    out_cross = [out_along] + [cross(out_along, m) for m in range(1, per)]
    cot_o = swap(cotangent)
    limit = (lengths[0] - zi * rows).reshape(1, 1)

    wide = pl.BlockSpec((Q, channels), step)
    gwide = pl.BlockSpec((Q, gc), step)
    bspec = pl.BlockSpec((Q, STATE), step)
    hspec = pl.BlockSpec((Q, heads), step)
    h2spec = pl.BlockSpec((Q, 2 * heads), step)
    tspec = pl.BlockSpec((heads, Q), lambda i: (0, i))
    tile = 2 * Q if rows % (2 * Q) == 0 else Q
    smem = pl.BlockSpec(memory_space=pltpu.SMEM)
    wout, masked, dyn = pl.pallas_call(
        functools.partial(pull_kernel, per, nz),
        grid=(rows // tile,),
        in_specs=[
            pl.BlockSpec((tile, half), step), pl.BlockSpec((tile, half), step), smem,
            *[whole(v) for v in out_own + out_cross],
        ],
        out_specs=[
            pl.BlockSpec((channels, model), fix), pl.BlockSpec((tile, model), step),
            pl.BlockSpec((tile, channels), step),
        ],
        out_shape=[shape((channels, model), BF), shape((rows, model), BF), full],
        compiler_params=params(),
        cost_estimate=cost(5),
        name="pull",
    )(cotangent, cot_o, limit, *out_own, *out_cross)
    out = pl.pallas_call(
        functools.partial(carry_kernel, groups, per),
        grid=(blocks,),
        in_specs=[
            *[gwide] * (3 * nz), wide, bspec, bspec, tspec, h2spec, h2spec, *[whole(v) for v in messages],
            whole(skip), whole(gain_out), whole(ex),
        ],
        out_specs=[
            *[gwide] * nz, *[pl.BlockSpec((1, gc, STATE), lambda i: (i, 0, 0))] * nz, wide,
            pl.BlockSpec((Q, 2), step),
        ],
        out_shape=[
            *[part] * nz, *[shape((blocks, gc, STATE), BF)] * nz, shape((rows, channels), BF),
            shape((rows, 2)),
        ],
        scratch_shapes=[pltpu.VMEM((channels, STATE), F32)],
        compiler_params=params(),
        cost_estimate=cost(10),
        name="carry",
    )(*y_in, *xs, *z, dyn, bs, cs, clt, e12, dttl2, *messages, skip, gain_out, ex)
    ys, states, gg, sums = out[:nz], out[nz : 2 * nz], out[2 * nz], out[2 * nz + 1]
    sums2 = swap(sums)

    def sum_products(a, w, count):
        tile = 2 * Q if count % (2 * Q) == 0 else count
        return pl.pallas_call(
            functools.partial(sum_products_kernel, len(a)),
            grid=(count // tile,),
            in_specs=[
                *[pl.BlockSpec((tile, v.shape[1]), step) for v in a], *[whole(v) for v in w]
            ],
            out_specs=[pl.BlockSpec((tile, half), step)] * 2,
            out_shape=[shape((count, half)), shape((count, half), BF)],
            compiler_params=params(),
            cost_estimate=cost(4),
            name="products",
        )(*a, *w)

    branch, branch_o = sum_products([gg], [wout], rows)
    branch_o = swap(branch_o)
    hhalf = pl.BlockSpec((Q, half), step)
    out = pl.pallas_call(
        functools.partial(gate_kernel, groups, per),
        grid=(blocks,),
        in_specs=[
            *[gwide] * (3 * nz), wide, pl.BlockSpec((Q, 2), step), pl.BlockSpec((Q, 2), step),
            whole(gain_out), h2spec, whole(ex), bspec, hhalf, hhalf, hhalf, smem,
        ],
        out_specs=[
            *[gwide] * nz, wide, wide, pl.BlockSpec((channels, STATE), fix),
            pl.BlockSpec((1, channels), fix), pl.BlockSpec((1, channels), fix), hhalf,
        ],
        out_shape=[
            *[part] * nz, shape((rows, channels), BF), shape((rows, channels), BF),
            shape((channels, STATE), BF), shape((1, channels)), shape((1, channels)),
            shape((rows, half), BF),
        ],
        scratch_shapes=[pltpu.VMEM((channels, STATE), F32)],
        compiler_params=params(),
        cost_estimate=cost(10),
        name="gate",
    )(
        *ys, *z, *xs, dyn, sums, sums2, gain_out, ec2, ex, cs, hidden, branch, branch_o, limit
    )
    dys = out[:nz]
    dz, yn, ds_local, g_gain, g_skip, out_hidden = out[nz:]
    messages = send_states([ds_local], -1)

    def plane_sum(parts):
        total = parts[0].astype(F32)
        for m in range(1, per):
            total = total + cross(parts[m], m).astype(F32)
        return total

    def to_owner(total):
        v = jnp.stack([total] + [cross(total, m) for m in range(1, per)])
        v = jnp.stack([pick(v, di ^ m) for m in range(per)])
        return v[:, :, :half], swap(v[:, :, half:])

    def by_head(mine, other):
        low_w = jnp.where(wi == 0, mine, other)
        high_w = jnp.where(wi == 0, other, mine)
        return jnp.concatenate([low_w, high_w], axis=0)

    gcol = pl.BlockSpec((rows, gc), lambda s: (0, s))
    early = pl.pallas_call(
        functools.partial(early_grad_kernel, per),
        grid=(nz,),
        in_specs=[gcol, whole(masked), gcol, whole(xn)],
        out_specs=[pl.BlockSpec((1, 2 * HEADDIM, model), lambda s: (s, 0, 0))] * per,
        out_shape=[shape((nz, 2 * HEADDIM, model), BF)] * per,
        compiler_params=params(),
        cost_estimate=cost(6),
        name="early_grad",
    )(yn, masked, dz, xn)
    early = plane_sum(early)
    early_low = early.astype(BF)

    out = pl.pallas_call(
        functools.partial(inside_back_kernel, groups, per),
        grid=(blocks,),
        in_specs=[*[gwide] * (2 * nz), bspec, bspec, hspec, tspec],
        out_specs=[*[gwide] * nz, bspec, bspec, hspec],
        out_shape=[*[part] * nz, shape((rows, STATE)), shape((rows, STATE)), shape((rows, heads))],
        scratch_shapes=[pltpu.VMEM((heads, Q), F32)],
        compiler_params=params(),
        cost_estimate=cost(15),
        name="inside_back",
    )(*xdt, *dys, bs, cs, cl, clt)
    dxi = out[:nz]
    dbi, dci, dai = out[nz:]
    rev = lambda i: (blocks - 1 - i, 0)
    rg = pl.BlockSpec((Q, gc), rev)
    rb = pl.BlockSpec((Q, STATE), rev)
    rh = pl.BlockSpec((Q, heads), rev)
    rh2 = pl.BlockSpec((Q, 2 * heads), rev)
    rbc = pl.BlockSpec((Q, 2 * STATE), rev)

    def back(some, final, dbi, dci, dti, wait):
        n = len(some)
        of = lambda values: [values[s] for s in some]
        out = pl.pallas_call(
            functools.partial(back_kernel, some, per, final),
            grid=(blocks,),
            in_specs=[
                *[rg] * (4 * n), *[pl.BlockSpec((HALO, gc), fix)] * n,
                *[pl.BlockSpec((1, gc, STATE), lambda i: (blocks - 1 - i, 0, 0))] * n,
                rb, rb, rb, rb, rh, rh, rh, rh,
                pl.BlockSpec((heads, Q), lambda i: (0, blocks - 1 - i)), rh2, rh2, rh2,
                rbc, rbc, whole(brawh), whole(taps), whole(taps_bc), whole(rate), whole(skip),
                whole(ex), whole(er), *[whole(v) for v in messages],
                pl.BlockSpec(memory_space=pl.ANY),
            ],
            out_specs=[
                *[rg] * n, *[pl.BlockSpec((HALO, gc), fix)] * n, *[pl.BlockSpec((4, gc), fix)] * n,
                rb, rb, rh, pl.BlockSpec((1, heads), fix), pl.BlockSpec((1, heads), fix),
                rbc, pl.BlockSpec((HALO, 2 * STATE), fix), pl.BlockSpec((4, 2 * STATE), fix),
            ],
            out_shape=[
                *[shape((rows, gc), BF)] * n, *[shape((HALO, gc), BF)] * n, *[shape((4, gc))] * n,
                shape((rows, STATE)), shape((rows, STATE)),
                shape((rows, heads), BF if final else F32), shape((1, heads)), shape((1, heads)),
                shape((rows, 2 * STATE), BF), shape((HALO, 2 * STATE), BF), shape((4, 2 * STATE)),
            ],
            scratch_shapes=[
                pltpu.VMEM((n * gc, STATE), F32), pltpu.VMEM((heads, STATE), F32),
                *[pltpu.VMEM((8, gc), F32)] * n, pltpu.VMEM((8, 2 * STATE), F32),
            ],
            compiler_params=params(),
            cost_estimate=cost(7 * n),
            name="back",
        )(
            *of(dxi), *of(dys), *of(u), *of(xr), *of(xrh), *of(states), bs, cs, dbi, dci, dai, dti,
            dt, sig, clt, dt2, e12, tl2, ubc, braw, brawh, taps, taps_bc, rate, skip, ex, er,
            *messages, wait,
        )
        return out[:n], out[n : 2 * n], out[2 * n : 3 * n], *out[3 * n :]

    halves = (groups[1 : nz // 2 + 1], groups[nz // 2 + 1 :] + groups[:1])
    dx, dxh, g_taps = [None] * nz, [None] * nz, [None] * nz
    dti = jnp.zeros((rows, heads), F32)
    g_rate, g_bias, late, wait = 0.0, 0.0, [], dti
    bc_rows = 2 * STATE // per
    for number, some in enumerate(halves):
        final = number == len(halves) - 1
        got, got_h, got_taps, dbi, dci, dti, one, two, dbc, dbch, g_taps_bc = back(
            some, final, dbi, dci, dti, wait
        )
        g_rate, g_bias = g_rate + one, g_bias + two
        for i, s in enumerate(some):
            dx[s], dxh[s], g_taps[s] = got[i], got_h[i], got_taps[i]
        n = len(some)
        spread_heads = pick_heads.T.astype(BF)
        more = [dbc, dbch, dti, spread_heads] if final else []
        out_rows = n * HEADDIM + (bc_rows + HALO if final else 0)
        g = pl.pallas_call(
            functools.partial(late_grad_kernel, n, per, final),
            out_shape=[shape((out_rows, model), BF)] * per,
            scratch_shapes=(
                [pltpu.VMEM((2 * STATE, model), F32), pltpu.VMEM((HEADS, model), F32)]
                if final
                else []
            ),
            compiler_params=params(),
            cost_estimate=cost(3),
            name="late_grad",
        )(*got, *got_h, xn, xnh, *more)
        late.append(plane_sum(g))
        wait = early_low if number == 0 else wait
    g_taps = jnp.concatenate(g_taps, axis=1)

    total = early[0]
    for s in range(1, nz):
        total = total + turn(early_low[s], -s).astype(F32)
    early_own, early_other = to_owner(total.astype(BF))
    share = late[-1][len(halves[-1]) * HEADDIM :]
    addend = {}
    for some, v in zip(halves, late):
        for i, s in enumerate(some):
            addend[s] = jnp.concatenate([v[i * HEADDIM : (i + 1) * HEADDIM], share], axis=0)
    total = addend[0]
    for s in range(1, nz):
        total = total + turn(addend[s].astype(BF), -s).astype(F32)
    late_own, late_other = to_owner(total.astype(BF))
    g_early = by_head(early_own, early_other)
    g_late = by_head(late_own[:, :HEADDIM], late_other[:, :HEADDIM])
    g_zx = jnp.concatenate([g_early[:, HEADDIM:], g_late], axis=1)
    g_bcdt = late_own[:, HEADDIM:].astype(F32) + late_other[:, HEADDIM:].astype(F32)
    grad_in_bcdt = jnp.transpose(
        jnp.concatenate(
            [
                g_bcdt[:, :bc_rows].reshape(2 * STATE, half),
                g_bcdt[:, bc_rows : bc_rows + HEADS // per].reshape(HEADS, half),
            ],
            axis=0,
        )
    )

    lhs = [dz] + dx + [dbc, dti]
    dxn, dxn_o = sum_products(lhs, [jnp.concatenate(wz, axis=0)] + wx + [wbc, wdt], rows)
    edge = sum(dot(v, w) for v, w in zip(dxh + [dbch], wx + [wbc]))
    edge = edge[:, :half] + swap(edge[:, half:])
    edge = shift(edge, -1)
    dxn = dxn + swap(dxn_o).astype(F32) + jnp.pad(edge, ((rows - HALO, 0), (0, 0)))
    source = hidden.astype(F32)
    gain_half = gain_in[:, :half]
    across = jnp.sum(dxn * gain_half * source, axis=1, keepdims=True)
    across = across + swap(across)
    grad_hidden = (
        cotangent.astype(F32)
        + r * gain_half * dxn
        - source * (r * r * r) / model * across
    ).astype(BF)
    g_norm = jnp.sum(dxn * source * r, axis=0)

    table = jnp.concatenate(
        [
            g_bias.reshape(heads, 1),
            (g_rate * rate).reshape(heads, 1),
            jnp.sum(g_skip.reshape(heads, HEADDIM), axis=1, keepdims=True),
            jnp.transpose(g_taps.reshape(4, heads, HEADDIM), (1, 0, 2)).reshape(heads, 4 * HEADDIM),
            g_gain.reshape(heads, HEADDIM),
        ],
        axis=1,
    )
    table = jnp.dot(pick_heads.T, table, precision=HIGH)
    side = (jnp.arange(2) == wi).astype(F32)[:, None] * g_norm[None]
    small = jnp.concatenate([table.reshape(-1), g_taps_bc.reshape(-1), side.reshape(-1)])
    small = small + swap(small)
    flip = 1
    while flip < ndp:
        small = small + cross(small, flip)
        flip *= 2
    flip = 1
    while flip < nz:
        small = small + lax.ppermute(small, "head", [(i, i ^ flip) for i in range(nz)])
        flip *= 2
    size = table.size
    table = lax.dynamic_slice_in_dim(
        small[:size].reshape(HEADS, -1), zi * own_heads, own_heads, 0
    )
    g_taps_bc = small[size : size + 8 * STATE].reshape(4, 2 * STATE)
    g_norm = pick(small[size + 8 * STATE :].reshape(2, half), wi)
    return (
        out_hidden,
        grad_hidden,
        g_norm,
        jnp.transpose(g_zx, (2, 0, 1)).astype(F32),
        grad_in_bcdt,
        jnp.transpose(
            table[:, 3 : 3 + 4 * HEADDIM].reshape(own_heads, 4, HEADDIM), (1, 0, 2)
        ).reshape(4, own_heads * HEADDIM),
        g_taps_bc,
        table[:, 0],
        table[:, 1],
        table[:, 2],
        table[:, 3 + 4 * HEADDIM :].reshape(-1),
        g_early[:, :HEADDIM].reshape(own_heads * HEADDIM, half).astype(F32),
    )


def fits(mesh):
    ndp, nz, nw = mesh.shape["dp"], mesh.shape["head"], mesh.shape["width"]
    return (
        nw == 2
        and ndp in (2, 4, 8)
        and nz & (nz - 1) == 0
        and HEADS == nz * nw * ndp
        and LEN % (nz * Q) == 0
        and SEQS == ndp
        and HEADS // nw * HEADDIM % Q == 0
        and HEADS // ndp <= HALO
    )


def solution(mesh):
    placed = (
        P(("dp", "head"), "width"),
        P("dp"),
        P(("dp", "head"), "width"),
        P("width"),
        P("width", "head", None),
        P("width", None),
        P(None, "head"),
        P(),
        P("head"),
        P("head"),
        P("head"),
        P("head"),
        P("head", "width"),
    )
    return jax.shard_map(
        sequence_device if fits(mesh) else per_device,
        mesh=mesh,
        in_specs=placed,
        out_specs=(
            P(("dp", "head"), "width"),
            P(("dp", "head"), "width"),
            P("width"),
            P("width", "head", None),
            P("width", None),
            P(None, "head"),
            P(),
            P("head"),
            P("head"),
            P("head"),
            P("head"),
            P("head", "width"),
        ),
        check_vma=False,
    )
```

```python
import functools

import jax
import jax.numpy as jnp
import numpy as np
from jax import lax
from jax.experimental import pallas as pl
from jax.experimental.pallas import tpu as pltpu
from jax.sharding import PartitionSpec as P

D = 1024
HEADS = 32
HEADDIM = 64
STATE = 128
SCAN_BLOCK = 256
LEN = 4096
INNER = 2048
SEQS = 4


EPS = 1e-05
HIGH = lax.Precision.HIGHEST


def conv_causal(values, kernel):
    taps = kernel.shape[0]
    padded = jnp.pad(values, ((taps - 1, 0), (0, 0)))
    total = jnp.zeros_like(values)
    for offset in range(taps):
        total = total + kernel[offset] * padded[offset : offset + values.shape[0]]
    return total


def block_scan(inputs, steps, rates, bmat, cmat, block):
    length, heads, hsize = inputs.shape
    count = length // block
    in_blocks = inputs.reshape(count, block, heads, hsize)
    step_blocks = steps.reshape(count, block, heads)
    b_blocks = bmat.reshape(count, block, bmat.shape[1])
    c_blocks = cmat.reshape(count, block, cmat.shape[1])
    places = jnp.arange(block)
    lower = (places[:, None] >= places[None, :])[:, :, None]

    def advance(state, pieces):
        x_part, dt_part, b_part, c_part = pieces
        cums = jnp.cumsum(dt_part * rates, axis=0)
        spread = cums[:, None, :] - cums[None, :, :]
        decay = jnp.where(lower, jnp.exp(jnp.where(lower, spread, 0.0)), 0.0)
        scores = jnp.dot(c_part, b_part.T, precision=HIGH)
        weights = scores[:, :, None] * decay * dt_part[None, :, :]
        inside = jnp.einsum("ijh,jhp->ihp", weights, x_part, precision=HIGH)
        carried = (
            jnp.einsum("in,hpn->ihp", c_part, state, precision=HIGH) * jnp.exp(cums)[:, :, None]
        )
        tails = jnp.exp(cums[-1][None, :] - cums) * dt_part
        state = jnp.exp(cums[-1])[:, None, None] * state + jnp.einsum(
            "jh,jhp,jn->hpn", tails, x_part, b_part, precision=HIGH
        )
        return (state, inside + carried)

    start_state = jnp.zeros((heads, hsize, bmat.shape[1]), jnp.float32)
    _, result = lax.scan(
        jax.checkpoint(advance), start_state, (in_blocks, step_blocks, b_blocks, c_blocks)
    )
    return result.reshape(length, heads, hsize)


def mixer(zx, bc_raw, dt_raw, kernel_x, kernel_bc, bias_dt, log_rate, skip):
    length, heads, double = zx.shape
    hsize = double // 2
    gate = zx[:, :, :hsize]
    x_raw = zx[:, :, hsize:].reshape(length, heads * hsize)
    xs_conv = jax.nn.silu(conv_causal(x_raw, kernel_x)).reshape(length, heads, hsize)
    bc_conv = jax.nn.silu(conv_causal(bc_raw, kernel_bc))
    half = bc_conv.shape[1] // 2
    steps = jax.nn.softplus(dt_raw + bias_dt)
    rates = -jnp.exp(log_rate)
    result = (
        block_scan(xs_conv, steps, rates, bc_conv[:, :half], bc_conv[:, half:], SCAN_BLOCK)
        + skip[:, None] * xs_conv
    )
    return (result * jax.nn.silu(gate)).reshape(length, heads * hsize)


def per_device(
    hidden,
    lengths,
    cotangent,
    norm_gain,
    in_zx,
    in_bcdt,
    conv_x,
    conv_bc,
    dt_bias,
    a_log,
    d_skip,
    gnorm_gain,
    out_w,
):
    slice_rows, half_width = hidden.shape
    local_heads = in_zx.shape[1]
    head_count = lax.axis_size("head")
    head_index = lax.axis_index("head")
    total_rows = slice_rows * head_count
    seq_local = lengths.shape[0]
    inner_local = local_heads * HEADDIM
    row_ids = head_index * slice_rows + jnp.arange(slice_rows, dtype=jnp.int32)
    owner = (row_ids // LEN)[:, None] == jnp.arange(seq_local, dtype=jnp.int32)[None, :]
    limits = jnp.sum(jnp.where(owner, lengths[None, :], 0), axis=1)
    keeper = (row_ids % LEN < limits).astype(jnp.float32)[:, None]
    source = hidden.astype(jnp.float32)
    squares = lax.psum(jnp.sum(source * source, axis=1), "width")
    scale = lax.rsqrt(squares / D + EPS)[:, None]
    gain_in = norm_gain.astype(jnp.float32)
    normed = (source * scale * gain_in).astype(jnp.bfloat16)
    gathered = lax.all_gather(normed, "head", axis=0, tiled=True)
    w_zx = in_zx.reshape(half_width, local_heads * 2 * HEADDIM)
    zx_part = jnp.dot(gathered, w_zx, preferred_element_type=jnp.float32)
    bcdt_part = jnp.dot(gathered, in_bcdt, preferred_element_type=jnp.float32)
    zx_full, bcdt_full = lax.psum((zx_part, bcdt_part), "width")
    zx_seq = zx_full.reshape(seq_local, LEN, local_heads, 2 * HEADDIM)
    bc_seq = bcdt_full[:, : 2 * STATE].reshape(seq_local, LEN, 2 * STATE)
    dt_seq = lax.dynamic_slice_in_dim(
        bcdt_full, 2 * STATE + head_index * local_heads, local_heads, 1
    ).reshape(seq_local, LEN, local_heads)

    def local_mix(zx_in, bc_in, dt_in, kernel_x, kernel_bc, bias_in, log_in, skip_in):
        per_sequence = jax.vmap(mixer, in_axes=(0, 0, 0, None, None, None, None, None))
        return per_sequence(
            zx_in, bc_in, dt_in, kernel_x, kernel_bc, bias_in, log_in, skip_in
        ).reshape(total_rows, inner_local)

    gated, mix_pull = jax.vjp(
        local_mix,
        zx_seq,
        bc_seq,
        dt_seq,
        conv_x.astype(jnp.float32),
        conv_bc.astype(jnp.float32),
        dt_bias,
        a_log,
        d_skip,
    )
    total_sq = lax.psum(jnp.sum(gated * gated, axis=1), "head")
    scale_out = lax.rsqrt(total_sq / INNER + EPS)[:, None]
    gain_out = gnorm_gain.astype(jnp.float32)
    mixed = (gated * scale_out * gain_out).astype(jnp.bfloat16)
    picked = mixed
    branch = lax.psum_scatter(
        jnp.dot(picked, out_w, preferred_element_type=jnp.float32),
        "head",
        scatter_dimension=0,
        tiled=True,
    )
    out_hidden = (source + keeper * branch).astype(jnp.bfloat16)
    grad_out = cotangent.astype(jnp.float32)
    masked = (grad_out * keeper).astype(jnp.bfloat16)
    piece = lax.all_gather(masked, "head", axis=0, tiled=True)
    picked = mixed
    acc_weight = jnp.einsum("tc,td->cd", picked, piece, preferred_element_type=jnp.float32)
    product = jnp.einsum("td,cd->tc", piece, out_w, preferred_element_type=jnp.float32)
    grad_mixed = lax.psum(product, "width")
    gain_out_grad = jnp.sum(grad_mixed * gated * scale_out, axis=0)
    inner_total = lax.psum(jnp.sum(grad_mixed * gain_out * gated, axis=1), "head")
    cubed = scale_out * scale_out * scale_out
    grad_gated = scale_out * gain_out * grad_mixed - gated * cubed / INNER * inner_total[:, None]
    (
        grad_zx_seq,
        grad_bc_seq,
        grad_dt_seq,
        kernel_x_grad,
        kernel_bc_grad,
        bias_grad,
        rate_grad,
        skip_grad,
    ) = mix_pull(grad_gated)
    grad_zx = grad_zx_seq.reshape(total_rows, local_heads * 2 * HEADDIM).astype(jnp.bfloat16)
    dt_columns = jnp.zeros((total_rows, HEADS), jnp.float32)
    dt_columns = lax.dynamic_update_slice_in_dim(
        dt_columns, grad_dt_seq.reshape(total_rows, local_heads), head_index * local_heads, 1
    )
    grad_bcdt_head = jnp.concatenate(
        [grad_bc_seq.reshape(total_rows, 2 * STATE), dt_columns], axis=1
    )
    weight_zx = jnp.einsum(
        "td,tc->dc", gathered, grad_zx, preferred_element_type=jnp.float32
    ).reshape(half_width, local_heads, 2 * HEADDIM)
    normed_part = jnp.einsum("tc,dc->td", grad_zx, w_zx, preferred_element_type=jnp.float32)
    grad_normed, bcdt_summed = (
        lax.psum_scatter(normed_part, "head", scatter_dimension=0, tiled=True),
        lax.psum_scatter(grad_bcdt_head, "head", scatter_dimension=0, tiled=True),
    )
    bcdt_low = bcdt_summed.astype(jnp.bfloat16)
    grad_normed = grad_normed + jnp.einsum(
        "tk,dk->td", bcdt_low, in_bcdt, preferred_element_type=jnp.float32
    )
    weight_bcdt = jnp.einsum("td,tk->dk", normed, bcdt_low, preferred_element_type=jnp.float32)
    gain_in_grad = jnp.sum(grad_normed * source * scale, axis=0)
    across = lax.psum(jnp.sum(grad_normed * gain_in * source, axis=1), "width")
    scale_cubed = scale * scale * scale
    grad_hidden = (
        grad_out + scale * gain_in * grad_normed - source * scale_cubed / D * across[:, None]
    ).astype(jnp.bfloat16)
    summed_dp = lax.psum(
        (weight_zx, acc_weight, kernel_x_grad, bias_grad, rate_grad, skip_grad, gain_out_grad), "dp"
    )
    summed_all = lax.psum((weight_bcdt, gain_in_grad, kernel_bc_grad), ("dp", "head"))
    return (
        out_hidden,
        grad_hidden,
        summed_all[1],
        summed_dp[0],
        summed_all[0],
        summed_dp[2],
        summed_all[2],
        summed_dp[3],
        summed_dp[4],
        summed_dp[5],
        summed_dp[6],
        summed_dp[1],
    )


BF = jnp.bfloat16
F32 = jnp.float32
Q = 128
HALO = 16
NEG = -1e30
MESH = pl.DeviceIdType.MESH
VMEM = 60 * 1024 * 1024


def dot(a, b, prec=None):
    return lax.dot_general(a, b, (((1,), (0,)), ((), ())), precision=prec, preferred_element_type=F32)


def dot_t(a, b, prec=None):
    return lax.dot_general(a, b, (((1,), (1,)), ((), ())), precision=prec, preferred_element_type=F32)


def t_dot(a, b, prec=None):
    return lax.dot_general(a, b, (((0,), (0,)), ((), ())), precision=prec, preferred_element_type=F32)


def split2(v, axis=1):
    hi = v.astype(BF)
    lo = (v - hi.astype(F32)).astype(BF)
    return jnp.concatenate([hi, lo], axis=axis)


def dot_split(v, m):
    hi = v.astype(BF)
    lo = (v - hi.astype(F32)).astype(BF)
    return dot(hi, m) + dot(lo, m)


def split_dot(m, v):
    hi = v.astype(BF)
    lo = (v - hi.astype(F32)).astype(BF)
    return dot(m, hi) + dot(m, lo)


def sigmoid(v):
    return 1.0 / (1.0 + jnp.exp(-v))


def tri(kind):
    row = lax.broadcasted_iota(jnp.int32, (Q, Q), 0)
    col = lax.broadcasted_iota(jnp.int32, (Q, Q), 1)
    return {"ge": row >= col, "le": row <= col, "gt": row > col}[kind]


def slot_heads(heads, per):
    nz = heads // per
    own = HEADS // nz
    bits = per.bit_length() - 1
    slot = lax.broadcasted_iota(jnp.int32, (heads, HEADS), 0)
    head = lax.broadcasted_iota(jnp.int32, (heads, HEADS), 1)
    z = (lax.axis_index("head") - (slot >> bits)) & (nz - 1)
    m = (slot & (per - 1)) ^ lax.axis_index("dp")
    return (head == z * own + lax.axis_index("width") * per + m).astype(F32)


def prep_kernel(
    per, zx, ow, bcdt, gain, cx, scal, gn,
    first_o, first2_o, rest_o, rest2_o, out_o, out2_o, bcdt_o, table_o,
):
    di = lax.axis_index("dp")
    wi = lax.axis_index("width")
    wide = 2 * HEADDIM
    for m in range(per):
        for w, whole_o, some_o, o_o in (
            (wi, first_o, rest_o, out_o), (1 - wi, first2_o, rest2_o, out2_o)
        ):
            head = w * per + jnp.bitwise_xor(di, m)
            v = jnp.transpose(zx[:, pl.ds(pl.multiple_of(head * wide, wide), wide)])
            if m == 0:
                whole_o[...] = v
            else:
                some_o[m - 1] = v
            o_o[m] = ow[pl.ds(pl.multiple_of(head * HEADDIM, HEADDIM), HEADDIM), :]
    n = bcdt.shape[1]
    bcdt_o[0:n, :] = jnp.transpose(bcdt[...])
    bcdt_o[n:, :] = jnp.broadcast_to(gain[...], (HALO, gain.shape[1]))
    rows = jnp.concatenate(
        [cx[...].astype(F32), gn[...].astype(F32), scal[...]], axis=0
    )
    half = rows.shape[1] // 2
    rows = jnp.where(wi == 0, rows[:, :half], rows[:, half:])
    step = 1
    while step < per:
        size = HEADDIM * step
        parts = [rows[:, i * size : (i + 1) * size] for i in range(half // size)]
        swapped = jnp.concatenate([parts[i ^ 1] for i in range(len(parts))], axis=1)
        rows = jnp.where(jnp.bitwise_and(di, step) != 0, swapped, rows)
        step *= 2
    table_o[...] = rows


def entry_kernel(
    per, hm, ho, hh, bcdt, table, cbc, sel,
    xn_o, xnh_o, r_o, raw_o, rawh_o, u_o, b_o, c_o, dt_o, sig_o, cl_o, clt_o, tot_o,
    dt2_o, e12_o, tl2_o, dttl2_o, ec2_o, edt2_o, rate_o, wdt_o, buf,
):
    rows = hm.shape[0]
    state = b_o.shape[1]
    per_head = dot(table[...], sel[...], HIGH)
    bias = per_head[5:6, :]
    rate = -jnp.exp(per_head[6:7, :])
    rate_o[...] = rate
    wbc = bcdt.at[0 : 2 * state, :]
    wdt_o[...] = dot(
        slot_heads(rate.shape[1], per).astype(BF), bcdt[2 * state : 2 * state + HEADS, :]
    ).astype(BF)
    wdt = wdt_o
    gain = bcdt[2 * state + HEADS : 2 * state + HEADS + 1, :].astype(F32)
    blocks = rows // Q
    lower = tri("ge").astype(F32)

    def norm(left, right):
        h = jnp.concatenate([left, right], axis=1).astype(F32)
        r = lax.rsqrt(jnp.mean(h * h, axis=1, keepdims=True) + EPS)
        return (h * r * gain).astype(BF), r

    half = hm.shape[1]
    xnh, _ = norm(hh[:, :half], hh[:, half:])
    xnh_o[...] = xnh
    buf[0:HALO, :] = dot_t(xnh, wbc[...])
    rawh_o[...] = buf[0:HALO, :]

    def first(i, carry):
        here = pl.ds(pl.multiple_of(i * Q, Q), Q)
        xn, r = norm(hm[here, :], ho[here, :])
        xn_o[here, :] = xn
        r_o[here, :] = r
        raw = dot_t(xn, wbc[...])
        raw_o[here, :] = raw
        buf[pl.ds(pl.multiple_of(HALO + i * Q, HALO), Q), :] = raw
        steps = dot_t(xn, wdt[...]) + bias
        dt = jax.nn.softplus(steps)
        dt_o[here, :] = dt
        sig_o[here, :] = sigmoid(steps)
        da = dt * rate
        cl_o[here, :] = dot(lower, da, HIGH)
        clt_o[:, here] = lax.dot_general(
            da, lower, (((0,), (1,)), ((), ())), precision=HIGH, preferred_element_type=F32
        )
        return carry

    lax.fori_loop(0, blocks, first, 0, unroll=2)

    def second(i, carry):
        here = pl.ds(pl.multiple_of(i * Q, Q), Q)
        win = buf[pl.ds(pl.multiple_of(i * Q, Q), Q + HALO), :]
        u = jnp.zeros((Q, win.shape[1]), F32)
        for k in range(4):
            u = u + cbc[k : k + 1, :] * win[HALO - 3 + k : HALO - 3 + k + Q, :]
        u_o[here, :] = u
        v = u * sigmoid(u)
        b_o[here, :] = v[:, :state].astype(BF)
        c_o[here, :] = v[:, state:].astype(BF)
        return carry

    lax.fori_loop(0, blocks, second, 0, unroll=2)
    tots = [cl_o[i * Q + Q - 1 : i * Q + Q, :] for i in range(blocks)]
    ctot = functools.reduce(lambda x, y: x + y, tots)
    heads = clt_o.shape[0]
    column = functools.reduce(
        lambda x, y: x + y, [clt_o[:, i * Q + Q - 1 : i * Q + Q] for i in range(blocks)]
    )
    hi = column.astype(BF)
    mid = (column - hi.astype(F32)).astype(BF)
    low = (column - hi.astype(F32) - mid.astype(F32)).astype(BF)
    lane = lax.broadcasted_iota(jnp.int32, (heads, tot_o.shape[1]), 1)
    tot_o[...] = jnp.where(
        lane == 0,
        hi.astype(F32),
        jnp.where(lane == 1, mid.astype(F32), jnp.where(lane == 2, low.astype(F32), 0.0)),
    ).astype(BF)
    off = jnp.zeros_like(ctot)
    for i in range(blocks):
        here = slice(i * Q, i * Q + Q)
        cl = cl_o[here, :]
        dt = dt_o[here, :]
        tail = jnp.exp(tots[i] - cl)
        dt2_o[here, :] = split2(dt)
        e12_o[here, :] = split2(jnp.exp(cl))
        tl2_o[here, :] = split2(tail)
        dttl2_o[here, :] = split2(dt * tail)
        ec2_o[here, :] = split2(jnp.exp(cl + off))
        edt2_o[here, :] = split2(dt * jnp.exp(ctot - cl - off))
        off = off + tots[i]


def decay(cl, clt, h, mask):
    return jnp.exp(jnp.where(mask, cl[:, h : h + 1] - clt[h : h + 1, :], NEG))


def lane_masks():
    lane = lax.broadcasted_iota(jnp.int32, (1, Q), 1)
    low = (lane < HEADDIM).astype(F32)
    return low.astype(BF), (1.0 - low).astype(BF)


def project_kernel(s, per, *refs):
    xn, xnh, pieces, cw, dt2, edt2, ex, b, rest = take(refs, 0, 0, per, 0, 0, 0, 0, 0)
    wz_o, wx_o, z_o, xr_o, xrh_o, u_o, xdt_o, s_o, buf, acc = rest
    rows = z_o.shape[0]
    gc = per * HEADDIM
    cols = slice(s * gc, s * gc + gc)
    wx = jnp.concatenate([v[HEADDIM:, :] for v in pieces], axis=0)
    wz = jnp.concatenate([v[:HEADDIM, :] for v in pieces], axis=0)

    @pl.when(pl.program_id(0) == 0)
    def _():
        wz_o[...] = wz
        wx_o[...] = wx
        xh = dot_t(xnh[...], wx)
        buf[0:HALO, :] = xh
        xrh_o[...] = xh
        acc[...] = jnp.zeros_like(acc)

    @pl.when(pl.program_id(0) > 0)
    def _():
        buf[0:HALO, :] = buf[rows : rows + HALO, :]

    buf[HALO:, :] = dot_t(xn[...], wx)
    z_o[...] = dot_t(xn[...], wz)
    for i in range(rows // Q):
        here = slice(i * Q, i * Q + Q)
        win = buf[i * Q : i * Q + Q + HALO, :]
        u = jnp.zeros((Q, gc), F32)
        for k in range(4):
            u = u + cw[k : k + 1, cols] * win[HALO - 3 + k : HALO - 3 + k + Q, :]
        xr_o[here, :] = win[HALO:, :].astype(BF)
        u_o[here, :] = u
        xs = u * sigmoid(u)
        xdt_o[here, :] = (xs * dot(dt2[here, :], ex[:, cols])).astype(BF)
        acc[...] += t_dot((xs * dot(edt2[here, :], ex[:, cols])).astype(BF), b[here, :])

    @pl.when(pl.program_id(0) == pl.num_programs(0) - 1)
    def _():
        s_o[...] = acc[...].astype(BF)


def inside_kernel(s, per, xdt, b, c, cl, clt, y_o):
    mask = tri("ge")
    low, high = lane_masks()
    for i in range(xdt.shape[0] // Q):
        rows = slice(i * Q, i * Q + Q)
        g = dot_t(c[rows, :], b[rows, :])
        clv, cltv = cl[rows, :], clt[:, rows]
        for p in range(xdt.shape[1] // Q):
            here = slice(p * Q, p * Q + Q)
            h = s * per + 2 * p
            ws = [(g * decay(clv, cltv, j, mask)).astype(BF) for j in (h, h + 1)]
            x = xdt[rows, here]
            y_o[rows, here] = dot(
                jnp.concatenate(ws, axis=1), jnp.concatenate([x * low, x * high], axis=0)
            ).astype(BF)


def head_scale(clt, first, per, state):
    return jnp.concatenate(
        [
            jnp.broadcast_to(jnp.exp(clt[h : h + 1, Q - 1 : Q]), (HEADDIM, state))
            for h in range(first, first + per)
        ],
        axis=0,
    )


def from_messages(messages, sign, groups, per, state, store, valid=None):
    nz = len(messages) + 1
    gc = per * HEADDIM
    top = nz * gc
    totals = [
        sum(m[top:, i : i + 1].astype(F32) for i in range(3)) for m in messages
    ]
    for at, j in enumerate(groups):
        total = jnp.zeros((gc, state), F32)
        faded = jnp.zeros((per, 1), F32)
        for k in range(1, nz):
            there = (j - sign * k) % nz
            scale = jnp.exp(faded)
            scale = jnp.concatenate(
                [jnp.broadcast_to(scale[h : h + 1, :], (HEADDIM, state)) for h in range(per)],
                axis=0,
            )
            part = scale * messages[k - 1][there * gc : there * gc + gc, :].astype(F32)
            if valid is not None:
                part = jnp.where(valid(k), part, 0.0)
            total = total + part
            faded = faded + totals[k - 1][there * per : there * per + per, :]
        store[at * gc : at * gc + gc, :] = total


def carry_kernel(groups, per, *refs):
    n = len(groups)
    y_in, us, z, dyn, b, c, clt, e12, dttl2, messages, dsk, gain, ex, rest = take(
        refs, n, n, n, 0, 0, 0, 0, 0, 0, n - 1, 0, 0, 0
    )
    ys_o, st_o, rest = take(rest, n, n)
    gg_o, sum_o, s = rest
    gc = per * HEADDIM

    @pl.when(pl.program_id(0) == 0)
    def _():
        from_messages(messages, 1, groups, per, s.shape[1], s)

    square = jnp.zeros((Q, gc), F32)
    inner = jnp.zeros((Q, gc), F32)
    for j in groups:
        here = slice(j * gc, j * gc + gc)
        sv = s[here, :]
        sb = sv.astype(BF)
        st_o[j][0] = sb
        x = us[j][...]
        x = x * sigmoid(x)
        e1 = dot(e12[...], ex[:, here])
        y = y_in[j][...].astype(F32) + e1 * dot_t(c[...], sb) + dsk[:, here] * x
        ys_o[j][...] = y
        xt = (x * dot(dttl2[...], ex[:, here])).astype(BF)
        s[here, :] = head_scale(clt, j * per, per, sv.shape[1]) * sv + t_dot(xt, b[...])
        zz = z[j][...]
        gz = y * (zz * sigmoid(zz))
        gg = gz * gain[:, here]
        gg_o[:, here] = gg.astype(BF)
        square = square + gz * gz
        inner = inner + gg * dyn[:, here]
    lane = lax.broadcasted_iota(jnp.int32, (Q, 2), 1)
    sum_o[...] = jnp.where(
        lane == 0,
        jnp.sum(square, axis=1, keepdims=True),
        jnp.sum(inner, axis=1, keepdims=True),
    )


def gate_kernel(groups, per, *refs):
    n = len(groups)
    ys, z, us, dyn, sums, sums2, gain, ec2, ex, c, rest = take(refs, n, n, n, *[0] * 7)
    hidden, branch, branch2, limit, rest = take(rest, 0, 0, 0, 0)
    dys_o, rest = take(rest, n)
    dz_o, yn_o, ds_o, gn_o, sk_o, out_o, acc = rest
    gc = per * HEADDIM

    @pl.when(pl.program_id(0) == 0)
    def _():
        acc[...] = jnp.zeros_like(acc)
        gn_o[...] = jnp.zeros_like(gn_o)
        sk_o[...] = jnp.zeros_like(sk_o)

    count = n * gc * 2
    both = sums[...] + sums2[...]
    r2 = lax.rsqrt(both[:, 0:1] / count + EPS)
    pull = both[:, 1:2] * (r2 * r2 * r2) / count
    row = lax.broadcasted_iota(jnp.int32, (Q, 1), 0) + pl.program_id(0) * Q
    keep = jnp.where(row < limit[0, 0], r2, 0.0)
    out_o[...] = (
        hidden[...].astype(F32) + keep * (branch[...] + branch2[...].astype(F32))
    ).astype(BF)
    for j in groups:
        here = slice(j * gc, j * gc + gc)
        gn = gain[:, here]
        zz = z[j][...]
        sz = sigmoid(zz)
        silu = zz * sz
        y = ys[j][...]
        gz = y * silu
        dy_n = dyn[:, here]
        gr = gz * r2
        yn_o[:, here] = (gr * gn).astype(BF)
        gn_o[:, here] += jnp.sum(dy_n * gr, axis=0, keepdims=True)
        dgz = r2 * gn * dy_n - gz * pull
        dys = dgz * silu
        dys_o[j][...] = dys.astype(BF)
        dz_o[:, here] = (dgz * y * (sz + silu * (1.0 - sz))).astype(BF)
        x = us[j][...]
        x = x * sigmoid(x)
        sk_o[:, here] += jnp.sum(dys * x, axis=0, keepdims=True)
        acc[here, :] += t_dot((dys * dot(ec2[...], ex[:, here])).astype(BF), c[...])

    @pl.when(pl.program_id(0) == pl.num_programs(0) - 1)
    def _():
        ds_o[...] = acc[...].astype(BF)


def line_peers(count, sign):
    z = lax.axis_index("head")
    return [{"head": lax.rem(z + sign * k + count, count)} for k in range(1, count)]


def plane_peers(count):
    d = lax.axis_index("dp")
    return [{"dp": jnp.bitwise_xor(d, m)} for m in range(1, count)]


def meet(peers):
    barrier = pltpu.get_barrier_semaphore()
    for peer in peers:
        pl.semaphore_signal(barrier, inc=1, device_id=peer, device_id_type=MESH)
    pl.semaphore_wait(barrier, len(peers))


def remote(source, target, sends, receives, i, peer):
    return pltpu.make_async_remote_copy(
        src_ref=source,
        dst_ref=target,
        send_sem=sends.at[i],
        recv_sem=receives.at[i],
        device_id=peer,
        device_id_type=MESH,
    )


def inside_back_kernel(groups, per, *refs):
    n = len(groups)
    xdt, dys, b, c, cl, clt, message, early, rest = take(refs, n, n, 0, 0, 0, 0, 0, per)
    dx_o, rest = take(rest, n)
    db_o, dc_o, da_o, rest = take(rest, 0, 0, 0)
    messages_o, early_o, rest = take(rest, n - 1, per - 1)
    kt, sends, receives = rest
    nz = n

    def copies():
        found = []
        for i, peer in enumerate(line_peers(nz, -1)):
            found.append(remote(message, messages_o[i], sends, receives, i, peer))
        for i, peer in enumerate(plane_peers(per)):
            found.append(remote(early[i + 1], early_o[i], sends, receives, nz - 1 + i, peer))
        return found

    @pl.when(pl.program_id(0) == 0)
    def _():
        meet(line_peers(nz, -1) + plane_peers(per))
        for copy in copies():
            copy.start()

    @pl.when(pl.program_id(0) == pl.num_programs(0) - 1)
    def _():
        for copy in copies():
            copy.wait()

    mask = tri("ge")
    low, high = lane_masks()
    g = dot_t(c[...], b[...])
    clv, cltv = cl[...], clt[...]
    heads = clt.shape[0]
    lane = lax.broadcasted_iota(jnp.int32, (Q, heads), 1)
    dg = jnp.zeros((Q, Q), F32)
    rsum = jnp.zeros((Q, heads), F32)
    for s in groups:
        for p in range(per // 2):
            here = slice(p * Q, p * Q + Q)
            x = xdt[s][:, here]
            dy = dys[s][:, here]
            pp = dot_t(dy, jnp.concatenate([x * low, x * high], axis=0))
            ws = []
            for j in range(2):
                h = s * per + 2 * p + j
                ell = decay(clv, cltv, h, mask)
                ws.append((g * ell).astype(BF))
                pe = pp[:, j * Q : j * Q + Q] * ell
                dg = dg + pe
                m = pe * g
                rsum = jnp.where(lane == h, jnp.sum(m, axis=1, keepdims=True), rsum)
                kt[h : h + 1, :] = jnp.sum(m, axis=0, keepdims=True)
            dx_o[s][:, here] = t_dot(
                jnp.concatenate(ws, axis=0), jnp.concatenate([dy * low, dy * high], axis=0)
            )
    dgb = dg.astype(BF)
    dc_o[...] = dot(dgb, b[...])
    db_o[...] = t_dot(dgb, c[...])
    upper = tri("le").astype(F32)
    da_o[...] = dot(upper, rsum, HIGH) - dot_t(upper, kt[...], HIGH)


def conv_back(d, nxt, taps, raw, rawh, grad_o, out_o, outh_o, last):
    win = jnp.concatenate([d, nxt[...]], axis=0)
    back = jnp.zeros_like(d)
    sums = []
    for k in range(4):
        part = win[3 - k : 3 - k + Q, :]
        back = back + taps[k : k + 1, :] * part
        sums.append(jnp.sum(raw * part, axis=0, keepdims=True))
    grad_o[...] += jnp.concatenate(sums, axis=0)
    out_o[...] = back.astype(BF)
    nxt[...] = d[0:8, :]

    @pl.when(last)
    def _():
        win_h = jnp.concatenate([jnp.zeros((HALO, d.shape[1]), F32), d[0:8, :]], axis=0)
        back_h = jnp.zeros((HALO, d.shape[1]), F32)
        sums_h = []
        for k in range(4):
            part = win_h[3 - k : 3 - k + HALO, :]
            back_h = back_h + taps[k : k + 1, :] * part
            sums_h.append(jnp.sum(rawh[...] * part, axis=0, keepdims=True))
        grad_o[...] += jnp.concatenate(sums_h, axis=0)
        outh_o[...] = back_h.astype(BF)


def back_kernel(groups, per, final, *refs):
    n = len(groups)
    dxi, dys, u, xr, xrh, st, rest = take(refs, n, n, n, n, n, n)
    (b, c, dbi, dci, dai, dti, dt, sig, clt, dt2, e12, tl2), rest = rest[:12], rest[12:]
    (ubc, braw, brawh, cw, cbc, rate, dsk, ex, er), rest = rest[:9], rest[9:]
    nz = dt.shape[1] // per
    messages, _, _, dx_o, dxh_o, gcx_o, rest = take(rest, nz - 1, 0, 0, n, n, n)
    db_o, dc_o, dt_o, ga_o, gbias_o, bc_o, bch_o, gcb_o, ds, vs = rest[:10]
    du_next, rest = take(rest[10:], n)
    (db_next,) = rest
    step = pl.program_id(0)
    blocks = pl.num_programs(0)
    heads = dt.shape[1]
    state = b.shape[1]
    gc = per * HEADDIM

    @pl.when(step == 0)
    def _():
        z = lax.axis_index("head")
        from_messages(messages, -1, groups, per, state, ds, lambda k: z + k < nz)
        for i in range(n):
            du_next[i][...] = jnp.zeros_like(du_next[i])
            gcx_o[i][...] = jnp.zeros_like(gcx_o[i])
        vs[...] = jnp.zeros_like(vs)
        db_next[...] = jnp.zeros_like(db_next)
        gcb_o[...] = jnp.zeros_like(gcb_o)
        ga_o[...] = jnp.zeros_like(ga_o)
        gbias_o[...] = jnp.zeros_like(gbias_o)

    last = step == blocks - 1
    rsum = jnp.zeros((Q, heads), F32)
    gsum = jnp.zeros((Q, heads), F32)
    ddt = jnp.zeros((Q, heads), F32)
    dbs = dbi[...]
    dcs = dci[...]
    for i, s in enumerate(groups):
        here = slice(s * gc, s * gc + gc)
        mine = slice(i * gc, i * gc + gc)
        ehere = er[here, :]
        sb = st[i][0]
        dsv = ds[mine, :]
        dsb = dsv.astype(BF)
        dy = dys[i][...].astype(F32)
        dye = dy * dot(e12[...], ex[:, here])
        dyb = dye.astype(BF)
        rsum = rsum + dot((dye * dot_t(c[...], sb)).astype(BF), ehere)
        dcs = dcs + dot(dyb, sb)
        bds = dot_t(b[...], dsb)
        tail = dot(tl2[...], ex[:, here])
        dtx = dot(dt2[...], ex[:, here])
        uu = u[i][...]
        su = sigmoid(uu)
        xs = uu * su
        xt = xs * dtx * tail
        gsum = gsum + dot((xt * bds).astype(BF), ehere)
        dbs = dbs + dot(xt.astype(BF), dsb)
        dxdt = dxi[i][...] + tail * bds
        ddt = ddt + dot((dxdt * xs).astype(BF), ehere)
        eds = head_scale(clt, s * per, per, state) * dsv
        ev = eds * sb.astype(F32)
        for j in range(per):
            h = s * per + j
            vs[h : h + 1, :] = jnp.sum(
                ev[j * HEADDIM : (j + 1) * HEADDIM, :], axis=0, keepdims=True
            )
        ds[mine, :] = eds + t_dot(dyb, c[...])
        du = (dxdt * dtx + dsk[:, here] * dy) * (su + xs * (1.0 - su))
        conv_back(
            du, du_next[i], cw.at[:, here], xr[i][...].astype(F32), xrh[i], gcx_o[i], dx_o[i], dxh_o[i], last
        )
    col = lax.broadcasted_iota(jnp.int32, (1, heads), 1)
    mine = functools.reduce(
        jnp.logical_or, [(col >= s * per) & (col < s * per + per) for s in groups]
    )
    vrow = dot_t(jnp.ones((8, state), F32), vs[...], HIGH)
    da = (
        dai[...]
        + split_dot(tri("le").astype(BF), rsum)
        + split_dot(tri("gt").astype(BF), gsum)
        + vrow[0:1, :]
    )
    da = jnp.where(mine, da, 0.0)
    draw = (rate[...] * da + ddt) * sig[...]
    dt_o[...] = (dti[...] + draw).astype(dt_o.dtype)
    ga_o[...] += jnp.sum(da * dt[...], axis=0, keepdims=True)
    gbias_o[...] += jnp.sum(draw, axis=0, keepdims=True)
    db_o[...] = dbs
    dc_o[...] = dcs
    if final:
        d = jnp.concatenate([dbs, dcs], axis=1)
        v = ubc[...]
        sv = sigmoid(v)
        conv_back(
            d * (sv + v * sv * (1.0 - sv)), db_next, cbc, braw[...], brawh, gcb_o, bc_o, bch_o, last
        )


def sum_products_kernel(n, *refs):
    a, w, _, rest = take(refs, n, n, 0)
    left_o, right_o = rest
    total = dot(a[0][...], w[0][...])
    for i in range(1, n):
        total = total + dot(a[i][...], w[i][...])
    half = left_o.shape[1]
    left_o[...] = total[:, :half]
    right_o[...] = total[:, half:].astype(BF)


def pull_kernel(per, nz, *refs):
    cot, cot2, limit, own, others, rest = take(refs, 0, 0, 0, per, per)
    w_o, mask_o, dyn_o = rest
    rows = cot.shape[0]
    half = cot.shape[1]

    @pl.when(pl.program_id(0) == 0)
    def _():
        for m in range(per):
            w_o[m * HEADDIM : (m + 1) * HEADDIM, :] = own[m][...]
            for s in range(1, nz):
                at = (s * per + m) * HEADDIM
                w_o[at : at + HEADDIM, :] = others[m][(s - 1) * HEADDIM : s * HEADDIM, :]

    row = lax.broadcasted_iota(jnp.int32, (rows, 1), 0) + pl.program_id(0) * rows
    keep = row < limit[0, 0]
    for i, v in enumerate((cot, cot2)):
        mask_o[:, i * half : i * half + half] = jnp.where(keep, v[...].astype(F32), 0.0).astype(BF)
    dyn_o[...] = dot_t(mask_o[...], w_o[...])


def early_grad_kernel(per, yn, masked, dz, xn, *outs):
    g_out = t_dot(yn[...], masked[...]).astype(BF)
    g_z = t_dot(dz[...], xn[...]).astype(BF)
    for m in range(per):
        here = slice(m * HEADDIM, (m + 1) * HEADDIM)
        outs[m][0, :HEADDIM, :] = g_out[here, :]
        outs[m][0, HEADDIM:, :] = g_z[here, :]


def late_grad_kernel(n, per, final, *refs):
    _, dx, dxh, xn, xnh, rest = take(refs, 0, n, n, 0, 0)
    if final:
        dbc, dbch, ddt, spread, rest = take(rest, 0, 0, 0, 0)
        outs, rest = take(rest, per)
        gbc, gdt = rest
        bc_rows = gbc.shape[0] // per
        dt_rows = gdt.shape[0] // per
        gbc[...] = t_dot(dbc[...], xn[...]) + t_dot(dbch[...], xnh[...])
        gdt[...] = split_dot(spread[...], t_dot(ddt[...], xn[...]))
    else:
        outs, rest = take(rest, per)
    for i in range(n):
        g = (t_dot(dx[i][...], xn[...]) + t_dot(dxh[i][...], xnh[...])).astype(BF)
        for m in range(per):
            outs[m][i * HEADDIM : (i + 1) * HEADDIM, :] = g[m * HEADDIM : (m + 1) * HEADDIM, :]
    if final:
        me = lax.axis_index("dp")
        for m in range(per):
            at = jnp.bitwise_xor(me, m)
            v = gbc[pl.ds(pl.multiple_of(at * bc_rows, bc_rows), bc_rows), :]
            w = gdt[pl.ds(pl.multiple_of(at * dt_rows, dt_rows), dt_rows), :]
            w = jnp.concatenate([w, jnp.zeros((HALO - dt_rows, w.shape[1]), F32)], axis=0)
            outs[m][n * HEADDIM : n * HEADDIM + bc_rows, :] = v.astype(BF)
            outs[m][n * HEADDIM + bc_rows :, :] = w.astype(BF)


def shape(dims, dtype=F32):
    return jax.ShapeDtypeStruct(dims, dtype)


def whole(array):
    rank = len(array.shape)
    return pl.BlockSpec(array.shape, lambda *_: (0,) * rank)


def params():
    return pltpu.CompilerParams(vmem_limit_bytes=VMEM)


def cost(us):
    return pl.CostEstimate(flops=int(us * 1.0e8), bytes_accessed=int(us * 1.0e3), transcendentals=0)


def take(refs, *counts):
    out, at = [], 0
    for n in counts:
        out.append(refs[at] if n == 0 else refs[at : at + n])
        at += max(n, 1)
    return out + [refs[at:]]


def sequence_device(
    hidden, lengths, cotangent, norm_gain, in_zx, in_bcdt, conv_x, conv_bc,
    dt_bias, a_log, d_skip, gnorm_gain, out_w,
):
    rows, half = hidden.shape
    own_heads = in_zx.shape[1]
    nz = lax.axis_size("head")
    ndp = lax.axis_size("dp")
    zi = lax.axis_index("head")
    di = lax.axis_index("dp")
    wi = lax.axis_index("width")
    per = ndp
    heads = nz * per
    channels = heads * HEADDIM
    model = 2 * half
    blocks = rows // Q

    def swap(v):
        return lax.ppermute(v, "width", [(0, 1), (1, 0)])

    def turn(v, s):
        return lax.ppermute(v, "head", [(i, (i + s) % nz) for i in range(nz)])

    def shift(v, s):
        return lax.ppermute(v, "head", [(i, i + s) for i in range(nz) if 0 <= i + s < nz])

    def cross(v, m):
        return lax.ppermute(v, "dp", [(i, i ^ m) for i in range(ndp)])

    def pick(v, index):
        return lax.dynamic_index_in_dim(v, index, 0, keepdims=False)

    gc = per * HEADDIM
    groups = tuple(range(nz))

    onehot = np.kron(np.eye(heads), np.ones((1, HEADDIM)))
    ex = jnp.asarray(np.concatenate([onehot, onehot], axis=0), BF)
    er = jnp.asarray(onehot.T, BF)
    sel = jnp.asarray(onehot.T * (np.arange(channels) % HEADDIM == 0)[:, None], F32)

    def after_that(v, w):
        return v + (w[(0,) * w.ndim] * 0).astype(v.dtype)

    def beside(mine, other):
        return jnp.concatenate([mine, swap(other)], axis=-1)

    scal = jnp.repeat(jnp.stack([dt_bias, a_log, d_skip]), HEADDIM, axis=1)
    piece = shape((2 * HEADDIM, half), BF)
    some = shape((per - 1, 2 * HEADDIM, half), BF)
    outs = shape((per, HEADDIM, half), BF)
    first, first2, rest, rest2, out_mine, out_mine2, bcdt_t, table = pl.pallas_call(
        functools.partial(prep_kernel, per),
        out_shape=[
            piece, piece, some, some, outs, outs,
            shape((2 * STATE + HEADS + HALO, half), BF), shape((8, gc)),
        ],
        compiler_params=params(),
        cost_estimate=cost(4),
        name="prep",
    )(
        in_zx.reshape(half, -1), out_w, in_bcdt, norm_gain[None], conv_x, scal,
        gnorm_gain[None],
    )
    own_first = beside(first, first2)
    along = [turn(own_first, s) for s in range(1, nz)]
    hidden_o = swap(hidden)
    bcdt_t = beside(bcdt_t, bcdt_t)
    table = jnp.concatenate([table] + [turn(table, s) for s in range(1, nz)], axis=1)
    rest = beside(rest, rest2)
    pieces = [[own_first] + [rest[m] for m in range(per - 1)]]
    for got in along:
        pieces.append([got] + [cross(got, m) for m in range(1, per)])
    wbc = bcdt_t[: 2 * STATE]
    taps, gain_out, skip = table[:4], table[4:5], table[7:8]
    taps_bc = conv_bc.astype(F32)
    slot = jnp.arange(heads)
    slot_head = ((zi - slot // per) % nz) * own_heads + wi * per + ((slot % per) ^ di)
    pick_heads = (slot_head[:, None] == jnp.arange(HEADS)[None, :]).astype(F32)

    edge = jnp.concatenate([hidden[rows - HALO :], hidden_o[rows - HALO :]], axis=1)
    edge = shift(edge, 1)
    ext_rows = rows + HALO
    narrow = shape((rows, 2 * heads), BF)
    (
        xn, xnh, r, braw, brawh, ubc, bs, cs, dt, sig, cl, clt, totals,
        dt2, e12, tl2, dttl2, ec2, edt2, rate, wdt,
    ) = pl.pallas_call(
        functools.partial(entry_kernel, per),
        out_shape=[
            shape((rows, model), BF), shape((HALO, model), BF), shape((rows, 1)),
            shape((rows, 2 * STATE)),
            shape((HALO, 2 * STATE)), shape((rows, 2 * STATE)), shape((rows, STATE), BF),
            shape((rows, STATE), BF), shape((rows, heads)), shape((rows, heads)),
            shape((rows, heads)), shape((heads, rows)), shape((heads, STATE), BF),
            narrow, narrow, narrow, narrow, narrow, narrow, shape((1, heads)),
            shape((heads, model), BF),
        ],
        scratch_shapes=[pltpu.VMEM((ext_rows, 2 * STATE), F32)],
        compiler_params=params(),
        cost_estimate=cost(12),
        name="entry",
    )(hidden, hidden_o, edge, bcdt_t, table, taps_bc, sel)

    def send_states(local, sign):
        message = jnp.concatenate([*local, totals], axis=0)
        return [shift(message, sign * k) for k in range(1, nz)]

    cut = rows // 2 if rows // 2 % Q == 0 else rows
    part = shape((rows, gc), BF)
    full = shape((rows, channels))
    step = lambda i: (i, 0)
    fix = lambda i: (0, 0)
    gspec = pl.BlockSpec((cut, gc), step)
    wz, wx, z, xr, xrh, u, xdt, s_local, y_in = ([] for _ in range(9))
    for s in groups:
        out = pl.pallas_call(
            functools.partial(project_kernel, s, per),
            grid=(rows // cut,),
            in_specs=[
                pl.BlockSpec((cut, model), step),
                pl.BlockSpec((HALO, model), fix),
                *[whole(v) for v in pieces[s]], whole(taps), pl.BlockSpec((cut, 2 * heads), step),
                pl.BlockSpec((cut, 2 * heads), step), whole(ex), pl.BlockSpec((cut, STATE), step),
            ],
            out_specs=[
                pl.BlockSpec((gc, model), fix), pl.BlockSpec((gc, model), fix), gspec, gspec,
                pl.BlockSpec((HALO, gc), fix), gspec, gspec, pl.BlockSpec((gc, STATE), fix),
            ],
            out_shape=[
                shape((gc, model), BF), shape((gc, model), BF), shape((rows, gc)), part,
                shape((HALO, gc)),
                shape((rows, gc)), part, shape((gc, STATE), BF),
            ],
            scratch_shapes=[pltpu.VMEM((cut + HALO, gc), F32), pltpu.VMEM((gc, STATE), F32)],
            compiler_params=params(),
            cost_estimate=cost(5),
            name="project",
        )(xn, xnh, *pieces[s], taps, dt2, edt2, ex, bs)
        for keep, v in zip((wz, wx, z, xr, xrh, u, xdt, s_local), out):
            keep.append(v)
        y_in.append(
            pl.pallas_call(
                functools.partial(inside_kernel, s, per),
                grid=(rows // cut,),
                in_specs=[
                    gspec, pl.BlockSpec((cut, STATE), step), pl.BlockSpec((cut, STATE), step),
                    pl.BlockSpec((cut, heads), step), pl.BlockSpec((heads, cut), lambda i: (0, i)),
                ],
                out_specs=gspec,
                out_shape=part,
                compiler_params=params(),
                cost_estimate=cost(3),
                name="inside",
            )(xdt[s], bs, cs, cl, clt)
        )
    messages = send_states(s_local, 1)

    out_mine2 = after_that(out_mine2, totals)
    out_both = beside(out_mine, out_mine2)
    out_own = [out_both[m] for m in range(per)]
    out_first = after_that(out_own[0], s_local[1])
    out_along = jnp.concatenate([turn(out_first, s) for s in range(1, nz)], axis=0)
    out_cross = [out_along] + [cross(out_along, m) for m in range(1, per)]
    cot_o = swap(after_that(cotangent, totals))
    limit = (lengths[0] - zi * rows).reshape(1, 1)

    wide = pl.BlockSpec((Q, channels), step)
    gwide = pl.BlockSpec((Q, gc), step)
    bspec = pl.BlockSpec((Q, STATE), step)
    hspec = pl.BlockSpec((Q, heads), step)
    h2spec = pl.BlockSpec((Q, 2 * heads), step)
    tspec = pl.BlockSpec((heads, Q), lambda i: (0, i))
    tile = 2 * Q if rows % (2 * Q) == 0 else Q
    smem = pl.BlockSpec(memory_space=pltpu.SMEM)
    wout, masked, dyn = pl.pallas_call(
        functools.partial(pull_kernel, per, nz),
        grid=(rows // tile,),
        in_specs=[
            pl.BlockSpec((tile, half), step), pl.BlockSpec((tile, half), step), smem,
            *[whole(v) for v in out_own + out_cross],
        ],
        out_specs=[
            pl.BlockSpec((channels, model), fix), pl.BlockSpec((tile, model), step),
            pl.BlockSpec((tile, channels), step),
        ],
        out_shape=[shape((channels, model), BF), shape((rows, model), BF), full],
        compiler_params=params(),
        cost_estimate=cost(5),
        name="pull",
    )(cotangent, cot_o, limit, *out_own, *out_cross)
    out = pl.pallas_call(
        functools.partial(carry_kernel, groups, per),
        grid=(blocks,),
        in_specs=[
            *[gwide] * (3 * nz), wide, bspec, bspec, tspec, h2spec, h2spec, *[whole(v) for v in messages],
            whole(skip), whole(gain_out), whole(ex),
        ],
        out_specs=[
            *[gwide] * nz, *[pl.BlockSpec((1, gc, STATE), lambda i: (i, 0, 0))] * nz, wide,
            pl.BlockSpec((Q, 2), step),
        ],
        out_shape=[
            *[shape((rows, gc))] * nz, *[shape((blocks, gc, STATE), BF)] * nz, shape((rows, channels), BF),
            shape((rows, 2)),
        ],
        scratch_shapes=[pltpu.VMEM((channels, STATE), F32)],
        compiler_params=params(),
        cost_estimate=cost(10),
        name="carry",
    )(*y_in, *u, *z, dyn, bs, cs, clt, e12, dttl2, *messages, skip, gain_out, ex)
    ys, states, gg, sums = out[:nz], out[nz : 2 * nz], out[2 * nz], out[2 * nz + 1]
    sums2 = swap(sums)

    def sum_products(a, columns, w, count, wait):
        tile = 2 * Q if count % (2 * Q) == 0 else count
        return pl.pallas_call(
            functools.partial(sum_products_kernel, len(a)),
            grid=(count // tile,),
            in_specs=[
                *[
                    pl.BlockSpec((tile, v.shape[0]), lambda i, j=j: (i, j))
                    for v, j in zip(w, columns)
                ],
                *[whole(v) for v in w],
                pl.BlockSpec(memory_space=pl.ANY),
            ],
            out_specs=[pl.BlockSpec((tile, half), step)] * 2,
            out_shape=[shape((count, half)), shape((count, half), BF)],
            compiler_params=params(),
            cost_estimate=cost(4),
            name="products",
        )(*a, *w, wait)

    branch, branch_o = sum_products([gg], [0], [wout], rows, sums)
    branch_o = swap(branch_o)
    hhalf = pl.BlockSpec((Q, half), step)
    out = pl.pallas_call(
        functools.partial(gate_kernel, groups, per),
        grid=(blocks,),
        in_specs=[
            *[gwide] * (3 * nz), wide, pl.BlockSpec((Q, 2), step), pl.BlockSpec((Q, 2), step),
            whole(gain_out), h2spec, whole(ex), bspec, hhalf, hhalf, hhalf, smem,
        ],
        out_specs=[
            *[gwide] * nz, wide, wide, pl.BlockSpec((channels, STATE), fix),
            pl.BlockSpec((1, channels), fix), pl.BlockSpec((1, channels), fix), hhalf,
        ],
        out_shape=[
            *[part] * nz, shape((rows, channels), BF), shape((rows, channels), BF),
            shape((channels, STATE), BF), shape((1, channels)), shape((1, channels)),
            shape((rows, half), BF),
        ],
        scratch_shapes=[pltpu.VMEM((channels, STATE), F32)],
        compiler_params=params(),
        cost_estimate=cost(10),
        name="gate",
    )(
        *ys, *z, *u, dyn, sums, sums2, gain_out, ec2, ex, cs, hidden, branch, branch_o, limit
    )
    dys = out[:nz]
    dz, yn, ds_local, g_gain, g_skip, out_hidden = out[nz:]
    message = jnp.concatenate([ds_local, totals], axis=0)

    def plane_sum(parts):
        total = parts[0].astype(F32)
        for m in range(1, per):
            total = total + cross(parts[m], m).astype(F32)
        return total

    def to_owner(total):
        v = jnp.stack([total] + [cross(total, m) for m in range(1, per)])
        v = jnp.stack([pick(v, di ^ m) for m in range(per)])
        return v[:, :, :half], swap(v[:, :, half:])

    def by_head(mine, other):
        low_w = jnp.where(wi == 0, mine, other)
        high_w = jnp.where(wi == 0, other, mine)
        return jnp.concatenate([low_w, high_w], axis=0)

    anywhere = pl.BlockSpec(memory_space=pl.ANY)
    gcol = pl.BlockSpec((rows, gc), lambda s: (0, s))
    early = pl.pallas_call(
        functools.partial(early_grad_kernel, per),
        grid=(nz,),
        in_specs=[gcol, whole(masked), gcol, whole(xn)],
        out_specs=[pl.BlockSpec((1, 2 * HEADDIM, model), lambda s: (s, 0, 0))] * per,
        out_shape=[shape((nz, 2 * HEADDIM, model), BF)] * per,
        compiler_params=params(),
        cost_estimate=cost(6),
        name="early_grad",
    )(yn, masked, dz, xn)
    out = pl.pallas_call(
        functools.partial(inside_back_kernel, groups, per),
        grid=(blocks,),
        in_specs=[
            *[gwide] * (2 * nz), bspec, bspec, hspec, tspec, *[anywhere] * (1 + per)
        ],
        out_specs=[*[gwide] * nz, bspec, bspec, hspec, *[anywhere] * (nz - 1 + per - 1)],
        out_shape=[
            *[shape((rows, gc))] * nz, shape((rows, STATE)), shape((rows, STATE)),
            shape((rows, heads)), *[shape(message.shape, BF)] * (nz - 1),
            *[shape(early[0].shape, BF)] * (per - 1),
        ],
        scratch_shapes=[
            pltpu.VMEM((heads, Q), F32), pltpu.SemaphoreType.DMA((nz + per - 2,)),
            pltpu.SemaphoreType.DMA((nz + per - 2,)),
        ],
        compiler_params=pltpu.CompilerParams(
            vmem_limit_bytes=VMEM, collective_id=0, has_side_effects=True
        ),
        cost_estimate=cost(15),
        name="inside_back",
    )(*xdt, *dys, bs, cs, cl, clt, message, *early)
    dxi = out[:nz]
    dbi, dci, dai = out[nz : nz + 3]
    messages = out[nz + 3 : 2 * nz + 2]
    early_sum = sum(v.astype(F32) for v in [early[0], *out[2 * nz + 2 :]])
    early_low = early_sum.astype(BF)
    early_total = early_sum[0]
    for s in range(1, nz):
        early_total = early_total + turn(early_low[s], -s).astype(F32)
    early_total = early_total.astype(BF)
    early_own, early_other = to_owner(early_total)
    rev = lambda i: (blocks - 1 - i, 0)
    rg = pl.BlockSpec((Q, gc), rev)
    rb = pl.BlockSpec((Q, STATE), rev)
    rh = pl.BlockSpec((Q, heads), rev)
    rh2 = pl.BlockSpec((Q, 2 * heads), rev)
    rbc = pl.BlockSpec((Q, 2 * STATE), rev)

    def back(some, final, dbi, dci, dti, wait):
        n = len(some)
        of = lambda values: [values[s] for s in some]
        out = pl.pallas_call(
            functools.partial(back_kernel, some, per, final),
            grid=(blocks,),
            in_specs=[
                *[rg] * (4 * n), *[pl.BlockSpec((HALO, gc), fix)] * n,
                *[pl.BlockSpec((1, gc, STATE), lambda i: (blocks - 1 - i, 0, 0))] * n,
                rb, rb, rb, rb, rh, rh, rh, rh,
                pl.BlockSpec((heads, Q), lambda i: (0, blocks - 1 - i)), rh2, rh2, rh2,
                rbc, rbc, whole(brawh), whole(taps), whole(taps_bc), whole(rate), whole(skip),
                whole(ex), whole(er), *[whole(v) for v in messages],
                pl.BlockSpec(memory_space=pl.ANY), pl.BlockSpec(memory_space=pl.ANY),
            ],
            out_specs=[
                *[rg] * n, *[pl.BlockSpec((HALO, gc), fix)] * n, *[pl.BlockSpec((4, gc), fix)] * n,
                rb, rb, rh, pl.BlockSpec((1, heads), fix), pl.BlockSpec((1, heads), fix),
                rbc, pl.BlockSpec((HALO, 2 * STATE), fix), pl.BlockSpec((4, 2 * STATE), fix),
            ],
            out_shape=[
                *[shape((rows, gc), BF)] * n, *[shape((HALO, gc), BF)] * n, *[shape((4, gc))] * n,
                shape((rows, STATE)), shape((rows, STATE)),
                shape((rows, heads), BF if final else F32), shape((1, heads)), shape((1, heads)),
                shape((rows, 2 * STATE), BF), shape((HALO, 2 * STATE), BF), shape((4, 2 * STATE)),
            ],
            scratch_shapes=[
                pltpu.VMEM((n * gc, STATE), F32), pltpu.VMEM((heads, STATE), F32),
                *[pltpu.VMEM((8, gc), F32)] * n, pltpu.VMEM((8, 2 * STATE), F32),
            ],
            compiler_params=params(),
            cost_estimate=cost(7 * n),
            name="back",
        )(
            *of(dxi), *of(dys), *of(u), *of(xr), *of(xrh), *of(states), bs, cs, dbi, dci, dai, dti,
            dt, sig, clt, dt2, e12, tl2, ubc, braw, brawh, taps, taps_bc, rate, skip, ex, er,
            *messages, *wait,
        )
        return out[:n], out[n : 2 * n], out[2 * n : 3 * n], *out[3 * n :]

    halves = (groups[1 : nz // 2 + 1], groups[nz // 2 + 1 :] + groups[:1])
    dx, dxh, g_taps = [None] * nz, [None] * nz, [None] * nz
    dti = jnp.zeros((rows, heads), F32)
    g_rate, g_bias, late, wait = 0.0, 0.0, [], (dti, dti)
    bc_rows = 2 * STATE // per
    for number, some in enumerate(halves):
        final = number == len(halves) - 1
        got, got_h, got_taps, dbi, dci, dti, one, two, dbc, dbch, g_taps_bc = back(
            some, final, dbi, dci, dti, wait
        )
        g_rate, g_bias = g_rate + one, g_bias + two
        for i, s in enumerate(some):
            dx[s], dxh[s], g_taps[s] = got[i], got_h[i], got_taps[i]
        n = len(some)
        spread_heads = pick_heads.T.astype(BF)
        more = [dbc, dbch, dti, spread_heads] if final else []
        out_rows = n * HEADDIM + (bc_rows + HALO if final else 0)
        g = pl.pallas_call(
            functools.partial(late_grad_kernel, n, per, final),
            in_specs=[
                pl.BlockSpec(memory_space=pl.ANY),
                *[whole(v) for v in [*got, *got_h, xn, xnh, *more]],
            ],
            out_shape=[shape((out_rows, model), BF)] * per,
            scratch_shapes=(
                [pltpu.VMEM((2 * STATE, model), F32), pltpu.VMEM((HEADS, model), F32)]
                if final
                else []
            ),
            compiler_params=params(),
            cost_estimate=cost(3),
            name="late_grad",
        )(early_total if final else dti, *got, *got_h, xn, xnh, *more)
        late.append(plane_sum(g))
        wait = (early_low, g[0])
    g_taps = jnp.concatenate(g_taps, axis=1)

    share = late[-1][len(halves[-1]) * HEADDIM :]
    addend = {}
    for some, v in zip(halves, late):
        for i, s in enumerate(some):
            addend[s] = jnp.concatenate([v[i * HEADDIM : (i + 1) * HEADDIM], share], axis=0)
    total = addend[0]
    for s in range(1, nz):
        total = total + turn(addend[s].astype(BF), -s).astype(F32)
    late_own, late_other = to_owner(total.astype(BF))
    g_early = by_head(early_own, early_other)
    g_late = by_head(late_own[:, :HEADDIM], late_other[:, :HEADDIM])
    g_zx = jnp.concatenate([g_early[:, HEADDIM:], g_late], axis=1)
    g_bcdt = late_own[:, HEADDIM:].astype(F32) + late_other[:, HEADDIM:].astype(F32)
    grad_in_bcdt = jnp.transpose(
        jnp.concatenate(
            [
                g_bcdt[:, :bc_rows].reshape(2 * STATE, half),
                g_bcdt[:, bc_rows : bc_rows + HEADS // per].reshape(HEADS, half),
            ],
            axis=0,
        )
    )

    lhs = [dz] * nz + dx + [dbc, dti]
    dxn, dxn_o = sum_products(
        lhs, [*groups] + [0] * (nz + 2), wz + wx + [wbc, wdt], rows, early_other
    )
    edge = sum(dot(v, w) for v, w in zip(dxh + [dbch], wx + [wbc]))
    edge = edge[:, :half] + swap(edge[:, half:])
    edge = shift(edge, -1)
    dxn = dxn + swap(dxn_o).astype(F32) + jnp.pad(edge, ((rows - HALO, 0), (0, 0)))
    source = hidden.astype(F32)
    gain_half = norm_gain[None].astype(F32)
    across = jnp.sum(dxn * gain_half * source, axis=1, keepdims=True)
    across = across + swap(across)
    grad_hidden = (
        cotangent.astype(F32)
        + r * gain_half * dxn
        - source * (r * r * r) / model * across
    ).astype(BF)
    g_norm = jnp.sum(dxn * source * r, axis=0)

    table = jnp.concatenate(
        [
            g_bias.reshape(heads, 1),
            (g_rate * rate).reshape(heads, 1),
            jnp.sum(g_skip.reshape(heads, HEADDIM), axis=1, keepdims=True),
            jnp.transpose(g_taps.reshape(4, heads, HEADDIM), (1, 0, 2)).reshape(heads, 4 * HEADDIM),
            g_gain.reshape(heads, HEADDIM),
        ],
        axis=1,
    )
    table = jnp.dot(pick_heads.T, table, precision=HIGH)
    side = (jnp.arange(2) == wi).astype(F32)[:, None] * g_norm[None]
    small = jnp.concatenate([table.reshape(-1), g_taps_bc.reshape(-1), side.reshape(-1)])
    small = small + swap(small)
    flip = 1
    while flip < ndp:
        small = small + cross(small, flip)
        flip *= 2
    flip = 1
    while flip < nz:
        small = small + lax.ppermute(small, "head", [(i, i ^ flip) for i in range(nz)])
        flip *= 2
    size = table.size
    table = lax.dynamic_slice_in_dim(
        small[:size].reshape(HEADS, -1), zi * own_heads, own_heads, 0
    )
    g_taps_bc = small[size : size + 8 * STATE].reshape(4, 2 * STATE)
    g_norm = pick(small[size + 8 * STATE :].reshape(2, half), wi)
    return (
        out_hidden,
        grad_hidden,
        g_norm,
        jnp.transpose(g_zx, (2, 0, 1)).astype(F32),
        grad_in_bcdt,
        jnp.transpose(
            table[:, 3 : 3 + 4 * HEADDIM].reshape(own_heads, 4, HEADDIM), (1, 0, 2)
        ).reshape(4, own_heads * HEADDIM),
        g_taps_bc,
        table[:, 0],
        table[:, 1],
        table[:, 2],
        table[:, 3 + 4 * HEADDIM :].reshape(-1),
        g_early[:, :HEADDIM].reshape(own_heads * HEADDIM, half).astype(F32),
    )


def fits(mesh):
    ndp, nz, nw = mesh.shape["dp"], mesh.shape["head"], mesh.shape["width"]
    return (
        nw == 2
        and ndp in (2, 4, 8)
        and nz & (nz - 1) == 0
        and HEADS == nz * nw * ndp
        and LEN % (nz * Q) == 0
        and SEQS == ndp
        and HEADS // nw * HEADDIM % Q == 0
        and HEADS // ndp <= HALO
    )


def solution(mesh):
    placed = (
        P(("dp", "head"), "width"),
        P("dp"),
        P(("dp", "head"), "width"),
        P("width"),
        P("width", "head", None),
        P("width", None),
        P(None, "head"),
        P(),
        P("head"),
        P("head"),
        P("head"),
        P("head"),
        P("head", "width"),
    )
    return jax.shard_map(
        sequence_device if fits(mesh) else per_device,
        mesh=mesh,
        in_specs=placed,
        out_specs=(
            P(("dp", "head"), "width"),
            P(("dp", "head"), "width"),
            P("width"),
            P("width", "head", None),
            P("width", None),
            P(None, "head"),
            P(),
            P("head"),
            P("head"),
            P("head"),
            P("head"),
            P("head", "width"),
        ),
        check_vma=False,
    )
```

```python
import functools

import jax
import jax.numpy as jnp
import numpy as np
from jax import lax
from jax.experimental import pallas as pl
from jax.experimental.pallas import tpu as pltpu
from jax.sharding import PartitionSpec as P

D = 1024
HEADS = 32
HEADDIM = 64
STATE = 128
SCAN_BLOCK = 256
LEN = 4096
INNER = 2048
SEQS = 4


EPS = 1e-05
HIGH = lax.Precision.HIGHEST


def conv_causal(values, kernel):
    taps = kernel.shape[0]
    padded = jnp.pad(values, ((taps - 1, 0), (0, 0)))
    total = jnp.zeros_like(values)
    for offset in range(taps):
        total = total + kernel[offset] * padded[offset : offset + values.shape[0]]
    return total


def block_scan(inputs, steps, rates, bmat, cmat, block):
    length, heads, hsize = inputs.shape
    count = length // block
    in_blocks = inputs.reshape(count, block, heads, hsize)
    step_blocks = steps.reshape(count, block, heads)
    b_blocks = bmat.reshape(count, block, bmat.shape[1])
    c_blocks = cmat.reshape(count, block, cmat.shape[1])
    places = jnp.arange(block)
    lower = (places[:, None] >= places[None, :])[:, :, None]

    def advance(state, pieces):
        x_part, dt_part, b_part, c_part = pieces
        cums = jnp.cumsum(dt_part * rates, axis=0)
        spread = cums[:, None, :] - cums[None, :, :]
        decay = jnp.where(lower, jnp.exp(jnp.where(lower, spread, 0.0)), 0.0)
        scores = jnp.dot(c_part, b_part.T, precision=HIGH)
        weights = scores[:, :, None] * decay * dt_part[None, :, :]
        inside = jnp.einsum("ijh,jhp->ihp", weights, x_part, precision=HIGH)
        carried = (
            jnp.einsum("in,hpn->ihp", c_part, state, precision=HIGH) * jnp.exp(cums)[:, :, None]
        )
        tails = jnp.exp(cums[-1][None, :] - cums) * dt_part
        state = jnp.exp(cums[-1])[:, None, None] * state + jnp.einsum(
            "jh,jhp,jn->hpn", tails, x_part, b_part, precision=HIGH
        )
        return (state, inside + carried)

    start_state = jnp.zeros((heads, hsize, bmat.shape[1]), jnp.float32)
    _, result = lax.scan(
        jax.checkpoint(advance), start_state, (in_blocks, step_blocks, b_blocks, c_blocks)
    )
    return result.reshape(length, heads, hsize)


def mixer(zx, bc_raw, dt_raw, kernel_x, kernel_bc, bias_dt, log_rate, skip):
    length, heads, double = zx.shape
    hsize = double // 2
    gate = zx[:, :, :hsize]
    x_raw = zx[:, :, hsize:].reshape(length, heads * hsize)
    xs_conv = jax.nn.silu(conv_causal(x_raw, kernel_x)).reshape(length, heads, hsize)
    bc_conv = jax.nn.silu(conv_causal(bc_raw, kernel_bc))
    half = bc_conv.shape[1] // 2
    steps = jax.nn.softplus(dt_raw + bias_dt)
    rates = -jnp.exp(log_rate)
    result = (
        block_scan(xs_conv, steps, rates, bc_conv[:, :half], bc_conv[:, half:], SCAN_BLOCK)
        + skip[:, None] * xs_conv
    )
    return (result * jax.nn.silu(gate)).reshape(length, heads * hsize)


def per_device(
    hidden,
    lengths,
    cotangent,
    norm_gain,
    in_zx,
    in_bcdt,
    conv_x,
    conv_bc,
    dt_bias,
    a_log,
    d_skip,
    gnorm_gain,
    out_w,
):
    slice_rows, half_width = hidden.shape
    local_heads = in_zx.shape[1]
    head_count = lax.axis_size("head")
    head_index = lax.axis_index("head")
    total_rows = slice_rows * head_count
    seq_local = lengths.shape[0]
    inner_local = local_heads * HEADDIM
    row_ids = head_index * slice_rows + jnp.arange(slice_rows, dtype=jnp.int32)
    owner = (row_ids // LEN)[:, None] == jnp.arange(seq_local, dtype=jnp.int32)[None, :]
    limits = jnp.sum(jnp.where(owner, lengths[None, :], 0), axis=1)
    keeper = (row_ids % LEN < limits).astype(jnp.float32)[:, None]
    source = hidden.astype(jnp.float32)
    squares = lax.psum(jnp.sum(source * source, axis=1), "width")
    scale = lax.rsqrt(squares / D + EPS)[:, None]
    gain_in = norm_gain.astype(jnp.float32)
    normed = (source * scale * gain_in).astype(jnp.bfloat16)
    gathered = lax.all_gather(normed, "head", axis=0, tiled=True)
    w_zx = in_zx.reshape(half_width, local_heads * 2 * HEADDIM)
    zx_part = jnp.dot(gathered, w_zx, preferred_element_type=jnp.float32)
    bcdt_part = jnp.dot(gathered, in_bcdt, preferred_element_type=jnp.float32)
    zx_full, bcdt_full = lax.psum((zx_part, bcdt_part), "width")
    zx_seq = zx_full.reshape(seq_local, LEN, local_heads, 2 * HEADDIM)
    bc_seq = bcdt_full[:, : 2 * STATE].reshape(seq_local, LEN, 2 * STATE)
    dt_seq = lax.dynamic_slice_in_dim(
        bcdt_full, 2 * STATE + head_index * local_heads, local_heads, 1
    ).reshape(seq_local, LEN, local_heads)

    def local_mix(zx_in, bc_in, dt_in, kernel_x, kernel_bc, bias_in, log_in, skip_in):
        per_sequence = jax.vmap(mixer, in_axes=(0, 0, 0, None, None, None, None, None))
        return per_sequence(
            zx_in, bc_in, dt_in, kernel_x, kernel_bc, bias_in, log_in, skip_in
        ).reshape(total_rows, inner_local)

    gated, mix_pull = jax.vjp(
        local_mix,
        zx_seq,
        bc_seq,
        dt_seq,
        conv_x.astype(jnp.float32),
        conv_bc.astype(jnp.float32),
        dt_bias,
        a_log,
        d_skip,
    )
    total_sq = lax.psum(jnp.sum(gated * gated, axis=1), "head")
    scale_out = lax.rsqrt(total_sq / INNER + EPS)[:, None]
    gain_out = gnorm_gain.astype(jnp.float32)
    mixed = (gated * scale_out * gain_out).astype(jnp.bfloat16)
    picked = mixed
    branch = lax.psum_scatter(
        jnp.dot(picked, out_w, preferred_element_type=jnp.float32),
        "head",
        scatter_dimension=0,
        tiled=True,
    )
    out_hidden = (source + keeper * branch).astype(jnp.bfloat16)
    grad_out = cotangent.astype(jnp.float32)
    masked = (grad_out * keeper).astype(jnp.bfloat16)
    piece = lax.all_gather(masked, "head", axis=0, tiled=True)
    picked = mixed
    acc_weight = jnp.einsum("tc,td->cd", picked, piece, preferred_element_type=jnp.float32)
    product = jnp.einsum("td,cd->tc", piece, out_w, preferred_element_type=jnp.float32)
    grad_mixed = lax.psum(product, "width")
    gain_out_grad = jnp.sum(grad_mixed * gated * scale_out, axis=0)
    inner_total = lax.psum(jnp.sum(grad_mixed * gain_out * gated, axis=1), "head")
    cubed = scale_out * scale_out * scale_out
    grad_gated = scale_out * gain_out * grad_mixed - gated * cubed / INNER * inner_total[:, None]
    (
        grad_zx_seq,
        grad_bc_seq,
        grad_dt_seq,
        kernel_x_grad,
        kernel_bc_grad,
        bias_grad,
        rate_grad,
        skip_grad,
    ) = mix_pull(grad_gated)
    grad_zx = grad_zx_seq.reshape(total_rows, local_heads * 2 * HEADDIM).astype(jnp.bfloat16)
    dt_columns = jnp.zeros((total_rows, HEADS), jnp.float32)
    dt_columns = lax.dynamic_update_slice_in_dim(
        dt_columns, grad_dt_seq.reshape(total_rows, local_heads), head_index * local_heads, 1
    )
    grad_bcdt_head = jnp.concatenate(
        [grad_bc_seq.reshape(total_rows, 2 * STATE), dt_columns], axis=1
    )
    weight_zx = jnp.einsum(
        "td,tc->dc", gathered, grad_zx, preferred_element_type=jnp.float32
    ).reshape(half_width, local_heads, 2 * HEADDIM)
    normed_part = jnp.einsum("tc,dc->td", grad_zx, w_zx, preferred_element_type=jnp.float32)
    grad_normed, bcdt_summed = (
        lax.psum_scatter(normed_part, "head", scatter_dimension=0, tiled=True),
        lax.psum_scatter(grad_bcdt_head, "head", scatter_dimension=0, tiled=True),
    )
    bcdt_low = bcdt_summed.astype(jnp.bfloat16)
    grad_normed = grad_normed + jnp.einsum(
        "tk,dk->td", bcdt_low, in_bcdt, preferred_element_type=jnp.float32
    )
    weight_bcdt = jnp.einsum("td,tk->dk", normed, bcdt_low, preferred_element_type=jnp.float32)
    gain_in_grad = jnp.sum(grad_normed * source * scale, axis=0)
    across = lax.psum(jnp.sum(grad_normed * gain_in * source, axis=1), "width")
    scale_cubed = scale * scale * scale
    grad_hidden = (
        grad_out + scale * gain_in * grad_normed - source * scale_cubed / D * across[:, None]
    ).astype(jnp.bfloat16)
    summed_dp = lax.psum(
        (weight_zx, acc_weight, kernel_x_grad, bias_grad, rate_grad, skip_grad, gain_out_grad), "dp"
    )
    summed_all = lax.psum((weight_bcdt, gain_in_grad, kernel_bc_grad), ("dp", "head"))
    return (
        out_hidden,
        grad_hidden,
        summed_all[1],
        summed_dp[0],
        summed_all[0],
        summed_dp[2],
        summed_all[2],
        summed_dp[3],
        summed_dp[4],
        summed_dp[5],
        summed_dp[6],
        summed_dp[1],
    )


BF = jnp.bfloat16
F32 = jnp.float32
Q = 128
HALO = 16
NEG = -1e30
MESH = pl.DeviceIdType.MESH
VMEM = 60 * 1024 * 1024


def dot(a, b, prec=None):
    return lax.dot_general(a, b, (((1,), (0,)), ((), ())), precision=prec, preferred_element_type=F32)


def dot_t(a, b, prec=None):
    return lax.dot_general(a, b, (((1,), (1,)), ((), ())), precision=prec, preferred_element_type=F32)


def t_dot(a, b, prec=None):
    return lax.dot_general(a, b, (((0,), (0,)), ((), ())), precision=prec, preferred_element_type=F32)


def split2(v, axis=1):
    hi = v.astype(BF)
    lo = (v - hi.astype(F32)).astype(BF)
    return jnp.concatenate([hi, lo], axis=axis)


def dot_split(v, m):
    hi = v.astype(BF)
    lo = (v - hi.astype(F32)).astype(BF)
    return dot(hi, m) + dot(lo, m)


def split_dot(m, v):
    hi = v.astype(BF)
    lo = (v - hi.astype(F32)).astype(BF)
    return dot(m, hi) + dot(m, lo)


def sigmoid(v):
    return 1.0 / (1.0 + jnp.exp(-v))


def tri(kind):
    row = lax.broadcasted_iota(jnp.int32, (Q, Q), 0)
    col = lax.broadcasted_iota(jnp.int32, (Q, Q), 1)
    return {"ge": row >= col, "le": row <= col, "gt": row > col}[kind]


def slot_heads(heads, per):
    nz = heads // per
    own = HEADS // nz
    bits = per.bit_length() - 1
    slot = lax.broadcasted_iota(jnp.int32, (heads, HEADS), 0)
    head = lax.broadcasted_iota(jnp.int32, (heads, HEADS), 1)
    z = (lax.axis_index("head") - (slot >> bits)) & (nz - 1)
    m = (slot & (per - 1)) ^ lax.axis_index("dp")
    return (head == z * own + lax.axis_index("width") * per + m).astype(F32)


def prep_kernel(
    per, zx, ow, bcdt, gain, cx, scal, gn,
    first_o, first2_o, rest_o, rest2_o, out_o, out2_o, bcdt_o, table_o,
):
    di = lax.axis_index("dp")
    wi = lax.axis_index("width")
    wide = 2 * HEADDIM
    for m in range(per):
        for w, whole_o, some_o, o_o in (
            (wi, first_o, rest_o, out_o), (1 - wi, first2_o, rest2_o, out2_o)
        ):
            head = w * per + jnp.bitwise_xor(di, m)
            v = jnp.transpose(zx[:, pl.ds(pl.multiple_of(head * wide, wide), wide)])
            for i in range(2):
                part = v[i * HEADDIM : (i + 1) * HEADDIM, :]
                if m == 0:
                    whole_o[i] = part
                else:
                    some_o[i, (m - 1) * HEADDIM : m * HEADDIM, :] = part
            o_o[m * HEADDIM : (m + 1) * HEADDIM, :] = ow[
                pl.ds(pl.multiple_of(head * HEADDIM, HEADDIM), HEADDIM), :
            ]
    n = bcdt.shape[1]
    bcdt_o[0:n, :] = jnp.transpose(bcdt[...])
    bcdt_o[n:, :] = jnp.broadcast_to(gain[...], (HALO, gain.shape[1]))
    rows = jnp.concatenate(
        [cx[...].astype(F32), gn[...].astype(F32), scal[...]], axis=0
    )
    half = rows.shape[1] // 2
    rows = jnp.where(wi == 0, rows[:, :half], rows[:, half:])
    step = 1
    while step < per:
        size = HEADDIM * step
        parts = [rows[:, i * size : (i + 1) * size] for i in range(half // size)]
        swapped = jnp.concatenate([parts[i ^ 1] for i in range(len(parts))], axis=1)
        rows = jnp.where(jnp.bitwise_and(di, step) != 0, swapped, rows)
        step *= 2
    table_o[...] = rows


def entry_first(per, hm, ho, hh, bcdt, table, cbc, sel, o, xn_o, buf):
    xnh_o, r_o, raw_o, rawh_o, dt_o, sig_o = o.xnh, o.r, o.raw, o.rawh, o.dt, o.sig
    cl_o, clt_o, rate_o, wdt_o, b_o = o.cl, o.clt, o.rate, o.wdt, o.b
    rows = hm.shape[0]
    state = b_o.shape[1]
    per_head = dot(table[...], sel[...], HIGH)
    bias = per_head[5:6, :]
    rate = -jnp.exp(per_head[6:7, :])
    rate_o[...] = rate
    wbc = bcdt.at[0 : 2 * state, :]
    wdt_o[...] = dot(
        slot_heads(rate.shape[1], per).astype(BF), bcdt[2 * state : 2 * state + HEADS, :]
    ).astype(BF)
    wdt = wdt_o
    gain = bcdt[2 * state + HEADS : 2 * state + HEADS + 1, :].astype(F32)
    blocks = rows // Q
    lower = tri("ge").astype(F32)

    def norm(left, right):
        h = jnp.concatenate([left, right], axis=1).astype(F32)
        r = lax.rsqrt(jnp.mean(h * h, axis=1, keepdims=True) + EPS)
        return (h * r * gain).astype(BF), r

    half = hm.shape[1]
    xnh, _ = norm(hh[:, :half], hh[:, half:])
    xnh = jnp.where(lax.axis_index("head") > 0, xnh.astype(F32), 0.0).astype(BF)
    xnh_o[...] = xnh
    buf[0:HALO, :] = dot_t(xnh, wbc[...])
    rawh_o[...] = buf[0:HALO, :]

    def first(i, carry):
        here = pl.ds(pl.multiple_of(i * Q, Q), Q)
        xn, r = norm(hm[here, :], ho[here, :])
        xn_o[here, :] = xn
        r_o[here, :] = r
        raw = dot_t(xn, wbc[...])
        raw_o[here, :] = raw
        buf[pl.ds(pl.multiple_of(HALO + i * Q, HALO), Q), :] = raw
        steps = dot_t(xn, wdt[...]) + bias
        dt = jax.nn.softplus(steps)
        dt_o[here, :] = dt
        sig_o[here, :] = sigmoid(steps)
        da = dt * rate
        cl_o[here, :] = dot(lower, da, HIGH)
        clt_o[:, here] = lax.dot_general(
            da, lower, (((0,), (1,)), ((), ())), precision=HIGH, preferred_element_type=F32
        )
        return carry

    lax.fori_loop(0, blocks, first, 0, unroll=2)


def entry_second(cbc, o, tot_o, buf):
    u_o, b_o, c_o, dt_o, cl_o, clt_o = o.ubc, o.b, o.c, o.dt, o.cl, o.clt
    dt2_o, e12_o, tl2_o, dttl2_o, ec2_o, edt2_o = o.dt2, o.e12, o.tl2, o.dttl2, o.ec2, o.edt2
    state = b_o.shape[1]
    blocks = b_o.shape[0] // Q

    def second(i, carry):
        here = pl.ds(pl.multiple_of(i * Q, Q), Q)
        win = buf[pl.ds(pl.multiple_of(i * Q, Q), Q + HALO), :]
        u = jnp.zeros((Q, win.shape[1]), F32)
        for k in range(4):
            u = u + cbc[k : k + 1, :] * win[HALO - 3 + k : HALO - 3 + k + Q, :]
        u_o[here, :] = u
        v = u * sigmoid(u)
        b_o[here, :] = v[:, :state].astype(BF)
        c_o[here, :] = v[:, state:].astype(BF)
        return carry

    lax.fori_loop(0, blocks, second, 0, unroll=2)
    tots = [cl_o[i * Q + Q - 1 : i * Q + Q, :] for i in range(blocks)]
    ctot = functools.reduce(lambda x, y: x + y, tots)
    heads = clt_o.shape[0]
    column = functools.reduce(
        lambda x, y: x + y, [clt_o[:, i * Q + Q - 1 : i * Q + Q] for i in range(blocks)]
    )
    hi = column.astype(BF)
    mid = (column - hi.astype(F32)).astype(BF)
    low = (column - hi.astype(F32) - mid.astype(F32)).astype(BF)
    lane = lax.broadcasted_iota(jnp.int32, (heads, tot_o.shape[1]), 1)
    tot_o[...] = jnp.where(
        lane == 0,
        hi.astype(F32),
        jnp.where(lane == 1, mid.astype(F32), jnp.where(lane == 2, low.astype(F32), 0.0)),
    ).astype(BF)
    off = jnp.zeros_like(ctot)
    for i in range(blocks):
        here = slice(i * Q, i * Q + Q)
        cl = cl_o[here, :]
        dt = dt_o[here, :]
        tail = jnp.exp(tots[i] - cl)
        dt2_o[here, :] = split2(dt)
        e12_o[here, :] = split2(jnp.exp(cl))
        tl2_o[here, :] = split2(tail)
        dttl2_o[here, :] = split2(dt * tail)
        ec2_o[here, :] = split2(jnp.exp(cl + off))
        edt2_o[here, :] = split2(dt * jnp.exp(ctot - cl - off))
        off = off + tots[i]


def decay(cl, clt, h, mask):
    return jnp.exp(jnp.where(mask, cl[:, h : h + 1] - clt[h : h + 1, :], NEG))


def lane_masks():
    lane = lax.broadcasted_iota(jnp.int32, (1, Q), 1)
    low = (lane < HEADDIM).astype(F32)
    return low.astype(BF), (1.0 - low).astype(BF)


def project(s, per, xn, o, w, cw, ex, z_o, xr_o, xrh_o, u_o, xdt_o, msg, buf, acc):
    rows = z_o.shape[0]
    gc = per * HEADDIM
    cols = slice(s * gc, s * gc + gc)
    xh = dot_t(o.xnh[...], w[1, cols, :])
    buf[0:HALO, :] = xh
    xrh_o[...] = xh
    acc[...] = jnp.zeros_like(acc)
    cut = rows // 2 if rows // 2 % Q == 0 else rows

    def part(j, carry):
        base = j * cut
        here = pl.ds(pl.multiple_of(base, Q), cut)
        buf[pl.ds(pl.multiple_of(base + HALO, HALO), cut), :] = dot_t(xn[here, :], w[1, cols, :])
        z_o[here, :] = dot_t(xn[here, :], w[0, cols, :])
        for i in range(cut // Q):
            here = pl.ds(pl.multiple_of(base + i * Q, Q), Q)
            win = buf[pl.ds(pl.multiple_of(base + i * Q, Q), Q + HALO), :]
            u = jnp.zeros((Q, gc), F32)
            for k in range(4):
                u = u + cw[k : k + 1, cols] * win[HALO - 3 + k : HALO - 3 + k + Q, :]
            xr_o[here, :] = win[HALO:, :].astype(BF)
            u_o[here, :] = u
            xs = u * sigmoid(u)
            xdt_o[here, :] = (xs * dot(o.dt2[here, :], ex[:, cols])).astype(BF)
            acc[...] += t_dot((xs * dot(o.edt2[here, :], ex[:, cols])).astype(BF), o.b[here, :])
        return carry

    lax.fori_loop(0, rows // cut, part, 0)
    msg[cols, :] = acc[...].astype(BF)


def inside(s, per, xdt, o, y_o):
    mask = tri("ge")
    low, high = lane_masks()
    rows = xdt.shape[0]
    some = 4 if rows % (4 * Q) == 0 else 1

    def part(j, carry):
        for i in range(some):
            here = pl.ds(pl.multiple_of((j * some + i) * Q, Q), Q)
            g = dot_t(o.c[here, :], o.b[here, :])
            clv, cltv = o.cl[here, :], o.clt[:, here]
            for p in range(xdt.shape[1] // Q):
                lanes = slice(p * Q, p * Q + Q)
                h = s * per + 2 * p
                ws = [(g * decay(clv, cltv, k, mask)).astype(BF) for k in (h, h + 1)]
                x = xdt[here, lanes]
                y_o[here, lanes] = dot(
                    jnp.concatenate(ws, axis=1), jnp.concatenate([x * low, x * high], axis=0)
                ).astype(BF)
        return carry

    lax.fori_loop(0, rows // (some * Q), part, 0)


class Named:
    def __init__(self, names, refs):
        for name, ref in zip(names, refs):
            setattr(self, name, ref)


KEPT = (
    "xnh", "r", "raw", "rawh", "ubc", "b", "c", "dt", "sig", "cl", "clt", "dt2", "e12", "tl2",
    "dttl2", "ec2", "edt2", "rate", "wdt", "tot", "table",
)


def front_kernel(per, nz, *refs):
    hidden, first, first2, rest, rest2, bcdt, table, cbc, sel, ex, refs = take(refs, *[0] * 10)
    out_mine, out2, cot, refs = take(refs, 0, 0, 0)
    w_o, wo_o, cot_o, xn_o, refs = take(refs, 0, 0, 0, 0)
    z_o, xr_o, u_o, xdt_o, y_o, messages_o, xrh_o, refs = take(refs, *[nz] * 5, nz - 1, nz)
    kept, refs = refs[: len(KEPT)], refs[len(KEPT) :]
    o = Named(KEPT, kept)
    z_v, xr_v, u_v, xdt_v, y_v, refs = take(refs, *[nz] * 5)
    w, ho, eh, bc, xn, msg, buf, bcbuf, acc, sends, receives, locals_ = refs
    rows, half = hidden.shape
    gc = per * HEADDIM
    top = nz * gc
    sibling = {"width": 1 - lax.axis_index("width")}
    z_peers = line_peers(nz, 1)
    d_peers = plane_peers(per)
    used = [0]

    def copy(source, target, peer):
        i = used[0]
        used[0] += 1
        return remote(source, target, sends, receives, i, peer)

    left, right = pl.ds(0, half), pl.ds(half, half)
    swap_first = copy(first2, w.at[:, pl.ds(0, HEADDIM), right], sibling)
    swap_rest = copy(rest2, w.at[:, pl.ds(HEADDIM, gc - HEADDIM), right], sibling)
    swap_hidden = copy(hidden, ho, sibling)
    swap_bc = copy(bcdt, bc.at[:, right], sibling)
    swap_out = copy(out2, wo_o.at[pl.ds(0, gc), right], sibling)
    swap_cot = copy(cot, cot_o, sibling)
    z_table, z_w, z_out, z_state, z_state2 = [], [], [], [], []
    for k, peer in enumerate(z_peers):
        s = k + 1
        z_table.append(copy(table, o.table.at[:, pl.ds(s * gc, gc)], peer))
        own = w.at[:, pl.ds(0, HEADDIM), :]
        z_w.append(copy(own, w.at[:, pl.ds(s * gc, HEADDIM), :], peer))
        z_out.append(
            copy(wo_o.at[pl.ds(0, HEADDIM), :], wo_o.at[pl.ds(s * gc, HEADDIM), :], peer)
        )
        most = pl.ds(0, top - gc)
        z_state.append(copy(msg.at[most, :], messages_o[k].at[most, :], peer))
        more = pl.ds(top - gc, gc + HALO)
        z_state2.append(copy(msg.at[more, :], messages_o[k].at[more, :], peer))
    last = pl.ds(rows - HALO, HALO)
    edge1 = copy(hidden.at[last, :], eh.at[:, left], z_peers[0])
    edge2 = copy(ho.at[last, :], eh.at[:, right], z_peers[0])
    p_w = {s: [] for s in range(1, nz)}
    p_out = {s: [] for s in range(1, nz)}
    for s in range(1, nz):
        for k, peer in enumerate(d_peers):
            mine = pl.ds(s * gc, HEADDIM)
            there = pl.ds(s * gc + (k + 1) * HEADDIM, HEADDIM)
            p_w[s].append(copy(w.at[:, mine, :], w.at[:, there, :], peer))
            p_out[s].append(copy(wo_o.at[mine, :], wo_o.at[there, :], peer))

    places = [0]

    def local(source, target):
        i = places[0]
        places[0] += 1
        found = pltpu.make_async_copy(source, target, locals_.at[i])
        found.start()
        return found

    def start(copies):
        for c in copies:
            c.start()

    def arrive(copies):
        for c in copies:
            c.wait_recv()

    ready = [
        local(first, w.at[:, pl.ds(0, HEADDIM), left]),
        local(rest, w.at[:, pl.ds(HEADDIM, gc - HEADDIM), left]),
        local(bcdt, bc.at[:, left]),
        local(table, o.table.at[:, pl.ds(0, gc)]),
        local(out_mine, wo_o.at[pl.ds(0, gc), left]),
    ]
    meet([sibling, *z_peers, *line_peers(nz, -1), *d_peers])
    start([swap_first, *z_table, swap_hidden, swap_bc, edge1, swap_rest, swap_out, swap_cot])
    ready[0].wait()
    arrive([swap_first])
    start(z_w)
    arrive([swap_hidden])
    start([edge2])
    for c in ready[1:]:
        c.wait()
    arrive([swap_bc, *z_table, edge1, edge2])
    entry_first(per, hidden, ho, eh, bc, o.table, cbc, sel, o, xn, bcbuf)
    arrive([z_w[0]])
    start(p_w[1])
    entry_second(cbc, o, o.tot, bcbuf)
    msg[top:, :] = o.tot[...]
    pending = [local(xn, xn_o)]
    arrive([swap_out])
    start(z_out)
    arrive([swap_rest])
    taps = o.table
    for s in range(nz):
        if s > 0:
            arrive(p_w[s])
        project(
            s, per, xn, o, w, taps, ex, z_v[s], xr_v[s], xrh_o[s], u_v[s], xdt_v[s], msg, buf, acc
        )
        for a, b in ((z_v, z_o), (xr_v, xr_o), (u_v, u_o), (xdt_v, xdt_o)):
            pending.append(local(a[s], b[s]))
        if s == 0:
            for k in range(2, nz):
                arrive([z_w[k - 1]])
                start(p_w[k])
        if s == nz - 2:
            start(z_state)
            for k in range(1, nz):
                arrive([z_out[k - 1]])
                start(p_out[k])
        if s == nz - 1:
            start(z_state2)
            pending.append(local(w, w_o))
        inside(s, per, xdt_v[s], o, y_v[s])
        pending.append(local(y_v[s], y_o[s]))
    everything = [swap_first, swap_rest, swap_hidden, swap_bc, swap_out, swap_cot, edge1, edge2]
    everything += [*z_table, *z_w, *z_out, *z_state, *z_state2]
    for s in range(1, nz):
        everything += p_w[s] + p_out[s]
        arrive(p_out[s])
    arrive([swap_cot, *z_state, *z_state2])
    for c in everything:
        c.wait_send()
    for c in pending:
        c.wait()


def head_scale(clt, first, per, state):
    return jnp.concatenate(
        [
            jnp.broadcast_to(jnp.exp(clt[h : h + 1, Q - 1 : Q]), (HEADDIM, state))
            for h in range(first, first + per)
        ],
        axis=0,
    )


def from_messages(messages, sign, groups, per, state, store, valid=None):
    nz = len(messages) + 1
    gc = per * HEADDIM
    top = nz * gc
    totals = [
        sum(m[top:, i : i + 1].astype(F32) for i in range(3)) for m in messages
    ]
    for at, j in enumerate(groups):
        total = jnp.zeros((gc, state), F32)
        faded = jnp.zeros((per, 1), F32)
        for k in range(1, nz):
            there = (j - sign * k) % nz
            scale = jnp.exp(faded)
            scale = jnp.concatenate(
                [jnp.broadcast_to(scale[h : h + 1, :], (HEADDIM, state)) for h in range(per)],
                axis=0,
            )
            part = scale * messages[k - 1][there * gc : there * gc + gc, :].astype(F32)
            if valid is not None:
                part = jnp.where(valid(k), part, 0.0)
            total = total + part
            faded = faded + totals[k - 1][there * per : there * per + per, :]
        store[at * gc : at * gc + gc, :] = total


def carry_kernel(groups, per, *refs):
    n = len(groups)
    y_in, us, z, dyn, b, c, clt, e12, dttl2, messages, dsk, gain, ex, rest = take(
        refs, n, n, n, 0, 0, 0, 0, 0, 0, n - 1, 0, 0, 0
    )
    ys_o, st_o, rest = take(rest, n, n)
    gg_o, sum_o, s = rest
    gc = per * HEADDIM

    @pl.when(pl.program_id(0) == 0)
    def _():
        z_index = lax.axis_index("head")
        from_messages(messages, 1, groups, per, s.shape[1], s, lambda k: z_index - k >= 0)

    square = jnp.zeros((Q, gc), F32)
    inner = jnp.zeros((Q, gc), F32)
    for j in groups:
        here = slice(j * gc, j * gc + gc)
        sv = s[here, :]
        sb = sv.astype(BF)
        st_o[j][0] = sb
        x = us[j][...]
        x = x * sigmoid(x)
        e1 = dot(e12[...], ex[:, here])
        y = y_in[j][...].astype(F32) + e1 * dot_t(c[...], sb) + dsk[:, here] * x
        ys_o[j][...] = y
        xt = (x * dot(dttl2[...], ex[:, here])).astype(BF)
        s[here, :] = head_scale(clt, j * per, per, sv.shape[1]) * sv + t_dot(xt, b[...])
        zz = z[j][...]
        gz = y * (zz * sigmoid(zz))
        gg = gz * gain[:, here]
        gg_o[:, here] = gg.astype(BF)
        square = square + gz * gz
        inner = inner + gg * dyn[:, here]
    lane = lax.broadcasted_iota(jnp.int32, (Q, 2), 1)
    sum_o[...] = jnp.where(
        lane == 0,
        jnp.sum(square, axis=1, keepdims=True),
        jnp.sum(inner, axis=1, keepdims=True),
    )


def gate_kernel(groups, per, *refs):
    n = len(groups)
    ys, z, us, dyn, sums, sums2, gain, ec2, ex, c, rest = take(refs, n, n, n, *[0] * 7)
    hidden, branch, branch2, limit, rest = take(rest, 0, 0, 0, 0)
    dys_o, rest = take(rest, n)
    dz_o, yn_o, ds_o, gn_o, sk_o, out_o, acc = rest
    gc = per * HEADDIM

    @pl.when(pl.program_id(0) == 0)
    def _():
        acc[...] = jnp.zeros_like(acc)
        gn_o[...] = jnp.zeros_like(gn_o)
        sk_o[...] = jnp.zeros_like(sk_o)

    count = n * gc * 2
    both = sums[...] + sums2[...]
    r2 = lax.rsqrt(both[:, 0:1] / count + EPS)
    pull = both[:, 1:2] * (r2 * r2 * r2) / count
    row = lax.broadcasted_iota(jnp.int32, (Q, 1), 0) + pl.program_id(0) * Q
    keep = jnp.where(row < limit[0, 0], r2, 0.0)
    out_o[...] = (
        hidden[...].astype(F32) + keep * (branch[...] + branch2[...].astype(F32))
    ).astype(BF)
    for j in groups:
        here = slice(j * gc, j * gc + gc)
        gn = gain[:, here]
        zz = z[j][...]
        sz = sigmoid(zz)
        silu = zz * sz
        y = ys[j][...]
        gz = y * silu
        dy_n = dyn[:, here]
        gr = gz * r2
        yn_o[:, here] = (gr * gn).astype(BF)
        gn_o[:, here] += jnp.sum(dy_n * gr, axis=0, keepdims=True)
        dgz = r2 * gn * dy_n - gz * pull
        dys = dgz * silu
        dys_o[j][...] = dys.astype(BF)
        dz_o[:, here] = (dgz * y * (sz + silu * (1.0 - sz))).astype(BF)
        x = us[j][...]
        x = x * sigmoid(x)
        sk_o[:, here] += jnp.sum(dys * x, axis=0, keepdims=True)
        acc[here, :] += t_dot((dys * dot(ec2[...], ex[:, here])).astype(BF), c[...])

    @pl.when(pl.program_id(0) == pl.num_programs(0) - 1)
    def _():
        ds_o[...] = acc[...].astype(BF)


def line_peers(count, sign):
    z = lax.axis_index("head")
    return [{"head": lax.rem(z + sign * k + count, count)} for k in range(1, count)]


def plane_peers(count):
    d = lax.axis_index("dp")
    return [{"dp": jnp.bitwise_xor(d, m)} for m in range(1, count)]


def meet(peers):
    barrier = pltpu.get_barrier_semaphore()
    for peer in peers:
        pl.semaphore_signal(barrier, inc=1, device_id=peer, device_id_type=MESH)
    pl.semaphore_wait(barrier, len(peers))


def remote(source, target, sends, receives, i, peer):
    return pltpu.make_async_remote_copy(
        src_ref=source,
        dst_ref=target,
        send_sem=sends.at[i],
        recv_sem=receives.at[i],
        device_id=peer,
        device_id_type=MESH,
    )


def conv_back(d, nxt, taps, raw, rawh, grad_o, out_o, outh_o, last):
    win = jnp.concatenate([d, nxt[...]], axis=0)
    back = jnp.zeros_like(d)
    sums = []
    for k in range(4):
        part = win[3 - k : 3 - k + Q, :]
        back = back + taps[k : k + 1, :] * part
        sums.append(jnp.sum(raw * part, axis=0, keepdims=True))
    grad_o[...] += jnp.concatenate(sums, axis=0)
    out_o[...] = back.astype(BF)
    nxt[...] = d[0:8, :]

    @pl.when(last)
    def _():
        win_h = jnp.concatenate([jnp.zeros((HALO, d.shape[1]), F32), d[0:8, :]], axis=0)
        back_h = jnp.zeros((HALO, d.shape[1]), F32)
        sums_h = []
        for k in range(4):
            part = win_h[3 - k : 3 - k + HALO, :]
            back_h = back_h + taps[k : k + 1, :] * part
            sums_h.append(jnp.sum(rawh[...] * part, axis=0, keepdims=True))
        grad_o[...] += jnp.concatenate(sums_h, axis=0)
        outh_o[...] = back_h.astype(BF)


def scan_back_kernel(groups, per, *refs):
    n = len(groups)
    nz = n
    xdt, dys, u, xr, st, xrh, rest = take(refs, n, n, n, n, n, n)
    (b, c, cl, clt, dt, sig, dt2, e12, tl2), rest = rest[:9], rest[9:]
    (ubc, braw, brawh, cw, cbc, rate, dsk, ex, er), rest = rest[:9], rest[9:]
    message, early, rest = take(rest, 0, per)
    dx_o, dxh_o, gcx_o, rest = take(rest, n, n, n)
    dt_o, ga_o, gbias_o, bc_o, bch_o, gcb_o, early_o = rest[:7]
    messages, got, rest = take(rest[7:], nz - 1, per - 1)
    du_next, line, rest = take(rest, n, nz - 1)
    db_next, own, low, dxi, dbi, dci, dai, kt, ds, vs, sends, receives, local = rest
    step = pl.program_id(0)
    blocks = pl.num_programs(0) // 2
    heads = dt.shape[1]
    state = b.shape[1]
    gc = per * HEADDIM
    line_at, back_at, plane_at = 0, nz - 1, 2 * nz - 2

    def state_copies():
        return [
            remote(message, messages[i], sends, receives, line_at + i, peer)
            for i, peer in enumerate(line_peers(nz, -1))
        ]

    def plane_copies(s):
        return [
            remote(
                early[i + 1].at[s], got[i].at[s], sends, receives, plane_at + s * (per - 1) + i, peer
            )
            for i, peer in enumerate(plane_peers(per))
        ]

    def line_copy(s):
        return remote(
            low.at[s], line[s - 1], sends, receives, back_at + s - 1, line_peers(nz, -1)[s - 1]
        )

    def own_copy():
        return pltpu.make_async_copy(early[0], own, local)

    @pl.when(step == 0)
    def _():
        own_copy().start()
        meet(line_peers(nz, -1) + line_peers(nz, 1) + plane_peers(per))
        for copy in plane_copies(1) + state_copies():
            copy.start()

    @pl.when(step < blocks)
    def _():
        rows = pl.ds(pl.multiple_of(step * Q, Q), Q)
        mask = tri("ge")
        lower, upper_lanes = lane_masks()
        g = dot_t(c[...], b[...])
        clv, cltv = cl[...], clt[...]
        lane = lax.broadcasted_iota(jnp.int32, (Q, heads), 1)
        dg = jnp.zeros((Q, Q), F32)
        rsum = jnp.zeros((Q, heads), F32)
        for s in groups:
            for p in range(per // 2):
                here = slice(p * Q, p * Q + Q)
                x = xdt[s][:, here]
                dy = dys[s][:, here]
                pp = dot_t(dy, jnp.concatenate([x * lower, x * upper_lanes], axis=0))
                ws = []
                for j in range(2):
                    h = s * per + 2 * p + j
                    ell = decay(clv, cltv, h, mask)
                    ws.append((g * ell).astype(BF))
                    pe = pp[:, j * Q : j * Q + Q] * ell
                    dg = dg + pe
                    m = pe * g
                    rsum = jnp.where(lane == h, jnp.sum(m, axis=1, keepdims=True), rsum)
                    kt[h : h + 1, :] = jnp.sum(m, axis=0, keepdims=True)
                dxi[rows, s * gc + p * Q : s * gc + p * Q + Q] = t_dot(
                    jnp.concatenate(ws, axis=0),
                    jnp.concatenate([dy * lower, dy * upper_lanes], axis=0),
                )
        dgb = dg.astype(BF)
        dci[rows, :] = dot(dgb, b[...])
        dbi[rows, :] = t_dot(dgb, c[...])
        upper = tri("le").astype(F32)
        dai[rows, :] = dot(upper, rsum, HIGH) - dot_t(upper, kt[...], HIGH)

    @pl.when(step == blocks)
    def _():
        for copy in state_copies():
            copy.wait()
        z = lax.axis_index("head")
        from_messages(messages, -1, groups, per, state, ds, lambda k: z + k < nz)
        for i in range(n):
            du_next[i][...] = jnp.zeros_like(du_next[i])
            gcx_o[i][...] = jnp.zeros_like(gcx_o[i])
        db_next[...] = jnp.zeros_like(db_next)
        gcb_o[...] = jnp.zeros_like(gcb_o)
        ga_o[...] = jnp.zeros_like(ga_o)
        gbias_o[...] = jnp.zeros_like(gbias_o)

    @pl.when(step >= blocks)
    def _():
        rows = pl.ds(pl.multiple_of((2 * blocks - 1 - step) * Q, Q), Q)
        last = step == 2 * blocks - 1
        rsum = jnp.zeros((Q, heads), F32)
        gsum = jnp.zeros((Q, heads), F32)
        ddt = jnp.zeros((Q, heads), F32)
        dbs = dbi[rows, :]
        dcs = dci[rows, :]
        for s in groups:
            here = slice(s * gc, s * gc + gc)
            ehere = er[here, :]
            sb = st[s][0]
            dsv = ds[here, :]
            dsb = dsv.astype(BF)
            dy = dys[s][...].astype(F32)
            dye = dy * dot(e12[...], ex[:, here])
            dyb = dye.astype(BF)
            rsum = rsum + dot((dye * dot_t(c[...], sb)).astype(BF), ehere)
            dcs = dcs + dot(dyb, sb)
            bds = dot_t(b[...], dsb)
            tail = dot(tl2[...], ex[:, here])
            dtx = dot(dt2[...], ex[:, here])
            uu = u[s][...]
            su = sigmoid(uu)
            xs = uu * su
            xt = xs * dtx * tail
            gsum = gsum + dot((xt * bds).astype(BF), ehere)
            dbs = dbs + dot(xt.astype(BF), dsb)
            dxdt = dxi[rows, here] + tail * bds
            ddt = ddt + dot((dxdt * xs).astype(BF), ehere)
            eds = head_scale(clt, s * per, per, state) * dsv
            ev = eds * sb.astype(F32)
            for j in range(per):
                h = s * per + j
                vs[h : h + 1, :] = jnp.sum(
                    ev[j * HEADDIM : (j + 1) * HEADDIM, :], axis=0, keepdims=True
                )
            ds[here, :] = eds + t_dot(dyb, c[...])
            du = (dxdt * dtx + dsk[:, here] * dy) * (su + xs * (1.0 - su))
            conv_back(
                du, du_next[s], cw.at[:, here], xr[s][...].astype(F32), xrh[s], gcx_o[s],
                dx_o[s], dxh_o[s], last,
            )
        vrow = dot_t(jnp.ones((8, state), F32), vs[...], HIGH)
        da = (
            dai[rows, :]
            + split_dot(tri("le").astype(BF), rsum)
            + split_dot(tri("gt").astype(BF), gsum)
            + vrow[0:1, :]
        )
        draw = (rate[...] * da + ddt) * sig[...]
        dt_o[...] = draw.astype(BF)
        ga_o[...] += jnp.sum(da * dt[...], axis=0, keepdims=True)
        gbias_o[...] += jnp.sum(draw, axis=0, keepdims=True)
        d = jnp.concatenate([dbs, dcs], axis=1)
        v = ubc[...]
        sv = sigmoid(v)
        conv_back(
            d * (sv + v * sv * (1.0 - sv)), db_next, cbc, braw[...], brawh, gcb_o, bc_o, bch_o,
            last,
        )

    def add(s):
        for copy in plane_copies(s):
            copy.wait()

        def piece(i, carry):
            part = pl.ds(pl.multiple_of(i * HALO, HALO), HALO)
            total = own[s, part, :].astype(F32)
            for v in got:
                total = total + v[s, part, :].astype(F32)
            low[s, part, :] = total.astype(BF)
            return carry

        lax.fori_loop(0, low.shape[1] // HALO, piece, 0, unroll=2)

    order = [*range(1, nz), 0]
    for k, s in enumerate(order):
        if k > 0:

            @pl.when(step == (blocks * k * 3) // (2 * nz))
            def _(s=s):
                for copy in plane_copies(s):
                    copy.start()

        if s > 0:

            @pl.when(step == blocks + (blocks * 3 * k) // (4 * (nz - 1)) + 1)
            def _(s=s):
                if s == 1:
                    own_copy().wait()
                add(s)
                line_copy(s).start()

    @pl.when(step == 2 * blocks - 1)
    def _():
        add(0)
        for s in range(1, nz):
            line_copy(s).wait()
        total = low[0].astype(F32)
        for v in line:
            total = total + v[...].astype(F32)
        early_o[...] = total.astype(BF)


def sum_products_kernel(n, *refs):
    a, w, _, rest = take(refs, n, n, 0)
    left_o, right_o = rest
    total = dot(a[0][...], w[0][...])
    for i in range(1, n):
        total = total + dot(a[i][...], w[i][...])
    half = left_o.shape[1]
    left_o[...] = total[:, :half]
    right_o[...] = total[:, half:].astype(BF)


def pull_kernel(cot, cot2, limit, w, mask_o, dyn_o):
    rows = cot.shape[0]
    half = cot.shape[1]
    row = lax.broadcasted_iota(jnp.int32, (rows, 1), 0) + pl.program_id(0) * rows
    keep = row < limit[0, 0]
    for i, v in enumerate((cot, cot2)):
        mask_o[:, i * half : i * half + half] = jnp.where(keep, v[...].astype(F32), 0.0).astype(BF)
    dyn_o[...] = dot_t(mask_o[...], w[...])


def early_grad_kernel(per, yn, masked, dz, xn, *outs):
    g_out = t_dot(yn[...], masked[...]).astype(BF)
    g_z = t_dot(dz[...], xn[...]).astype(BF)
    for m in range(per):
        here = slice(m * HEADDIM, (m + 1) * HEADDIM)
        outs[m][0, :HEADDIM, :] = g_out[here, :]
        outs[m][0, HEADDIM:, :] = g_z[here, :]


def late_grad_kernel(n, per, final, *refs):
    _, dx, dxh, xn, xnh, rest = take(refs, 0, n, n, 0, 0)
    if final:
        dbc, dbch, ddt, spread, rest = take(rest, 0, 0, 0, 0)
        outs, rest = take(rest, per)
        gbc, gdt = rest
        bc_rows = gbc.shape[0] // per
        dt_rows = gdt.shape[0] // per
        gbc[...] = t_dot(dbc[...], xn[...]) + t_dot(dbch[...], xnh[...])
        gdt[...] = split_dot(spread[...], t_dot(ddt[...], xn[...]))
    else:
        outs, rest = take(rest, per)
    for i in range(n):
        g = (t_dot(dx[i][...], xn[...]) + t_dot(dxh[i][...], xnh[...])).astype(BF)
        for m in range(per):
            outs[m][i * HEADDIM : (i + 1) * HEADDIM, :] = g[m * HEADDIM : (m + 1) * HEADDIM, :]
    if final:
        me = lax.axis_index("dp")
        for m in range(per):
            at = jnp.bitwise_xor(me, m)
            v = gbc[pl.ds(pl.multiple_of(at * bc_rows, bc_rows), bc_rows), :]
            w = gdt[pl.ds(pl.multiple_of(at * dt_rows, dt_rows), dt_rows), :]
            w = jnp.concatenate([w, jnp.zeros((HALO - dt_rows, w.shape[1]), F32)], axis=0)
            outs[m][n * HEADDIM : n * HEADDIM + bc_rows, :] = v.astype(BF)
            outs[m][n * HEADDIM + bc_rows :, :] = w.astype(BF)


def shape(dims, dtype=F32):
    return jax.ShapeDtypeStruct(dims, dtype)


def whole(array):
    rank = len(array.shape)
    return pl.BlockSpec(array.shape, lambda *_: (0,) * rank)


def params():
    return pltpu.CompilerParams(vmem_limit_bytes=VMEM)


def cost(us):
    return pl.CostEstimate(flops=int(us * 1.0e8), bytes_accessed=int(us * 1.0e3), transcendentals=0)


def take(refs, *counts):
    out, at = [], 0
    for n in counts:
        out.append(refs[at] if n == 0 else refs[at : at + n])
        at += max(n, 1)
    return out + [refs[at:]]


def sequence_device(
    hidden, lengths, cotangent, norm_gain, in_zx, in_bcdt, conv_x, conv_bc,
    dt_bias, a_log, d_skip, gnorm_gain, out_w,
):
    rows, half = hidden.shape
    own_heads = in_zx.shape[1]
    nz = lax.axis_size("head")
    ndp = lax.axis_size("dp")
    zi = lax.axis_index("head")
    di = lax.axis_index("dp")
    wi = lax.axis_index("width")
    per = ndp
    heads = nz * per
    channels = heads * HEADDIM
    model = 2 * half
    blocks = rows // Q

    def swap(v):
        return lax.ppermute(v, "width", [(0, 1), (1, 0)])

    def turn(v, s):
        return lax.ppermute(v, "head", [(i, (i + s) % nz) for i in range(nz)])

    def shift(v, s):
        return lax.ppermute(v, "head", [(i, i + s) for i in range(nz) if 0 <= i + s < nz])

    def cross(v, m):
        return lax.ppermute(v, "dp", [(i, i ^ m) for i in range(ndp)])

    def pick(v, index):
        return lax.dynamic_index_in_dim(v, index, 0, keepdims=False)

    gc = per * HEADDIM
    groups = tuple(range(nz))

    onehot = np.kron(np.eye(heads), np.ones((1, HEADDIM)))
    ex = jnp.asarray(np.concatenate([onehot, onehot], axis=0), BF)
    er = jnp.asarray(onehot.T, BF)
    sel = jnp.asarray(onehot.T * (np.arange(channels) % HEADDIM == 0)[:, None], F32)

    scal = jnp.repeat(jnp.stack([dt_bias, a_log, d_skip]), HEADDIM, axis=1)
    piece = shape((2, HEADDIM, half), BF)
    some = shape((2, gc - HEADDIM, half), BF)
    outs = shape((gc, half), BF)
    first, first2, rest, rest2, out_mine, out_mine2, bcdt_t, table = pl.pallas_call(
        functools.partial(prep_kernel, per),
        out_shape=[
            piece, piece, some, some, outs, outs,
            shape((2 * STATE + HEADS + HALO, half), BF), shape((8, gc)),
        ],
        compiler_params=params(),
        cost_estimate=cost(4),
        name="prep",
    )(
        in_zx.reshape(half, -1), out_w, in_bcdt, norm_gain[None], conv_x, scal,
        gnorm_gain[None],
    )
    taps_bc = conv_bc.astype(F32)
    slot = jnp.arange(heads)
    slot_head = ((zi - slot // per) % nz) * own_heads + wi * per + ((slot % per) ^ di)
    pick_heads = (slot_head[:, None] == jnp.arange(HEADS)[None, :]).astype(F32)

    step = lambda i: (i, 0)
    fix = lambda i: (0, 0)
    part = shape((rows, gc), BF)
    full = shape((rows, channels))
    anywhere = pl.BlockSpec(memory_space=pl.ANY)
    vmem = pl.BlockSpec(memory_space=pltpu.VMEM)
    narrow = shape((rows, 2 * heads), BF)
    kept = dict(
        xnh=shape((HALO, model), BF), r=shape((rows, 1)), raw=shape((rows, 2 * STATE)),
        rawh=shape((HALO, 2 * STATE)), ubc=shape((rows, 2 * STATE)), b=shape((rows, STATE), BF),
        c=shape((rows, STATE), BF), dt=shape((rows, heads)), sig=shape((rows, heads)),
        cl=shape((rows, heads)), clt=shape((heads, rows)), dt2=narrow, e12=narrow, tl2=narrow,
        dttl2=narrow, ec2=narrow, edt2=narrow, rate=shape((1, heads)),
        wdt=shape((heads, model), BF), tot=shape((heads, STATE), BF), table=shape((8, channels)),
    )
    wide_part = shape((rows, gc))
    message_shape = shape((channels + HALO, STATE), BF)
    out_shapes = [
        shape((2, channels, model), BF), shape((channels, model), BF), shape((rows, half), BF),
        shape((rows, model), BF), *[wide_part] * nz, *[part] * nz, *[wide_part] * nz,
        *[part] * nz, *[part] * nz, *[message_shape] * (nz - 1), *[shape((HALO, gc))] * nz,
        *[kept[name] for name in KEPT],
    ]
    held = lambda v: pltpu.VMEM(v.shape, v.dtype)
    remotes = 6 + 5 * (nz - 1) + 2 + 2 * (nz - 1) * (per - 1)
    out = pl.pallas_call(
        functools.partial(front_kernel, per, nz),
        in_specs=[vmem] * 10 + [anywhere] * 3,
        out_specs=[anywhere] * (4 + 5 * nz + nz - 1) + [vmem] * (nz + len(KEPT)),
        out_shape=out_shapes,
        scratch_shapes=[
            *[held(wide_part)] * nz, *[held(part)] * nz, *[held(wide_part)] * nz,
            *[held(part)] * nz, *[held(part)] * nz, pltpu.VMEM((2, channels, model), BF),
            pltpu.VMEM((rows, half), BF), pltpu.VMEM((HALO, model), BF),
            pltpu.VMEM((2 * STATE + HEADS + HALO, model), BF), pltpu.VMEM((rows, model), BF),
            held(message_shape), pltpu.VMEM((rows + HALO, gc), F32),
            pltpu.VMEM((rows + HALO, 2 * STATE), F32), pltpu.VMEM((gc, STATE), F32),
            pltpu.SemaphoreType.DMA((remotes,)), pltpu.SemaphoreType.DMA((remotes,)),
            pltpu.SemaphoreType.DMA((7 + 5 * nz,)),
        ],
        compiler_params=pltpu.CompilerParams(
            vmem_limit_bytes=VMEM, collective_id=1, has_side_effects=True
        ),
        cost_estimate=cost(90),
        name="front",
    )(
        hidden, first, first2, rest, rest2, bcdt_t, table, taps_bc, sel, ex, out_mine, out_mine2,
        cotangent,
    )
    weights, wout, cot_o, xn, out = out[0], out[1], out[2], out[3], out[4:]
    z, xr, u, xdt, y_in, messages, xrh, out = take(out, *[nz] * 5, nz - 1, nz)
    o = Named(KEPT, out)
    xnh, r, braw, brawh, ubc, bs, cs = o.xnh, o.r, o.raw, o.rawh, o.ubc, o.b, o.c
    dt, sig, cl, clt, rate, wdt, totals, table = o.dt, o.sig, o.cl, o.clt, o.rate, o.wdt, o.tot, o.table
    dt2, e12, tl2, dttl2, ec2, edt2 = o.dt2, o.e12, o.tl2, o.dttl2, o.ec2, o.edt2
    taps, gain_out, skip = table[:4], table[4:5], table[7:8]
    bcdt_t = jnp.concatenate([bcdt_t, swap(bcdt_t)], axis=-1)
    wbc = bcdt_t[: 2 * STATE]
    limit = (lengths[0] - zi * rows).reshape(1, 1)

    wide = pl.BlockSpec((Q, channels), step)
    gwide = pl.BlockSpec((Q, gc), step)
    bspec = pl.BlockSpec((Q, STATE), step)
    hspec = pl.BlockSpec((Q, heads), step)
    h2spec = pl.BlockSpec((Q, 2 * heads), step)
    tspec = pl.BlockSpec((heads, Q), lambda i: (0, i))
    tile = 2 * Q if rows % (2 * Q) == 0 else Q
    smem = pl.BlockSpec(memory_space=pltpu.SMEM)
    masked, dyn = pl.pallas_call(
        pull_kernel,
        grid=(rows // tile,),
        in_specs=[
            pl.BlockSpec((tile, half), step), pl.BlockSpec((tile, half), step), smem, whole(wout),
        ],
        out_specs=[pl.BlockSpec((tile, model), step), pl.BlockSpec((tile, channels), step)],
        out_shape=[shape((rows, model), BF), full],
        compiler_params=params(),
        cost_estimate=cost(5),
        name="pull",
    )(cotangent, cot_o, limit, wout)
    out = pl.pallas_call(
        functools.partial(carry_kernel, groups, per),
        grid=(blocks,),
        in_specs=[
            *[gwide] * (3 * nz), wide, bspec, bspec, tspec, h2spec, h2spec, *[whole(v) for v in messages],
            whole(skip), whole(gain_out), whole(ex),
        ],
        out_specs=[
            *[gwide] * nz, *[pl.BlockSpec((1, gc, STATE), lambda i: (i, 0, 0))] * nz, wide,
            pl.BlockSpec((Q, 2), step),
        ],
        out_shape=[
            *[shape((rows, gc))] * nz, *[shape((blocks, gc, STATE), BF)] * nz, shape((rows, channels), BF),
            shape((rows, 2)),
        ],
        scratch_shapes=[pltpu.VMEM((channels, STATE), F32)],
        compiler_params=params(),
        cost_estimate=cost(10),
        name="carry",
    )(*y_in, *u, *z, dyn, bs, cs, clt, e12, dttl2, *messages, skip, gain_out, ex)
    ys, states, gg, sums = out[:nz], out[nz : 2 * nz], out[2 * nz], out[2 * nz + 1]
    sums2 = swap(sums)

    def sum_products(a, columns, w, count, wait):
        tile = 2 * Q if count % (2 * Q) == 0 else count
        return pl.pallas_call(
            functools.partial(sum_products_kernel, len(a)),
            grid=(count // tile,),
            in_specs=[
                *[
                    pl.BlockSpec((tile, v.shape[0]), lambda i, j=j: (i, j))
                    for v, j in zip(w, columns)
                ],
                *[whole(v) for v in w],
                pl.BlockSpec(memory_space=pl.ANY),
            ],
            out_specs=[pl.BlockSpec((tile, half), step)] * 2,
            out_shape=[shape((count, half)), shape((count, half), BF)],
            compiler_params=params(),
            cost_estimate=cost(4),
            name="products",
        )(*a, *w, wait)

    branch, branch_o = sum_products([gg], [0], [wout], rows, sums)
    branch_o = swap(branch_o)
    hhalf = pl.BlockSpec((Q, half), step)
    out = pl.pallas_call(
        functools.partial(gate_kernel, groups, per),
        grid=(blocks,),
        in_specs=[
            *[gwide] * (3 * nz), wide, pl.BlockSpec((Q, 2), step), pl.BlockSpec((Q, 2), step),
            whole(gain_out), h2spec, whole(ex), bspec, hhalf, hhalf, hhalf, smem,
        ],
        out_specs=[
            *[gwide] * nz, wide, wide, pl.BlockSpec((channels, STATE), fix),
            pl.BlockSpec((1, channels), fix), pl.BlockSpec((1, channels), fix), hhalf,
        ],
        out_shape=[
            *[part] * nz, shape((rows, channels), BF), shape((rows, channels), BF),
            shape((channels, STATE), BF), shape((1, channels)), shape((1, channels)),
            shape((rows, half), BF),
        ],
        scratch_shapes=[pltpu.VMEM((channels, STATE), F32)],
        compiler_params=params(),
        cost_estimate=cost(10),
        name="gate",
    )(
        *ys, *z, *u, dyn, sums, sums2, gain_out, ec2, ex, cs, hidden, branch, branch_o, limit
    )
    dys = out[:nz]
    dz, yn, ds_local, g_gain, g_skip, out_hidden = out[nz:]
    message = jnp.concatenate([ds_local, totals], axis=0)

    def plane_sum(parts):
        total = parts[0].astype(F32)
        for m in range(1, per):
            total = total + cross(parts[m], m).astype(F32)
        return total

    def to_owner(total):
        v = jnp.stack([total] + [cross(total, m) for m in range(1, per)])
        v = jnp.stack([pick(v, di ^ m) for m in range(per)])
        return v[:, :, :half], swap(v[:, :, half:])

    def by_head(mine, other):
        low_w = jnp.where(wi == 0, mine, other)
        high_w = jnp.where(wi == 0, other, mine)
        return jnp.concatenate([low_w, high_w], axis=0)

    gcol = pl.BlockSpec((rows, gc), lambda s: (0, s))
    early = pl.pallas_call(
        functools.partial(early_grad_kernel, per),
        grid=(nz,),
        in_specs=[gcol, whole(masked), gcol, whole(xn)],
        out_specs=[pl.BlockSpec((1, 2 * HEADDIM, model), lambda s: (s, 0, 0))] * per,
        out_shape=[shape((nz, 2 * HEADDIM, model), BF)] * per,
        compiler_params=params(),
        cost_estimate=cost(6),
        name="early_grad",
    )(yn, masked, dz, xn)
    one = lambda i: (jnp.minimum(i, blocks - 1), 0)
    two = lambda i: (jnp.minimum(blocks - 1, 2 * blocks - 1 - i), 0)
    both = lambda i: (jnp.minimum(i, 2 * blocks - 1 - i), 0)
    head_columns = lambda v: pl.BlockSpec((Q, v), two)
    early_shape = early[0].shape
    exchange = 2 * (nz - 1) + nz * (per - 1)
    out = pl.pallas_call(
        functools.partial(scan_back_kernel, groups, per),
        grid=(2 * blocks,),
        in_specs=[
            *[pl.BlockSpec((Q, gc), one)] * nz, *[pl.BlockSpec((Q, gc), both)] * nz,
            *[pl.BlockSpec((Q, gc), two)] * (2 * nz),
            *[
                pl.BlockSpec(
                    (1, gc, STATE), lambda i: (jnp.minimum(blocks - 1, 2 * blocks - 1 - i), 0, 0)
                )
            ] * nz,
            *[pl.BlockSpec((HALO, gc), fix)] * nz,
            pl.BlockSpec((Q, STATE), both), pl.BlockSpec((Q, STATE), both),
            pl.BlockSpec((Q, heads), one),
            pl.BlockSpec((heads, Q), lambda i: (0, jnp.minimum(i, 2 * blocks - 1 - i))),
            head_columns(heads), head_columns(heads), head_columns(2 * heads),
            head_columns(2 * heads), head_columns(2 * heads), head_columns(2 * STATE),
            head_columns(2 * STATE), whole(brawh), whole(taps), whole(taps_bc), whole(rate),
            whole(skip), whole(ex), whole(er), *[anywhere] * (1 + per),
        ],
        out_specs=[
            *[pl.BlockSpec((Q, gc), two)] * nz, *[pl.BlockSpec((HALO, gc), fix)] * nz,
            *[pl.BlockSpec((4, gc), fix)] * nz, head_columns(heads),
            pl.BlockSpec((1, heads), fix), pl.BlockSpec((1, heads), fix),
            head_columns(2 * STATE), pl.BlockSpec((HALO, 2 * STATE), fix),
            pl.BlockSpec((4, 2 * STATE), fix), pl.BlockSpec((2 * HEADDIM, model), fix),
        ],
        out_shape=[
            *[shape((rows, gc), BF)] * nz, *[shape((HALO, gc), BF)] * nz, *[shape((4, gc))] * nz,
            shape((rows, heads), BF), shape((1, heads)), shape((1, heads)),
            shape((rows, 2 * STATE), BF), shape((HALO, 2 * STATE), BF), shape((4, 2 * STATE)),
            shape((2 * HEADDIM, model), BF),
        ],
        scratch_shapes=[
            *[pltpu.VMEM(message.shape, BF)] * (nz - 1), *[pltpu.VMEM(early_shape, BF)] * (per - 1),
            *[pltpu.VMEM((8, gc), F32)] * nz, *[pltpu.VMEM((2 * HEADDIM, model), BF)] * (nz - 1),
            pltpu.VMEM((8, 2 * STATE), F32), pltpu.VMEM(early_shape, BF),
            pltpu.VMEM(early_shape, BF), pltpu.VMEM((rows, channels), F32),
            pltpu.VMEM((rows, STATE), F32), pltpu.VMEM((rows, STATE), F32),
            pltpu.VMEM((rows, heads), F32), pltpu.VMEM((heads, Q), F32),
            pltpu.VMEM((channels, STATE), F32), pltpu.VMEM((heads, STATE), F32),
            pltpu.SemaphoreType.DMA((exchange,)), pltpu.SemaphoreType.DMA((exchange,)),
            pltpu.SemaphoreType.DMA,
        ],
        compiler_params=pltpu.CompilerParams(
            vmem_limit_bytes=VMEM, collective_id=0, has_side_effects=True
        ),
        cost_estimate=cost(50),
        name="scan_back",
    )(
        *xdt, *dys, *u, *xr, *states, *xrh, bs, cs, cl, clt, dt, sig, dt2, e12, tl2, ubc, braw,
        brawh, taps, taps_bc, rate, skip, ex, er, message, *early,
    )
    dx, dxh, g_taps = list(out[:nz]), list(out[nz : 2 * nz]), out[2 * nz : 3 * nz]
    dti, g_rate, g_bias, dbc, dbch, g_taps_bc, early_total = out[3 * nz :]
    g_taps = jnp.concatenate(g_taps, axis=1)
    early_own, early_other = to_owner(early_total)
    spread_heads = pick_heads.T.astype(BF)
    bc_rows = 2 * STATE // per
    order = groups[1:] + groups[:1]
    operands = [
        early_total, *[dx[s] for s in order], *[dxh[s] for s in order], xn, xnh, dbc, dbch, dti,
        spread_heads,
    ]
    late = pl.pallas_call(
        functools.partial(late_grad_kernel, nz, per, True),
        in_specs=[anywhere, *[whole(v) for v in operands[1:]]],
        out_shape=[shape((nz * HEADDIM + bc_rows + HALO, model), BF)] * per,
        scratch_shapes=[pltpu.VMEM((2 * STATE, model), F32), pltpu.VMEM((HEADS, model), F32)],
        compiler_params=params(),
        cost_estimate=cost(8),
        name="late_grad",
    )(*operands)
    halves = (order,)
    late = [plane_sum(late)]

    share = late[-1][len(halves[-1]) * HEADDIM :]
    addend = {}
    for some, v in zip(halves, late):
        for i, s in enumerate(some):
            addend[s] = jnp.concatenate([v[i * HEADDIM : (i + 1) * HEADDIM], share], axis=0)
    total = addend[0]
    for s in range(1, nz):
        total = total + turn(addend[s].astype(BF), -s).astype(F32)
    late_own, late_other = to_owner(total.astype(BF))
    g_early = by_head(early_own, early_other)
    g_late = by_head(late_own[:, :HEADDIM], late_other[:, :HEADDIM])
    g_zx = jnp.concatenate([g_early[:, HEADDIM:], g_late], axis=1)
    g_bcdt = late_own[:, HEADDIM:].astype(F32) + late_other[:, HEADDIM:].astype(F32)
    grad_in_bcdt = jnp.transpose(
        jnp.concatenate(
            [
                g_bcdt[:, :bc_rows].reshape(2 * STATE, half),
                g_bcdt[:, bc_rows : bc_rows + HEADS // per].reshape(HEADS, half),
            ],
            axis=0,
        )
    )

    wz = [weights[0, s * gc : (s + 1) * gc] for s in groups]
    wx = [weights[1, s * gc : (s + 1) * gc] for s in groups]
    lhs = [dz] * nz + dx + [dbc, dti]
    dxn, dxn_o = sum_products(
        lhs, [*groups] + [0] * (nz + 2), wz + wx + [wbc, wdt], rows, early_other
    )
    edge = sum(dot(v, w) for v, w in zip(dxh + [dbch], wx + [wbc]))
    edge = edge[:, :half] + swap(edge[:, half:])
    edge = shift(edge, -1)
    dxn = dxn + swap(dxn_o).astype(F32) + jnp.pad(edge, ((rows - HALO, 0), (0, 0)))
    source = hidden.astype(F32)
    gain_half = norm_gain[None].astype(F32)
    across = jnp.sum(dxn * gain_half * source, axis=1, keepdims=True)
    across = across + swap(across)
    grad_hidden = (
        cotangent.astype(F32)
        + r * gain_half * dxn
        - source * (r * r * r) / model * across
    ).astype(BF)
    g_norm = jnp.sum(dxn * source * r, axis=0)

    table = jnp.concatenate(
        [
            g_bias.reshape(heads, 1),
            (g_rate * rate).reshape(heads, 1),
            jnp.sum(g_skip.reshape(heads, HEADDIM), axis=1, keepdims=True),
            jnp.transpose(g_taps.reshape(4, heads, HEADDIM), (1, 0, 2)).reshape(heads, 4 * HEADDIM),
            g_gain.reshape(heads, HEADDIM),
        ],
        axis=1,
    )
    table = jnp.dot(pick_heads.T, table, precision=HIGH)
    side = (jnp.arange(2) == wi).astype(F32)[:, None] * g_norm[None]
    small = jnp.concatenate([table.reshape(-1), g_taps_bc.reshape(-1), side.reshape(-1)])
    small = small + swap(small)
    flip = 1
    while flip < ndp:
        small = small + cross(small, flip)
        flip *= 2
    flip = 1
    while flip < nz:
        small = small + lax.ppermute(small, "head", [(i, i ^ flip) for i in range(nz)])
        flip *= 2
    size = table.size
    table = lax.dynamic_slice_in_dim(
        small[:size].reshape(HEADS, -1), zi * own_heads, own_heads, 0
    )
    g_taps_bc = small[size : size + 8 * STATE].reshape(4, 2 * STATE)
    g_norm = pick(small[size + 8 * STATE :].reshape(2, half), wi)
    return (
        out_hidden,
        grad_hidden,
        g_norm,
        jnp.transpose(g_zx, (2, 0, 1)).astype(F32),
        grad_in_bcdt,
        jnp.transpose(
            table[:, 3 : 3 + 4 * HEADDIM].reshape(own_heads, 4, HEADDIM), (1, 0, 2)
        ).reshape(4, own_heads * HEADDIM),
        g_taps_bc,
        table[:, 0],
        table[:, 1],
        table[:, 2],
        table[:, 3 + 4 * HEADDIM :].reshape(-1),
        g_early[:, :HEADDIM].reshape(own_heads * HEADDIM, half).astype(F32),
    )


def fits(mesh):
    ndp, nz, nw = mesh.shape["dp"], mesh.shape["head"], mesh.shape["width"]
    return (
        nw == 2
        and ndp in (2, 4, 8)
        and nz & (nz - 1) == 0
        and HEADS == nz * nw * ndp
        and LEN % (nz * Q) == 0
        and SEQS == ndp
        and HEADS // nw * HEADDIM % Q == 0
        and HEADS // ndp <= HALO
    )


def solution(mesh):
    placed = (
        P(("dp", "head"), "width"),
        P("dp"),
        P(("dp", "head"), "width"),
        P("width"),
        P("width", "head", None),
        P("width", None),
        P(None, "head"),
        P(),
        P("head"),
        P("head"),
        P("head"),
        P("head"),
        P("head", "width"),
    )
    return jax.shard_map(
        sequence_device if fits(mesh) else per_device,
        mesh=mesh,
        in_specs=placed,
        out_specs=(
            P(("dp", "head"), "width"),
            P(("dp", "head"), "width"),
            P("width"),
            P("width", "head", None),
            P("width", None),
            P(None, "head"),
            P(),
            P("head"),
            P("head"),
            P("head"),
            P("head"),
            P("head", "width"),
        ),
        check_vma=False,
    )
```

```python
import functools

import jax
import jax.numpy as jnp
import numpy as np
from jax import lax
from jax.experimental import pallas as pl
from jax.experimental.pallas import tpu as pltpu
from jax.sharding import PartitionSpec as P

D = 1024
HEADS = 32
HEADDIM = 64
STATE = 128
SCAN_BLOCK = 256
LEN = 4096
INNER = 2048
SEQS = 4


EPS = 1e-05
HIGH = lax.Precision.HIGHEST


def conv_causal(values, kernel):
    taps = kernel.shape[0]
    padded = jnp.pad(values, ((taps - 1, 0), (0, 0)))
    total = jnp.zeros_like(values)
    for offset in range(taps):
        total = total + kernel[offset] * padded[offset : offset + values.shape[0]]
    return total


def block_scan(inputs, steps, rates, bmat, cmat, block):
    length, heads, hsize = inputs.shape
    count = length // block
    in_blocks = inputs.reshape(count, block, heads, hsize)
    step_blocks = steps.reshape(count, block, heads)
    b_blocks = bmat.reshape(count, block, bmat.shape[1])
    c_blocks = cmat.reshape(count, block, cmat.shape[1])
    places = jnp.arange(block)
    lower = (places[:, None] >= places[None, :])[:, :, None]

    def advance(state, pieces):
        x_part, dt_part, b_part, c_part = pieces
        cums = jnp.cumsum(dt_part * rates, axis=0)
        spread = cums[:, None, :] - cums[None, :, :]
        decay = jnp.where(lower, jnp.exp(jnp.where(lower, spread, 0.0)), 0.0)
        scores = jnp.dot(c_part, b_part.T, precision=HIGH)
        weights = scores[:, :, None] * decay * dt_part[None, :, :]
        inside = jnp.einsum("ijh,jhp->ihp", weights, x_part, precision=HIGH)
        carried = (
            jnp.einsum("in,hpn->ihp", c_part, state, precision=HIGH) * jnp.exp(cums)[:, :, None]
        )
        tails = jnp.exp(cums[-1][None, :] - cums) * dt_part
        state = jnp.exp(cums[-1])[:, None, None] * state + jnp.einsum(
            "jh,jhp,jn->hpn", tails, x_part, b_part, precision=HIGH
        )
        return (state, inside + carried)

    start_state = jnp.zeros((heads, hsize, bmat.shape[1]), jnp.float32)
    _, result = lax.scan(
        jax.checkpoint(advance), start_state, (in_blocks, step_blocks, b_blocks, c_blocks)
    )
    return result.reshape(length, heads, hsize)


def mixer(zx, bc_raw, dt_raw, kernel_x, kernel_bc, bias_dt, log_rate, skip):
    length, heads, double = zx.shape
    hsize = double // 2
    gate = zx[:, :, :hsize]
    x_raw = zx[:, :, hsize:].reshape(length, heads * hsize)
    xs_conv = jax.nn.silu(conv_causal(x_raw, kernel_x)).reshape(length, heads, hsize)
    bc_conv = jax.nn.silu(conv_causal(bc_raw, kernel_bc))
    half = bc_conv.shape[1] // 2
    steps = jax.nn.softplus(dt_raw + bias_dt)
    rates = -jnp.exp(log_rate)
    result = (
        block_scan(xs_conv, steps, rates, bc_conv[:, :half], bc_conv[:, half:], SCAN_BLOCK)
        + skip[:, None] * xs_conv
    )
    return (result * jax.nn.silu(gate)).reshape(length, heads * hsize)


def per_device(
    hidden,
    lengths,
    cotangent,
    norm_gain,
    in_zx,
    in_bcdt,
    conv_x,
    conv_bc,
    dt_bias,
    a_log,
    d_skip,
    gnorm_gain,
    out_w,
):
    slice_rows, half_width = hidden.shape
    local_heads = in_zx.shape[1]
    head_count = lax.axis_size("head")
    head_index = lax.axis_index("head")
    total_rows = slice_rows * head_count
    seq_local = lengths.shape[0]
    inner_local = local_heads * HEADDIM
    row_ids = head_index * slice_rows + jnp.arange(slice_rows, dtype=jnp.int32)
    owner = (row_ids // LEN)[:, None] == jnp.arange(seq_local, dtype=jnp.int32)[None, :]
    limits = jnp.sum(jnp.where(owner, lengths[None, :], 0), axis=1)
    keeper = (row_ids % LEN < limits).astype(jnp.float32)[:, None]
    source = hidden.astype(jnp.float32)
    squares = lax.psum(jnp.sum(source * source, axis=1), "width")
    scale = lax.rsqrt(squares / D + EPS)[:, None]
    gain_in = norm_gain.astype(jnp.float32)
    normed = (source * scale * gain_in).astype(jnp.bfloat16)
    gathered = lax.all_gather(normed, "head", axis=0, tiled=True)
    w_zx = in_zx.reshape(half_width, local_heads * 2 * HEADDIM)
    zx_part = jnp.dot(gathered, w_zx, preferred_element_type=jnp.float32)
    bcdt_part = jnp.dot(gathered, in_bcdt, preferred_element_type=jnp.float32)
    zx_full, bcdt_full = lax.psum((zx_part, bcdt_part), "width")
    zx_seq = zx_full.reshape(seq_local, LEN, local_heads, 2 * HEADDIM)
    bc_seq = bcdt_full[:, : 2 * STATE].reshape(seq_local, LEN, 2 * STATE)
    dt_seq = lax.dynamic_slice_in_dim(
        bcdt_full, 2 * STATE + head_index * local_heads, local_heads, 1
    ).reshape(seq_local, LEN, local_heads)

    def local_mix(zx_in, bc_in, dt_in, kernel_x, kernel_bc, bias_in, log_in, skip_in):
        per_sequence = jax.vmap(mixer, in_axes=(0, 0, 0, None, None, None, None, None))
        return per_sequence(
            zx_in, bc_in, dt_in, kernel_x, kernel_bc, bias_in, log_in, skip_in
        ).reshape(total_rows, inner_local)

    gated, mix_pull = jax.vjp(
        local_mix,
        zx_seq,
        bc_seq,
        dt_seq,
        conv_x.astype(jnp.float32),
        conv_bc.astype(jnp.float32),
        dt_bias,
        a_log,
        d_skip,
    )
    total_sq = lax.psum(jnp.sum(gated * gated, axis=1), "head")
    scale_out = lax.rsqrt(total_sq / INNER + EPS)[:, None]
    gain_out = gnorm_gain.astype(jnp.float32)
    mixed = (gated * scale_out * gain_out).astype(jnp.bfloat16)
    picked = mixed
    branch = lax.psum_scatter(
        jnp.dot(picked, out_w, preferred_element_type=jnp.float32),
        "head",
        scatter_dimension=0,
        tiled=True,
    )
    out_hidden = (source + keeper * branch).astype(jnp.bfloat16)
    grad_out = cotangent.astype(jnp.float32)
    masked = (grad_out * keeper).astype(jnp.bfloat16)
    piece = lax.all_gather(masked, "head", axis=0, tiled=True)
    picked = mixed
    acc_weight = jnp.einsum("tc,td->cd", picked, piece, preferred_element_type=jnp.float32)
    product = jnp.einsum("td,cd->tc", piece, out_w, preferred_element_type=jnp.float32)
    grad_mixed = lax.psum(product, "width")
    gain_out_grad = jnp.sum(grad_mixed * gated * scale_out, axis=0)
    inner_total = lax.psum(jnp.sum(grad_mixed * gain_out * gated, axis=1), "head")
    cubed = scale_out * scale_out * scale_out
    grad_gated = scale_out * gain_out * grad_mixed - gated * cubed / INNER * inner_total[:, None]
    (
        grad_zx_seq,
        grad_bc_seq,
        grad_dt_seq,
        kernel_x_grad,
        kernel_bc_grad,
        bias_grad,
        rate_grad,
        skip_grad,
    ) = mix_pull(grad_gated)
    grad_zx = grad_zx_seq.reshape(total_rows, local_heads * 2 * HEADDIM).astype(jnp.bfloat16)
    dt_columns = jnp.zeros((total_rows, HEADS), jnp.float32)
    dt_columns = lax.dynamic_update_slice_in_dim(
        dt_columns, grad_dt_seq.reshape(total_rows, local_heads), head_index * local_heads, 1
    )
    grad_bcdt_head = jnp.concatenate(
        [grad_bc_seq.reshape(total_rows, 2 * STATE), dt_columns], axis=1
    )
    weight_zx = jnp.einsum(
        "td,tc->dc", gathered, grad_zx, preferred_element_type=jnp.float32
    ).reshape(half_width, local_heads, 2 * HEADDIM)
    normed_part = jnp.einsum("tc,dc->td", grad_zx, w_zx, preferred_element_type=jnp.float32)
    grad_normed, bcdt_summed = (
        lax.psum_scatter(normed_part, "head", scatter_dimension=0, tiled=True),
        lax.psum_scatter(grad_bcdt_head, "head", scatter_dimension=0, tiled=True),
    )
    bcdt_low = bcdt_summed.astype(jnp.bfloat16)
    grad_normed = grad_normed + jnp.einsum(
        "tk,dk->td", bcdt_low, in_bcdt, preferred_element_type=jnp.float32
    )
    weight_bcdt = jnp.einsum("td,tk->dk", normed, bcdt_low, preferred_element_type=jnp.float32)
    gain_in_grad = jnp.sum(grad_normed * source * scale, axis=0)
    across = lax.psum(jnp.sum(grad_normed * gain_in * source, axis=1), "width")
    scale_cubed = scale * scale * scale
    grad_hidden = (
        grad_out + scale * gain_in * grad_normed - source * scale_cubed / D * across[:, None]
    ).astype(jnp.bfloat16)
    summed_dp = lax.psum(
        (weight_zx, acc_weight, kernel_x_grad, bias_grad, rate_grad, skip_grad, gain_out_grad), "dp"
    )
    summed_all = lax.psum((weight_bcdt, gain_in_grad, kernel_bc_grad), ("dp", "head"))
    return (
        out_hidden,
        grad_hidden,
        summed_all[1],
        summed_dp[0],
        summed_all[0],
        summed_dp[2],
        summed_all[2],
        summed_dp[3],
        summed_dp[4],
        summed_dp[5],
        summed_dp[6],
        summed_dp[1],
    )


BF = jnp.bfloat16
F32 = jnp.float32
Q = 128
HALO = 16
NEG = -1e30
MESH = pl.DeviceIdType.MESH
VMEM = 60 * 1024 * 1024


def dot(a, b, prec=None):
    return lax.dot_general(a, b, (((1,), (0,)), ((), ())), precision=prec, preferred_element_type=F32)


def dot_t(a, b, prec=None):
    return lax.dot_general(a, b, (((1,), (1,)), ((), ())), precision=prec, preferred_element_type=F32)


def t_dot(a, b, prec=None):
    return lax.dot_general(a, b, (((0,), (0,)), ((), ())), precision=prec, preferred_element_type=F32)


def split2(v, axis=1):
    hi = v.astype(BF)
    lo = (v - hi.astype(F32)).astype(BF)
    return jnp.concatenate([hi, lo], axis=axis)


def dot_split(v, m):
    hi = v.astype(BF)
    lo = (v - hi.astype(F32)).astype(BF)
    return dot(hi, m) + dot(lo, m)


def split_dot(m, v):
    hi = v.astype(BF)
    lo = (v - hi.astype(F32)).astype(BF)
    return dot(m, hi) + dot(m, lo)


def sigmoid(v):
    return 1.0 / (1.0 + jnp.exp(-v))


def tri(kind):
    row = lax.broadcasted_iota(jnp.int32, (Q, Q), 0)
    col = lax.broadcasted_iota(jnp.int32, (Q, Q), 1)
    return {"ge": row >= col, "le": row <= col, "gt": row > col}[kind]


def slot_heads(heads, per):
    nz = heads // per
    own = HEADS // nz
    bits = per.bit_length() - 1
    slot = lax.broadcasted_iota(jnp.int32, (heads, HEADS), 0)
    head = lax.broadcasted_iota(jnp.int32, (heads, HEADS), 1)
    z = (lax.axis_index("head") - (slot >> bits)) & (nz - 1)
    m = (slot & (per - 1)) ^ lax.axis_index("dp")
    return (head == z * own + lax.axis_index("width") * per + m).astype(F32)


def prep_kernel(
    per, zx, ow, bcdt, gain, cx, scal, gn,
    first_o, first2_o, rest_o, rest2_o, out_o, out2_o, bcdt_o, table_o,
):
    di = lax.axis_index("dp")
    wi = lax.axis_index("width")
    wide = 2 * HEADDIM
    for m in range(per):
        for w, whole_o, some_o, o_o in (
            (wi, first_o, rest_o, out_o), (1 - wi, first2_o, rest2_o, out2_o)
        ):
            head = w * per + jnp.bitwise_xor(di, m)
            v = jnp.transpose(zx[:, pl.ds(pl.multiple_of(head * wide, wide), wide)])
            for i in range(2):
                part = v[i * HEADDIM : (i + 1) * HEADDIM, :]
                if m == 0:
                    whole_o[i] = part
                else:
                    some_o[i, (m - 1) * HEADDIM : m * HEADDIM, :] = part
            o_o[m * HEADDIM : (m + 1) * HEADDIM, :] = ow[
                pl.ds(pl.multiple_of(head * HEADDIM, HEADDIM), HEADDIM), :
            ]
    n = bcdt.shape[1]
    bcdt_o[0:n, :] = jnp.transpose(bcdt[...])
    bcdt_o[n:, :] = jnp.broadcast_to(gain[...], (HALO, gain.shape[1]))
    rows = jnp.concatenate(
        [cx[...].astype(F32), gn[...].astype(F32), scal[...]], axis=0
    )
    half = rows.shape[1] // 2
    rows = jnp.where(wi == 0, rows[:, :half], rows[:, half:])
    step = 1
    while step < per:
        size = HEADDIM * step
        parts = [rows[:, i * size : (i + 1) * size] for i in range(half // size)]
        swapped = jnp.concatenate([parts[i ^ 1] for i in range(len(parts))], axis=1)
        rows = jnp.where(jnp.bitwise_and(di, step) != 0, swapped, rows)
        step *= 2
    table_o[...] = rows


def entry_first(per, hm, ho, hh, bcdt, table, cbc, sel, o, xn_o, buf):
    xnh_o, r_o, raw_o, rawh_o, dt_o, sig_o = o.xnh, o.r, o.raw, o.rawh, o.dt, o.sig
    cl_o, clt_o, rate_o, wdt_o, b_o = o.cl, o.clt, o.rate, o.wdt, o.b
    rows = hm.shape[0]
    state = b_o.shape[1]
    per_head = dot(table[...], sel[...], HIGH)
    bias = per_head[5:6, :]
    rate = -jnp.exp(per_head[6:7, :])
    rate_o[...] = rate
    wbc = bcdt.at[0 : 2 * state, :]
    wdt_o[...] = dot(
        slot_heads(rate.shape[1], per).astype(BF), bcdt[2 * state : 2 * state + HEADS, :]
    ).astype(BF)
    wdt = wdt_o
    gain = bcdt[2 * state + HEADS : 2 * state + HEADS + 1, :].astype(F32)
    blocks = rows // Q
    lower = tri("ge").astype(F32)

    def norm(left, right):
        h = jnp.concatenate([left, right], axis=1).astype(F32)
        r = lax.rsqrt(jnp.mean(h * h, axis=1, keepdims=True) + EPS)
        return (h * r * gain).astype(BF), r

    half = hm.shape[1]
    xnh, _ = norm(hh[:, :half], hh[:, half:])
    xnh = jnp.where(lax.axis_index("head") > 0, xnh.astype(F32), 0.0).astype(BF)
    xnh_o[...] = xnh
    buf[0:HALO, :] = dot_t(xnh, wbc[...])
    rawh_o[...] = buf[0:HALO, :]

    def first(i, carry):
        here = pl.ds(pl.multiple_of(i * Q, Q), Q)
        xn, r = norm(hm[here, :], ho[here, :])
        xn_o[here, :] = xn
        r_o[here, :] = r
        raw = dot_t(xn, wbc[...])
        raw_o[here, :] = raw
        buf[pl.ds(pl.multiple_of(HALO + i * Q, HALO), Q), :] = raw
        steps = dot_t(xn, wdt[...]) + bias
        dt = jax.nn.softplus(steps)
        dt_o[here, :] = dt
        sig_o[here, :] = sigmoid(steps)
        da = dt * rate
        cl_o[here, :] = dot(lower, da, HIGH)
        clt_o[:, here] = lax.dot_general(
            da, lower, (((0,), (1,)), ((), ())), precision=HIGH, preferred_element_type=F32
        )
        return carry

    lax.fori_loop(0, blocks, first, 0, unroll=2)


def entry_second(cbc, o, tot_o, buf):
    u_o, b_o, c_o, dt_o, cl_o, clt_o = o.ubc, o.b, o.c, o.dt, o.cl, o.clt
    dt2_o, e12_o, tl2_o, dttl2_o, ec2_o, edt2_o = o.dt2, o.e12, o.tl2, o.dttl2, o.ec2, o.edt2
    state = b_o.shape[1]
    blocks = b_o.shape[0] // Q

    def second(i, carry):
        here = pl.ds(pl.multiple_of(i * Q, Q), Q)
        win = buf[pl.ds(pl.multiple_of(i * Q, Q), Q + HALO), :]
        u = jnp.zeros((Q, win.shape[1]), F32)
        for k in range(4):
            u = u + cbc[k : k + 1, :] * win[HALO - 3 + k : HALO - 3 + k + Q, :]
        u_o[here, :] = u
        v = u * sigmoid(u)
        b_o[here, :] = v[:, :state].astype(BF)
        c_o[here, :] = v[:, state:].astype(BF)
        return carry

    lax.fori_loop(0, blocks, second, 0, unroll=2)
    tots = [cl_o[i * Q + Q - 1 : i * Q + Q, :] for i in range(blocks)]
    ctot = functools.reduce(lambda x, y: x + y, tots)
    heads = clt_o.shape[0]
    column = functools.reduce(
        lambda x, y: x + y, [clt_o[:, i * Q + Q - 1 : i * Q + Q] for i in range(blocks)]
    )
    hi = column.astype(BF)
    mid = (column - hi.astype(F32)).astype(BF)
    low = (column - hi.astype(F32) - mid.astype(F32)).astype(BF)
    lane = lax.broadcasted_iota(jnp.int32, (heads, tot_o.shape[1]), 1)
    tot_o[...] = jnp.where(
        lane == 0,
        hi.astype(F32),
        jnp.where(lane == 1, mid.astype(F32), jnp.where(lane == 2, low.astype(F32), 0.0)),
    ).astype(BF)
    off = jnp.zeros_like(ctot)
    for i in range(blocks):
        here = slice(i * Q, i * Q + Q)
        cl = cl_o[here, :]
        dt = dt_o[here, :]
        tail = jnp.exp(tots[i] - cl)
        dt2_o[here, :] = split2(dt)
        e12_o[here, :] = split2(jnp.exp(cl))
        tl2_o[here, :] = split2(tail)
        dttl2_o[here, :] = split2(dt * tail)
        ec2_o[here, :] = split2(jnp.exp(cl + off))
        edt2_o[here, :] = split2(dt * jnp.exp(ctot - cl - off))
        off = off + tots[i]


def decay(cl, clt, h, mask):
    return jnp.exp(jnp.where(mask, cl[:, h : h + 1] - clt[h : h + 1, :], NEG))


def lane_masks():
    lane = lax.broadcasted_iota(jnp.int32, (1, Q), 1)
    low = (lane < HEADDIM).astype(F32)
    return low.astype(BF), (1.0 - low).astype(BF)


def project(s, per, xn, o, w, cw, ex, z_o, xr_o, xrh_o, u_o, xdt_o, msg, buf, acc):
    rows = z_o.shape[0]
    gc = per * HEADDIM
    cols = slice(s * gc, s * gc + gc)
    xh = dot_t(o.xnh[...], w[1, cols, :])
    buf[0:HALO, :] = xh
    xrh_o[...] = xh
    acc[...] = jnp.zeros_like(acc)
    cut = rows // 2 if rows // 2 % Q == 0 else rows

    def part(j, carry):
        base = j * cut
        here = pl.ds(pl.multiple_of(base, Q), cut)
        buf[pl.ds(pl.multiple_of(base + HALO, HALO), cut), :] = dot_t(xn[here, :], w[1, cols, :])
        z_o[here, :] = dot_t(xn[here, :], w[0, cols, :])
        for i in range(cut // Q):
            here = pl.ds(pl.multiple_of(base + i * Q, Q), Q)
            win = buf[pl.ds(pl.multiple_of(base + i * Q, Q), Q + HALO), :]
            u = jnp.zeros((Q, gc), F32)
            for k in range(4):
                u = u + cw[k : k + 1, cols] * win[HALO - 3 + k : HALO - 3 + k + Q, :]
            xr_o[here, :] = win[HALO:, :].astype(BF)
            u_o[here, :] = u
            xs = u * sigmoid(u)
            xdt_o[here, :] = (xs * dot(o.dt2[here, :], ex[:, cols])).astype(BF)
            acc[...] += t_dot((xs * dot(o.edt2[here, :], ex[:, cols])).astype(BF), o.b[here, :])
        return carry

    lax.fori_loop(0, rows // cut, part, 0)
    msg[cols, :] = acc[...].astype(BF)


def inside(s, per, xdt, o, y_o):
    mask = tri("ge")
    low, high = lane_masks()
    rows = xdt.shape[0]
    some = 4 if rows % (4 * Q) == 0 else 1

    def part(j, carry):
        for i in range(some):
            here = pl.ds(pl.multiple_of((j * some + i) * Q, Q), Q)
            g = dot_t(o.c[here, :], o.b[here, :])
            clv, cltv = o.cl[here, :], o.clt[:, here]
            for p in range(xdt.shape[1] // Q):
                lanes = slice(p * Q, p * Q + Q)
                h = s * per + 2 * p
                ws = [(g * decay(clv, cltv, k, mask)).astype(BF) for k in (h, h + 1)]
                x = xdt[here, lanes]
                y_o[here, lanes] = dot(
                    jnp.concatenate(ws, axis=1), jnp.concatenate([x * low, x * high], axis=0)
                ).astype(BF)
        return carry

    lax.fori_loop(0, rows // (some * Q), part, 0)


class Named:
    def __init__(self, names, refs):
        for name, ref in zip(names, refs):
            setattr(self, name, ref)


KEPT = (
    "xnh", "r", "raw", "rawh", "ubc", "b", "c", "dt", "sig", "cl", "clt", "dt2", "e12", "tl2",
    "dttl2", "ec2", "edt2", "rate", "wdt", "tot", "table", "bcdt",
)


def front_kernel(per, nz, *refs):
    hidden, first, first2, rest, rest2, bcdt, table, cbc, sel, ex, refs = take(refs, *[0] * 10)
    out_mine, out2, cot, refs = take(refs, 0, 0, 0)
    w_o, wo_o, cot_o, xn_o, refs = take(refs, 0, 0, 0, 0)
    z_o, xr_o, u_o, xdt_o, y_o, messages_o, xrh_o, refs = take(refs, *[nz] * 5, nz - 1, nz)
    kept, refs = refs[: len(KEPT)], refs[len(KEPT) :]
    o = Named(KEPT, kept)
    z_v, xr_v, u_v, xdt_v, y_v, refs = take(refs, *[nz] * 5)
    w, ho, eh, xn, msg, buf, bcbuf, acc, sends, receives, locals_ = refs
    bc = o.bcdt
    rows, half = hidden.shape
    gc = per * HEADDIM
    top = nz * gc
    sibling = {"width": 1 - lax.axis_index("width")}
    z_peers = line_peers(nz, 1)
    d_peers = plane_peers(per)
    used = [0]

    def copy(source, target, peer):
        i = used[0]
        used[0] += 1
        return remote(source, target, sends, receives, i, peer)

    left, right = pl.ds(0, half), pl.ds(half, half)
    swap_first = copy(first2, w.at[:, pl.ds(0, HEADDIM), right], sibling)
    swap_rest = copy(rest2, w.at[:, pl.ds(HEADDIM, gc - HEADDIM), right], sibling)
    swap_hidden = copy(hidden, ho, sibling)
    swap_bc = copy(bcdt, bc.at[:, right], sibling)
    swap_out = copy(out2, wo_o.at[pl.ds(0, gc), right], sibling)
    swap_cot = copy(cot, cot_o, sibling)
    z_table, z_w, z_out, z_state, z_state2 = [], [], [], [], []
    for k, peer in enumerate(z_peers):
        s = k + 1
        z_table.append(copy(table, o.table.at[:, pl.ds(s * gc, gc)], peer))
        own = w.at[:, pl.ds(0, HEADDIM), :]
        z_w.append(copy(own, w.at[:, pl.ds(s * gc, HEADDIM), :], peer))
        z_out.append(
            copy(wo_o.at[pl.ds(0, HEADDIM), :], wo_o.at[pl.ds(s * gc, HEADDIM), :], peer)
        )
        most = pl.ds(0, top - gc)
        z_state.append(copy(msg.at[most, :], messages_o[k].at[most, :], peer))
        more = pl.ds(top - gc, gc + HALO)
        z_state2.append(copy(msg.at[more, :], messages_o[k].at[more, :], peer))
    last = pl.ds(rows - HALO, HALO)
    edge1 = copy(hidden.at[last, :], eh.at[:, left], z_peers[0])
    edge2 = copy(ho.at[last, :], eh.at[:, right], z_peers[0])
    p_w = {s: [] for s in range(1, nz)}
    p_out = {s: [] for s in range(1, nz)}
    for s in range(1, nz):
        for k, peer in enumerate(d_peers):
            mine = pl.ds(s * gc, HEADDIM)
            there = pl.ds(s * gc + (k + 1) * HEADDIM, HEADDIM)
            p_w[s].append(copy(w.at[:, mine, :], w.at[:, there, :], peer))
            p_out[s].append(copy(wo_o.at[mine, :], wo_o.at[there, :], peer))

    places = [0]

    def local(source, target):
        i = places[0]
        places[0] += 1
        found = pltpu.make_async_copy(source, target, locals_.at[i])
        found.start()
        return found

    ready = [
        local(first, w.at[:, pl.ds(0, HEADDIM), left]),
        local(rest, w.at[:, pl.ds(HEADDIM, gc - HEADDIM), left]),
        local(bcdt, bc.at[:, left]),
        local(table, o.table.at[:, pl.ds(0, gc)]),
        local(out_mine, wo_o.at[pl.ds(0, gc), left]),
    ]
    meet([sibling, *z_peers, *line_peers(nz, -1), *d_peers])
    start([swap_first, *z_table, swap_hidden, swap_bc, edge1, swap_rest, swap_out, swap_cot])
    ready[0].wait()
    arrive([swap_first])
    start(z_w)
    arrive([swap_hidden])
    start([edge2])
    for c in ready[1:]:
        c.wait()
    arrive([swap_bc, *z_table, edge1, edge2])
    entry_first(per, hidden, ho, eh, bc, o.table, cbc, sel, o, xn, bcbuf)
    arrive([z_w[0]])
    start(p_w[1])
    entry_second(cbc, o, o.tot, bcbuf)
    msg[top:, :] = o.tot[...]
    pending = [local(xn, xn_o)]
    arrive([swap_out])
    start(z_out)
    arrive([swap_rest])
    taps = o.table
    for s in range(nz):
        if s > 0:
            arrive(p_w[s])
        project(
            s, per, xn, o, w, taps, ex, z_v[s], xr_v[s], xrh_o[s], u_v[s], xdt_v[s], msg, buf, acc
        )
        for a, b in ((z_v, z_o), (xr_v, xr_o), (u_v, u_o), (xdt_v, xdt_o)):
            pending.append(local(a[s], b[s]))
        if s == 0:
            for k in range(2, nz):
                arrive([z_w[k - 1]])
                start(p_w[k])
        if s == nz - 2:
            start(z_state)
            for k in range(1, nz):
                arrive([z_out[k - 1]])
                start(p_out[k])
        if s == nz - 1:
            start(z_state2)
            pending.append(local(w, w_o))
        inside(s, per, xdt_v[s], o, y_v[s])
        pending.append(local(y_v[s], y_o[s]))
    everything = [swap_first, swap_rest, swap_hidden, swap_bc, swap_out, swap_cot, edge1, edge2]
    everything += [*z_table, *z_w, *z_out, *z_state, *z_state2]
    for s in range(1, nz):
        everything += p_w[s] + p_out[s]
        arrive(p_out[s])
    arrive([swap_cot, *z_state, *z_state2])
    for c in everything:
        c.wait_send()
    for c in pending:
        c.wait()


def head_scale(clt, first, per, state):
    return jnp.concatenate(
        [
            jnp.broadcast_to(jnp.exp(clt[h : h + 1, Q - 1 : Q]), (HEADDIM, state))
            for h in range(first, first + per)
        ],
        axis=0,
    )


def from_messages(messages, sign, groups, per, state, store, valid=None):
    nz = len(messages) + 1
    gc = per * HEADDIM
    top = nz * gc
    totals = [
        sum(m[top:, i : i + 1].astype(F32) for i in range(3)) for m in messages
    ]
    for at, j in enumerate(groups):
        total = jnp.zeros((gc, state), F32)
        faded = jnp.zeros((per, 1), F32)
        for k in range(1, nz):
            there = (j - sign * k) % nz
            scale = jnp.exp(faded)
            scale = jnp.concatenate(
                [jnp.broadcast_to(scale[h : h + 1, :], (HEADDIM, state)) for h in range(per)],
                axis=0,
            )
            part = scale * messages[k - 1][there * gc : there * gc + gc, :].astype(F32)
            if valid is not None:
                part = jnp.where(valid(k), part, 0.0)
            total = total + part
            faded = faded + totals[k - 1][there * per : there * per + per, :]
        store[at * gc : at * gc + gc, :] = total


def carry_kernel(groups, per, *refs):
    n = len(groups)
    y_in, us, z, dyn, b, c, clt, e12, dttl2, messages, dsk, gain, ex, rest = take(
        refs, n, n, n, 0, 0, 0, 0, 0, 0, n - 1, 0, 0, 0
    )
    ys_o, st_o, rest = take(rest, n, n)
    gg_o, sum_o, s = rest
    gc = per * HEADDIM

    @pl.when(pl.program_id(0) == 0)
    def _():
        z_index = lax.axis_index("head")
        from_messages(messages, 1, groups, per, s.shape[1], s, lambda k: z_index - k >= 0)

    square = jnp.zeros((Q, gc), F32)
    inner = jnp.zeros((Q, gc), F32)
    for j in groups:
        here = slice(j * gc, j * gc + gc)
        sv = s[here, :]
        sb = sv.astype(BF)
        st_o[j][0] = sb
        x = us[j][...]
        x = x * sigmoid(x)
        e1 = dot(e12[...], ex[:, here])
        y = y_in[j][...].astype(F32) + e1 * dot_t(c[...], sb) + dsk[:, here] * x
        ys_o[j][...] = y
        xt = (x * dot(dttl2[...], ex[:, here])).astype(BF)
        s[here, :] = head_scale(clt, j * per, per, sv.shape[1]) * sv + t_dot(xt, b[...])
        zz = z[j][...]
        gz = y * (zz * sigmoid(zz))
        gg = gz * gain[:, here]
        gg_o[:, here] = gg.astype(BF)
        square = square + gz * gz
        inner = inner + gg * dyn[:, here]
    lane = lax.broadcasted_iota(jnp.int32, (Q, 2), 1)
    sum_o[...] = jnp.where(
        lane == 0,
        jnp.sum(square, axis=1, keepdims=True),
        jnp.sum(inner, axis=1, keepdims=True),
    )


def gate_kernel(groups, per, *refs):
    n = len(groups)
    ys, z, us, dyn, sums, sums2, gain, ec2, ex, c, rest = take(refs, n, n, n, *[0] * 7)
    hidden, branch, branch2, limit, rest = take(rest, 0, 0, 0, 0)
    dys_o, rest = take(rest, n)
    dz_o, yn_o, ds_o, gn_o, sk_o, out_o, acc = rest
    gc = per * HEADDIM

    @pl.when(pl.program_id(0) == 0)
    def _():
        acc[...] = jnp.zeros_like(acc)
        gn_o[...] = jnp.zeros_like(gn_o)
        sk_o[...] = jnp.zeros_like(sk_o)

    count = n * gc * 2
    both = sums[...] + sums2[...]
    r2 = lax.rsqrt(both[:, 0:1] / count + EPS)
    pull = both[:, 1:2] * (r2 * r2 * r2) / count
    row = lax.broadcasted_iota(jnp.int32, (Q, 1), 0) + pl.program_id(0) * Q
    keep = jnp.where(row < limit[0, 0], r2, 0.0)
    out_o[...] = (
        hidden[...].astype(F32) + keep * (branch[...] + branch2[...].astype(F32))
    ).astype(BF)
    for j in groups:
        here = slice(j * gc, j * gc + gc)
        gn = gain[:, here]
        zz = z[j][...]
        sz = sigmoid(zz)
        silu = zz * sz
        y = ys[j][...]
        gz = y * silu
        dy_n = dyn[:, here]
        gr = gz * r2
        yn_o[:, here] = (gr * gn).astype(BF)
        gn_o[:, here] += jnp.sum(dy_n * gr, axis=0, keepdims=True)
        dgz = r2 * gn * dy_n - gz * pull
        dys = dgz * silu
        dys_o[j][...] = dys.astype(BF)
        dz_o[:, here] = (dgz * y * (sz + silu * (1.0 - sz))).astype(BF)
        x = us[j][...]
        x = x * sigmoid(x)
        sk_o[:, here] += jnp.sum(dys * x, axis=0, keepdims=True)
        acc[here, :] += t_dot((dys * dot(ec2[...], ex[:, here])).astype(BF), c[...])

    @pl.when(pl.program_id(0) == pl.num_programs(0) - 1)
    def _():
        ds_o[...] = acc[...].astype(BF)


def line_peers(count, sign):
    z = lax.axis_index("head")
    return [{"head": lax.rem(z + sign * k + count, count)} for k in range(1, count)]


def plane_peers(count):
    d = lax.axis_index("dp")
    return [{"dp": jnp.bitwise_xor(d, m)} for m in range(1, count)]


def meet(peers):
    barrier = pltpu.get_barrier_semaphore()
    for peer in peers:
        pl.semaphore_signal(barrier, inc=1, device_id=peer, device_id_type=MESH)
    pl.semaphore_wait(barrier, len(peers))


def remote(source, target, sends, receives, i, peer):
    return pltpu.make_async_remote_copy(
        src_ref=source,
        dst_ref=target,
        send_sem=sends.at[i],
        recv_sem=receives.at[i],
        device_id=peer,
        device_id_type=MESH,
    )


def conv_back(d, nxt, taps, raw, rawh, grad_o, out_o, outh_o, last):
    win = jnp.concatenate([d, nxt[...]], axis=0)
    back = jnp.zeros_like(d)
    sums = []
    for k in range(4):
        part = win[3 - k : 3 - k + Q, :]
        back = back + taps[k : k + 1, :] * part
        sums.append(jnp.sum(raw * part, axis=0, keepdims=True))
    grad_o[...] += jnp.concatenate(sums, axis=0)
    out_o[...] = back.astype(BF)
    nxt[...] = d[0:8, :]

    @pl.when(last)
    def _():
        win_h = jnp.concatenate([jnp.zeros((HALO, d.shape[1]), F32), d[0:8, :]], axis=0)
        back_h = jnp.zeros((HALO, d.shape[1]), F32)
        sums_h = []
        for k in range(4):
            part = win_h[3 - k : 3 - k + HALO, :]
            back_h = back_h + taps[k : k + 1, :] * part
            sums_h.append(jnp.sum(rawh[...] * part, axis=0, keepdims=True))
        grad_o[...] += jnp.concatenate(sums_h, axis=0)
        outh_o[...] = back_h.astype(BF)


def scan_back_kernel(groups, per, *refs):
    n = len(groups)
    nz = n
    xdt, dys, u, xr, st, xrh, rest = take(refs, n, n, n, n, n, n)
    (b, c, cl, clt, dt, sig, dt2, e12, tl2), rest = rest[:9], rest[9:]
    (ubc, braw, brawh, cw, cbc, rate, dsk, ex, er), rest = rest[:9], rest[9:]
    message, early, rest = take(rest, 0, per)
    dx_o, dxh_o, gcx_o, rest = take(rest, n, n, n)
    dt_o, ga_o, gbias_o, bc_o, bch_o, gcb_o, early_o = rest[:7]
    messages, got, rest = take(rest[7:], nz - 1, per - 1)
    du_next, line, rest = take(rest, n, nz - 1)
    db_next, own, low, dxi, dbi, dci, dai, kt, ds, vs, sends, receives, local = rest
    step = pl.program_id(0)
    blocks = pl.num_programs(0) // 2
    heads = dt.shape[1]
    state = b.shape[1]
    gc = per * HEADDIM
    line_at, back_at, plane_at = 0, nz - 1, 2 * nz - 2

    def state_copies():
        return [
            remote(message, messages[i], sends, receives, line_at + i, peer)
            for i, peer in enumerate(line_peers(nz, -1))
        ]

    def plane_copies(s):
        return [
            remote(
                early[i + 1].at[s], got[i].at[s], sends, receives, plane_at + s * (per - 1) + i, peer
            )
            for i, peer in enumerate(plane_peers(per))
        ]

    def line_copy(s):
        return remote(
            low.at[s], line[s - 1], sends, receives, back_at + s - 1, line_peers(nz, -1)[s - 1]
        )

    def own_copy():
        return pltpu.make_async_copy(early[0], own, local)

    @pl.when(step == 0)
    def _():
        own_copy().start()
        meet(line_peers(nz, -1) + line_peers(nz, 1) + plane_peers(per))
        for copy in plane_copies(1) + state_copies():
            copy.start()

    @pl.when(step < blocks)
    def _():
        rows = pl.ds(pl.multiple_of(step * Q, Q), Q)
        mask = tri("ge")
        lower, upper_lanes = lane_masks()
        g = dot_t(c[...], b[...])
        clv, cltv = cl[...], clt[...]
        lane = lax.broadcasted_iota(jnp.int32, (Q, heads), 1)
        dg = jnp.zeros((Q, Q), F32)
        rsum = jnp.zeros((Q, heads), F32)
        for s in groups:
            for p in range(per // 2):
                here = slice(p * Q, p * Q + Q)
                x = xdt[s][:, here]
                dy = dys[s][:, here]
                pp = dot_t(dy, jnp.concatenate([x * lower, x * upper_lanes], axis=0))
                ws = []
                for j in range(2):
                    h = s * per + 2 * p + j
                    ell = decay(clv, cltv, h, mask)
                    ws.append((g * ell).astype(BF))
                    pe = pp[:, j * Q : j * Q + Q] * ell
                    dg = dg + pe
                    m = pe * g
                    rsum = jnp.where(lane == h, jnp.sum(m, axis=1, keepdims=True), rsum)
                    kt[h : h + 1, :] = jnp.sum(m, axis=0, keepdims=True)
                dxi[rows, s * gc + p * Q : s * gc + p * Q + Q] = t_dot(
                    jnp.concatenate(ws, axis=0),
                    jnp.concatenate([dy * lower, dy * upper_lanes], axis=0),
                )
        dgb = dg.astype(BF)
        dci[rows, :] = dot(dgb, b[...])
        dbi[rows, :] = t_dot(dgb, c[...])
        upper = tri("le").astype(F32)
        dai[rows, :] = dot(upper, rsum, HIGH) - dot_t(upper, kt[...], HIGH)

    @pl.when(step == blocks)
    def _():
        for copy in state_copies():
            copy.wait()
        z = lax.axis_index("head")
        from_messages(messages, -1, groups, per, state, ds, lambda k: z + k < nz)
        for i in range(n):
            du_next[i][...] = jnp.zeros_like(du_next[i])
            gcx_o[i][...] = jnp.zeros_like(gcx_o[i])
        db_next[...] = jnp.zeros_like(db_next)
        gcb_o[...] = jnp.zeros_like(gcb_o)
        ga_o[...] = jnp.zeros_like(ga_o)
        gbias_o[...] = jnp.zeros_like(gbias_o)

    @pl.when(step >= blocks)
    def _():
        rows = pl.ds(pl.multiple_of((2 * blocks - 1 - step) * Q, Q), Q)
        last = step == 2 * blocks - 1
        rsum = jnp.zeros((Q, heads), F32)
        gsum = jnp.zeros((Q, heads), F32)
        ddt = jnp.zeros((Q, heads), F32)
        dbs = dbi[rows, :]
        dcs = dci[rows, :]
        for s in groups:
            here = slice(s * gc, s * gc + gc)
            ehere = er[here, :]
            sb = st[s][0]
            dsv = ds[here, :]
            dsb = dsv.astype(BF)
            dy = dys[s][...].astype(F32)
            dye = dy * dot(e12[...], ex[:, here])
            dyb = dye.astype(BF)
            rsum = rsum + dot((dye * dot_t(c[...], sb)).astype(BF), ehere)
            dcs = dcs + dot(dyb, sb)
            bds = dot_t(b[...], dsb)
            tail = dot(tl2[...], ex[:, here])
            dtx = dot(dt2[...], ex[:, here])
            uu = u[s][...]
            su = sigmoid(uu)
            xs = uu * su
            xt = xs * dtx * tail
            gsum = gsum + dot((xt * bds).astype(BF), ehere)
            dbs = dbs + dot(xt.astype(BF), dsb)
            dxdt = dxi[rows, here] + tail * bds
            ddt = ddt + dot((dxdt * xs).astype(BF), ehere)
            eds = head_scale(clt, s * per, per, state) * dsv
            ev = eds * sb.astype(F32)
            for j in range(per):
                h = s * per + j
                vs[h : h + 1, :] = jnp.sum(
                    ev[j * HEADDIM : (j + 1) * HEADDIM, :], axis=0, keepdims=True
                )
            ds[here, :] = eds + t_dot(dyb, c[...])
            du = (dxdt * dtx + dsk[:, here] * dy) * (su + xs * (1.0 - su))
            conv_back(
                du, du_next[s], cw.at[:, here], xr[s][...].astype(F32), xrh[s], gcx_o[s],
                dx_o[s], dxh_o[s], last,
            )
        vrow = dot_t(jnp.ones((8, state), F32), vs[...], HIGH)
        da = (
            dai[rows, :]
            + split_dot(tri("le").astype(BF), rsum)
            + split_dot(tri("gt").astype(BF), gsum)
            + vrow[0:1, :]
        )
        draw = (rate[...] * da + ddt) * sig[...]
        dt_o[...] = draw.astype(BF)
        ga_o[...] += jnp.sum(da * dt[...], axis=0, keepdims=True)
        gbias_o[...] += jnp.sum(draw, axis=0, keepdims=True)
        d = jnp.concatenate([dbs, dcs], axis=1)
        v = ubc[...]
        sv = sigmoid(v)
        conv_back(
            d * (sv + v * sv * (1.0 - sv)), db_next, cbc, braw[...], brawh, gcb_o, bc_o, bch_o,
            last,
        )

    def add(s):
        for copy in plane_copies(s):
            copy.wait()

        def piece(i, carry):
            part = pl.ds(pl.multiple_of(i * HALO, HALO), HALO)
            total = own[s, part, :].astype(F32)
            for v in got:
                total = total + v[s, part, :].astype(F32)
            low[s, part, :] = total.astype(BF)
            return carry

        lax.fori_loop(0, low.shape[1] // HALO, piece, 0, unroll=2)

    order = [*range(1, nz), 0]
    for k, s in enumerate(order):
        if k > 0:

            @pl.when(step == (blocks * k * 3) // (2 * nz))
            def _(s=s):
                for copy in plane_copies(s):
                    copy.start()

        if s > 0:

            @pl.when(step == blocks + (blocks * 3 * k) // (4 * (nz - 1)) + 1)
            def _(s=s):
                if s == 1:
                    own_copy().wait()
                add(s)
                line_copy(s).start()

    @pl.when(step == 2 * blocks - 1)
    def _():
        add(0)
        for s in range(1, nz):
            line_copy(s).wait()
        total = low[0].astype(F32)
        for v in line:
            total = total + v[...].astype(F32)
        early_o[...] = total.astype(BF)


def sum_products_kernel(n, *refs):
    a, w, _, rest = take(refs, n, n, 0)
    left_o, right_o = rest
    total = dot(a[0][...], w[0][...])
    for i in range(1, n):
        total = total + dot(a[i][...], w[i][...])
    half = left_o.shape[1]
    left_o[...] = total[:, :half]
    right_o[...] = total[:, half:].astype(BF)


def pull_kernel(cot, cot2, limit, w, mask_o, dyn_o):
    rows = cot.shape[0]
    half = cot.shape[1]
    row = lax.broadcasted_iota(jnp.int32, (rows, 1), 0) + pl.program_id(0) * rows
    keep = row < limit[0, 0]
    for i, v in enumerate((cot, cot2)):
        mask_o[:, i * half : i * half + half] = jnp.where(keep, v[...].astype(F32), 0.0).astype(BF)
    dyn_o[...] = dot_t(mask_o[...], w[...])


def early_grad_kernel(per, yn, masked, dz, xn, *outs):
    g_out = t_dot(yn[...], masked[...]).astype(BF)
    g_z = t_dot(dz[...], xn[...]).astype(BF)
    for m in range(per):
        here = slice(m * HEADDIM, (m + 1) * HEADDIM)
        outs[m][0, :HEADDIM, :] = g_out[here, :]
        outs[m][0, HEADDIM:, :] = g_z[here, :]


class Copies:
    def __init__(self, sends, receives):
        self.sends, self.receives, self.all = sends, receives, []

    def __call__(self, source, target, peer):
        copy = remote(source, target, self.sends, self.receives, len(self.all), peer)
        self.all.append(copy)
        return copy


def start(copies):
    for c in copies:
        c.start()


def arrive(copies):
    for c in copies:
        c.wait_recv()


def tail_kernel(per, nz, *refs):
    dx, dxh, taps, refs = take(refs, nz, nz, nz)
    (dz, dbc, dbch, dti, xn, xnh, w, bc, wdt, early, hidden, cot, r), refs = refs[:13], refs[13:]
    (gain, gbc, grate, gbias, gskip, ggain, rate, ex), refs = refs[:8], refs[8:]
    zx_o, ow_o, bcdt_o, hid_o, norm_o, tbc_o, small_o, refs = take(refs, *[0] * 7)
    ea, la, gx, gs, gdt, lx, ls, sw_out, sw_in, dxn, dxn_out, dxn_in, refs = take(refs, *[0] * 12)
    edge_out, edge_in, edge_sum, edge_next, across, across_in, nrm, nrm2, sums, refs = take(
        refs, *[0] * 9
    )
    rx, rs, zx, zs, nr, nz_r, refs = take(refs, per - 1, per - 1, nz - 1, nz - 1, per - 1, nz - 1)
    stage, sends, receives = refs
    copy = Copies(sends, receives)
    rows, half = hidden.shape
    gc = per * HEADDIM
    channels = nz * gc
    state2 = dbc.shape[1]
    quarter = state2 // per
    share = quarter + HALO
    some_dt = HEADS // per
    wi, di, zi = lax.axis_index("width"), lax.axis_index("dp"), lax.axis_index("head")
    sibling = {"width": 1 - wi}
    d_peers, z_back = plane_peers(per), line_peers(nz, -1)
    left, right = pl.ds(0, half), pl.ds(half, half)
    block = rows // nz

    early_swap = copy(early.at[:, right], ea.at[0, wi], sibling)
    late_swap = copy(sw_out, sw_in, sibling)
    dxn_swap = [
        copy(dxn_out.at[pl.ds(i * block, block), :], dxn_in.at[pl.ds(i * block, block), :], sibling)
        for i in range(nz)
    ]
    edge_swap = copy(edge_out, edge_in, sibling)
    across_swap = copy(across, across_in, sibling)
    p_share, p_x, p_early, p_norm, p_late = [], {s: [] for s in range(nz)}, [], [], []
    for k, peer in enumerate(d_peers):
        m = k + 1
        p_share.append(copy(gs.at[m], rs[k], peer))
        for s in range(nz):
            p_x[s].append(copy(gx.at[s, m], rx[k].at[s], peer))
        p_early.append(copy(ea.at[0], ea.at[m], peer))
        p_norm.append(copy(nrm, nr[k], peer))
        p_late.append(copy(la.at[0], la.at[m], peer))
    z_x, z_share, z_norm = [], [], []
    for k, peer in enumerate(z_back):
        z_x.append(copy(lx.at[k + 1], zx[k], peer))
        z_share.append(copy(ls, zs[k], peer))
        z_norm.append(copy(nrm2, nz_r[k], peer))
    z_edge = copy(edge_sum, edge_next, z_back[0])

    meet([sibling, *z_back, *line_peers(nz, 1), *d_peers])
    start([early_swap])
    ea[0, wi] = early[:, :half]

    g = t_dot(dbc[...], xn[...]) + t_dot(dbch[...], xnh[...])
    stage[0:state2, :] = g
    gdt[...] = split_dot_tr(slot_heads(dti.shape[1], per), t_dot(dti[...], xn[...]))
    per_head = jnp.concatenate([gbias[...], grate[...] * rate[...]], axis=0)
    small = jnp.concatenate(
        [
            jnp.concatenate([v[...] for v in taps], axis=1),
            ggain[...],
            gskip[...],
            dot(split2(per_head), ex[...]),
        ],
        axis=0,
    )
    both = split2(gbc[...])
    both = jnp.concatenate([both, jnp.zeros((4, 2 * state2), BF)], axis=0)
    for m in range(per):
        at = jnp.bitwise_xor(di, m)
        gs[m, 0:quarter, :] = stage[pl.ds(pl.multiple_of(at * quarter, quarter), quarter), :].astype(
            BF
        )
        lanes = jnp.concatenate(
            [
                small[:, (s * per + m) * HEADDIM : (s * per + m + 1) * HEADDIM]
                for s in range(nz)
            ],
            axis=1,
        )
        lower = jnp.concatenate([split2(lanes), both], axis=1)
        upper = gdt[pl.ds(pl.multiple_of(at * some_dt, some_dt), some_dt), :].astype(BF)
        gs[m, quarter:, :] = jnp.concatenate(
            [upper.astype(F32), lower.astype(F32)], axis=0
        ).astype(BF)
    start(p_share)
    order = [*range(1, nz), 0]
    for s in order:
        g = t_dot(dx[s][...], xn[...]) + t_dot(dxh[s][...], xnh[...])
        for m in range(per):
            gx[s, m] = g[m * HEADDIM : (m + 1) * HEADDIM, :].astype(BF)
        start(p_x[s])
    arrive([early_swap])
    start(p_early)

    def add_share():
        arrive(p_share)
        for i in range(share // HALO):
            here = slice(i * HALO, i * HALO + HALO)
            total = gs[0, here, :].astype(F32)
            for v in rs:
                total = total + v[here, :].astype(F32)
            sums[here, :] = total
        pack(sums)
        start(z_share)

    def pack(v):
        ls[0:quarter, :] = v[0:quarter, :].astype(BF)
        n = nz * HEADDIM
        rest = v[quarter:, :]
        a = rest[:, 0:n] + rest[:, n : 2 * n]
        b = rest[:, 2 * n : 2 * n + state2] + rest[:, 2 * n + state2 :]
        low_rows = jnp.concatenate([split2(a), split2(b)], axis=1)
        row = lax.broadcasted_iota(jnp.int32, (HALO, 1), 0)
        ls[quarter:, :] = jnp.where(row < some_dt, rest, low_rows.astype(F32)).astype(BF)

    def add_x(s):
        arrive(p_x[s])
        for i in range(HEADDIM // HALO):
            here = slice(i * HALO, i * HALO + HALO)
            total = gx[s, 0, here, :].astype(F32)
            for v in rx:
                total = total + v[s, here, :].astype(F32)
            lx[s, here, :] = total.astype(BF)
        if s > 0:
            start([z_x[s - 1]])

    for i in range(nz):
        here = slice(i * block, i * block + block)
        total = dot(dz[here, :], w[0])
        for s in range(nz):
            total = total + dot(dx[s][here, :], w[1, s * gc : (s + 1) * gc, :])
        total = total + dot(dbc[here, :], bc[0:state2, :]) + dot(dti[here, :], wdt[...])
        dxn[here, :] = total[:, :half]
        dxn_out[here, :] = total[:, half:].astype(BF)
        start([dxn_swap[i]])
        if i == 0:
            add_share()
            total = dot(dbch[...], bc[0:state2, :])
            for s in range(nz):
                total = total + dot(dxh[s][...], w[1, s * gc : (s + 1) * gc, :])
            edge_sum[...] = total[:, :half]
            edge_out[...] = total[:, half:]
            start([edge_swap])
        if i == 1:
            add_x(order[0])
            arrive([edge_swap])
            edge_sum[...] = edge_sum[...] + edge_in[...]
            start([z_edge])
    if nz > 2:
        add_x(order[1])

    arrive([*dxn_swap, z_edge])
    late_edge = jnp.where(zi < nz - 1, edge_next[...], 0.0)
    gain_v = gain[...]
    norm_sum = jnp.zeros((8, half), F32)
    ones = jnp.ones((8, half), BF)
    for i in range(rows // Q):
        here = slice(i * Q, i * Q + Q)
        v = dxn[here, :] + dxn_in[here, :].astype(F32)
        if i == rows // Q - 1:
            v = v + jnp.concatenate([jnp.zeros((Q - HALO, half), F32), late_edge], axis=0)
        dxn[here, :] = v
        h = hidden[here, :].astype(F32)
        vh = v * h
        norm_sum = norm_sum + jnp.sum(
            (vh * r[here, :]).reshape(Q // 8, 8, half), axis=0
        )
        across[:, here] = split_dot_t(ones, vh * gain_v)
    start([across_swap])
    nrm[...] = norm_sum
    start(p_norm)
    for s in order[2:]:
        add_x(s)
    arrive([across_swap])
    eighth = jnp.full((8, Q), 0.125, F32)
    for i in range(rows // Q):
        here = slice(i * Q, i * Q + Q)
        total = across[:, here] + across_in[:, here]
        total = t_dot(total, eighth, HIGH)
        rr = r[here, :]
        scale = rr * rr * rr / (2 * half)
        rg = rr * gain_v
        for j in range(half // Q):
            lanes = slice(j * Q, j * Q + Q)
            hid_o[here, lanes] = (
                cot[here, lanes].astype(F32)
                + rg[:, lanes] * dxn[here, lanes]
                - hidden[here, lanes].astype(F32) * (scale * total)
            ).astype(BF)
    arrive(p_norm)
    total = nrm[...]
    for v in nr:
        total = total + v[...]
    nrm2[...] = total
    start(z_norm)

    arrive([*z_x, *z_share])
    total = lx[0].astype(F32)
    for v in zx:
        total = total + v[...].astype(F32)
    mine = total.astype(BF)
    la[0, pl.ds(pl.multiple_of(wi * HEADDIM, HEADDIM), HEADDIM), :] = mine[:, :half]
    sw_out[0:HEADDIM, :] = mine[:, half:]
    n = nz * HEADDIM
    total = ls[0:quarter, :].astype(F32)
    for v in zs:
        total = total + v[0:quarter, :].astype(F32)
    sums[0:quarter, :] = total
    sw_out[HEADDIM : HEADDIM + quarter, :] = total[:, half:].astype(BF)
    total = ls[quarter:, :].astype(F32)
    own_small = total[:, 0:HEADDIM] + total[:, n : n + HEADDIM]
    for k, v in enumerate(zs):
        part = v[quarter:, :].astype(F32)
        total = total + part
        at = (k + 1) * HEADDIM
        own_small = own_small + (
            part[:, at : at + HEADDIM] + part[:, n + at : n + at + HEADDIM]
        )
    sums[quarter:, :] = total
    taps_bc = total[:, 2 * n : 2 * n + state2] + total[:, 2 * n + state2 :]
    at = HEADDIM + quarter
    sw_out[at : at + HALO, :] = total[:, half:].astype(BF)
    own_small = split2(own_small)
    own_small = jnp.concatenate(
        [own_small, jnp.zeros((HALO, half - 2 * HEADDIM), BF)], axis=1
    )
    taps_bc2 = split2(taps_bc)
    sw_out[at + HALO : at + 2 * HALO, :] = own_small
    sw_out[at + 2 * HALO : at + 3 * HALO, :] = taps_bc2
    start([late_swap])
    arrive([late_swap])
    there = pl.ds(pl.multiple_of((1 - wi) * HEADDIM, HEADDIM), HEADDIM)
    la[0, there, :] = sw_in[0:HEADDIM, :]
    base = 2 * HEADDIM
    la[0, base : base + share, :] = (
        sums[:, :half] + sw_in[HEADDIM : HEADDIM + share, :].astype(F32)
    ).astype(BF)
    base = base + share
    la[0, pl.ds(pl.multiple_of(base + wi * HALO, HALO), HALO), :] = own_small
    la[0, pl.ds(pl.multiple_of(base + (1 - wi) * HALO, HALO), HALO), :] = sw_in[
        at + HALO : at + 2 * HALO, :
    ]
    start(p_late)
    got = sw_in[at + 2 * HALO : at + 3 * HALO, :].astype(F32)
    taps_bc = taps_bc + got[:, :state2] + got[:, state2:]
    tbc_o[...] = taps_bc[some_dt : some_dt + 4, :]
    arrive(z_norm)
    total = nrm2[...]
    for v in nz_r:
        total = total + v[...]
    norm_o[...] = jnp.sum(total, axis=0, keepdims=True)

    arrive(p_early)
    for m in range(per):
        for k in range(2):
            head = k * per + jnp.bitwise_xor(di, m)
            v = ea[m, k].astype(F32)
            ow_o[pl.ds(pl.multiple_of(head * HEADDIM, HEADDIM), HEADDIM), :] = v[:HEADDIM, :]
    arrive(p_late)
    for m in range(per):
        at = jnp.bitwise_xor(di, m)
        for k in range(2):
            head = k * per + at
            z_part = ea[m, k, HEADDIM:, :].astype(F32)
            x_part = la[m, k * HEADDIM : (k + 1) * HEADDIM, :].astype(F32)
            zx_o[:, pl.ds(pl.multiple_of(head * 2 * HEADDIM, 2 * HEADDIM), 2 * HEADDIM)] = (
                jnp.transpose(jnp.concatenate([z_part, x_part], axis=0))
            )
            v = la[m, base + k * HALO : base + (k + 1) * HALO, :].astype(F32)
            small_o[head] = (v[:, :HEADDIM] + v[:, HEADDIM : 2 * HEADDIM])[some_dt:, :]
        v = la[m, 2 * HEADDIM : base, :].astype(F32)
        stage[pl.ds(pl.multiple_of(at * quarter, quarter), quarter), left] = v[:quarter, :]
        stage[pl.ds(pl.multiple_of(state2 + at * some_dt, some_dt), some_dt), left] = v[
            quarter : quarter + some_dt, :
        ]
    bcdt_o[...] = jnp.transpose(stage[:, :half])
    for c in copy.all:
        c.wait_send()


def split_dot_tr(m, v):
    hi = v.astype(BF)
    lo = (v - hi.astype(F32)).astype(BF)
    m = m.astype(BF)
    return t_dot(m, hi) + t_dot(m, lo)


def split_dot_t(m, v):
    hi = v.astype(BF)
    lo = (v - hi.astype(F32)).astype(BF)
    return dot_t(m, hi) + dot_t(m, lo)


def shape(dims, dtype=F32):
    return jax.ShapeDtypeStruct(dims, dtype)


def whole(array):
    rank = len(array.shape)
    return pl.BlockSpec(array.shape, lambda *_: (0,) * rank)


def params():
    return pltpu.CompilerParams(vmem_limit_bytes=VMEM)


def cost(us):
    return pl.CostEstimate(flops=int(us * 1.0e8), bytes_accessed=int(us * 1.0e3), transcendentals=0)


def take(refs, *counts):
    out, at = [], 0
    for n in counts:
        out.append(refs[at] if n == 0 else refs[at : at + n])
        at += max(n, 1)
    return out + [refs[at:]]


def sequence_device(
    hidden, lengths, cotangent, norm_gain, in_zx, in_bcdt, conv_x, conv_bc,
    dt_bias, a_log, d_skip, gnorm_gain, out_w,
):
    rows, half = hidden.shape
    own_heads = in_zx.shape[1]
    nz = lax.axis_size("head")
    ndp = lax.axis_size("dp")
    zi = lax.axis_index("head")
    di = lax.axis_index("dp")
    wi = lax.axis_index("width")
    per = ndp
    heads = nz * per
    channels = heads * HEADDIM
    model = 2 * half
    blocks = rows // Q

    def swap(v):
        return lax.ppermute(v, "width", [(0, 1), (1, 0)])

    gc = per * HEADDIM
    groups = tuple(range(nz))

    onehot = np.kron(np.eye(heads), np.ones((1, HEADDIM)))
    ex = jnp.asarray(np.concatenate([onehot, onehot], axis=0), BF)
    er = jnp.asarray(onehot.T, BF)
    sel = jnp.asarray(onehot.T * (np.arange(channels) % HEADDIM == 0)[:, None], F32)

    scal = jnp.repeat(jnp.stack([dt_bias, a_log, d_skip]), HEADDIM, axis=1)
    piece = shape((2, HEADDIM, half), BF)
    some = shape((2, gc - HEADDIM, half), BF)
    outs = shape((gc, half), BF)
    first, first2, rest, rest2, out_mine, out_mine2, bcdt_t, table = pl.pallas_call(
        functools.partial(prep_kernel, per),
        out_shape=[
            piece, piece, some, some, outs, outs,
            shape((2 * STATE + HEADS + HALO, half), BF), shape((8, gc)),
        ],
        compiler_params=params(),
        cost_estimate=cost(4),
        name="prep",
    )(
        in_zx.reshape(half, -1), out_w, in_bcdt, norm_gain[None], conv_x, scal,
        gnorm_gain[None],
    )
    taps_bc = conv_bc.astype(F32)

    step = lambda i: (i, 0)
    fix = lambda i: (0, 0)
    part = shape((rows, gc), BF)
    full = shape((rows, channels))
    anywhere = pl.BlockSpec(memory_space=pl.ANY)
    vmem = pl.BlockSpec(memory_space=pltpu.VMEM)
    narrow = shape((rows, 2 * heads), BF)
    kept = dict(
        xnh=shape((HALO, model), BF), r=shape((rows, 1)), raw=shape((rows, 2 * STATE)),
        rawh=shape((HALO, 2 * STATE)), ubc=shape((rows, 2 * STATE)), b=shape((rows, STATE), BF),
        c=shape((rows, STATE), BF), dt=shape((rows, heads)), sig=shape((rows, heads)),
        cl=shape((rows, heads)), clt=shape((heads, rows)), dt2=narrow, e12=narrow, tl2=narrow,
        dttl2=narrow, ec2=narrow, edt2=narrow, rate=shape((1, heads)),
        wdt=shape((heads, model), BF),
        bcdt=shape((2 * STATE + HEADS + HALO, model), BF), tot=shape((heads, STATE), BF), table=shape((8, channels)),
    )
    wide_part = shape((rows, gc))
    message_shape = shape((channels + HALO, STATE), BF)
    out_shapes = [
        shape((2, channels, model), BF), shape((channels, model), BF), shape((rows, half), BF),
        shape((rows, model), BF), *[wide_part] * nz, *[part] * nz, *[wide_part] * nz,
        *[part] * nz, *[part] * nz, *[message_shape] * (nz - 1), *[shape((HALO, gc))] * nz,
        *[kept[name] for name in KEPT],
    ]
    held = lambda v: pltpu.VMEM(v.shape, v.dtype)
    remotes = 6 + 5 * (nz - 1) + 2 + 2 * (nz - 1) * (per - 1)
    out = pl.pallas_call(
        functools.partial(front_kernel, per, nz),
        in_specs=[vmem] * 10 + [anywhere] * 3,
        out_specs=[anywhere] * (4 + 5 * nz + nz - 1) + [vmem] * (nz + len(KEPT)),
        out_shape=out_shapes,
        scratch_shapes=[
            *[held(wide_part)] * nz, *[held(part)] * nz, *[held(wide_part)] * nz,
            *[held(part)] * nz, *[held(part)] * nz, pltpu.VMEM((2, channels, model), BF),
            pltpu.VMEM((rows, half), BF), pltpu.VMEM((HALO, model), BF),
            pltpu.VMEM((rows, model), BF),
            held(message_shape), pltpu.VMEM((rows + HALO, gc), F32),
            pltpu.VMEM((rows + HALO, 2 * STATE), F32), pltpu.VMEM((gc, STATE), F32),
            pltpu.SemaphoreType.DMA((remotes,)), pltpu.SemaphoreType.DMA((remotes,)),
            pltpu.SemaphoreType.DMA((7 + 5 * nz,)),
        ],
        compiler_params=pltpu.CompilerParams(
            vmem_limit_bytes=VMEM, collective_id=1, has_side_effects=True
        ),
        cost_estimate=cost(90),
        name="front",
    )(
        hidden, first, first2, rest, rest2, bcdt_t, table, taps_bc, sel, ex, out_mine, out_mine2,
        cotangent,
    )
    weights, wout, cot_o, xn, out = out[0], out[1], out[2], out[3], out[4:]
    z, xr, u, xdt, y_in, messages, xrh, out = take(out, *[nz] * 5, nz - 1, nz)
    o = Named(KEPT, out)
    xnh, r, braw, brawh, ubc, bs, cs = o.xnh, o.r, o.raw, o.rawh, o.ubc, o.b, o.c
    dt, sig, cl, clt, rate, wdt, totals, table = o.dt, o.sig, o.cl, o.clt, o.rate, o.wdt, o.tot, o.table
    dt2, e12, tl2, dttl2, ec2, edt2 = o.dt2, o.e12, o.tl2, o.dttl2, o.ec2, o.edt2
    taps, gain_out, skip = table[:4], table[4:5], table[7:8]
    limit = (lengths[0] - zi * rows).reshape(1, 1)

    wide = pl.BlockSpec((Q, channels), step)
    gwide = pl.BlockSpec((Q, gc), step)
    bspec = pl.BlockSpec((Q, STATE), step)
    hspec = pl.BlockSpec((Q, heads), step)
    h2spec = pl.BlockSpec((Q, 2 * heads), step)
    tspec = pl.BlockSpec((heads, Q), lambda i: (0, i))
    tile = 2 * Q if rows % (2 * Q) == 0 else Q
    smem = pl.BlockSpec(memory_space=pltpu.SMEM)
    masked, dyn = pl.pallas_call(
        pull_kernel,
        grid=(rows // tile,),
        in_specs=[
            pl.BlockSpec((tile, half), step), pl.BlockSpec((tile, half), step), smem, whole(wout),
        ],
        out_specs=[pl.BlockSpec((tile, model), step), pl.BlockSpec((tile, channels), step)],
        out_shape=[shape((rows, model), BF), full],
        compiler_params=params(),
        cost_estimate=cost(5),
        name="pull",
    )(cotangent, cot_o, limit, wout)
    out = pl.pallas_call(
        functools.partial(carry_kernel, groups, per),
        grid=(blocks,),
        in_specs=[
            *[gwide] * (3 * nz), wide, bspec, bspec, tspec, h2spec, h2spec, *[whole(v) for v in messages],
            whole(skip), whole(gain_out), whole(ex),
        ],
        out_specs=[
            *[gwide] * nz, *[pl.BlockSpec((1, gc, STATE), lambda i: (i, 0, 0))] * nz, wide,
            pl.BlockSpec((Q, 2), step),
        ],
        out_shape=[
            *[shape((rows, gc))] * nz, *[shape((blocks, gc, STATE), BF)] * nz, shape((rows, channels), BF),
            shape((rows, 2)),
        ],
        scratch_shapes=[pltpu.VMEM((channels, STATE), F32)],
        compiler_params=params(),
        cost_estimate=cost(10),
        name="carry",
    )(*y_in, *u, *z, dyn, bs, cs, clt, e12, dttl2, *messages, skip, gain_out, ex)
    ys, states, gg, sums = out[:nz], out[nz : 2 * nz], out[2 * nz], out[2 * nz + 1]
    sums2 = swap(sums)

    def sum_products(a, columns, w, count, wait):
        tile = 2 * Q if count % (2 * Q) == 0 else count
        return pl.pallas_call(
            functools.partial(sum_products_kernel, len(a)),
            grid=(count // tile,),
            in_specs=[
                *[
                    pl.BlockSpec((tile, v.shape[0]), lambda i, j=j: (i, j))
                    for v, j in zip(w, columns)
                ],
                *[whole(v) for v in w],
                pl.BlockSpec(memory_space=pl.ANY),
            ],
            out_specs=[pl.BlockSpec((tile, half), step)] * 2,
            out_shape=[shape((count, half)), shape((count, half), BF)],
            compiler_params=params(),
            cost_estimate=cost(4),
            name="products",
        )(*a, *w, wait)

    branch, branch_o = sum_products([gg], [0], [wout], rows, sums)
    branch_o = swap(branch_o)
    hhalf = pl.BlockSpec((Q, half), step)
    out = pl.pallas_call(
        functools.partial(gate_kernel, groups, per),
        grid=(blocks,),
        in_specs=[
            *[gwide] * (3 * nz), wide, pl.BlockSpec((Q, 2), step), pl.BlockSpec((Q, 2), step),
            whole(gain_out), h2spec, whole(ex), bspec, hhalf, hhalf, hhalf, smem,
        ],
        out_specs=[
            *[gwide] * nz, wide, wide, pl.BlockSpec((channels, STATE), fix),
            pl.BlockSpec((1, channels), fix), pl.BlockSpec((1, channels), fix), hhalf,
        ],
        out_shape=[
            *[part] * nz, shape((rows, channels), BF), shape((rows, channels), BF),
            shape((channels, STATE), BF), shape((1, channels)), shape((1, channels)),
            shape((rows, half), BF),
        ],
        scratch_shapes=[pltpu.VMEM((channels, STATE), F32)],
        compiler_params=params(),
        cost_estimate=cost(10),
        name="gate",
    )(
        *ys, *z, *u, dyn, sums, sums2, gain_out, ec2, ex, cs, hidden, branch, branch_o, limit
    )
    dys = out[:nz]
    dz, yn, ds_local, g_gain, g_skip, out_hidden = out[nz:]
    message = jnp.concatenate([ds_local, totals], axis=0)

    gcol = pl.BlockSpec((rows, gc), lambda s: (0, s))
    early = pl.pallas_call(
        functools.partial(early_grad_kernel, per),
        grid=(nz,),
        in_specs=[gcol, whole(masked), gcol, whole(xn)],
        out_specs=[pl.BlockSpec((1, 2 * HEADDIM, model), lambda s: (s, 0, 0))] * per,
        out_shape=[shape((nz, 2 * HEADDIM, model), BF)] * per,
        compiler_params=params(),
        cost_estimate=cost(6),
        name="early_grad",
    )(yn, masked, dz, xn)
    one = lambda i: (jnp.minimum(i, blocks - 1), 0)
    two = lambda i: (jnp.minimum(blocks - 1, 2 * blocks - 1 - i), 0)
    both = lambda i: (jnp.minimum(i, 2 * blocks - 1 - i), 0)
    head_columns = lambda v: pl.BlockSpec((Q, v), two)
    early_shape = early[0].shape
    exchange = 2 * (nz - 1) + nz * (per - 1)
    out = pl.pallas_call(
        functools.partial(scan_back_kernel, groups, per),
        grid=(2 * blocks,),
        in_specs=[
            *[pl.BlockSpec((Q, gc), one)] * nz, *[pl.BlockSpec((Q, gc), both)] * nz,
            *[pl.BlockSpec((Q, gc), two)] * (2 * nz),
            *[
                pl.BlockSpec(
                    (1, gc, STATE), lambda i: (jnp.minimum(blocks - 1, 2 * blocks - 1 - i), 0, 0)
                )
            ] * nz,
            *[pl.BlockSpec((HALO, gc), fix)] * nz,
            pl.BlockSpec((Q, STATE), both), pl.BlockSpec((Q, STATE), both),
            pl.BlockSpec((Q, heads), one),
            pl.BlockSpec((heads, Q), lambda i: (0, jnp.minimum(i, 2 * blocks - 1 - i))),
            head_columns(heads), head_columns(heads), head_columns(2 * heads),
            head_columns(2 * heads), head_columns(2 * heads), head_columns(2 * STATE),
            head_columns(2 * STATE), whole(brawh), whole(taps), whole(taps_bc), whole(rate),
            whole(skip), whole(ex), whole(er), *[anywhere] * (1 + per),
        ],
        out_specs=[
            *[pl.BlockSpec((Q, gc), two)] * nz, *[pl.BlockSpec((HALO, gc), fix)] * nz,
            *[pl.BlockSpec((4, gc), fix)] * nz, head_columns(heads),
            pl.BlockSpec((1, heads), fix), pl.BlockSpec((1, heads), fix),
            head_columns(2 * STATE), pl.BlockSpec((HALO, 2 * STATE), fix),
            pl.BlockSpec((4, 2 * STATE), fix), pl.BlockSpec((2 * HEADDIM, model), fix),
        ],
        out_shape=[
            *[shape((rows, gc), BF)] * nz, *[shape((HALO, gc), BF)] * nz, *[shape((4, gc))] * nz,
            shape((rows, heads), BF), shape((1, heads)), shape((1, heads)),
            shape((rows, 2 * STATE), BF), shape((HALO, 2 * STATE), BF), shape((4, 2 * STATE)),
            shape((2 * HEADDIM, model), BF),
        ],
        scratch_shapes=[
            *[pltpu.VMEM(message.shape, BF)] * (nz - 1), *[pltpu.VMEM(early_shape, BF)] * (per - 1),
            *[pltpu.VMEM((8, gc), F32)] * nz, *[pltpu.VMEM((2 * HEADDIM, model), BF)] * (nz - 1),
            pltpu.VMEM((8, 2 * STATE), F32), pltpu.VMEM(early_shape, BF),
            pltpu.VMEM(early_shape, BF), pltpu.VMEM((rows, channels), F32),
            pltpu.VMEM((rows, STATE), F32), pltpu.VMEM((rows, STATE), F32),
            pltpu.VMEM((rows, heads), F32), pltpu.VMEM((heads, Q), F32),
            pltpu.VMEM((channels, STATE), F32), pltpu.VMEM((heads, STATE), F32),
            pltpu.SemaphoreType.DMA((exchange,)), pltpu.SemaphoreType.DMA((exchange,)),
            pltpu.SemaphoreType.DMA,
        ],
        compiler_params=pltpu.CompilerParams(
            vmem_limit_bytes=VMEM, collective_id=0, has_side_effects=True
        ),
        cost_estimate=cost(50),
        name="scan_back",
    )(
        *xdt, *dys, *u, *xr, *states, *xrh, bs, cs, cl, clt, dt, sig, dt2, e12, tl2, ubc, braw,
        brawh, taps, taps_bc, rate, skip, ex, er, message, *early,
    )
    dx, dxh, g_taps = list(out[:nz]), list(out[nz : 2 * nz]), out[2 * nz : 3 * nz]
    dti, g_rate, g_bias, dbc, dbch, g_taps_bc, early_total = out[3 * nz :]
    quarter = 2 * STATE // per
    share = quarter + HALO
    late_rows = 2 * HEADDIM + share + 2 * HALO
    swap_rows = HEADDIM + share + 2 * HALO
    tail_copies = 4 + nz + (per - 1) * (4 + nz) + 3 * (nz - 1) + 1
    operands = [
        *dx, *dxh, *g_taps, dz, dbc, dbch, dti, xn, xnh, weights, o.bcdt, wdt, early_total, hidden,
        cotangent, r, norm_gain[None].astype(F32), g_taps_bc, g_rate, g_bias, g_skip, g_gain, rate,
        ex,
    ]
    line16 = pltpu.VMEM((HALO, half), F32)
    line8 = pltpu.VMEM((8, half), F32)
    g_zx, g_out, grad_in_bcdt, grad_hidden, g_norm, g_taps_bc, small = pl.pallas_call(
        functools.partial(tail_kernel, per, nz),
        in_specs=[vmem] * len(operands),
        out_specs=[vmem] * 7,
        out_shape=[
            shape((half, own_heads * 2 * HEADDIM)), shape((own_heads * HEADDIM, half)),
            shape((half, 2 * STATE + HEADS)), shape((rows, half), BF), shape((1, half)),
            shape((4, 2 * STATE)), shape((own_heads, 8, HEADDIM)),
        ],
        scratch_shapes=[
            pltpu.VMEM((per, 2, 2 * HEADDIM, half), BF), pltpu.VMEM((per, late_rows, half), BF),
            pltpu.VMEM((nz, per, HEADDIM, model), BF), pltpu.VMEM((per, share, model), BF),
            pltpu.VMEM((HEADS, model), F32), pltpu.VMEM((nz, HEADDIM, model), BF),
            pltpu.VMEM((share, model), BF), pltpu.VMEM((swap_rows, half), BF),
            pltpu.VMEM((swap_rows, half), BF), pltpu.VMEM((rows, half), F32),
            pltpu.VMEM((rows, half), BF), pltpu.VMEM((rows, half), BF), line16, line16, line16,
            line16, pltpu.VMEM((8, rows), F32), pltpu.VMEM((8, rows), F32), line8, line8,
            pltpu.VMEM((share, model), F32),
            *[pltpu.VMEM((nz, HEADDIM, model), BF)] * (per - 1),
            *[pltpu.VMEM((share, model), BF)] * (per - 1),
            *[pltpu.VMEM((HEADDIM, model), BF)] * (nz - 1),
            *[pltpu.VMEM((share, model), BF)] * (nz - 1), *[line8] * (per - 1),
            *[line8] * (nz - 1), pltpu.VMEM((2 * STATE + HEADS, model), F32),
            pltpu.SemaphoreType.DMA((tail_copies,)), pltpu.SemaphoreType.DMA((tail_copies,)),
        ],
        compiler_params=pltpu.CompilerParams(
            vmem_limit_bytes=VMEM, collective_id=2, has_side_effects=True
        ),
        cost_estimate=cost(60),
        name="tail",
    )(*operands)
    return (
        out_hidden,
        grad_hidden,
        g_norm.reshape(half),
        g_zx.reshape(half, own_heads, 2 * HEADDIM),
        grad_in_bcdt,
        jnp.transpose(small[:, :4], (1, 0, 2)).reshape(4, own_heads * HEADDIM),
        g_taps_bc,
        small[:, 6, 0],
        small[:, 7, 0],
        jnp.sum(small[:, 5], axis=1),
        small[:, 4].reshape(-1),
        g_out,
    )


def fits(mesh):
    ndp, nz, nw = mesh.shape["dp"], mesh.shape["head"], mesh.shape["width"]
    return (
        nw == 2
        and ndp in (2, 4, 8)
        and nz & (nz - 1) == 0
        and HEADS == nz * nw * ndp
        and LEN % (nz * Q) == 0
        and SEQS == ndp
        and HEADS // nw * HEADDIM % Q == 0
        and HEADS // ndp == 8
    )


def solution(mesh):
    placed = (
        P(("dp", "head"), "width"),
        P("dp"),
        P(("dp", "head"), "width"),
        P("width"),
        P("width", "head", None),
        P("width", None),
        P(None, "head"),
        P(),
        P("head"),
        P("head"),
        P("head"),
        P("head"),
        P("head", "width"),
    )
    return jax.shard_map(
        sequence_device if fits(mesh) else per_device,
        mesh=mesh,
        in_specs=placed,
        out_specs=(
            P(("dp", "head"), "width"),
            P(("dp", "head"), "width"),
            P("width"),
            P("width", "head", None),
            P("width", None),
            P(None, "head"),
            P(),
            P("head"),
            P("head"),
            P("head"),
            P("head"),
            P("head", "width"),
        ),
        check_vma=False,
    )
```

```python
import functools

import jax
import jax.numpy as jnp
import numpy as np
from jax import lax
from jax.experimental import pallas as pl
from jax.experimental.pallas import tpu as pltpu
from jax.sharding import PartitionSpec as P

D = 1024
HEADS = 32
HEADDIM = 64
STATE = 128
SCAN_BLOCK = 256
LEN = 4096
INNER = 2048
SEQS = 4


EPS = 1e-05
HIGH = lax.Precision.HIGHEST


def conv_causal(values, kernel):
    taps = kernel.shape[0]
    padded = jnp.pad(values, ((taps - 1, 0), (0, 0)))
    total = jnp.zeros_like(values)
    for offset in range(taps):
        total = total + kernel[offset] * padded[offset : offset + values.shape[0]]
    return total


def block_scan(inputs, steps, rates, bmat, cmat, block):
    length, heads, hsize = inputs.shape
    count = length // block
    in_blocks = inputs.reshape(count, block, heads, hsize)
    step_blocks = steps.reshape(count, block, heads)
    b_blocks = bmat.reshape(count, block, bmat.shape[1])
    c_blocks = cmat.reshape(count, block, cmat.shape[1])
    places = jnp.arange(block)
    lower = (places[:, None] >= places[None, :])[:, :, None]

    def advance(state, pieces):
        x_part, dt_part, b_part, c_part = pieces
        cums = jnp.cumsum(dt_part * rates, axis=0)
        spread = cums[:, None, :] - cums[None, :, :]
        decay = jnp.where(lower, jnp.exp(jnp.where(lower, spread, 0.0)), 0.0)
        scores = jnp.dot(c_part, b_part.T, precision=HIGH)
        weights = scores[:, :, None] * decay * dt_part[None, :, :]
        inside = jnp.einsum("ijh,jhp->ihp", weights, x_part, precision=HIGH)
        carried = (
            jnp.einsum("in,hpn->ihp", c_part, state, precision=HIGH) * jnp.exp(cums)[:, :, None]
        )
        tails = jnp.exp(cums[-1][None, :] - cums) * dt_part
        state = jnp.exp(cums[-1])[:, None, None] * state + jnp.einsum(
            "jh,jhp,jn->hpn", tails, x_part, b_part, precision=HIGH
        )
        return (state, inside + carried)

    start_state = jnp.zeros((heads, hsize, bmat.shape[1]), jnp.float32)
    _, result = lax.scan(
        jax.checkpoint(advance), start_state, (in_blocks, step_blocks, b_blocks, c_blocks)
    )
    return result.reshape(length, heads, hsize)


def mixer(zx, bc_raw, dt_raw, kernel_x, kernel_bc, bias_dt, log_rate, skip):
    length, heads, double = zx.shape
    hsize = double // 2
    gate = zx[:, :, :hsize]
    x_raw = zx[:, :, hsize:].reshape(length, heads * hsize)
    xs_conv = jax.nn.silu(conv_causal(x_raw, kernel_x)).reshape(length, heads, hsize)
    bc_conv = jax.nn.silu(conv_causal(bc_raw, kernel_bc))
    half = bc_conv.shape[1] // 2
    steps = jax.nn.softplus(dt_raw + bias_dt)
    rates = -jnp.exp(log_rate)
    result = (
        block_scan(xs_conv, steps, rates, bc_conv[:, :half], bc_conv[:, half:], SCAN_BLOCK)
        + skip[:, None] * xs_conv
    )
    return (result * jax.nn.silu(gate)).reshape(length, heads * hsize)


def per_device(
    hidden,
    lengths,
    cotangent,
    norm_gain,
    in_zx,
    in_bcdt,
    conv_x,
    conv_bc,
    dt_bias,
    a_log,
    d_skip,
    gnorm_gain,
    out_w,
):
    slice_rows, half_width = hidden.shape
    local_heads = in_zx.shape[1]
    head_count = lax.axis_size("head")
    head_index = lax.axis_index("head")
    total_rows = slice_rows * head_count
    seq_local = lengths.shape[0]
    inner_local = local_heads * HEADDIM
    row_ids = head_index * slice_rows + jnp.arange(slice_rows, dtype=jnp.int32)
    owner = (row_ids // LEN)[:, None] == jnp.arange(seq_local, dtype=jnp.int32)[None, :]
    limits = jnp.sum(jnp.where(owner, lengths[None, :], 0), axis=1)
    keeper = (row_ids % LEN < limits).astype(jnp.float32)[:, None]
    source = hidden.astype(jnp.float32)
    squares = lax.psum(jnp.sum(source * source, axis=1), "width")
    scale = lax.rsqrt(squares / D + EPS)[:, None]
    gain_in = norm_gain.astype(jnp.float32)
    normed = (source * scale * gain_in).astype(jnp.bfloat16)
    gathered = lax.all_gather(normed, "head", axis=0, tiled=True)
    w_zx = in_zx.reshape(half_width, local_heads * 2 * HEADDIM)
    zx_part = jnp.dot(gathered, w_zx, preferred_element_type=jnp.float32)
    bcdt_part = jnp.dot(gathered, in_bcdt, preferred_element_type=jnp.float32)
    zx_full, bcdt_full = lax.psum((zx_part, bcdt_part), "width")
    zx_seq = zx_full.reshape(seq_local, LEN, local_heads, 2 * HEADDIM)
    bc_seq = bcdt_full[:, : 2 * STATE].reshape(seq_local, LEN, 2 * STATE)
    dt_seq = lax.dynamic_slice_in_dim(
        bcdt_full, 2 * STATE + head_index * local_heads, local_heads, 1
    ).reshape(seq_local, LEN, local_heads)

    def local_mix(zx_in, bc_in, dt_in, kernel_x, kernel_bc, bias_in, log_in, skip_in):
        per_sequence = jax.vmap(mixer, in_axes=(0, 0, 0, None, None, None, None, None))
        return per_sequence(
            zx_in, bc_in, dt_in, kernel_x, kernel_bc, bias_in, log_in, skip_in
        ).reshape(total_rows, inner_local)

    gated, mix_pull = jax.vjp(
        local_mix,
        zx_seq,
        bc_seq,
        dt_seq,
        conv_x.astype(jnp.float32),
        conv_bc.astype(jnp.float32),
        dt_bias,
        a_log,
        d_skip,
    )
    total_sq = lax.psum(jnp.sum(gated * gated, axis=1), "head")
    scale_out = lax.rsqrt(total_sq / INNER + EPS)[:, None]
    gain_out = gnorm_gain.astype(jnp.float32)
    mixed = (gated * scale_out * gain_out).astype(jnp.bfloat16)
    picked = mixed
    branch = lax.psum_scatter(
        jnp.dot(picked, out_w, preferred_element_type=jnp.float32),
        "head",
        scatter_dimension=0,
        tiled=True,
    )
    out_hidden = (source + keeper * branch).astype(jnp.bfloat16)
    grad_out = cotangent.astype(jnp.float32)
    masked = (grad_out * keeper).astype(jnp.bfloat16)
    piece = lax.all_gather(masked, "head", axis=0, tiled=True)
    picked = mixed
    acc_weight = jnp.einsum("tc,td->cd", picked, piece, preferred_element_type=jnp.float32)
    product = jnp.einsum("td,cd->tc", piece, out_w, preferred_element_type=jnp.float32)
    grad_mixed = lax.psum(product, "width")
    gain_out_grad = jnp.sum(grad_mixed * gated * scale_out, axis=0)
    inner_total = lax.psum(jnp.sum(grad_mixed * gain_out * gated, axis=1), "head")
    cubed = scale_out * scale_out * scale_out
    grad_gated = scale_out * gain_out * grad_mixed - gated * cubed / INNER * inner_total[:, None]
    (
        grad_zx_seq,
        grad_bc_seq,
        grad_dt_seq,
        kernel_x_grad,
        kernel_bc_grad,
        bias_grad,
        rate_grad,
        skip_grad,
    ) = mix_pull(grad_gated)
    grad_zx = grad_zx_seq.reshape(total_rows, local_heads * 2 * HEADDIM).astype(jnp.bfloat16)
    dt_columns = jnp.zeros((total_rows, HEADS), jnp.float32)
    dt_columns = lax.dynamic_update_slice_in_dim(
        dt_columns, grad_dt_seq.reshape(total_rows, local_heads), head_index * local_heads, 1
    )
    grad_bcdt_head = jnp.concatenate(
        [grad_bc_seq.reshape(total_rows, 2 * STATE), dt_columns], axis=1
    )
    weight_zx = jnp.einsum(
        "td,tc->dc", gathered, grad_zx, preferred_element_type=jnp.float32
    ).reshape(half_width, local_heads, 2 * HEADDIM)
    normed_part = jnp.einsum("tc,dc->td", grad_zx, w_zx, preferred_element_type=jnp.float32)
    grad_normed, bcdt_summed = (
        lax.psum_scatter(normed_part, "head", scatter_dimension=0, tiled=True),
        lax.psum_scatter(grad_bcdt_head, "head", scatter_dimension=0, tiled=True),
    )
    bcdt_low = bcdt_summed.astype(jnp.bfloat16)
    grad_normed = grad_normed + jnp.einsum(
        "tk,dk->td", bcdt_low, in_bcdt, preferred_element_type=jnp.float32
    )
    weight_bcdt = jnp.einsum("td,tk->dk", normed, bcdt_low, preferred_element_type=jnp.float32)
    gain_in_grad = jnp.sum(grad_normed * source * scale, axis=0)
    across = lax.psum(jnp.sum(grad_normed * gain_in * source, axis=1), "width")
    scale_cubed = scale * scale * scale
    grad_hidden = (
        grad_out + scale * gain_in * grad_normed - source * scale_cubed / D * across[:, None]
    ).astype(jnp.bfloat16)
    summed_dp = lax.psum(
        (weight_zx, acc_weight, kernel_x_grad, bias_grad, rate_grad, skip_grad, gain_out_grad), "dp"
    )
    summed_all = lax.psum((weight_bcdt, gain_in_grad, kernel_bc_grad), ("dp", "head"))
    return (
        out_hidden,
        grad_hidden,
        summed_all[1],
        summed_dp[0],
        summed_all[0],
        summed_dp[2],
        summed_all[2],
        summed_dp[3],
        summed_dp[4],
        summed_dp[5],
        summed_dp[6],
        summed_dp[1],
    )


BF = jnp.bfloat16
F32 = jnp.float32
Q = 128
HALO = 16
NEG = -1e30
MESH = pl.DeviceIdType.MESH
VMEM = 60 * 1024 * 1024


def dot(a, b, prec=None):
    return lax.dot_general(a, b, (((1,), (0,)), ((), ())), precision=prec, preferred_element_type=F32)


def dot_t(a, b, prec=None):
    return lax.dot_general(a, b, (((1,), (1,)), ((), ())), precision=prec, preferred_element_type=F32)


def t_dot(a, b, prec=None):
    return lax.dot_general(a, b, (((0,), (0,)), ((), ())), precision=prec, preferred_element_type=F32)


def split2(v, axis=1):
    hi = v.astype(BF)
    lo = (v - hi.astype(F32)).astype(BF)
    return jnp.concatenate([hi, lo], axis=axis)


def dot_split(v, m):
    hi = v.astype(BF)
    lo = (v - hi.astype(F32)).astype(BF)
    return dot(hi, m) + dot(lo, m)


def split_dot(m, v):
    hi = v.astype(BF)
    lo = (v - hi.astype(F32)).astype(BF)
    return dot(m, hi) + dot(m, lo)


def sigmoid(v):
    return 1.0 / (1.0 + jnp.exp(-v))


def tri(kind):
    row = lax.broadcasted_iota(jnp.int32, (Q, Q), 0)
    col = lax.broadcasted_iota(jnp.int32, (Q, Q), 1)
    return {"ge": row >= col, "le": row <= col, "gt": row > col}[kind]


def slot_heads(heads, per):
    nz = heads // per
    own = HEADS // nz
    bits = per.bit_length() - 1
    slot = lax.broadcasted_iota(jnp.int32, (heads, HEADS), 0)
    head = lax.broadcasted_iota(jnp.int32, (heads, HEADS), 1)
    z = (lax.axis_index("head") - (slot >> bits)) & (nz - 1)
    m = (slot & (per - 1)) ^ lax.axis_index("dp")
    return (head == z * own + lax.axis_index("width") * per + m).astype(F32)


def prep_kernel(
    per, zx, ow, bcdt, rows_in,
    first_o, first2_o, rest_o, rest2_o, out_o, out2_o, bcdt_o, table_o,
):
    di = lax.axis_index("dp")
    wi = lax.axis_index("width")
    wide = 2 * HEADDIM
    for m in range(per):
        for w, whole_o, some_o, o_o in (
            (wi, first_o, rest_o, out_o), (1 - wi, first2_o, rest2_o, out2_o)
        ):
            head = w * per + jnp.bitwise_xor(di, m)
            v = jnp.transpose(zx[:, pl.ds(pl.multiple_of(head * wide, wide), wide)])
            for i in range(2):
                part = v[i * HEADDIM : (i + 1) * HEADDIM, :]
                if m == 0:
                    whole_o[i] = part
                else:
                    some_o[i, (m - 1) * HEADDIM : m * HEADDIM, :] = part
            o_o[m * HEADDIM : (m + 1) * HEADDIM, :] = ow[
                pl.ds(pl.multiple_of(head * HEADDIM, HEADDIM), HEADDIM), :
            ]
    n = bcdt.shape[0]
    bcdt_o[0:n, :] = bcdt[...]
    bcdt_o[n:, :] = jnp.broadcast_to(rows_in[8:9, :], (HALO, bcdt.shape[1])).astype(BF)
    rows = rows_in[0:8, :]
    half = rows.shape[1] // 2
    rows = jnp.where(wi == 0, rows[:, :half], rows[:, half:])
    step = 1
    while step < per:
        size = HEADDIM * step
        parts = [rows[:, i * size : (i + 1) * size] for i in range(half // size)]
        swapped = jnp.concatenate([parts[i ^ 1] for i in range(len(parts))], axis=1)
        rows = jnp.where(jnp.bitwise_and(di, step) != 0, swapped, rows)
        step *= 2
    table_o[...] = rows


def entry_first(per, hm, ho, hh, bcdt, table, sel, o, xn_o, buf, between, edges):
    xnh_o, r_o, raw_o, rawh_o, dt_o, sig_o = o.xnh, o.r, o.raw, o.rawh, o.dt, o.sig
    cl_o, clt_o, rate_o, wdt_o, b_o = o.cl, o.clt, o.rate, o.wdt, o.b
    rows = hm.shape[0]
    state = b_o.shape[1]
    per_head = dot(table[...], sel[...], HIGH)
    bias = per_head[5:6, :]
    rate = -jnp.exp(per_head[6:7, :])
    rate_o[...] = rate
    wbc = bcdt.at[0 : 2 * state, :]
    wdt_o[...] = dot(
        slot_heads(rate.shape[1], per).astype(BF), bcdt[2 * state : 2 * state + HEADS, :]
    ).astype(BF)
    wdt = wdt_o
    gain = bcdt[2 * state + HEADS : 2 * state + HEADS + 1, :].astype(F32)
    blocks = rows // Q
    lower = tri("ge").astype(F32)

    def norm(left, right):
        h = jnp.concatenate([left, right], axis=1).astype(F32)
        r = lax.rsqrt(jnp.mean(h * h, axis=1, keepdims=True) + EPS)
        return (h * r * gain).astype(BF), r

    def first(i, carry):
        here = pl.ds(pl.multiple_of(i * Q, Q), Q)
        xn, r = norm(hm[here, :], ho[here, :])
        xn_o[here, :] = xn
        r_o[here, :] = r
        raw = dot_t(xn, wbc[...])
        raw_o[here, :] = raw
        buf[pl.ds(pl.multiple_of(HALO + i * Q, HALO), Q), :] = raw
        steps = dot_t(xn, wdt[...]) + bias
        dt = jax.nn.softplus(steps)
        dt_o[here, :] = dt
        sig_o[here, :] = sigmoid(steps)
        da = dt * rate
        cl_o[here, :] = dot(lower, da, HIGH)
        clt_o[:, here] = lax.dot_general(
            da, lower, (((0,), (1,)), ((), ())), precision=HIGH, preferred_element_type=F32
        )
        return carry

    lax.fori_loop(0, blocks // 2, first, 0, unroll=2)
    between()
    lax.fori_loop(blocks // 2, blocks, first, 0, unroll=2)
    edges()
    half = hm.shape[1]
    xnh, _ = norm(hh[:, :half], hh[:, half:])
    xnh = jnp.where(lax.axis_index("head") > 0, xnh.astype(F32), 0.0).astype(BF)
    xnh_o[...] = xnh
    buf[0:HALO, :] = dot_t(xnh, wbc[...])
    rawh_o[...] = buf[0:HALO, :]


def entry_second(cbc, o, tot_o, buf):
    u_o, b_o, c_o, dt_o, cl_o, clt_o = o.ubc, o.b, o.c, o.dt, o.cl, o.clt
    dt2_o, e12_o, tl2_o, dttl2_o, ec2_o, edt2_o = o.dt2, o.e12, o.tl2, o.dttl2, o.ec2, o.edt2
    state = b_o.shape[1]
    blocks = b_o.shape[0] // Q

    def second(i, carry):
        here = pl.ds(pl.multiple_of(i * Q, Q), Q)
        win = buf[pl.ds(pl.multiple_of(i * Q, Q), Q + HALO), :]
        u = jnp.zeros((Q, win.shape[1]), F32)
        for k in range(4):
            u = u + cbc[k : k + 1, :] * win[HALO - 3 + k : HALO - 3 + k + Q, :]
        u_o[here, :] = u
        v = u * sigmoid(u)
        b_o[here, :] = v[:, :state].astype(BF)
        c_o[here, :] = v[:, state:].astype(BF)
        return carry

    lax.fori_loop(0, blocks, second, 0, unroll=2)
    tots = [cl_o[i * Q + Q - 1 : i * Q + Q, :] for i in range(blocks)]
    ctot = functools.reduce(lambda x, y: x + y, tots)
    heads = clt_o.shape[0]
    column = functools.reduce(
        lambda x, y: x + y, [clt_o[:, i * Q + Q - 1 : i * Q + Q] for i in range(blocks)]
    )
    hi = column.astype(BF)
    mid = (column - hi.astype(F32)).astype(BF)
    low = (column - hi.astype(F32) - mid.astype(F32)).astype(BF)
    lane = lax.broadcasted_iota(jnp.int32, (heads, tot_o.shape[1]), 1)
    tot_o[...] = jnp.where(
        lane == 0,
        hi.astype(F32),
        jnp.where(lane == 1, mid.astype(F32), jnp.where(lane == 2, low.astype(F32), 0.0)),
    ).astype(BF)
    off = jnp.zeros_like(ctot)
    for i in range(blocks):
        here = slice(i * Q, i * Q + Q)
        cl = cl_o[here, :]
        dt = dt_o[here, :]
        tail = jnp.exp(tots[i] - cl)
        dt2_o[here, :] = split2(dt)
        e12_o[here, :] = split2(jnp.exp(cl))
        tl2_o[here, :] = split2(tail)
        dttl2_o[here, :] = split2(dt * tail)
        ec2_o[here, :] = split2(jnp.exp(cl + off))
        edt2_o[here, :] = split2(dt * jnp.exp(ctot - cl - off))
        off = off + tots[i]


def decay(cl, clt, h, mask):
    return jnp.exp(jnp.where(mask, cl[:, h : h + 1] - clt[h : h + 1, :], NEG))


def lane_masks():
    lane = lax.broadcasted_iota(jnp.int32, (1, Q), 1)
    low = (lane < HEADDIM).astype(F32)
    return low.astype(BF), (1.0 - low).astype(BF)


def project(s, per, xn, o, w, cw, ex, z_o, xr_o, xrh_o, u_o, xdt_o, msg, buf, acc):
    rows = z_o.shape[0]
    gc = per * HEADDIM
    cols = slice(s * gc, s * gc + gc)
    xh = dot_t(o.xnh[...], w[1, cols, :])
    buf[0:HALO, :] = xh
    xrh_o[...] = xh
    acc[...] = jnp.zeros_like(acc)
    cut = rows // 2 if rows // 2 % Q == 0 else rows

    def part(j, carry):
        base = j * cut
        here = pl.ds(pl.multiple_of(base, Q), cut)
        buf[pl.ds(pl.multiple_of(base + HALO, HALO), cut), :] = dot_t(xn[here, :], w[1, cols, :])
        z_o[here, :] = dot_t(xn[here, :], w[0, cols, :])
        for i in range(cut // Q):
            here = pl.ds(pl.multiple_of(base + i * Q, Q), Q)
            win = buf[pl.ds(pl.multiple_of(base + i * Q, Q), Q + HALO), :]
            u = jnp.zeros((Q, gc), F32)
            for k in range(4):
                u = u + cw[k : k + 1, cols] * win[HALO - 3 + k : HALO - 3 + k + Q, :]
            xr_o[here, :] = win[HALO:, :].astype(BF)
            u_o[here, :] = u
            xs = u * sigmoid(u)
            xdt_o[here, :] = (xs * dot(o.dt2[here, :], ex[:, cols])).astype(BF)
            acc[...] += t_dot((xs * dot(o.edt2[here, :], ex[:, cols])).astype(BF), o.b[here, :])
        return carry

    lax.fori_loop(0, rows // cut, part, 0)
    msg[cols, :] = acc[...].astype(BF)


def inside(s, per, xdt, o, y_o):
    mask = tri("ge")
    low, high = lane_masks()
    rows = xdt.shape[0]
    some = 4 if rows % (4 * Q) == 0 else 1

    def part(j, carry):
        for i in range(some):
            here = pl.ds(pl.multiple_of((j * some + i) * Q, Q), Q)
            g = dot_t(o.c[here, :], o.b[here, :])
            clv, cltv = o.cl[here, :], o.clt[:, here]
            for p in range(xdt.shape[1] // Q):
                lanes = slice(p * Q, p * Q + Q)
                h = s * per + 2 * p
                ws = [(g * decay(clv, cltv, k, mask)).astype(BF) for k in (h, h + 1)]
                x = xdt[here, lanes]
                y_o[here, lanes] = dot(
                    jnp.concatenate(ws, axis=1), jnp.concatenate([x * low, x * high], axis=0)
                ).astype(BF)
        return carry

    lax.fori_loop(0, rows // (some * Q), part, 0)


class Named:
    def __init__(self, names, refs):
        for name, ref in zip(names, refs):
            setattr(self, name, ref)


KEPT = (
    "xnh", "r", "raw", "rawh", "ubc", "b", "c", "dt", "sig", "cl", "clt", "dt2", "e12", "tl2",
    "dttl2", "ec2", "edt2", "rate", "wdt", "tot", "table", "bcdt",
)


def front_kernel(per, nz, *refs):
    hidden, first, first2, rest, rest2, bcdt, table, cbc, sel, ex, refs = take(refs, *[0] * 10)
    out_mine, out2, cot, refs = take(refs, 0, 0, 0)
    w_o, wo_o, cot_o, xn_o, refs = take(refs, 0, 0, 0, 0)
    z_o, xr_o, u_o, xdt_o, y_o, messages_o, xrh_o, refs = take(refs, *[nz] * 5, nz - 1, nz)
    kept, refs = refs[: len(KEPT)], refs[len(KEPT) :]
    o = Named(KEPT, kept)
    z_v, xr_v, u_v, xdt_v, y_v, refs = take(refs, *[nz] * 5)
    w, ho, eh, xn, msg, buf, bcbuf, acc, sends, receives, locals_ = refs
    bc = o.bcdt
    rows, half = hidden.shape
    gc = per * HEADDIM
    top = nz * gc
    sibling = {"width": 1 - lax.axis_index("width")}
    z_peers = line_peers(nz, 1)
    d_peers = plane_peers(per)
    used = [0]

    def copy(source, target, peer):
        i = used[0]
        used[0] += 1
        return remote(source, target, sends, receives, i, peer)

    left, right = pl.ds(0, half), pl.ds(half, half)
    swap_first = copy(first2, w.at[:, pl.ds(0, HEADDIM), right], sibling)
    swap_rest = copy(rest2, w.at[:, pl.ds(HEADDIM, gc - HEADDIM), right], sibling)
    swap_hidden = copy(hidden, ho, sibling)
    swap_bc = copy(bcdt, bc.at[:, right], sibling)
    swap_out = copy(out2, wo_o.at[pl.ds(0, gc), right], sibling)
    swap_cot = copy(cot, cot_o, sibling)
    z_table, z_w, z_out, z_state, z_state2 = [], [], [], [], []
    for k, peer in enumerate(z_peers):
        s = k + 1
        z_table.append(copy(table, o.table.at[:, pl.ds(s * gc, gc)], peer))
        own = w.at[:, pl.ds(0, HEADDIM), :]
        z_w.append(copy(own, w.at[:, pl.ds(s * gc, HEADDIM), :], peer))
        z_out.append(
            copy(wo_o.at[pl.ds(0, HEADDIM), :], wo_o.at[pl.ds(s * gc, HEADDIM), :], peer)
        )
        most = pl.ds(0, top - gc)
        z_state.append(copy(msg.at[most, :], messages_o[k].at[most, :], peer))
        more = pl.ds(top - gc, gc + HALO)
        z_state2.append(copy(msg.at[more, :], messages_o[k].at[more, :], peer))
    last = pl.ds(rows - HALO, HALO)
    edge1 = copy(hidden.at[last, :], eh.at[:, left], z_peers[0])
    edge2 = copy(ho.at[last, :], eh.at[:, right], z_peers[0])
    p_w = {s: [] for s in range(1, nz)}
    p_out = {s: [] for s in range(1, nz)}
    for s in range(1, nz):
        for k, peer in enumerate(d_peers):
            mine = pl.ds(s * gc, HEADDIM)
            there = pl.ds(s * gc + (k + 1) * HEADDIM, HEADDIM)
            via, to = k, peer
            if k + 1 == per - 1:
                first_hop = s % 2
                mine = pl.ds(s * gc + (first_hop + 1) * HEADDIM, HEADDIM)
                to = d_peers[1 - first_hop]
            p_w[s].append(copy(w.at[:, mine, :], w.at[:, there, :], to))
            p_out[s].append(copy(wo_o.at[mine, :], wo_o.at[there, :], to))

    places = [0]

    def local(source, target):
        i = places[0]
        places[0] += 1
        found = pltpu.make_async_copy(source, target, locals_.at[i])
        found.start()
        return found

    ready = [
        local(first, w.at[:, pl.ds(0, HEADDIM), left]),
        local(rest, w.at[:, pl.ds(HEADDIM, gc - HEADDIM), left]),
        local(bcdt, bc.at[:, left]),
        local(table, o.table.at[:, pl.ds(0, gc)]),
        local(out_mine, wo_o.at[pl.ds(0, gc), left]),
    ]
    meet([sibling, *z_peers, *line_peers(nz, -1), *d_peers])
    start([swap_first, *z_table, swap_hidden, swap_bc, edge1])
    ready[0].wait()
    arrive([swap_first])
    start([z_w[0], swap_rest, swap_out, swap_cot])
    for c in ready[1:]:
        c.wait()
    arrive([swap_hidden])
    start([edge2])
    arrive([swap_bc, *z_table])
    pending = []

    def pass_on(copies, s):
        arrive([copies[s % 2]])
        start([copies[2]])

    def between():
        arrive([z_w[0]])
        start([*p_w[1][:2], *z_w[1:]])

    def edges():
        arrive([edge1, edge2])

    entry_first(per, hidden, ho, eh, bc, o.table, sel, o, xn, bcbuf, between, edges)
    pass_on(p_w[1], 1)
    arrive([z_w[1], swap_rest])
    start(p_w[2][:2])
    entry_second(cbc, o, o.tot, bcbuf)
    msg[top:, :] = o.tot[...]
    pending.append(local(xn, xn_o))
    for k in range(3, nz):
        arrive([z_w[k - 1]])
        start(p_w[k][:2])
    arrive([swap_out])
    start(z_out)
    taps = o.table

    def project_group(s):
        project(
            s, per, xn, o, w, taps, ex, z_v[s], xr_v[s], xrh_o[s], u_v[s], xdt_v[s], msg, buf, acc
        )
        for a, b in ((z_v, z_o), (xr_v, xr_o), (u_v, u_o), (xdt_v, xdt_o)):
            pending.append(local(a[s], b[s]))

    def inside_group(s):
        inside(s, per, xdt_v[s], o, y_v[s])
        pending.append(local(y_v[s], y_o[s]))

    project_group(0)
    for k in range(2, nz):
        pass_on(p_w[k], k)
    inside_group(0)
    for k in range(1, nz):
        arrive([z_out[k - 1]])
        start(p_out[k][:2])
    for s in range(1, nz):
        arrive([p_w[s][1 - s % 2], p_w[s][2]])
        project_group(s)
        if s == nz - 2:
            start(z_state)
            for k in range(1, nz):
                pass_on(p_out[k], k)
    start(z_state2)
    pending.append(local(w, w_o))
    for s in range(1, nz):
        inside_group(s)
    everything = [swap_first, swap_rest, swap_hidden, swap_bc, swap_out, swap_cot, edge1, edge2]
    everything += [*z_table, *z_w, *z_out, *z_state, *z_state2]
    for s in range(1, nz):
        everything += p_w[s] + p_out[s]
        arrive([p_out[s][1 - s % 2], p_out[s][2]])
    arrive([swap_cot, *z_state, *z_state2])
    for c in everything:
        c.wait_send()
    for c in pending:
        c.wait()


def head_scale(clt, first, per, state):
    return jnp.concatenate(
        [
            jnp.broadcast_to(jnp.exp(clt[h : h + 1, Q - 1 : Q]), (HEADDIM, state))
            for h in range(first, first + per)
        ],
        axis=0,
    )


def from_messages(messages, sign, groups, per, state, store, valid=None):
    nz = len(messages) + 1
    gc = per * HEADDIM
    top = nz * gc
    totals = [
        sum(m[top:, i : i + 1].astype(F32) for i in range(3)) for m in messages
    ]
    for at, j in enumerate(groups):
        total = jnp.zeros((gc, state), F32)
        faded = jnp.zeros((per, 1), F32)
        for k in range(1, nz):
            there = (j - sign * k) % nz
            scale = jnp.exp(faded)
            scale = jnp.concatenate(
                [jnp.broadcast_to(scale[h : h + 1, :], (HEADDIM, state)) for h in range(per)],
                axis=0,
            )
            part = scale * messages[k - 1][there * gc : there * gc + gc, :].astype(F32)
            if valid is not None:
                part = jnp.where(valid(k), part, 0.0)
            total = total + part
            faded = faded + totals[k - 1][there * per : there * per + per, :]
        store[at * gc : at * gc + gc, :] = total


def mid_kernel(groups, per, *refs):
    nz = len(groups)
    y_in, u, z, cot, cot2, b, c, clt, e12, dttl2, refs = take(refs, nz, nz, nz, *[0] * 7)
    u2, z2, ec2, c2, hidden, refs = take(refs, nz, nz, 0, 0, 0)
    messages, tot, table, ex, wout, limit, refs = take(refs, nz - 1, *[0] * 5)
    gain, dsk = table.at[4:5, :], table.at[7:8, :]
    st_o, mask_o, dys_o, dz_o, yn_o, out_o, msg_o, gn_o, sk_o, refs = take(
        refs, nz, 0, nz, *[0] * 6
    )
    s, acc, yv, dv, br, br_out, br_in, sm_out, sm_in, gg, sends, receives = refs
    step = pl.program_id(0)
    tiles = pl.num_programs(0) - 1
    rows, half = cot.shape
    gc = per * HEADDIM
    state = s.shape[1]
    sibling = {"width": 1 - lax.axis_index("width")}

    def copies(k):
        return [
            remote(sm_out.at[k], sm_in.at[k], sends, receives, 2 * k, sibling),
            remote(br_out.at[k], br_in.at[k], sends, receives, 2 * k + 1, sibling),
        ]

    @pl.when(step == 0)
    def _():
        meet([sibling])
        z_index = lax.axis_index("head")
        from_messages(messages, 1, groups, per, state, s, lambda k: z_index - k >= 0)
        acc[...] = jnp.zeros_like(acc)
        gn_o[...] = jnp.zeros_like(gn_o)
        sk_o[...] = jnp.zeros_like(sk_o)

    @pl.when(step < tiles)
    def _():
        slot = lax.rem(step, 2)
        row = lax.broadcasted_iota(jnp.int32, (rows, 1), 0) + step * rows
        keep = row < limit[0, 0]
        for i, v in enumerate((cot, cot2)):
            mask_o[:, i * half : i * half + half] = jnp.where(keep, v[...].astype(F32), 0.0).astype(
                BF
            )
        dv[slot] = dot_t(mask_o[...], wout[...])
        lane = lax.broadcasted_iota(jnp.int32, (Q, Q), 1)
        for i in range(rows // Q):
            part = slice(i * Q, i * Q + Q)
            cc, bb = c[part, :], b[part, :]
            square = jnp.zeros((Q, gc), F32)
            inner = jnp.zeros((Q, gc), F32)
            for j in groups:
                here = slice(j * gc, j * gc + gc)
                sv = s[here, :]
                sb = sv.astype(BF)
                st_o[j][i] = sb
                x = u[j][part, :]
                x = x * sigmoid(x)
                e1 = dot(e12[part, :], ex[:, here])
                y = y_in[j][part, :].astype(F32) + e1 * dot_t(cc, sb) + dsk[:, here] * x
                yv[slot, part, here] = y
                xt = (x * dot(dttl2[part, :], ex[:, here])).astype(BF)
                s[here, :] = head_scale(clt.at[:, part], j * per, per, state) * sv + t_dot(xt, bb)
                zz = z[j][part, :]
                gz = y * (zz * sigmoid(zz))
                g = gz * gain[:, here]
                gg[part, here] = g.astype(BF)
                square = square + gz * gz
                inner = inner + g * dv[slot, part, here]
            sm_out[step, part, :] = jnp.where(
                lane == 0,
                jnp.sum(square, axis=1, keepdims=True),
                jnp.sum(inner, axis=1, keepdims=True),
            )
        branch = dot(gg[...], wout[...])
        br[slot] = branch[:, :half]
        br_out[step] = branch[:, half:].astype(BF)
        for copy in copies(step):
            copy.start()

    @pl.when(step > 0)
    def _():
        k = step - 1
        slot = lax.rem(k, 2)
        for copy in copies(k):
            copy.wait()
        count = nz * gc * 2
        for i in range(rows // Q):
            part = slice(i * Q, i * Q + Q)
            both = sm_out[k, part, :] + sm_in[k, part, :]
            r2 = lax.rsqrt(both[:, 0:1] / count + EPS)
            pull = both[:, 1:2] * (r2 * r2 * r2) / count
            row = lax.broadcasted_iota(jnp.int32, (Q, 1), 0) + k * rows + i * Q
            keep = jnp.where(row < limit[0, 0], r2, 0.0)
            out_o[part, :] = (
                hidden[part, :].astype(F32)
                + keep * (br[slot, part, :] + br_in[k, part, :].astype(F32))
            ).astype(BF)
            for j in groups:
                here = slice(j * gc, j * gc + gc)
                gn = gain[:, here]
                zz = z2[j][part, :]
                sz = sigmoid(zz)
                silu = zz * sz
                y = yv[slot, part, here]
                gz = y * silu
                dy_n = dv[slot, part, here]
                gr = gz * r2
                yn_o[part, here] = (gr * gn).astype(BF)
                gn_o[:, here] += jnp.sum(dy_n * gr, axis=0, keepdims=True)
                dgz = r2 * gn * dy_n - gz * pull
                dys = dgz * silu
                dys_o[j][part, :] = dys.astype(BF)
                dz_o[part, here] = (dgz * y * (sz + silu * (1.0 - sz))).astype(BF)
                x = u2[j][part, :]
                x = x * sigmoid(x)
                sk_o[:, here] += jnp.sum(dys * x, axis=0, keepdims=True)
                acc[here, :] += t_dot(
                    (dys * dot(ec2[part, :], ex[:, here])).astype(BF), c2[part, :]
                )

    @pl.when(step == tiles)
    def _():
        top = nz * gc
        msg_o[0:top, :] = acc[...].astype(BF)
        msg_o[top:, :] = tot[...]


def line_peers(count, sign):
    z = lax.axis_index("head")
    return [{"head": lax.rem(z + sign * k + count, count)} for k in range(1, count)]


def plane_peers(count):
    d = lax.axis_index("dp")
    return [{"dp": jnp.bitwise_xor(d, m)} for m in range(1, count)]


def meet(peers):
    barrier = pltpu.get_barrier_semaphore()
    for peer in peers:
        pl.semaphore_signal(barrier, inc=1, device_id=peer, device_id_type=MESH)
    pl.semaphore_wait(barrier, len(peers))


def remote(source, target, sends, receives, i, peer):
    return pltpu.make_async_remote_copy(
        src_ref=source,
        dst_ref=target,
        send_sem=sends.at[i],
        recv_sem=receives.at[i],
        device_id=peer,
        device_id_type=MESH,
    )


def conv_back(d, nxt, taps, raw, rawh, grad_o, out_o, outh_o, last):
    win = jnp.concatenate([d, nxt[...]], axis=0)
    back = jnp.zeros_like(d)
    sums = []
    for k in range(4):
        part = win[3 - k : 3 - k + Q, :]
        back = back + taps[k : k + 1, :] * part
        sums.append(jnp.sum(raw * part, axis=0, keepdims=True))
    grad_o[...] += jnp.concatenate(sums, axis=0)
    out_o[...] = back.astype(BF)
    nxt[...] = d[0:8, :]

    @pl.when(last)
    def _():
        win_h = jnp.concatenate([jnp.zeros((HALO, d.shape[1]), F32), d[0:8, :]], axis=0)
        back_h = jnp.zeros((HALO, d.shape[1]), F32)
        sums_h = []
        for k in range(4):
            part = win_h[3 - k : 3 - k + HALO, :]
            back_h = back_h + taps[k : k + 1, :] * part
            sums_h.append(jnp.sum(rawh[...] * part, axis=0, keepdims=True))
        grad_o[...] += jnp.concatenate(sums_h, axis=0)
        outh_o[...] = back_h.astype(BF)


def scan_back_kernel(groups, per, *refs):
    n = len(groups)
    nz = n
    xdt, dys, u, xr, st, xrh, rest = take(refs, n, n, n, n, n, n)
    (b, c, cl, clt, dt, sig, dt2, e12, tl2), rest = rest[:9], rest[9:]
    (ubc, braw, brawh, table, cbc, rate, ex, er), rest = rest[:8], rest[8:]
    cw, dsk = table.at[0:4, :], table.at[7:8, :]
    message, early, rest = take(rest, 0, per)
    dx_o, dxh_o, gcx_o, rest = take(rest, n, n, n)
    dt_o, ga_o, gbias_o, bc_o, bch_o, gcb_o, low = rest[:7]
    messages, got, rest = take(rest[7:], nz - 1, per - 1)
    du_next, rest = take(rest, n)
    db_next, own, dxi, dbi, dci, dai, kt, ds, vs, sends, receives, local = rest
    step = pl.program_id(0)
    blocks = pl.num_programs(0) // 2
    heads = dt.shape[1]
    state = b.shape[1]
    gc = per * HEADDIM
    line_at, plane_at = 0, nz - 1

    def state_copies():
        return [
            remote(message, messages[i], sends, receives, line_at + i, peer)
            for i, peer in enumerate(line_peers(nz, -1))
        ]

    def plane_copies(s):
        return [
            remote(
                early[i + 1].at[s], got[i].at[s], sends, receives, plane_at + s * (per - 1) + i, peer
            )
            for i, peer in enumerate(plane_peers(per))
        ]

    def own_copy():
        return pltpu.make_async_copy(early[0], own, local)

    @pl.when(step == 0)
    def _():
        own_copy().start()
        meet(line_peers(nz, -1) + line_peers(nz, 1) + plane_peers(per))
        for copy in plane_copies(1) + state_copies():
            copy.start()

    @pl.when(step < blocks)
    def _():
        rows = pl.ds(pl.multiple_of(step * Q, Q), Q)
        mask = tri("ge")
        lower, upper_lanes = lane_masks()
        g = dot_t(c[...], b[...])
        clv, cltv = cl[...], clt[...]
        lane = lax.broadcasted_iota(jnp.int32, (Q, heads), 1)
        dg = jnp.zeros((Q, Q), F32)
        rsum = jnp.zeros((Q, heads), F32)
        for s in groups:
            for p in range(per // 2):
                here = slice(p * Q, p * Q + Q)
                x = xdt[s][:, here]
                dy = dys[s][:, here]
                pp = dot_t(dy, jnp.concatenate([x * lower, x * upper_lanes], axis=0))
                ws = []
                for j in range(2):
                    h = s * per + 2 * p + j
                    ell = decay(clv, cltv, h, mask)
                    ws.append((g * ell).astype(BF))
                    pe = pp[:, j * Q : j * Q + Q] * ell
                    dg = dg + pe
                    m = pe * g
                    rsum = jnp.where(lane == h, jnp.sum(m, axis=1, keepdims=True), rsum)
                    kt[h : h + 1, :] = jnp.sum(m, axis=0, keepdims=True)
                dxi[rows, s * gc + p * Q : s * gc + p * Q + Q] = t_dot(
                    jnp.concatenate(ws, axis=0),
                    jnp.concatenate([dy * lower, dy * upper_lanes], axis=0),
                )
        dgb = dg.astype(BF)
        dci[rows, :] = dot(dgb, b[...])
        dbi[rows, :] = t_dot(dgb, c[...])
        upper = tri("le").astype(F32)
        dai[rows, :] = dot(upper, rsum, HIGH) - dot_t(upper, kt[...], HIGH)

    @pl.when(step == blocks)
    def _():
        for copy in state_copies():
            copy.wait()
        z = lax.axis_index("head")
        from_messages(messages, -1, groups, per, state, ds, lambda k: z + k < nz)
        for i in range(n):
            du_next[i][...] = jnp.zeros_like(du_next[i])
            gcx_o[i][...] = jnp.zeros_like(gcx_o[i])
        db_next[...] = jnp.zeros_like(db_next)
        gcb_o[...] = jnp.zeros_like(gcb_o)
        ga_o[...] = jnp.zeros_like(ga_o)
        gbias_o[...] = jnp.zeros_like(gbias_o)

    @pl.when(step >= blocks)
    def _():
        rows = pl.ds(pl.multiple_of((2 * blocks - 1 - step) * Q, Q), Q)
        last = step == 2 * blocks - 1
        rsum = jnp.zeros((Q, heads), F32)
        gsum = jnp.zeros((Q, heads), F32)
        ddt = jnp.zeros((Q, heads), F32)
        dbs = dbi[rows, :]
        dcs = dci[rows, :]
        for s in groups:
            here = slice(s * gc, s * gc + gc)
            ehere = er[here, :]
            sb = st[s][0]
            dsv = ds[here, :]
            dsb = dsv.astype(BF)
            dy = dys[s][...].astype(F32)
            dye = dy * dot(e12[...], ex[:, here])
            dyb = dye.astype(BF)
            rsum = rsum + dot((dye * dot_t(c[...], sb)).astype(BF), ehere)
            dcs = dcs + dot(dyb, sb)
            bds = dot_t(b[...], dsb)
            tail = dot(tl2[...], ex[:, here])
            dtx = dot(dt2[...], ex[:, here])
            uu = u[s][...]
            su = sigmoid(uu)
            xs = uu * su
            xt = xs * dtx * tail
            gsum = gsum + dot((xt * bds).astype(BF), ehere)
            dbs = dbs + dot(xt.astype(BF), dsb)
            dxdt = dxi[rows, here] + tail * bds
            ddt = ddt + dot((dxdt * xs).astype(BF), ehere)
            eds = head_scale(clt, s * per, per, state) * dsv
            ev = eds * sb.astype(F32)
            for j in range(per):
                h = s * per + j
                vs[h : h + 1, :] = jnp.sum(
                    ev[j * HEADDIM : (j + 1) * HEADDIM, :], axis=0, keepdims=True
                )
            ds[here, :] = eds + t_dot(dyb, c[...])
            du = (dxdt * dtx + dsk[:, here] * dy) * (su + xs * (1.0 - su))
            conv_back(
                du, du_next[s], cw.at[:, here], xr[s][...].astype(F32), xrh[s], gcx_o[s],
                dx_o[s], dxh_o[s], last,
            )
        vrow = dot_t(jnp.ones((8, state), F32), vs[...], HIGH)
        da = (
            dai[rows, :]
            + split_dot(tri("le").astype(BF), rsum)
            + split_dot(tri("gt").astype(BF), gsum)
            + vrow[0:1, :]
        )
        draw = (rate[...] * da + ddt) * sig[...]
        dt_o[...] = draw.astype(BF)
        ga_o[...] += jnp.sum(da * dt[...], axis=0, keepdims=True)
        gbias_o[...] += jnp.sum(draw, axis=0, keepdims=True)
        d = jnp.concatenate([dbs, dcs], axis=1)
        v = ubc[...]
        sv = sigmoid(v)
        conv_back(
            d * (sv + v * sv * (1.0 - sv)), db_next, cbc, braw[...], brawh, gcb_o, bc_o, bch_o,
            last,
        )

    def add(s):
        for copy in plane_copies(s):
            copy.wait()

        def piece(i, carry):
            part = pl.ds(pl.multiple_of(i * HALO, HALO), HALO)
            total = own[s, part, :].astype(F32)
            for v in got:
                total = total + v[s, part, :].astype(F32)
            low[s, part, :] = total.astype(BF)
            return carry

        lax.fori_loop(0, low.shape[1] // HALO, piece, 0, unroll=2)

    order = [*range(1, nz), 0]
    for k, s in enumerate(order):
        if k > 0:

            @pl.when(step == (blocks * k * 3) // (2 * nz))
            def _(s=s):
                for copy in plane_copies(s):
                    copy.start()

        if s > 0:

            @pl.when(step == blocks + (blocks * 3 * k) // (4 * (nz - 1)) + 1)
            def _(s=s):
                if s == 1:
                    own_copy().wait()
                add(s)

    @pl.when(step == 2 * blocks - 1)
    def _():
        add(0)


def early_grad_kernel(per, yn, masked, dz, xn, *outs):
    g_out = t_dot(yn[...], masked[...]).astype(BF)
    g_z = t_dot(dz[...], xn[...]).astype(BF)
    for m in range(per):
        here = slice(m * HEADDIM, (m + 1) * HEADDIM)
        outs[m][0, :HEADDIM, :] = g_out[here, :]
        outs[m][0, HEADDIM:, :] = g_z[here, :]


class Copies:
    def __init__(self, sends, receives):
        self.sends, self.receives, self.all = sends, receives, []

    def __call__(self, source, target, peer):
        copy = remote(source, target, self.sends, self.receives, len(self.all), peer)
        self.all.append(copy)
        return copy


def start(copies):
    for c in copies:
        c.start()


def arrive(copies):
    for c in copies:
        c.wait_recv()


def tail_kernel(per, nz, *refs):
    dx, dxh, taps, refs = take(refs, nz, nz, nz)
    (dz, dbc, dbch, dti, xn, xnh, w, bc, wdt, early, hidden, cot, r), refs = refs[:13], refs[13:]
    (gain, gbc, grate, gbias, gskip, ggain, rate, ex), refs = refs[:8], refs[8:]
    ea, la, hid_o, norm_o, tbc_o, refs = take(refs, *[0] * 5)
    etot, gx, gs, gdt, lx, ls, sw_out, sw_in, dxn, dxn_out, dxn_in, refs = take(refs, *[0] * 11)
    edge_out, edge_in, edge_sum, edge_next, across, across_in, nrm, nrm2, sums, refs = take(
        refs, *[0] * 9
    )
    rx, rs, zx, zs, nr, nz_r, ze, refs = take(
        refs, per - 1, per - 1, nz - 1, nz - 1, per - 1, nz - 1, nz - 1
    )
    stage, sends, receives = refs
    copy = Copies(sends, receives)
    rows, half = hidden.shape
    gc = per * HEADDIM
    channels = nz * gc
    state2 = dbc.shape[1]
    quarter = state2 // per
    share = quarter + HALO
    some_dt = HEADS // per
    wi, di, zi = lax.axis_index("width"), lax.axis_index("dp"), lax.axis_index("head")
    sibling = {"width": 1 - wi}
    d_peers, z_back = plane_peers(per), line_peers(nz, -1)
    left, right = pl.ds(0, half), pl.ds(half, half)
    block = rows // nz

    early_swap = copy(etot.at[:, right], ea.at[0, wi], sibling)
    late_swap = copy(sw_out, sw_in, sibling)
    dxn_swap = [
        copy(dxn_out.at[pl.ds(i * block, block), :], dxn_in.at[pl.ds(i * block, block), :], sibling)
        for i in range(nz)
    ]
    edge_swap = copy(edge_out, edge_in, sibling)
    across_swap = copy(across, across_in, sibling)
    p_share, p_x, p_early, p_norm, p_late = [], {s: [] for s in range(nz)}, [], [], []
    for k, peer in enumerate(d_peers):
        m = k + 1
        p_share.append(copy(gs.at[m], rs[k], peer))
        for s in range(nz):
            p_x[s].append(copy(gx.at[s, m], rx[k].at[s], peer))
        p_early.append(copy(ea.at[0], ea.at[m], peer))
        p_norm.append(copy(nrm, nr[k], peer))
        p_late.append(copy(la.at[0], la.at[m], peer))
    z_x, z_share, z_norm, z_early = [], [], [], []
    for k, peer in enumerate(z_back):
        z_x.append(copy(lx.at[k + 1], zx[k], peer))
        z_early.append(copy(early.at[k + 1], ze[k], peer))
        z_share.append(copy(ls, zs[k], peer))
        z_norm.append(copy(nrm2, nz_r[k], peer))
    z_edge = copy(edge_sum, edge_next, z_back[0])

    meet([sibling, *z_back, *line_peers(nz, 1), *d_peers])
    start(z_early)

    g = t_dot(dbc[...], xn[...]) + t_dot(dbch[...], xnh[...])
    stage[0:state2, :] = g
    gdt[...] = split_dot_tr(slot_heads(dti.shape[1], per), t_dot(dti[...], xn[...]))
    per_head = jnp.concatenate([gbias[...], grate[...] * rate[...]], axis=0)
    small = jnp.concatenate(
        [
            jnp.concatenate([v[...] for v in taps], axis=1),
            ggain[...],
            gskip[...],
            dot(split2(per_head), ex[...]),
        ],
        axis=0,
    )
    both = split2(gbc[...])
    both = jnp.concatenate([both, jnp.zeros((4, 2 * state2), BF)], axis=0)
    for m in range(per):
        at = jnp.bitwise_xor(di, m)
        gs[m, 0:quarter, :] = stage[pl.ds(pl.multiple_of(at * quarter, quarter), quarter), :].astype(
            BF
        )
        lanes = jnp.concatenate(
            [
                small[:, (s * per + m) * HEADDIM : (s * per + m + 1) * HEADDIM]
                for s in range(nz)
            ],
            axis=1,
        )
        lower = jnp.concatenate([split2(lanes), both], axis=1)
        upper = gdt[pl.ds(pl.multiple_of(at * some_dt, some_dt), some_dt), :].astype(BF)
        gs[m, quarter:, :] = jnp.concatenate(
            [upper.astype(F32), lower.astype(F32)], axis=0
        ).astype(BF)
    start(p_share)
    order = [*range(1, nz), 0]
    for s in order:
        g = t_dot(dx[s][...], xn[...]) + t_dot(dxh[s][...], xnh[...])
        for m in range(per):
            gx[s, m] = g[m * HEADDIM : (m + 1) * HEADDIM, :].astype(BF)
        start(p_x[s])
    def add_share():
        arrive(p_share)
        for i in range(share // HALO):
            here = slice(i * HALO, i * HALO + HALO)
            total = gs[0, here, :].astype(F32)
            for v in rs:
                total = total + v[here, :].astype(F32)
            sums[here, :] = total
        pack(sums)
        start(z_share)

    def pack(v):
        ls[0:quarter, :] = v[0:quarter, :].astype(BF)
        n = nz * HEADDIM
        rest = v[quarter:, :]
        a = rest[:, 0:n] + rest[:, n : 2 * n]
        b = rest[:, 2 * n : 2 * n + state2] + rest[:, 2 * n + state2 :]
        low_rows = jnp.concatenate([split2(a), split2(b)], axis=1)
        row = lax.broadcasted_iota(jnp.int32, (HALO, 1), 0)
        ls[quarter:, :] = jnp.where(row < some_dt, rest, low_rows.astype(F32)).astype(BF)

    def add_x(s):
        arrive(p_x[s])
        for i in range(HEADDIM // HALO):
            here = slice(i * HALO, i * HALO + HALO)
            total = gx[s, 0, here, :].astype(F32)
            for v in rx:
                total = total + v[s, here, :].astype(F32)
            lx[s, here, :] = total.astype(BF)
        if s > 0:
            start([z_x[s - 1]])

    for i in range(nz):
        here = slice(i * block, i * block + block)
        total = dot(dz[here, :], w[0])
        for s in range(nz):
            total = total + dot(dx[s][here, :], w[1, s * gc : (s + 1) * gc, :])
        total = total + dot(dbc[here, :], bc[0:state2, :]) + dot(dti[here, :], wdt[...])
        dxn[here, :] = total[:, :half]
        dxn_out[here, :] = total[:, half:].astype(BF)
        start([dxn_swap[i]])
        if i == 0:
            add_share()
            total = dot(dbch[...], bc[0:state2, :])
            for s in range(nz):
                total = total + dot(dxh[s][...], w[1, s * gc : (s + 1) * gc, :])
            edge_sum[...] = total[:, :half]
            edge_out[...] = total[:, half:]
            start([edge_swap])
        if i == 1:
            arrive(z_early)
            for j in range(early.shape[1] // HALO):
                part = slice(j * HALO, j * HALO + HALO)
                total = early[0, part, :].astype(F32)
                for v in ze:
                    total = total + v[part, :].astype(F32)
                etot[part, :] = total.astype(BF)
            start([early_swap])
            ea[0, wi] = etot[:, :half]
            add_x(order[0])
            arrive([edge_swap])
            edge_sum[...] = edge_sum[...] + edge_in[...]
            start([z_edge])
        if i == 2:
            arrive([early_swap])
            start(p_early)
    if nz > 2:
        add_x(order[1])

    arrive([*dxn_swap, z_edge])
    late_edge = jnp.where(zi < nz - 1, edge_next[...], 0.0)
    gain_v = gain[...]
    norm_sum = jnp.zeros((8, half), F32)
    ones = jnp.ones((8, half), BF)
    for i in range(rows // Q):
        here = slice(i * Q, i * Q + Q)
        v = dxn[here, :] + dxn_in[here, :].astype(F32)
        if i == rows // Q - 1:
            v = v + jnp.concatenate([jnp.zeros((Q - HALO, half), F32), late_edge], axis=0)
        dxn[here, :] = v
        h = hidden[here, :].astype(F32)
        vh = v * h
        norm_sum = norm_sum + jnp.sum(
            (vh * r[here, :]).reshape(Q // 8, 8, half), axis=0
        )
        across[:, here] = split_dot_t(ones, vh * gain_v)
    start([across_swap])
    nrm[...] = norm_sum
    start(p_norm)
    for s in order[2:]:
        add_x(s)
    arrive([across_swap])
    eighth = jnp.full((8, Q), 0.125, F32)
    for i in range(rows // Q):
        here = slice(i * Q, i * Q + Q)
        total = across[:, here] + across_in[:, here]
        total = t_dot(total, eighth, HIGH)
        rr = r[here, :]
        scale = rr * rr * rr / (2 * half)
        rg = rr * gain_v
        for j in range(half // Q):
            lanes = slice(j * Q, j * Q + Q)
            hid_o[here, lanes] = (
                cot[here, lanes].astype(F32)
                + rg[:, lanes] * dxn[here, lanes]
                - hidden[here, lanes].astype(F32) * (scale * total)
            ).astype(BF)
    arrive(p_norm)
    total = nrm[...]
    for v in nr:
        total = total + v[...]
    nrm2[...] = total
    start(z_norm)

    arrive([*z_x, *z_share])
    total = lx[0].astype(F32)
    for v in zx:
        total = total + v[...].astype(F32)
    mine = total.astype(BF)
    la[0, pl.ds(pl.multiple_of(wi * HEADDIM, HEADDIM), HEADDIM), :] = mine[:, :half]
    sw_out[0:HEADDIM, :] = mine[:, half:]
    n = nz * HEADDIM
    total = ls[0:quarter, :].astype(F32)
    for v in zs:
        total = total + v[0:quarter, :].astype(F32)
    sums[0:quarter, :] = total
    sw_out[HEADDIM : HEADDIM + quarter, :] = total[:, half:].astype(BF)
    total = ls[quarter:, :].astype(F32)
    own_small = total[:, 0:HEADDIM] + total[:, n : n + HEADDIM]
    for k, v in enumerate(zs):
        part = v[quarter:, :].astype(F32)
        total = total + part
        at = (k + 1) * HEADDIM
        own_small = own_small + (
            part[:, at : at + HEADDIM] + part[:, n + at : n + at + HEADDIM]
        )
    sums[quarter:, :] = total
    taps_bc = total[:, 2 * n : 2 * n + state2] + total[:, 2 * n + state2 :]
    at = HEADDIM + quarter
    sw_out[at : at + HALO, :] = total[:, half:].astype(BF)
    own_small = split2(own_small)
    own_small = jnp.concatenate(
        [own_small, jnp.zeros((HALO, half - 2 * HEADDIM), BF)], axis=1
    )
    taps_bc2 = split2(taps_bc)
    sw_out[at + HALO : at + 2 * HALO, :] = own_small
    sw_out[at + 2 * HALO : at + 3 * HALO, :] = taps_bc2
    start([late_swap])
    arrive([late_swap])
    there = pl.ds(pl.multiple_of((1 - wi) * HEADDIM, HEADDIM), HEADDIM)
    la[0, there, :] = sw_in[0:HEADDIM, :]
    base = 2 * HEADDIM
    la[0, base : base + share, :] = (
        sums[:, :half] + sw_in[HEADDIM : HEADDIM + share, :].astype(F32)
    ).astype(BF)
    base = base + share
    la[0, pl.ds(pl.multiple_of(base + wi * HALO, HALO), HALO), :] = own_small
    la[0, pl.ds(pl.multiple_of(base + (1 - wi) * HALO, HALO), HALO), :] = sw_in[
        at + HALO : at + 2 * HALO, :
    ]
    start(p_late)
    got = sw_in[at + 2 * HALO : at + 3 * HALO, :].astype(F32)
    taps_bc = taps_bc + got[:, :state2] + got[:, state2:]
    tbc_o[...] = taps_bc[some_dt : some_dt + 4, :]
    arrive(z_norm)
    total = nrm2[...]
    for v in nz_r:
        total = total + v[...]
    norm_o[...] = jnp.sum(total, axis=0, keepdims=True)

    arrive([*p_early, *p_late])
    for c in copy.all:
        c.wait_send()


def finish_kernel(per, ea, la, las, ones, zx_o, ow_o, bcdt_o, cx_o, gn_o, sk_o, bias_o, rate_o):
    di = lax.axis_index("dp")
    some_dt = HEADS // per
    quarter = (bcdt_o.shape[0] - HEADS) // per
    base = 2 * HEADDIM + quarter + HALO
    small = []
    for h in range(2 * per):
        k, j = h // per, h % per
        m = jnp.bitwise_xor(di, j)
        z_part = ea[m, k, HEADDIM:, :].astype(F32)
        x_part = la[m, k * HEADDIM : (k + 1) * HEADDIM, :].astype(F32)
        zx_o[:, h, :] = jnp.transpose(jnp.concatenate([z_part, x_part], axis=0))
        ow_o[h * HEADDIM : (h + 1) * HEADDIM, :] = ea[m, k, :HEADDIM, :].astype(F32)
        v = las[m, base + k * HALO : base + (k + 1) * HALO, :].astype(F32)
        small.append((v[:, :HEADDIM] + v[:, HEADDIM : 2 * HEADDIM])[some_dt:, :])
    for j in range(per):
        m = jnp.bitwise_xor(di, j)
        v = la[m, 2 * HEADDIM : base, :].astype(F32)
        bcdt_o[j * quarter : (j + 1) * quarter, :] = v[:quarter, :]
        at = per * quarter + j * some_dt
        bcdt_o[at : at + some_dt, :] = v[quarter : quarter + some_dt, :]

    @pl.when(pl.program_id(0) == 0)
    def _():
        rows = jnp.concatenate(small, axis=1)
        cx_o[...] = rows[0:4, :]
        gn_o[...] = rows[4:5, :]
        total = dot(rows, ones[...], HIGH)
        sk_o[...] = total[5:6, :]
        bias_o[...] = total[6:7, :] / HEADDIM
        rate_o[...] = total[7:8, :] / HEADDIM


def split_dot_tr(m, v):
    hi = v.astype(BF)
    lo = (v - hi.astype(F32)).astype(BF)
    m = m.astype(BF)
    return t_dot(m, hi) + t_dot(m, lo)


def split_dot_t(m, v):
    hi = v.astype(BF)
    lo = (v - hi.astype(F32)).astype(BF)
    return dot_t(m, hi) + dot_t(m, lo)


def shape(dims, dtype=F32):
    return jax.ShapeDtypeStruct(dims, dtype)


def whole(array):
    rank = len(array.shape)
    return pl.BlockSpec(array.shape, lambda *_: (0,) * rank)


def params():
    return pltpu.CompilerParams(vmem_limit_bytes=VMEM)


def cost(us):
    return pl.CostEstimate(flops=int(us * 1.0e8), bytes_accessed=int(us * 1.0e3), transcendentals=0)


def take(refs, *counts):
    out, at = [], 0
    for n in counts:
        out.append(refs[at] if n == 0 else refs[at : at + n])
        at += max(n, 1)
    return out + [refs[at:]]


def sequence_device(
    hidden, lengths, cotangent, norm_gain, in_zx, in_bcdt, conv_x, conv_bc,
    dt_bias, a_log, d_skip, gnorm_gain, out_w,
):
    rows, half = hidden.shape
    own_heads = in_zx.shape[1]
    nz = lax.axis_size("head")
    ndp = lax.axis_size("dp")
    zi = lax.axis_index("head")
    di = lax.axis_index("dp")
    wi = lax.axis_index("width")
    per = ndp
    heads = nz * per
    channels = heads * HEADDIM
    model = 2 * half
    blocks = rows // Q

    def swap(v):
        return lax.ppermute(v, "width", [(0, 1), (1, 0)])

    gc = per * HEADDIM
    groups = tuple(range(nz))

    onehot = np.kron(np.eye(heads), np.ones((1, HEADDIM)))
    ex = jnp.asarray(np.concatenate([onehot, onehot], axis=0), BF)
    er = jnp.asarray(onehot.T, BF)
    sel = jnp.asarray(onehot.T * (np.arange(channels) % HEADDIM == 0)[:, None], F32)

    each = lambda v: jnp.broadcast_to(v[:, None], (own_heads, HEADDIM)).reshape(1, -1)
    parameter_rows = jnp.concatenate(
        [
            conv_x.astype(F32), gnorm_gain[None].astype(F32), each(dt_bias), each(a_log),
            each(d_skip), jnp.broadcast_to(norm_gain[None].astype(F32), (8, half)),
        ],
        axis=0,
    )
    piece = shape((2, HEADDIM, half), BF)
    some = shape((2, gc - HEADDIM, half), BF)
    outs = shape((gc, half), BF)
    first, first2, rest, rest2, out_mine, out_mine2, bcdt_t, table = pl.pallas_call(
        functools.partial(prep_kernel, per),
        out_shape=[
            piece, piece, some, some, outs, outs,
            shape((2 * STATE + HEADS + HALO, half), BF), shape((8, gc)),
        ],
        compiler_params=params(),
        cost_estimate=cost(4),
        name="prep",
    )(
        in_zx.reshape(half, -1), out_w, jnp.transpose(in_bcdt), parameter_rows
    )
    taps_bc = conv_bc.astype(F32)

    step = lambda i: (i, 0)
    fix = lambda i: (0, 0)
    part = shape((rows, gc), BF)
    full = shape((rows, channels))
    anywhere = pl.BlockSpec(memory_space=pl.ANY)
    vmem = pl.BlockSpec(memory_space=pltpu.VMEM)
    narrow = shape((rows, 2 * heads), BF)
    kept = dict(
        xnh=shape((HALO, model), BF), r=shape((rows, 1)), raw=shape((rows, 2 * STATE)),
        rawh=shape((HALO, 2 * STATE)), ubc=shape((rows, 2 * STATE)), b=shape((rows, STATE), BF),
        c=shape((rows, STATE), BF), dt=shape((rows, heads)), sig=shape((rows, heads)),
        cl=shape((rows, heads)), clt=shape((heads, rows)), dt2=narrow, e12=narrow, tl2=narrow,
        dttl2=narrow, ec2=narrow, edt2=narrow, rate=shape((1, heads)),
        wdt=shape((heads, model), BF),
        bcdt=shape((2 * STATE + HEADS + HALO, model), BF), tot=shape((heads, STATE), BF), table=shape((8, channels)),
    )
    wide_part = shape((rows, gc))
    message_shape = shape((channels + HALO, STATE), BF)
    out_shapes = [
        shape((2, channels, model), BF), shape((channels, model), BF), shape((rows, half), BF),
        shape((rows, model), BF), *[wide_part] * nz, *[part] * nz, *[wide_part] * nz,
        *[part] * nz, *[part] * nz, *[message_shape] * (nz - 1), *[shape((HALO, gc))] * nz,
        *[kept[name] for name in KEPT],
    ]
    held = lambda v: pltpu.VMEM(v.shape, v.dtype)
    remotes = 6 + 5 * (nz - 1) + 2 + 2 * (nz - 1) * (per - 1)
    out = pl.pallas_call(
        functools.partial(front_kernel, per, nz),
        in_specs=[vmem] * 10 + [anywhere] * 3,
        out_specs=[anywhere] * (4 + 5 * nz + nz - 1) + [vmem] * (nz + len(KEPT)),
        out_shape=out_shapes,
        scratch_shapes=[
            *[held(wide_part)] * nz, *[held(part)] * nz, *[held(wide_part)] * nz,
            *[held(part)] * nz, *[held(part)] * nz, pltpu.VMEM((2, channels, model), BF),
            pltpu.VMEM((rows, half), BF), pltpu.VMEM((HALO, model), BF),
            pltpu.VMEM((rows, model), BF),
            held(message_shape), pltpu.VMEM((rows + HALO, gc), F32),
            pltpu.VMEM((rows + HALO, 2 * STATE), F32), pltpu.VMEM((gc, STATE), F32),
            pltpu.SemaphoreType.DMA((remotes,)), pltpu.SemaphoreType.DMA((remotes,)),
            pltpu.SemaphoreType.DMA((7 + 5 * nz,)),
        ],
        compiler_params=pltpu.CompilerParams(
            vmem_limit_bytes=VMEM, collective_id=1, has_side_effects=True
        ),
        cost_estimate=cost(90),
        name="front",
    )(
        hidden, first, first2, rest, rest2, bcdt_t, table, taps_bc, sel, ex, out_mine, out_mine2,
        cotangent,
    )
    weights, wout, cot_o, xn, out = out[0], out[1], out[2], out[3], out[4:]
    z, xr, u, xdt, y_in, messages, xrh, out = take(out, *[nz] * 5, nz - 1, nz)
    o = Named(KEPT, out)
    xnh, r, braw, brawh, ubc, bs, cs = o.xnh, o.r, o.raw, o.rawh, o.ubc, o.b, o.c
    dt, sig, cl, clt, rate, wdt, totals, table = o.dt, o.sig, o.cl, o.clt, o.rate, o.wdt, o.tot, o.table
    dt2, e12, tl2, dttl2, ec2, edt2 = o.dt2, o.e12, o.tl2, o.dttl2, o.ec2, o.edt2
    limit = (lengths[0] - zi * rows).reshape(1, 1)

    smem = pl.BlockSpec(memory_space=pltpu.SMEM)
    tile = 2 * Q if rows % (2 * Q) == 0 else Q
    tiles = rows // tile
    now = lambda columns: pl.BlockSpec((tile, columns), lambda i: (jnp.minimum(i, tiles - 1), 0))
    then = lambda columns: pl.BlockSpec((tile, columns), lambda i: (jnp.maximum(i - 1, 0), 0))
    out = pl.pallas_call(
        functools.partial(mid_kernel, groups, per),
        grid=(tiles + 1,),
        in_specs=[
            *[now(gc)] * (3 * nz), now(half), now(half), now(STATE), now(STATE),
            pl.BlockSpec((heads, tile), lambda i: (0, jnp.minimum(i, tiles - 1))),
            now(2 * heads), now(2 * heads), *[then(gc)] * (2 * nz), then(2 * heads), then(STATE),
            then(half), *[whole(v) for v in messages], whole(totals), whole(table),
            whole(ex), whole(wout), smem,
        ],
        out_specs=[
            *[
                pl.BlockSpec((tile // Q, gc, STATE), lambda i: (jnp.minimum(i, tiles - 1), 0, 0))
            ] * nz,
            now(model), *[then(gc)] * nz, then(channels), then(channels), then(half),
            pl.BlockSpec((channels + HALO, STATE), fix), pl.BlockSpec((1, channels), fix),
            pl.BlockSpec((1, channels), fix),
        ],
        out_shape=[
            *[shape((blocks, gc, STATE), BF)] * nz, shape((rows, model), BF), *[part] * nz,
            shape((rows, channels), BF), shape((rows, channels), BF), shape((rows, half), BF),
            message_shape, shape((1, channels)), shape((1, channels)),
        ],
        scratch_shapes=[
            pltpu.VMEM((channels, STATE), F32), pltpu.VMEM((channels, STATE), F32),
            pltpu.VMEM((2, tile, channels), F32), pltpu.VMEM((2, tile, channels), F32),
            pltpu.VMEM((2, tile, half), F32), pltpu.VMEM((tiles, tile, half), BF),
            pltpu.VMEM((tiles, tile, half), BF), pltpu.VMEM((tiles, tile, Q), F32),
            pltpu.VMEM((tiles, tile, Q), F32), pltpu.VMEM((tile, channels), BF),
            pltpu.SemaphoreType.DMA((2 * tiles,)), pltpu.SemaphoreType.DMA((2 * tiles,)),
        ],
        compiler_params=pltpu.CompilerParams(
            vmem_limit_bytes=VMEM, collective_id=3, has_side_effects=True
        ),
        cost_estimate=cost(30),
        name="mid",
    )(
        *y_in, *u, *z, cotangent, cot_o, bs, cs, clt, e12, dttl2, *u, *z, ec2, cs, hidden,
        *messages, totals, table, ex, wout, limit,
    )
    states, masked, dys, out = take(out, nz, 0, nz)
    dz, yn, out_hidden, message, g_gain, g_skip = out

    gcol = pl.BlockSpec((rows, gc), lambda s: (0, s))
    early = pl.pallas_call(
        functools.partial(early_grad_kernel, per),
        grid=(nz,),
        in_specs=[gcol, whole(masked), gcol, whole(xn)],
        out_specs=[pl.BlockSpec((1, 2 * HEADDIM, model), lambda s: (s, 0, 0))] * per,
        out_shape=[shape((nz, 2 * HEADDIM, model), BF)] * per,
        compiler_params=params(),
        cost_estimate=cost(6),
        name="early_grad",
    )(yn, masked, dz, xn)
    one = lambda i: (jnp.minimum(i, blocks - 1), 0)
    two = lambda i: (jnp.minimum(blocks - 1, 2 * blocks - 1 - i), 0)
    both = lambda i: (jnp.minimum(i, 2 * blocks - 1 - i), 0)
    head_columns = lambda v: pl.BlockSpec((Q, v), two)
    early_shape = early[0].shape
    exchange = nz - 1 + nz * (per - 1)
    out = pl.pallas_call(
        functools.partial(scan_back_kernel, groups, per),
        grid=(2 * blocks,),
        in_specs=[
            *[pl.BlockSpec((Q, gc), one)] * nz, *[pl.BlockSpec((Q, gc), both)] * nz,
            *[pl.BlockSpec((Q, gc), two)] * (2 * nz),
            *[
                pl.BlockSpec(
                    (1, gc, STATE), lambda i: (jnp.minimum(blocks - 1, 2 * blocks - 1 - i), 0, 0)
                )
            ] * nz,
            *[pl.BlockSpec((HALO, gc), fix)] * nz,
            pl.BlockSpec((Q, STATE), both), pl.BlockSpec((Q, STATE), both),
            pl.BlockSpec((Q, heads), one),
            pl.BlockSpec((heads, Q), lambda i: (0, jnp.minimum(i, 2 * blocks - 1 - i))),
            head_columns(heads), head_columns(heads), head_columns(2 * heads),
            head_columns(2 * heads), head_columns(2 * heads), head_columns(2 * STATE),
            head_columns(2 * STATE), whole(brawh), whole(table), whole(taps_bc), whole(rate),
            whole(ex), whole(er), *[anywhere] * (1 + per),
        ],
        out_specs=[
            *[pl.BlockSpec((Q, gc), two)] * nz, *[pl.BlockSpec((HALO, gc), fix)] * nz,
            *[pl.BlockSpec((4, gc), fix)] * nz, head_columns(heads),
            pl.BlockSpec((1, heads), fix), pl.BlockSpec((1, heads), fix),
            head_columns(2 * STATE), pl.BlockSpec((HALO, 2 * STATE), fix),
            pl.BlockSpec((4, 2 * STATE), fix), pl.BlockSpec(early_shape, lambda i: (0, 0, 0)),
        ],
        out_shape=[
            *[shape((rows, gc), BF)] * nz, *[shape((HALO, gc), BF)] * nz, *[shape((4, gc))] * nz,
            shape((rows, heads), BF), shape((1, heads)), shape((1, heads)),
            shape((rows, 2 * STATE), BF), shape((HALO, 2 * STATE), BF), shape((4, 2 * STATE)),
            shape(early_shape, BF),
        ],
        scratch_shapes=[
            *[pltpu.VMEM(message.shape, BF)] * (nz - 1), *[pltpu.VMEM(early_shape, BF)] * (per - 1),
            *[pltpu.VMEM((8, gc), F32)] * nz,
            pltpu.VMEM((8, 2 * STATE), F32), pltpu.VMEM(early_shape, BF), pltpu.VMEM((rows, channels), F32),
            pltpu.VMEM((rows, STATE), F32), pltpu.VMEM((rows, STATE), F32),
            pltpu.VMEM((rows, heads), F32), pltpu.VMEM((heads, Q), F32),
            pltpu.VMEM((channels, STATE), F32), pltpu.VMEM((heads, STATE), F32),
            pltpu.SemaphoreType.DMA((exchange,)), pltpu.SemaphoreType.DMA((exchange,)),
            pltpu.SemaphoreType.DMA,
        ],
        compiler_params=pltpu.CompilerParams(
            vmem_limit_bytes=VMEM, collective_id=0, has_side_effects=True
        ),
        cost_estimate=cost(50),
        name="scan_back",
    )(
        *xdt, *dys, *u, *xr, *states, *xrh, bs, cs, cl, clt, dt, sig, dt2, e12, tl2, ubc, braw,
        brawh, table, taps_bc, rate, ex, er, message, *early,
    )
    dx, dxh, g_taps = list(out[:nz]), list(out[nz : 2 * nz]), out[2 * nz : 3 * nz]
    dti, g_rate, g_bias, dbc, dbch, g_taps_bc, early_low = out[3 * nz :]
    quarter = 2 * STATE // per
    share = quarter + HALO
    late_rows = 2 * HEADDIM + share + 2 * HALO
    swap_rows = HEADDIM + share + 2 * HALO
    tail_copies = 4 + nz + (per - 1) * (4 + nz) + 4 * (nz - 1) + 1
    operands = [
        *dx, *dxh, *g_taps, dz, dbc, dbch, dti, xn, xnh, weights, o.bcdt, wdt, early_low, hidden,
        cotangent, r, norm_gain[None].astype(F32), g_taps_bc, g_rate, g_bias, g_skip, g_gain, rate,
        ex,
    ]
    line16 = pltpu.VMEM((HALO, half), F32)
    line8 = pltpu.VMEM((8, half), F32)
    early_all, late_all, grad_hidden, g_norm, g_taps_bc = pl.pallas_call(
        functools.partial(tail_kernel, per, nz),
        in_specs=[vmem] * len(operands),
        out_specs=[vmem] * 5,
        out_shape=[
            shape((per, 2, 2 * HEADDIM, half), BF), shape((per, late_rows, half), BF),
            shape((rows, half), BF), shape((1, half)), shape((4, 2 * STATE)),
        ],
        scratch_shapes=[
            pltpu.VMEM((2 * HEADDIM, model), BF),
            pltpu.VMEM((nz, per, HEADDIM, model), BF), pltpu.VMEM((per, share, model), BF),
            pltpu.VMEM((HEADS, model), F32), pltpu.VMEM((nz, HEADDIM, model), BF),
            pltpu.VMEM((share, model), BF), pltpu.VMEM((swap_rows, half), BF),
            pltpu.VMEM((swap_rows, half), BF), pltpu.VMEM((rows, half), F32),
            pltpu.VMEM((rows, half), BF), pltpu.VMEM((rows, half), BF), line16, line16, line16,
            line16, pltpu.VMEM((8, rows), F32), pltpu.VMEM((8, rows), F32), line8, line8,
            pltpu.VMEM((share, model), F32),
            *[pltpu.VMEM((nz, HEADDIM, model), BF)] * (per - 1),
            *[pltpu.VMEM((share, model), BF)] * (per - 1),
            *[pltpu.VMEM((HEADDIM, model), BF)] * (nz - 1),
            *[pltpu.VMEM((share, model), BF)] * (nz - 1), *[line8] * (per - 1),
            *[line8] * (nz - 1), *[pltpu.VMEM((2 * HEADDIM, model), BF)] * (nz - 1),
            pltpu.VMEM((2 * STATE, model), F32),
            pltpu.SemaphoreType.DMA((tail_copies,)), pltpu.SemaphoreType.DMA((tail_copies,)),
        ],
        compiler_params=pltpu.CompilerParams(
            vmem_limit_bytes=VMEM, collective_id=2, has_side_effects=True
        ),
        cost_estimate=cost(60),
        name="tail",
    )(*operands)
    inner = own_heads * HEADDIM
    each_head = jnp.asarray(np.kron(np.eye(own_heads), np.ones((HEADDIM, 1))), F32)
    row_heads = shape((1, own_heads))
    g_zx, g_out, g_bcdt, g_cx, g_gain, g_skip, g_bias, g_rate = pl.pallas_call(
        functools.partial(finish_kernel, per),
        grid=(half // Q,),
        in_specs=[
            pl.BlockSpec((per, 2, 2 * HEADDIM, Q), lambda i: (0, 0, 0, i)),
            pl.BlockSpec((per, late_rows, Q), lambda i: (0, 0, i)),
            pl.BlockSpec((per, late_rows, Q), lambda i: (0, 0, 0)), whole(each_head),
        ],
        out_specs=[
            pl.BlockSpec((Q, own_heads, 2 * HEADDIM), lambda i: (i, 0, 0)),
            pl.BlockSpec((inner, Q), lambda i: (0, i)),
            pl.BlockSpec((2 * STATE + HEADS, Q), lambda i: (0, i)), pl.BlockSpec((4, inner), fix),
            pl.BlockSpec((1, inner), fix), *[pl.BlockSpec((1, own_heads), fix)] * 3,
        ],
        out_shape=[
            shape((half, own_heads, 2 * HEADDIM)), shape((inner, half)),
            shape((2 * STATE + HEADS, half)), shape((4, inner)), shape((1, inner)), row_heads,
            row_heads, row_heads,
        ],
        compiler_params=params(),
        cost_estimate=cost(5),
        name="finish",
    )(early_all, late_all, late_all, each_head)
    return (
        out_hidden,
        grad_hidden,
        g_norm.reshape(-1),
        g_zx,
        jnp.transpose(g_bcdt),
        g_cx,
        g_taps_bc,
        g_bias.reshape(-1),
        g_rate.reshape(-1),
        g_skip.reshape(-1),
        g_gain.reshape(-1),
        g_out,
    )


def fits(mesh):
    ndp, nz, nw = mesh.shape["dp"], mesh.shape["head"], mesh.shape["width"]
    return (
        nw == 2
        and ndp in (2, 4, 8)
        and nz & (nz - 1) == 0
        and HEADS == nz * nw * ndp
        and LEN % (nz * Q) == 0
        and SEQS == ndp
        and HEADS // nw * HEADDIM % Q == 0
        and HEADS // ndp == 8
    )


def solution(mesh):
    placed = (
        P(("dp", "head"), "width"),
        P("dp"),
        P(("dp", "head"), "width"),
        P("width"),
        P("width", "head", None),
        P("width", None),
        P(None, "head"),
        P(),
        P("head"),
        P("head"),
        P("head"),
        P("head"),
        P("head", "width"),
    )
    return jax.shard_map(
        sequence_device if fits(mesh) else per_device,
        mesh=mesh,
        in_specs=placed,
        out_specs=(
            P(("dp", "head"), "width"),
            P(("dp", "head"), "width"),
            P("width"),
            P("width", "head", None),
            P("width", None),
            P(None, "head"),
            P(),
            P("head"),
            P("head"),
            P("head"),
            P("head"),
            P("head", "width"),
        ),
        check_vma=False,
    )
```

```python
import functools

import jax
import jax.numpy as jnp
import numpy as np
from jax import lax
from jax.experimental import pallas as pl
from jax.experimental.pallas import tpu as pltpu
from jax.sharding import PartitionSpec as P

D = 1024
HEADS = 32
HEADDIM = 64
STATE = 128
SCAN_BLOCK = 256
LEN = 4096
INNER = 2048
SEQS = 4


EPS = 1e-05
HIGH = lax.Precision.HIGHEST


def conv_causal(values, kernel):
    taps = kernel.shape[0]
    padded = jnp.pad(values, ((taps - 1, 0), (0, 0)))
    total = jnp.zeros_like(values)
    for offset in range(taps):
        total = total + kernel[offset] * padded[offset : offset + values.shape[0]]
    return total


def block_scan(inputs, steps, rates, bmat, cmat, block):
    length, heads, hsize = inputs.shape
    count = length // block
    in_blocks = inputs.reshape(count, block, heads, hsize)
    step_blocks = steps.reshape(count, block, heads)
    b_blocks = bmat.reshape(count, block, bmat.shape[1])
    c_blocks = cmat.reshape(count, block, cmat.shape[1])
    places = jnp.arange(block)
    lower = (places[:, None] >= places[None, :])[:, :, None]

    def advance(state, pieces):
        x_part, dt_part, b_part, c_part = pieces
        cums = jnp.cumsum(dt_part * rates, axis=0)
        spread = cums[:, None, :] - cums[None, :, :]
        decay = jnp.where(lower, jnp.exp(jnp.where(lower, spread, 0.0)), 0.0)
        scores = jnp.dot(c_part, b_part.T, precision=HIGH)
        weights = scores[:, :, None] * decay * dt_part[None, :, :]
        inside = jnp.einsum("ijh,jhp->ihp", weights, x_part, precision=HIGH)
        carried = (
            jnp.einsum("in,hpn->ihp", c_part, state, precision=HIGH) * jnp.exp(cums)[:, :, None]
        )
        tails = jnp.exp(cums[-1][None, :] - cums) * dt_part
        state = jnp.exp(cums[-1])[:, None, None] * state + jnp.einsum(
            "jh,jhp,jn->hpn", tails, x_part, b_part, precision=HIGH
        )
        return (state, inside + carried)

    start_state = jnp.zeros((heads, hsize, bmat.shape[1]), jnp.float32)
    _, result = lax.scan(
        jax.checkpoint(advance), start_state, (in_blocks, step_blocks, b_blocks, c_blocks)
    )
    return result.reshape(length, heads, hsize)


def mixer(zx, bc_raw, dt_raw, kernel_x, kernel_bc, bias_dt, log_rate, skip):
    length, heads, double = zx.shape
    hsize = double // 2
    gate = zx[:, :, :hsize]
    x_raw = zx[:, :, hsize:].reshape(length, heads * hsize)
    xs_conv = jax.nn.silu(conv_causal(x_raw, kernel_x)).reshape(length, heads, hsize)
    bc_conv = jax.nn.silu(conv_causal(bc_raw, kernel_bc))
    half = bc_conv.shape[1] // 2
    steps = jax.nn.softplus(dt_raw + bias_dt)
    rates = -jnp.exp(log_rate)
    result = (
        block_scan(xs_conv, steps, rates, bc_conv[:, :half], bc_conv[:, half:], SCAN_BLOCK)
        + skip[:, None] * xs_conv
    )
    return (result * jax.nn.silu(gate)).reshape(length, heads * hsize)


def per_device(
    hidden,
    lengths,
    cotangent,
    norm_gain,
    in_zx,
    in_bcdt,
    conv_x,
    conv_bc,
    dt_bias,
    a_log,
    d_skip,
    gnorm_gain,
    out_w,
):
    slice_rows, half_width = hidden.shape
    local_heads = in_zx.shape[1]
    head_count = lax.axis_size("head")
    head_index = lax.axis_index("head")
    total_rows = slice_rows * head_count
    seq_local = lengths.shape[0]
    inner_local = local_heads * HEADDIM
    row_ids = head_index * slice_rows + jnp.arange(slice_rows, dtype=jnp.int32)
    owner = (row_ids // LEN)[:, None] == jnp.arange(seq_local, dtype=jnp.int32)[None, :]
    limits = jnp.sum(jnp.where(owner, lengths[None, :], 0), axis=1)
    keeper = (row_ids % LEN < limits).astype(jnp.float32)[:, None]
    source = hidden.astype(jnp.float32)
    squares = lax.psum(jnp.sum(source * source, axis=1), "width")
    scale = lax.rsqrt(squares / D + EPS)[:, None]
    gain_in = norm_gain.astype(jnp.float32)
    normed = (source * scale * gain_in).astype(jnp.bfloat16)
    gathered = lax.all_gather(normed, "head", axis=0, tiled=True)
    w_zx = in_zx.reshape(half_width, local_heads * 2 * HEADDIM)
    zx_part = jnp.dot(gathered, w_zx, preferred_element_type=jnp.float32)
    bcdt_part = jnp.dot(gathered, in_bcdt, preferred_element_type=jnp.float32)
    zx_full, bcdt_full = lax.psum((zx_part, bcdt_part), "width")
    zx_seq = zx_full.reshape(seq_local, LEN, local_heads, 2 * HEADDIM)
    bc_seq = bcdt_full[:, : 2 * STATE].reshape(seq_local, LEN, 2 * STATE)
    dt_seq = lax.dynamic_slice_in_dim(
        bcdt_full, 2 * STATE + head_index * local_heads, local_heads, 1
    ).reshape(seq_local, LEN, local_heads)

    def local_mix(zx_in, bc_in, dt_in, kernel_x, kernel_bc, bias_in, log_in, skip_in):
        per_sequence = jax.vmap(mixer, in_axes=(0, 0, 0, None, None, None, None, None))
        return per_sequence(
            zx_in, bc_in, dt_in, kernel_x, kernel_bc, bias_in, log_in, skip_in
        ).reshape(total_rows, inner_local)

    gated, mix_pull = jax.vjp(
        local_mix,
        zx_seq,
        bc_seq,
        dt_seq,
        conv_x.astype(jnp.float32),
        conv_bc.astype(jnp.float32),
        dt_bias,
        a_log,
        d_skip,
    )
    total_sq = lax.psum(jnp.sum(gated * gated, axis=1), "head")
    scale_out = lax.rsqrt(total_sq / INNER + EPS)[:, None]
    gain_out = gnorm_gain.astype(jnp.float32)
    mixed = (gated * scale_out * gain_out).astype(jnp.bfloat16)
    picked = mixed
    branch = lax.psum_scatter(
        jnp.dot(picked, out_w, preferred_element_type=jnp.float32),
        "head",
        scatter_dimension=0,
        tiled=True,
    )
    out_hidden = (source + keeper * branch).astype(jnp.bfloat16)
    grad_out = cotangent.astype(jnp.float32)
    masked = (grad_out * keeper).astype(jnp.bfloat16)
    piece = lax.all_gather(masked, "head", axis=0, tiled=True)
    picked = mixed
    acc_weight = jnp.einsum("tc,td->cd", picked, piece, preferred_element_type=jnp.float32)
    product = jnp.einsum("td,cd->tc", piece, out_w, preferred_element_type=jnp.float32)
    grad_mixed = lax.psum(product, "width")
    gain_out_grad = jnp.sum(grad_mixed * gated * scale_out, axis=0)
    inner_total = lax.psum(jnp.sum(grad_mixed * gain_out * gated, axis=1), "head")
    cubed = scale_out * scale_out * scale_out
    grad_gated = scale_out * gain_out * grad_mixed - gated * cubed / INNER * inner_total[:, None]
    (
        grad_zx_seq,
        grad_bc_seq,
        grad_dt_seq,
        kernel_x_grad,
        kernel_bc_grad,
        bias_grad,
        rate_grad,
        skip_grad,
    ) = mix_pull(grad_gated)
    grad_zx = grad_zx_seq.reshape(total_rows, local_heads * 2 * HEADDIM).astype(jnp.bfloat16)
    dt_columns = jnp.zeros((total_rows, HEADS), jnp.float32)
    dt_columns = lax.dynamic_update_slice_in_dim(
        dt_columns, grad_dt_seq.reshape(total_rows, local_heads), head_index * local_heads, 1
    )
    grad_bcdt_head = jnp.concatenate(
        [grad_bc_seq.reshape(total_rows, 2 * STATE), dt_columns], axis=1
    )
    weight_zx = jnp.einsum(
        "td,tc->dc", gathered, grad_zx, preferred_element_type=jnp.float32
    ).reshape(half_width, local_heads, 2 * HEADDIM)
    normed_part = jnp.einsum("tc,dc->td", grad_zx, w_zx, preferred_element_type=jnp.float32)
    grad_normed, bcdt_summed = (
        lax.psum_scatter(normed_part, "head", scatter_dimension=0, tiled=True),
        lax.psum_scatter(grad_bcdt_head, "head", scatter_dimension=0, tiled=True),
    )
    bcdt_low = bcdt_summed.astype(jnp.bfloat16)
    grad_normed = grad_normed + jnp.einsum(
        "tk,dk->td", bcdt_low, in_bcdt, preferred_element_type=jnp.float32
    )
    weight_bcdt = jnp.einsum("td,tk->dk", normed, bcdt_low, preferred_element_type=jnp.float32)
    gain_in_grad = jnp.sum(grad_normed * source * scale, axis=0)
    across = lax.psum(jnp.sum(grad_normed * gain_in * source, axis=1), "width")
    scale_cubed = scale * scale * scale
    grad_hidden = (
        grad_out + scale * gain_in * grad_normed - source * scale_cubed / D * across[:, None]
    ).astype(jnp.bfloat16)
    summed_dp = lax.psum(
        (weight_zx, acc_weight, kernel_x_grad, bias_grad, rate_grad, skip_grad, gain_out_grad), "dp"
    )
    summed_all = lax.psum((weight_bcdt, gain_in_grad, kernel_bc_grad), ("dp", "head"))
    return (
        out_hidden,
        grad_hidden,
        summed_all[1],
        summed_dp[0],
        summed_all[0],
        summed_dp[2],
        summed_all[2],
        summed_dp[3],
        summed_dp[4],
        summed_dp[5],
        summed_dp[6],
        summed_dp[1],
    )


BF = jnp.bfloat16
F32 = jnp.float32
Q = 128
HALO = 16
NEG = -1e30
MESH = pl.DeviceIdType.MESH
VMEM = 60 * 1024 * 1024


def dot(a, b, prec=None):
    return lax.dot_general(a, b, (((1,), (0,)), ((), ())), precision=prec, preferred_element_type=F32)


def dot_t(a, b, prec=None):
    return lax.dot_general(a, b, (((1,), (1,)), ((), ())), precision=prec, preferred_element_type=F32)


def t_dot(a, b, prec=None):
    return lax.dot_general(a, b, (((0,), (0,)), ((), ())), precision=prec, preferred_element_type=F32)


def split2(v, axis=1):
    hi = v.astype(BF)
    lo = (v - hi.astype(F32)).astype(BF)
    return jnp.concatenate([hi, lo], axis=axis)


def dot_split(v, m):
    hi = v.astype(BF)
    lo = (v - hi.astype(F32)).astype(BF)
    return dot(hi, m) + dot(lo, m)


def split_dot(m, v):
    hi = v.astype(BF)
    lo = (v - hi.astype(F32)).astype(BF)
    return dot(m, hi) + dot(m, lo)


def sigmoid(v):
    return 1.0 / (1.0 + jnp.exp(-v))


def tri(kind):
    row = lax.broadcasted_iota(jnp.int32, (Q, Q), 0)
    col = lax.broadcasted_iota(jnp.int32, (Q, Q), 1)
    return {"ge": row >= col, "le": row <= col, "gt": row > col}[kind]


def slot_heads(heads, per):
    nz = heads // per
    own = HEADS // nz
    bits = per.bit_length() - 1
    slot = lax.broadcasted_iota(jnp.int32, (heads, HEADS), 0)
    head = lax.broadcasted_iota(jnp.int32, (heads, HEADS), 1)
    z = (lax.axis_index("head") - (slot >> bits)) & (nz - 1)
    m = (slot & (per - 1)) ^ lax.axis_index("dp")
    return (head == z * own + lax.axis_index("width") * per + m).astype(F32)


def prep_kernel(
    per, zx, ow, bcdt, rows_in,
    first_o, first2_o, rest_o, rest2_o, out_o, out2_o, bcdt_o, table_o,
):
    di = lax.axis_index("dp")
    wi = lax.axis_index("width")
    wide = 2 * HEADDIM
    for m in range(per):
        for w, whole_o, some_o, o_o in (
            (wi, first_o, rest_o, out_o), (1 - wi, first2_o, rest2_o, out2_o)
        ):
            head = w * per + jnp.bitwise_xor(di, m)
            v = jnp.transpose(zx[:, pl.ds(pl.multiple_of(head * wide, wide), wide)])
            for i in range(2):
                part = v[i * HEADDIM : (i + 1) * HEADDIM, :]
                if m == 0:
                    whole_o[i] = part
                else:
                    some_o[i, (m - 1) * HEADDIM : m * HEADDIM, :] = part
            o_o[m * HEADDIM : (m + 1) * HEADDIM, :] = ow[
                pl.ds(pl.multiple_of(head * HEADDIM, HEADDIM), HEADDIM), :
            ]
    n = bcdt.shape[0]
    bcdt_o[0:n, :] = bcdt[...]
    bcdt_o[n:, :] = jnp.broadcast_to(rows_in[8:9, :], (HALO, bcdt.shape[1])).astype(BF)
    rows = rows_in[0:8, :]
    half = rows.shape[1] // 2
    rows = jnp.where(wi == 0, rows[:, :half], rows[:, half:])
    step = 1
    while step < per:
        size = HEADDIM * step
        parts = [rows[:, i * size : (i + 1) * size] for i in range(half // size)]
        swapped = jnp.concatenate([parts[i ^ 1] for i in range(len(parts))], axis=1)
        rows = jnp.where(jnp.bitwise_and(di, step) != 0, swapped, rows)
        step *= 2
    table_o[...] = rows


def entry_first(per, hm, ho, hh, bcdt, table, sel, o, xn_o, buf, between, edges):
    xnh_o, r_o, raw_o, rawh_o, dt_o, sig_o = o.xnh, o.r, o.raw, o.rawh, o.dt, o.sig
    cl_o, clt_o, rate_o, wdt_o, b_o = o.cl, o.clt, o.rate, o.wdt, o.b
    rows = hm.shape[0]
    state = b_o.shape[1]
    per_head = dot(table[...], sel[...], HIGH)
    bias = per_head[5:6, :]
    rate = -jnp.exp(per_head[6:7, :])
    rate_o[...] = rate
    wbc = bcdt.at[0 : 2 * state, :]
    wdt_o[...] = dot(
        slot_heads(rate.shape[1], per).astype(BF), bcdt[2 * state : 2 * state + HEADS, :]
    ).astype(BF)
    wdt = wdt_o
    gain = bcdt[2 * state + HEADS : 2 * state + HEADS + 1, :].astype(F32)
    blocks = rows // Q
    lower = tri("ge").astype(F32)

    def norm(left, right):
        h = jnp.concatenate([left, right], axis=1).astype(F32)
        r = lax.rsqrt(jnp.mean(h * h, axis=1, keepdims=True) + EPS)
        return (h * r * gain).astype(BF), r

    def first(i, carry):
        here = pl.ds(pl.multiple_of(i * Q, Q), Q)
        xn, r = norm(hm[here, :], ho[here, :])
        xn_o[here, :] = xn
        r_o[here, :] = r
        raw = dot_t(xn, wbc[...])
        raw_o[here, :] = raw
        buf[pl.ds(pl.multiple_of(HALO + i * Q, HALO), Q), :] = raw
        steps = dot_t(xn, wdt[...]) + bias
        dt = jax.nn.softplus(steps)
        dt_o[here, :] = dt
        sig_o[here, :] = sigmoid(steps)
        da = dt * rate
        cl_o[here, :] = dot(lower, da, HIGH)
        clt_o[:, here] = lax.dot_general(
            da, lower, (((0,), (1,)), ((), ())), precision=HIGH, preferred_element_type=F32
        )
        return carry

    lax.fori_loop(0, blocks // 2, first, 0, unroll=2)
    between()
    lax.fori_loop(blocks // 2, blocks, first, 0, unroll=2)
    edges()
    half = hm.shape[1]
    xnh, _ = norm(hh[:, :half], hh[:, half:])
    xnh = jnp.where(lax.axis_index("head") > 0, xnh.astype(F32), 0.0).astype(BF)
    xnh_o[...] = xnh
    buf[0:HALO, :] = dot_t(xnh, wbc[...])
    rawh_o[...] = buf[0:HALO, :]


def entry_second(cbc, o, tot_o, buf):
    u_o, b_o, c_o, dt_o, cl_o, clt_o = o.ubc, o.b, o.c, o.dt, o.cl, o.clt
    dt2_o, e12_o, tl2_o, dttl2_o, ec2_o, edt2_o = o.dt2, o.e12, o.tl2, o.dttl2, o.ec2, o.edt2
    state = b_o.shape[1]
    blocks = b_o.shape[0] // Q

    def second(i, carry):
        here = pl.ds(pl.multiple_of(i * Q, Q), Q)
        win = buf[pl.ds(pl.multiple_of(i * Q, Q), Q + HALO), :]
        u = jnp.zeros((Q, win.shape[1]), F32)
        for k in range(4):
            u = u + cbc[k : k + 1, :] * win[HALO - 3 + k : HALO - 3 + k + Q, :]
        u_o[here, :] = u
        v = u * sigmoid(u)
        b_o[here, :] = v[:, :state].astype(BF)
        c_o[here, :] = v[:, state:].astype(BF)
        return carry

    lax.fori_loop(0, blocks, second, 0, unroll=2)
    tots = [cl_o[i * Q + Q - 1 : i * Q + Q, :] for i in range(blocks)]
    ctot = functools.reduce(lambda x, y: x + y, tots)
    heads = clt_o.shape[0]
    column = functools.reduce(
        lambda x, y: x + y, [clt_o[:, i * Q + Q - 1 : i * Q + Q] for i in range(blocks)]
    )
    hi = column.astype(BF)
    mid = (column - hi.astype(F32)).astype(BF)
    low = (column - hi.astype(F32) - mid.astype(F32)).astype(BF)
    lane = lax.broadcasted_iota(jnp.int32, (heads, tot_o.shape[1]), 1)
    tot_o[...] = jnp.where(
        lane == 0,
        hi.astype(F32),
        jnp.where(lane == 1, mid.astype(F32), jnp.where(lane == 2, low.astype(F32), 0.0)),
    ).astype(BF)
    off = jnp.zeros_like(ctot)
    for i in range(blocks):
        here = slice(i * Q, i * Q + Q)
        cl = cl_o[here, :]
        dt = dt_o[here, :]
        tail = jnp.exp(tots[i] - cl)
        dt2_o[here, :] = split2(dt)
        e12_o[here, :] = split2(jnp.exp(cl))
        tl2_o[here, :] = split2(tail)
        dttl2_o[here, :] = split2(dt * tail)
        ec2_o[here, :] = split2(jnp.exp(cl + off))
        edt2_o[here, :] = split2(dt * jnp.exp(ctot - cl - off))
        off = off + tots[i]


def decay(cl, clt, h, mask):
    return jnp.exp(jnp.where(mask, cl[:, h : h + 1] - clt[h : h + 1, :], NEG))


def lane_masks():
    lane = lax.broadcasted_iota(jnp.int32, (1, Q), 1)
    low = (lane < HEADDIM).astype(F32)
    return low.astype(BF), (1.0 - low).astype(BF)


def project(s, per, xn, o, w, cw, ex, z_o, xr_o, xrh_o, u_o, xdt_o, msg, buf, acc):
    rows = z_o.shape[0]
    gc = per * HEADDIM
    cols = slice(s * gc, s * gc + gc)
    xh = dot_t(o.xnh[...], w[1, cols, :])
    buf[0:HALO, :] = xh
    xrh_o[...] = xh
    acc[...] = jnp.zeros_like(acc)
    cut = rows // 2 if rows // 2 % Q == 0 else rows

    def part(j, carry):
        base = j * cut
        here = pl.ds(pl.multiple_of(base, Q), cut)
        buf[pl.ds(pl.multiple_of(base + HALO, HALO), cut), :] = dot_t(xn[here, :], w[1, cols, :])
        z_o[here, :] = dot_t(xn[here, :], w[0, cols, :])
        for i in range(cut // Q):
            here = pl.ds(pl.multiple_of(base + i * Q, Q), Q)
            win = buf[pl.ds(pl.multiple_of(base + i * Q, Q), Q + HALO), :]
            u = jnp.zeros((Q, gc), F32)
            for k in range(4):
                u = u + cw[k : k + 1, cols] * win[HALO - 3 + k : HALO - 3 + k + Q, :]
            xr_o[here, :] = win[HALO:, :].astype(BF)
            u_o[here, :] = u
            xs = u * sigmoid(u)
            xdt_o[here, :] = (xs * dot(o.dt2[here, :], ex[:, cols])).astype(BF)
            acc[...] += t_dot((xs * dot(o.edt2[here, :], ex[:, cols])).astype(BF), o.b[here, :])
        return carry

    lax.fori_loop(0, rows // cut, part, 0)
    msg[cols, :] = acc[...].astype(BF)


def inside(s, per, xdt, o, y_o):
    mask = tri("ge")
    low, high = lane_masks()
    rows = xdt.shape[0]
    some = 4 if rows % (4 * Q) == 0 else 1

    def part(j, carry):
        for i in range(some):
            here = pl.ds(pl.multiple_of((j * some + i) * Q, Q), Q)
            g = dot_t(o.c[here, :], o.b[here, :])
            clv, cltv = o.cl[here, :], o.clt[:, here]
            for p in range(xdt.shape[1] // Q):
                lanes = slice(p * Q, p * Q + Q)
                h = s * per + 2 * p
                ws = [(g * decay(clv, cltv, k, mask)).astype(BF) for k in (h, h + 1)]
                x = xdt[here, lanes]
                y_o[here, lanes] = dot(
                    jnp.concatenate(ws, axis=1), jnp.concatenate([x * low, x * high], axis=0)
                ).astype(BF)
        return carry

    lax.fori_loop(0, rows // (some * Q), part, 0)


class Named:
    def __init__(self, names, refs):
        for name, ref in zip(names, refs):
            setattr(self, name, ref)


KEPT = (
    "xnh", "r", "raw", "rawh", "ubc", "b", "c", "dt", "sig", "cl", "clt", "dt2", "e12", "tl2",
    "dttl2", "ec2", "edt2", "rate", "wdt", "tot", "table", "bcdt",
)


def front_kernel(per, nz, *refs):
    hidden, first, first2, rest, rest2, bcdt, table, cbc, sel, ex, refs = take(refs, *[0] * 10)
    out_mine, out2, cot, refs = take(refs, 0, 0, 0)
    w_o, wo_o, cot_o, xn_o, refs = take(refs, 0, 0, 0, 0)
    z_o, xr_o, u_o, xdt_o, y_o, messages_o, xrh_o, refs = take(refs, *[nz] * 5, nz - 1, nz)
    kept, refs = refs[: len(KEPT)], refs[len(KEPT) :]
    o = Named(KEPT, kept)
    z_v, xr_v, u_v, xdt_v, y_v, refs = take(refs, *[nz] * 5)
    w, ho, eh, xn, msg, buf, bcbuf, acc, sends, receives, locals_ = refs
    bc = o.bcdt
    rows, half = hidden.shape
    gc = per * HEADDIM
    top = nz * gc
    sibling = {"width": 1 - lax.axis_index("width")}
    z_peers = line_peers(nz, 1)
    d_peers = plane_peers(per)
    used = [0]

    def copy(source, target, peer):
        i = used[0]
        used[0] += 1
        return remote(source, target, sends, receives, i, peer)

    left, right = pl.ds(0, half), pl.ds(half, half)
    swap_first = copy(first2, w.at[:, pl.ds(0, HEADDIM), right], sibling)
    swap_rest = copy(rest2, w.at[:, pl.ds(HEADDIM, gc - HEADDIM), right], sibling)
    swap_hidden = copy(hidden, ho, sibling)
    swap_bc = copy(bcdt, bc.at[:, right], sibling)
    swap_out = copy(out2, wo_o.at[pl.ds(0, gc), right], sibling)
    swap_cot = copy(cot, cot_o, sibling)
    z_table, z_w, z_out, z_state, z_state2 = [], [], [], [], []
    for k, peer in enumerate(z_peers):
        s = k + 1
        z_table.append(copy(table, o.table.at[:, pl.ds(s * gc, gc)], peer))
        own = w.at[:, pl.ds(0, HEADDIM), :]
        z_w.append(copy(own, w.at[:, pl.ds(s * gc, HEADDIM), :], peer))
        z_out.append(
            copy(wo_o.at[pl.ds(0, HEADDIM), :], wo_o.at[pl.ds(s * gc, HEADDIM), :], peer)
        )
        most = pl.ds(0, top - gc)
        z_state.append(copy(msg.at[most, :], messages_o[k].at[most, :], peer))
        more = pl.ds(top - gc, gc + HALO)
        z_state2.append(copy(msg.at[more, :], messages_o[k].at[more, :], peer))
    last = pl.ds(rows - HALO, HALO)
    edge1 = copy(hidden.at[last, :], eh.at[:, left], z_peers[0])
    edge2 = copy(ho.at[last, :], eh.at[:, right], z_peers[0])
    p_w = {s: [] for s in range(1, nz)}
    p_out = {s: [] for s in range(1, nz)}
    for s in range(1, nz):
        for k, peer in enumerate(d_peers):
            mine = pl.ds(s * gc, HEADDIM)
            there = pl.ds(s * gc + (k + 1) * HEADDIM, HEADDIM)
            via, to = k, peer
            if k + 1 == per - 1:
                first_hop = s % 2
                mine = pl.ds(s * gc + (first_hop + 1) * HEADDIM, HEADDIM)
                to = d_peers[1 - first_hop]
            p_w[s].append(copy(w.at[:, mine, :], w.at[:, there, :], to))
            p_out[s].append(copy(wo_o.at[mine, :], wo_o.at[there, :], to))

    places = [0]

    def local(source, target):
        i = places[0]
        places[0] += 1
        found = pltpu.make_async_copy(source, target, locals_.at[i])
        found.start()
        return found

    ready = [
        local(first, w.at[:, pl.ds(0, HEADDIM), left]),
        local(rest, w.at[:, pl.ds(HEADDIM, gc - HEADDIM), left]),
        local(bcdt, bc.at[:, left]),
        local(table, o.table.at[:, pl.ds(0, gc)]),
        local(out_mine, wo_o.at[pl.ds(0, gc), left]),
    ]
    meet([sibling, *z_peers, *line_peers(nz, -1), *d_peers])
    start([swap_first, *z_table, swap_hidden, swap_bc, edge1])
    ready[0].wait()
    arrive([swap_first])
    start([z_w[0], swap_rest, swap_out, swap_cot])
    for c in ready[1:]:
        c.wait()
    arrive([swap_hidden])
    start([edge2])
    arrive([swap_bc, *z_table])
    pending = []

    def pass_on(copies, s):
        arrive([copies[s % 2]])
        start([copies[2]])

    def between():
        arrive([z_w[0]])
        start([*p_w[1][:2], *z_w[1:]])

    def edges():
        arrive([edge1, edge2])

    entry_first(per, hidden, ho, eh, bc, o.table, sel, o, xn, bcbuf, between, edges)
    pass_on(p_w[1], 1)
    arrive([z_w[1], swap_rest])
    start(p_w[2][:2])
    entry_second(cbc, o, o.tot, bcbuf)
    msg[top:, :] = o.tot[...]
    pending.append(local(xn, xn_o))
    for k in range(3, nz):
        arrive([z_w[k - 1]])
        start(p_w[k][:2])
    arrive([swap_out])
    start(z_out)
    taps = o.table

    def project_group(s):
        project(
            s, per, xn, o, w, taps, ex, z_v[s], xr_v[s], xrh_o[s], u_v[s], xdt_v[s], msg, buf, acc
        )
        for a, b in ((z_v, z_o), (xr_v, xr_o), (u_v, u_o), (xdt_v, xdt_o)):
            pending.append(local(a[s], b[s]))

    def inside_group(s):
        inside(s, per, xdt_v[s], o, y_v[s])
        pending.append(local(y_v[s], y_o[s]))

    project_group(0)
    for k in range(2, nz):
        pass_on(p_w[k], k)
    inside_group(0)
    for k in range(1, nz):
        arrive([z_out[k - 1]])
        start(p_out[k][:2])
    for s in range(1, nz):
        arrive([p_w[s][1 - s % 2], p_w[s][2]])
        project_group(s)
        if s == nz - 2:
            start(z_state)
            for k in range(1, nz):
                pass_on(p_out[k], k)
    start(z_state2)
    pending.append(local(w, w_o))
    for s in range(1, nz):
        inside_group(s)
    everything = [swap_first, swap_rest, swap_hidden, swap_bc, swap_out, swap_cot, edge1, edge2]
    everything += [*z_table, *z_w, *z_out, *z_state, *z_state2]
    for s in range(1, nz):
        everything += p_w[s] + p_out[s]
        arrive([p_out[s][1 - s % 2], p_out[s][2]])
    arrive([swap_cot, *z_state, *z_state2])
    for c in everything:
        c.wait_send()
    for c in pending:
        c.wait()


def head_scale(clt, first, per, state):
    return jnp.concatenate(
        [
            jnp.broadcast_to(jnp.exp(clt[h : h + 1, Q - 1 : Q]), (HEADDIM, state))
            for h in range(first, first + per)
        ],
        axis=0,
    )


def from_messages(messages, sign, groups, per, state, store, valid=None):
    nz = len(messages) + 1
    gc = per * HEADDIM
    top = nz * gc
    totals = [
        sum(m[top:, i : i + 1].astype(F32) for i in range(3)) for m in messages
    ]
    for at, j in enumerate(groups):
        total = jnp.zeros((gc, state), F32)
        faded = jnp.zeros((per, 1), F32)
        for k in range(1, nz):
            there = (j - sign * k) % nz
            scale = jnp.exp(faded)
            scale = jnp.concatenate(
                [jnp.broadcast_to(scale[h : h + 1, :], (HEADDIM, state)) for h in range(per)],
                axis=0,
            )
            part = scale * messages[k - 1][there * gc : there * gc + gc, :].astype(F32)
            if valid is not None:
                part = jnp.where(valid(k), part, 0.0)
            total = total + part
            faded = faded + totals[k - 1][there * per : there * per + per, :]
        store[at * gc : at * gc + gc, :] = total


def mid_kernel(groups, per, *refs):
    nz = len(groups)
    y_in, u, z, cot, cot2, b, c, clt, e12, dttl2, refs = take(refs, nz, nz, nz, *[0] * 7)
    u2, z2, ec2, c2, hidden, refs = take(refs, nz, nz, 0, 0, 0)
    messages, tot, table, ex, wout, limit, refs = take(refs, nz - 1, *[0] * 5)
    gain, dsk = table.at[4:5, :], table.at[7:8, :]
    st_o, mask_o, dys_o, dz_o, yn_o, out_o, msg_o, gn_o, sk_o, refs = take(
        refs, nz, 0, nz, *[0] * 6
    )
    s, acc, yv, dv, br, br_out, br_in, sm_out, sm_in, gg, sends, receives = refs
    step = pl.program_id(0)
    tiles = pl.num_programs(0) - 1
    rows, half = cot.shape
    gc = per * HEADDIM
    state = s.shape[1]
    sibling = {"width": 1 - lax.axis_index("width")}

    def copies(k):
        return [
            remote(sm_out.at[k], sm_in.at[k], sends, receives, 2 * k, sibling),
            remote(br_out.at[k], br_in.at[k], sends, receives, 2 * k + 1, sibling),
        ]

    @pl.when(step == 0)
    def _():
        meet([sibling])
        z_index = lax.axis_index("head")
        from_messages(messages, 1, groups, per, state, s, lambda k: z_index - k >= 0)
        acc[...] = jnp.zeros_like(acc)
        gn_o[...] = jnp.zeros_like(gn_o)
        sk_o[...] = jnp.zeros_like(sk_o)

    @pl.when(step < tiles)
    def _():
        slot = lax.rem(step, 2)
        row = lax.broadcasted_iota(jnp.int32, (rows, 1), 0) + step * rows
        keep = row < limit[0, 0]
        for i, v in enumerate((cot, cot2)):
            mask_o[:, i * half : i * half + half] = jnp.where(keep, v[...].astype(F32), 0.0).astype(
                BF
            )
        dv[slot] = dot_t(mask_o[...], wout[...])
        lane = lax.broadcasted_iota(jnp.int32, (Q, Q), 1)
        for i in range(rows // Q):
            part = slice(i * Q, i * Q + Q)
            cc, bb = c[part, :], b[part, :]
            square = jnp.zeros((Q, gc), F32)
            inner = jnp.zeros((Q, gc), F32)
            for j in groups:
                here = slice(j * gc, j * gc + gc)
                sv = s[here, :]
                sb = sv.astype(BF)
                st_o[j][i] = sb
                x = u[j][part, :]
                x = x * sigmoid(x)
                e1 = dot(e12[part, :], ex[:, here])
                y = y_in[j][part, :].astype(F32) + e1 * dot_t(cc, sb) + dsk[:, here] * x
                yv[slot, part, here] = y
                xt = (x * dot(dttl2[part, :], ex[:, here])).astype(BF)
                s[here, :] = head_scale(clt.at[:, part], j * per, per, state) * sv + t_dot(xt, bb)
                zz = z[j][part, :]
                gz = y * (zz * sigmoid(zz))
                g = gz * gain[:, here]
                gg[part, here] = g.astype(BF)
                square = square + gz * gz
                inner = inner + g * dv[slot, part, here]
            sm_out[step, part, :] = jnp.where(
                lane == 0,
                jnp.sum(square, axis=1, keepdims=True),
                jnp.sum(inner, axis=1, keepdims=True),
            )
        branch = dot(gg[...], wout[...])
        br[slot] = branch[:, :half]
        br_out[step] = branch[:, half:].astype(BF)
        for copy in copies(step):
            copy.start()

    @pl.when(step > 0)
    def _():
        k = step - 1
        slot = lax.rem(k, 2)
        for copy in copies(k):
            copy.wait()
        count = nz * gc * 2
        for i in range(rows // Q):
            part = slice(i * Q, i * Q + Q)
            both = sm_out[k, part, :] + sm_in[k, part, :]
            r2 = lax.rsqrt(both[:, 0:1] / count + EPS)
            pull = both[:, 1:2] * (r2 * r2 * r2) / count
            row = lax.broadcasted_iota(jnp.int32, (Q, 1), 0) + k * rows + i * Q
            keep = jnp.where(row < limit[0, 0], r2, 0.0)
            out_o[part, :] = (
                hidden[part, :].astype(F32)
                + keep * (br[slot, part, :] + br_in[k, part, :].astype(F32))
            ).astype(BF)
            for j in groups:
                here = slice(j * gc, j * gc + gc)
                gn = gain[:, here]
                zz = z2[j][part, :]
                sz = sigmoid(zz)
                silu = zz * sz
                y = yv[slot, part, here]
                gz = y * silu
                dy_n = dv[slot, part, here]
                gr = gz * r2
                yn_o[part, here] = (gr * gn).astype(BF)
                gn_o[:, here] += jnp.sum(dy_n * gr, axis=0, keepdims=True)
                dgz = r2 * gn * dy_n - gz * pull
                dys = dgz * silu
                dys_o[j][part, :] = dys.astype(BF)
                dz_o[part, here] = (dgz * y * (sz + silu * (1.0 - sz))).astype(BF)
                x = u2[j][part, :]
                x = x * sigmoid(x)
                sk_o[:, here] += jnp.sum(dys * x, axis=0, keepdims=True)
                acc[here, :] += t_dot(
                    (dys * dot(ec2[part, :], ex[:, here])).astype(BF), c2[part, :]
                )

    @pl.when(step == tiles)
    def _():
        top = nz * gc
        msg_o[0:top, :] = acc[...].astype(BF)
        msg_o[top:, :] = tot[...]


def line_peers(count, sign):
    z = lax.axis_index("head")
    return [{"head": lax.rem(z + sign * k + count, count)} for k in range(1, count)]


def plane_peers(count):
    d = lax.axis_index("dp")
    return [{"dp": jnp.bitwise_xor(d, m)} for m in range(1, count)]


def meet(peers):
    barrier = pltpu.get_barrier_semaphore()
    for peer in peers:
        pl.semaphore_signal(barrier, inc=1, device_id=peer, device_id_type=MESH)
    pl.semaphore_wait(barrier, len(peers))


def remote(source, target, sends, receives, i, peer):
    return pltpu.make_async_remote_copy(
        src_ref=source,
        dst_ref=target,
        send_sem=sends.at[i],
        recv_sem=receives.at[i],
        device_id=peer,
        device_id_type=MESH,
    )


def conv_back(d, nxt, taps, raw, grad_o, out_o):
    win = jnp.concatenate([d, nxt[...]], axis=0)
    back = jnp.zeros_like(d)
    sums = []
    for k in range(4):
        part = win[3 - k : 3 - k + Q, :]
        back = back + taps[k : k + 1, :] * part
        sums.append(jnp.sum(raw * part, axis=0, keepdims=True))
    grad_o[...] += jnp.concatenate(sums, axis=0)
    out_o[...] = back.astype(BF)
    nxt[...] = d[0:8, :]


def conv_edge(first, taps, rawh, grad_o, outh_o):
    first = first[...]
    win = jnp.concatenate([jnp.zeros((HALO, first.shape[1]), F32), first], axis=0)
    back = jnp.zeros((HALO, first.shape[1]), F32)
    sums = []
    for k in range(4):
        part = win[3 - k : 3 - k + HALO, :]
        back = back + taps[k : k + 1, :] * part
        sums.append(jnp.sum(rawh[...] * part, axis=0, keepdims=True))
    grad_o[...] += jnp.concatenate(sums, axis=0)
    outh_o[...] = back.astype(BF)


def scan_back_kernel(groups, per, *refs):
    n = len(groups)
    nz = n
    xdt, dys, u, xr, st, xrh, rest = take(refs, n, n, n, n, n, n)
    (b, c, cl, clt, dt, sig, dt2, e12, tl2), rest = rest[:9], rest[9:]
    (ubc, braw, brawh, table, cbc, rate, ex, er), rest = rest[:8], rest[8:]
    cw, dsk = table.at[0:4, :], table.at[7:8, :]
    message, yn, masked, dz, xn, rest = take(rest, *[0] * 5)
    dx_o, dxh_o, gcx_o, rest = take(rest, n, n, n)
    dt_o, ga_o, gbias_o, bc_o, bch_o, gcb_o, etot = rest[:7]
    messages, got, line, rest = take(rest[7:], nz - 1, per - 1, nz - 1)
    du_next, rest = take(rest, n)
    db_next, early, low, dxi, dbi, dci, dai, kt, ds, vs, sends, receives = rest
    turn = pl.program_id(0)
    step = turn - nz
    blocks = (pl.num_programs(0) - nz) // 2
    heads = dt.shape[1]
    state = b.shape[1]
    gc = per * HEADDIM
    line_at, plane_at = 0, nz - 1
    back_at = plane_at + nz * (per - 1)

    def state_copies():
        return [
            remote(message, messages[i], sends, receives, line_at + i, peer)
            for i, peer in enumerate(line_peers(nz, -1))
        ]

    def plane_copies(s):
        return [
            remote(
                early.at[i + 1, s], got[i].at[s], sends, receives, plane_at + s * (per - 1) + i, peer
            )
            for i, peer in enumerate(plane_peers(per))
        ]

    def line_copy(s):
        return remote(
            low.at[s], line[s - 1], sends, receives, back_at + s - 1, line_peers(nz, -1)[s - 1]
        )

    order = [*range(1, nz), 0]
    leave = [0, nz + blocks // 4, nz + blocks - 1, nz + blocks + blocks // 4]
    added = [nz + blocks // 2, nz + blocks, nz + blocks + 3 * blocks // 8, nz + 2 * blocks - 1]

    @pl.when(turn == 0)
    def _():
        meet([*line_peers(nz, -1), *line_peers(nz, 1), *plane_peers(per)])
        for copy in state_copies():
            copy.start()

    @pl.when(turn < nz)
    def _():
        s = lax.rem(turn + 1, nz)
        g = t_dot(yn[...], masked[...]).astype(BF)
        for m in range(per):
            early[m, s, :HEADDIM, :] = g[m * HEADDIM : (m + 1) * HEADDIM, :]
        g = t_dot(dz[...], xn[...]).astype(BF)
        for m in range(per):
            early[m, s, HEADDIM:, :] = g[m * HEADDIM : (m + 1) * HEADDIM, :]

    for s, when in zip(order, leave):

        @pl.when(turn == when)
        def _(s=s):
            for copy in plane_copies(s):
                copy.start()

    @pl.when(jnp.logical_and(step >= 0, step < blocks))
    def _():
        rows = pl.ds(pl.multiple_of(step * Q, Q), Q)
        mask = tri("ge")
        lower, upper_lanes = lane_masks()
        g = dot_t(c[...], b[...])
        clv, cltv = cl[...], clt[...]
        lane = lax.broadcasted_iota(jnp.int32, (Q, heads), 1)
        dg = jnp.zeros((Q, Q), F32)
        rsum = jnp.zeros((Q, heads), F32)
        for s in groups:
            for p in range(per // 2):
                here = slice(p * Q, p * Q + Q)
                x = xdt[s][:, here]
                dy = dys[s][:, here]
                pp = dot_t(dy, jnp.concatenate([x * lower, x * upper_lanes], axis=0))
                ws = []
                for j in range(2):
                    h = s * per + 2 * p + j
                    ell = decay(clv, cltv, h, mask)
                    ws.append((g * ell).astype(BF))
                    pe = pp[:, j * Q : j * Q + Q] * ell
                    dg = dg + pe
                    m = pe * g
                    rsum = jnp.where(lane == h, jnp.sum(m, axis=1, keepdims=True), rsum)
                    kt[h : h + 1, :] = jnp.sum(m, axis=0, keepdims=True)
                dxi[rows, s * gc + p * Q : s * gc + p * Q + Q] = t_dot(
                    jnp.concatenate(ws, axis=0),
                    jnp.concatenate([dy * lower, dy * upper_lanes], axis=0),
                )
        dgb = dg.astype(BF)
        dci[rows, :] = dot(dgb, b[...])
        dbi[rows, :] = t_dot(dgb, c[...])
        upper = tri("le").astype(F32)
        dai[rows, :] = dot(upper, rsum, HIGH) - dot_t(upper, kt[...], HIGH)

    @pl.when(step == blocks)
    def _():
        for copy in state_copies():
            copy.wait()
        z = lax.axis_index("head")
        from_messages(messages, -1, groups, per, state, ds, lambda k: z + k < nz)
        for i in range(n):
            du_next[i][...] = jnp.zeros_like(du_next[i])
            gcx_o[i][...] = jnp.zeros_like(gcx_o[i])
        db_next[...] = jnp.zeros_like(db_next)
        gcb_o[...] = jnp.zeros_like(gcb_o)
        ga_o[...] = jnp.zeros_like(ga_o)
        gbias_o[...] = jnp.zeros_like(gbias_o)

    @pl.when(step >= blocks)
    def _():
        rows = pl.ds(pl.multiple_of((2 * blocks - 1 - step) * Q, Q), Q)
        rsum = jnp.zeros((Q, heads), F32)
        gsum = jnp.zeros((Q, heads), F32)
        ddt = jnp.zeros((Q, heads), F32)
        dbs = dbi[rows, :]
        dcs = dci[rows, :]
        for s in groups:
            here = slice(s * gc, s * gc + gc)
            ehere = er[here, :]
            sb = st[s][0]
            dsv = ds[here, :]
            dsb = dsv.astype(BF)
            dy = dys[s][...].astype(F32)
            dye = dy * dot(e12[...], ex[:, here])
            dyb = dye.astype(BF)
            rsum = rsum + dot((dye * dot_t(c[...], sb)).astype(BF), ehere)
            dcs = dcs + dot(dyb, sb)
            bds = dot_t(b[...], dsb)
            tail = dot(tl2[...], ex[:, here])
            dtx = dot(dt2[...], ex[:, here])
            uu = u[s][...]
            su = sigmoid(uu)
            xs = uu * su
            xt = xs * dtx * tail
            gsum = gsum + dot((xt * bds).astype(BF), ehere)
            dbs = dbs + dot(xt.astype(BF), dsb)
            dxdt = dxi[rows, here] + tail * bds
            ddt = ddt + dot((dxdt * xs).astype(BF), ehere)
            eds = head_scale(clt, s * per, per, state) * dsv
            ev = eds * sb.astype(F32)
            for j in range(per):
                h = s * per + j
                vs[h : h + 1, :] = jnp.sum(
                    ev[j * HEADDIM : (j + 1) * HEADDIM, :], axis=0, keepdims=True
                )
            ds[here, :] = eds + t_dot(dyb, c[...])
            du = (dxdt * dtx + dsk[:, here] * dy) * (su + xs * (1.0 - su))
            conv_back(
                du, du_next[s], cw.at[:, here], xr[s][...].astype(F32), gcx_o[s], dx_o[s]
            )
        vrow = dot_t(jnp.ones((8, state), F32), vs[...], HIGH)
        da = (
            dai[rows, :]
            + split_dot(tri("le").astype(BF), rsum)
            + split_dot(tri("gt").astype(BF), gsum)
            + vrow[0:1, :]
        )
        draw = (rate[...] * da + ddt) * sig[...]
        dt_o[...] = draw.astype(BF)
        ga_o[...] += jnp.sum(da * dt[...], axis=0, keepdims=True)
        gbias_o[...] += jnp.sum(draw, axis=0, keepdims=True)
        d = jnp.concatenate([dbs, dcs], axis=1)
        v = ubc[...]
        sv = sigmoid(v)
        conv_back(d * (sv + v * sv * (1.0 - sv)), db_next, cbc, braw[...], gcb_o, bc_o)

    @pl.when(step == 2 * blocks - 1)
    def _():
        for s in groups:
            here = slice(s * gc, s * gc + gc)
            conv_edge(du_next[s], cw.at[:, here], xrh[s], gcx_o[s], dxh_o[s])
        conv_edge(db_next, cbc, brawh, gcb_o, bch_o)

    def add(s):
        for copy in plane_copies(s):
            copy.wait()

        def piece(i, carry):
            part = pl.ds(pl.multiple_of(i * HALO, HALO), HALO)
            total = early[0, s, part, :].astype(F32)
            for v in got:
                total = total + v[s, part, :].astype(F32)
            low[s, part, :] = total.astype(BF)
            return carry

        lax.fori_loop(0, low.shape[1] // HALO, piece, 0, unroll=2)

    for s, when in zip(order, added):

        @pl.when(turn == when)
        def _(s=s):
            add(s)
            if s > 0:
                line_copy(s).start()

    @pl.when(step == 2 * blocks - 1)
    def _():
        for s in range(1, nz):
            line_copy(s).wait()
        for i in range(low.shape[1] // HALO):
            part = slice(i * HALO, i * HALO + HALO)
            total = low[0, part, :].astype(F32)
            for v in line:
                total = total + v[part, :].astype(F32)
            etot[part, :] = total.astype(BF)


class Copies:
    def __init__(self, sends, receives):
        self.sends, self.receives, self.all = sends, receives, []

    def __call__(self, source, target, peer):
        copy = remote(source, target, self.sends, self.receives, len(self.all), peer)
        self.all.append(copy)
        return copy


def start(copies):
    for c in copies:
        c.start()


def arrive(copies):
    for c in copies:
        c.wait_recv()


def tail_kernel(per, nz, *refs):
    dx, dxh, taps, refs = take(refs, nz, nz, nz)
    (dz, dbc, dbch, dti, xn, xnh, w, bc, wdt, early, hidden, cot, r), refs = refs[:13], refs[13:]
    (gain, gbc, grate, gbias, gskip, ggain, rate, ex), refs = refs[:8], refs[8:]
    ea, la, hid_o, norm_o, tbc_o, refs = take(refs, *[0] * 5)
    gx, gs, gdt, lx, ls, sw_out, sw_in, dxn, dxn_out, dxn_in, refs = take(refs, *[0] * 10)
    edge_out, edge_in, edge_sum, edge_next, across, across_in, nrm, nrm2, sums, refs = take(
        refs, *[0] * 9
    )
    rx, rs, zx, zs, nr, nz_r, refs = take(refs, per - 1, per - 1, nz - 1, nz - 1, per - 1, nz - 1)
    stage, sends, receives = refs
    copy = Copies(sends, receives)
    rows, half = hidden.shape
    gc = per * HEADDIM
    channels = nz * gc
    state2 = dbc.shape[1]
    quarter = state2 // per
    share = quarter + HALO
    some_dt = HEADS // per
    wi, di, zi = lax.axis_index("width"), lax.axis_index("dp"), lax.axis_index("head")
    sibling = {"width": 1 - wi}
    d_peers, z_back = plane_peers(per), line_peers(nz, -1)
    left, right = pl.ds(0, half), pl.ds(half, half)
    block = rows // nz

    early_swap = copy(early.at[:, right], ea.at[0, wi], sibling)
    late_swap = copy(sw_out, sw_in, sibling)
    dxn_swap = [
        copy(dxn_out.at[pl.ds(i * block, block), :], dxn_in.at[pl.ds(i * block, block), :], sibling)
        for i in range(nz)
    ]
    edge_swap = copy(edge_out, edge_in, sibling)
    across_swap = copy(across, across_in, sibling)
    p_share, p_x, p_early, p_norm, p_late = [], {s: [] for s in range(nz)}, [], [], []
    for k, peer in enumerate(d_peers):
        m = k + 1
        p_share.append(copy(gs.at[m], rs[k], peer))
        for s in range(nz):
            p_x[s].append(copy(gx.at[s, m], rx[k].at[s], peer))
        p_early.append(copy(ea.at[0], ea.at[m], peer))
        p_norm.append(copy(nrm, nr[k], peer))
        p_late.append(copy(la.at[0], la.at[m], peer))
    z_x, z_share, z_norm = [], [], []
    for k, peer in enumerate(z_back):
        z_x.append(copy(lx.at[k + 1], zx[k], peer))
        z_share.append(copy(ls, zs[k], peer))
        z_norm.append(copy(nrm2, nz_r[k], peer))
    z_edge = copy(edge_sum, edge_next, z_back[0])

    meet([sibling, *z_back, *line_peers(nz, 1), *d_peers])

    start([early_swap])
    ea[0, wi] = early[:, :half]

    g = t_dot(dbc[...], xn[...]) + t_dot(dbch[...], xnh[...])
    stage[0:state2, :] = g
    gdt[...] = split_dot_tr(slot_heads(dti.shape[1], per), t_dot(dti[...], xn[...]))
    per_head = jnp.concatenate([gbias[...], grate[...] * rate[...]], axis=0)
    small = jnp.concatenate(
        [
            jnp.concatenate([v[...] for v in taps], axis=1),
            ggain[...],
            gskip[...],
            dot(split2(per_head), ex[...]),
        ],
        axis=0,
    )
    both = split2(gbc[...])
    both = jnp.concatenate([both, jnp.zeros((4, 2 * state2), BF)], axis=0)
    for m in range(per):
        at = jnp.bitwise_xor(di, m)
        gs[m, 0:quarter, :] = stage[pl.ds(pl.multiple_of(at * quarter, quarter), quarter), :].astype(
            BF
        )
        lanes = jnp.concatenate(
            [
                small[:, (s * per + m) * HEADDIM : (s * per + m + 1) * HEADDIM]
                for s in range(nz)
            ],
            axis=1,
        )
        lower = jnp.concatenate([split2(lanes), both], axis=1)
        upper = gdt[pl.ds(pl.multiple_of(at * some_dt, some_dt), some_dt), :].astype(BF)
        gs[m, quarter:, :] = jnp.concatenate(
            [upper.astype(F32), lower.astype(F32)], axis=0
        ).astype(BF)
    start(p_share)
    arrive([early_swap])
    order = [*range(1, nz), 0]
    for s in order:
        g = t_dot(dx[s][...], xn[...]) + t_dot(dxh[s][...], xnh[...])
        for m in range(per):
            gx[s, m] = g[m * HEADDIM : (m + 1) * HEADDIM, :].astype(BF)
        start(p_x[s])
    start(p_early)

    def add_share():
        arrive(p_share)
        for i in range(share // HALO):
            here = slice(i * HALO, i * HALO + HALO)
            total = gs[0, here, :].astype(F32)
            for v in rs:
                total = total + v[here, :].astype(F32)
            sums[here, :] = total
        pack(sums)
        start(z_share)

    def pack(v):
        ls[0:quarter, :] = v[0:quarter, :].astype(BF)
        n = nz * HEADDIM
        rest = v[quarter:, :]
        a = rest[:, 0:n] + rest[:, n : 2 * n]
        b = rest[:, 2 * n : 2 * n + state2] + rest[:, 2 * n + state2 :]
        low_rows = jnp.concatenate([split2(a), split2(b)], axis=1)
        row = lax.broadcasted_iota(jnp.int32, (HALO, 1), 0)
        ls[quarter:, :] = jnp.where(row < some_dt, rest, low_rows.astype(F32)).astype(BF)

    def add_x(s):
        arrive(p_x[s])
        for i in range(HEADDIM // HALO):
            here = slice(i * HALO, i * HALO + HALO)
            total = gx[s, 0, here, :].astype(F32)
            for v in rx:
                total = total + v[s, here, :].astype(F32)
            lx[s, here, :] = total.astype(BF)
        if s > 0:
            start([z_x[s - 1]])

    for i in range(nz):
        here = slice(i * block, i * block + block)
        total = dot(dz[here, :], w[0])
        for s in range(nz):
            total = total + dot(dx[s][here, :], w[1, s * gc : (s + 1) * gc, :])
        total = total + dot(dbc[here, :], bc[0:state2, :]) + dot(dti[here, :], wdt[...])
        dxn[here, :] = total[:, :half]
        dxn_out[here, :] = total[:, half:].astype(BF)
        start([dxn_swap[i]])
        if i == 0:
            add_share()
            total = dot(dbch[...], bc[0:state2, :])
            for s in range(nz):
                total = total + dot(dxh[s][...], w[1, s * gc : (s + 1) * gc, :])
            edge_sum[...] = total[:, :half]
            edge_out[...] = total[:, half:]
            start([edge_swap])
        if i == 1:
            add_x(order[0])
            arrive([edge_swap])
            edge_sum[...] = edge_sum[...] + edge_in[...]
            start([z_edge])
    if nz > 2:
        add_x(order[1])

    arrive([*dxn_swap, z_edge])
    late_edge = jnp.where(zi < nz - 1, edge_next[...], 0.0)
    gain_v = gain[...]
    norm_sum = jnp.zeros((8, half), F32)
    ones = jnp.ones((8, half), BF)
    for i in range(rows // Q):
        here = slice(i * Q, i * Q + Q)
        v = dxn[here, :] + dxn_in[here, :].astype(F32)
        if i == rows // Q - 1:
            v = v + jnp.concatenate([jnp.zeros((Q - HALO, half), F32), late_edge], axis=0)
        dxn[here, :] = v
        h = hidden[here, :].astype(F32)
        vh = v * h
        norm_sum = norm_sum + jnp.sum(
            (vh * r[here, :]).reshape(Q // 8, 8, half), axis=0
        )
        across[:, here] = split_dot_t(ones, vh * gain_v)
    start([across_swap])
    nrm[...] = norm_sum
    start(p_norm)
    for s in order[2:]:
        add_x(s)
    arrive([across_swap])
    eighth = jnp.full((8, Q), 0.125, F32)
    for i in range(rows // Q):
        here = slice(i * Q, i * Q + Q)
        total = across[:, here] + across_in[:, here]
        total = t_dot(total, eighth, HIGH)
        rr = r[here, :]
        scale = rr * rr * rr / (2 * half)
        rg = rr * gain_v
        for j in range(half // Q):
            lanes = slice(j * Q, j * Q + Q)
            hid_o[here, lanes] = (
                cot[here, lanes].astype(F32)
                + rg[:, lanes] * dxn[here, lanes]
                - hidden[here, lanes].astype(F32) * (scale * total)
            ).astype(BF)
    arrive(p_norm)
    total = nrm[...]
    for v in nr:
        total = total + v[...]
    nrm2[...] = total
    start(z_norm)

    arrive([*z_x, *z_share])
    total = lx[0].astype(F32)
    for v in zx:
        total = total + v[...].astype(F32)
    mine = total.astype(BF)
    la[0, pl.ds(pl.multiple_of(wi * HEADDIM, HEADDIM), HEADDIM), :] = mine[:, :half]
    sw_out[0:HEADDIM, :] = mine[:, half:]
    n = nz * HEADDIM
    total = ls[0:quarter, :].astype(F32)
    for v in zs:
        total = total + v[0:quarter, :].astype(F32)
    sums[0:quarter, :] = total
    sw_out[HEADDIM : HEADDIM + quarter, :] = total[:, half:].astype(BF)
    total = ls[quarter:, :].astype(F32)
    own_small = total[:, 0:HEADDIM] + total[:, n : n + HEADDIM]
    for k, v in enumerate(zs):
        part = v[quarter:, :].astype(F32)
        total = total + part
        at = (k + 1) * HEADDIM
        own_small = own_small + (
            part[:, at : at + HEADDIM] + part[:, n + at : n + at + HEADDIM]
        )
    sums[quarter:, :] = total
    taps_bc = total[:, 2 * n : 2 * n + state2] + total[:, 2 * n + state2 :]
    at = HEADDIM + quarter
    sw_out[at : at + HALO, :] = total[:, half:].astype(BF)
    own_small = split2(own_small)
    own_small = jnp.concatenate(
        [own_small, jnp.zeros((HALO, half - 2 * HEADDIM), BF)], axis=1
    )
    taps_bc2 = split2(taps_bc)
    sw_out[at + HALO : at + 2 * HALO, :] = own_small
    sw_out[at + 2 * HALO : at + 3 * HALO, :] = taps_bc2
    start([late_swap])
    arrive([late_swap])
    there = pl.ds(pl.multiple_of((1 - wi) * HEADDIM, HEADDIM), HEADDIM)
    la[0, there, :] = sw_in[0:HEADDIM, :]
    base = 2 * HEADDIM
    la[0, base : base + share, :] = (
        sums[:, :half] + sw_in[HEADDIM : HEADDIM + share, :].astype(F32)
    ).astype(BF)
    base = base + share
    la[0, pl.ds(pl.multiple_of(base + wi * HALO, HALO), HALO), :] = own_small
    la[0, pl.ds(pl.multiple_of(base + (1 - wi) * HALO, HALO), HALO), :] = sw_in[
        at + HALO : at + 2 * HALO, :
    ]
    start(p_late)
    got = sw_in[at + 2 * HALO : at + 3 * HALO, :].astype(F32)
    taps_bc = taps_bc + got[:, :state2] + got[:, state2:]
    tbc_o[...] = taps_bc[some_dt : some_dt + 4, :]
    arrive(z_norm)
    total = nrm2[...]
    for v in nz_r:
        total = total + v[...]
    norm_o[...] = jnp.sum(total, axis=0, keepdims=True)

    arrive([*p_early, *p_late])
    for c in copy.all:
        c.wait_send()


def finish_kernel(per, ea, la, las, ones, zx_o, ow_o, bcdt_o, cx_o, gn_o, sk_o, bias_o, rate_o):
    di = lax.axis_index("dp")
    some_dt = HEADS // per
    quarter = (bcdt_o.shape[0] - HEADS) // per
    base = 2 * HEADDIM + quarter + HALO
    small = []
    for h in range(2 * per):
        k, j = h // per, h % per
        m = jnp.bitwise_xor(di, j)
        z_part = ea[m, k, HEADDIM:, :].astype(F32)
        x_part = la[m, k * HEADDIM : (k + 1) * HEADDIM, :].astype(F32)
        zx_o[:, h, :] = jnp.transpose(jnp.concatenate([z_part, x_part], axis=0))
        ow_o[h * HEADDIM : (h + 1) * HEADDIM, :] = ea[m, k, :HEADDIM, :].astype(F32)
        v = las[m, base + k * HALO : base + (k + 1) * HALO, :].astype(F32)
        small.append((v[:, :HEADDIM] + v[:, HEADDIM : 2 * HEADDIM])[some_dt:, :])
    for j in range(per):
        m = jnp.bitwise_xor(di, j)
        v = la[m, 2 * HEADDIM : base, :].astype(F32)
        bcdt_o[j * quarter : (j + 1) * quarter, :] = v[:quarter, :]
        at = per * quarter + j * some_dt
        bcdt_o[at : at + some_dt, :] = v[quarter : quarter + some_dt, :]

    @pl.when(pl.program_id(0) == 0)
    def _():
        rows = jnp.concatenate(small, axis=1)
        cx_o[...] = rows[0:4, :]
        gn_o[...] = rows[4:5, :]
        total = dot(rows, ones[...], HIGH)
        sk_o[...] = total[5:6, :]
        bias_o[...] = total[6:7, :] / HEADDIM
        rate_o[...] = total[7:8, :] / HEADDIM


def split_dot_tr(m, v):
    hi = v.astype(BF)
    lo = (v - hi.astype(F32)).astype(BF)
    m = m.astype(BF)
    return t_dot(m, hi) + t_dot(m, lo)


def split_dot_t(m, v):
    hi = v.astype(BF)
    lo = (v - hi.astype(F32)).astype(BF)
    return dot_t(m, hi) + dot_t(m, lo)


def shape(dims, dtype=F32):
    return jax.ShapeDtypeStruct(dims, dtype)


def whole(array):
    rank = len(array.shape)
    return pl.BlockSpec(array.shape, lambda *_: (0,) * rank)


def params():
    return pltpu.CompilerParams(vmem_limit_bytes=VMEM)


def cost(us):
    return pl.CostEstimate(flops=int(us * 1.0e8), bytes_accessed=int(us * 1.0e3), transcendentals=0)


def take(refs, *counts):
    out, at = [], 0
    for n in counts:
        out.append(refs[at] if n == 0 else refs[at : at + n])
        at += max(n, 1)
    return out + [refs[at:]]


def sequence_device(
    hidden, lengths, cotangent, norm_gain, in_zx, in_bcdt, conv_x, conv_bc,
    dt_bias, a_log, d_skip, gnorm_gain, out_w,
):
    rows, half = hidden.shape
    own_heads = in_zx.shape[1]
    nz = lax.axis_size("head")
    ndp = lax.axis_size("dp")
    zi = lax.axis_index("head")
    di = lax.axis_index("dp")
    wi = lax.axis_index("width")
    per = ndp
    heads = nz * per
    channels = heads * HEADDIM
    model = 2 * half
    blocks = rows // Q

    def swap(v):
        return lax.ppermute(v, "width", [(0, 1), (1, 0)])

    gc = per * HEADDIM
    groups = tuple(range(nz))

    onehot = np.kron(np.eye(heads), np.ones((1, HEADDIM)))
    ex = jnp.asarray(np.concatenate([onehot, onehot], axis=0), BF)
    er = jnp.asarray(onehot.T, BF)
    sel = jnp.asarray(onehot.T * (np.arange(channels) % HEADDIM == 0)[:, None], F32)

    each = lambda v: jnp.broadcast_to(v[:, None], (own_heads, HEADDIM)).reshape(1, -1)
    parameter_rows = jnp.concatenate(
        [
            conv_x.astype(F32), gnorm_gain[None].astype(F32), each(dt_bias), each(a_log),
            each(d_skip), jnp.broadcast_to(norm_gain[None].astype(F32), (8, half)),
        ],
        axis=0,
    )
    piece = shape((2, HEADDIM, half), BF)
    some = shape((2, gc - HEADDIM, half), BF)
    outs = shape((gc, half), BF)
    first, first2, rest, rest2, out_mine, out_mine2, bcdt_t, table = pl.pallas_call(
        functools.partial(prep_kernel, per),
        out_shape=[
            piece, piece, some, some, outs, outs,
            shape((2 * STATE + HEADS + HALO, half), BF), shape((8, gc)),
        ],
        compiler_params=params(),
        cost_estimate=cost(4),
        name="prep",
    )(
        in_zx.reshape(half, -1), out_w, jnp.transpose(in_bcdt), parameter_rows
    )
    taps_bc = conv_bc.astype(F32)

    step = lambda i: (i, 0)
    fix = lambda i: (0, 0)
    part = shape((rows, gc), BF)
    full = shape((rows, channels))
    anywhere = pl.BlockSpec(memory_space=pl.ANY)
    vmem = pl.BlockSpec(memory_space=pltpu.VMEM)
    narrow = shape((rows, 2 * heads), BF)
    kept = dict(
        xnh=shape((HALO, model), BF), r=shape((rows, 1)), raw=shape((rows, 2 * STATE)),
        rawh=shape((HALO, 2 * STATE)), ubc=shape((rows, 2 * STATE)), b=shape((rows, STATE), BF),
        c=shape((rows, STATE), BF), dt=shape((rows, heads)), sig=shape((rows, heads)),
        cl=shape((rows, heads)), clt=shape((heads, rows)), dt2=narrow, e12=narrow, tl2=narrow,
        dttl2=narrow, ec2=narrow, edt2=narrow, rate=shape((1, heads)),
        wdt=shape((heads, model), BF),
        bcdt=shape((2 * STATE + HEADS + HALO, model), BF), tot=shape((heads, STATE), BF), table=shape((8, channels)),
    )
    wide_part = shape((rows, gc))
    message_shape = shape((channels + HALO, STATE), BF)
    out_shapes = [
        shape((2, channels, model), BF), shape((channels, model), BF), shape((rows, half), BF),
        shape((rows, model), BF), *[wide_part] * nz, *[part] * nz, *[wide_part] * nz,
        *[part] * nz, *[part] * nz, *[message_shape] * (nz - 1), *[shape((HALO, gc))] * nz,
        *[kept[name] for name in KEPT],
    ]
    held = lambda v: pltpu.VMEM(v.shape, v.dtype)
    remotes = 6 + 5 * (nz - 1) + 2 + 2 * (nz - 1) * (per - 1)
    out = pl.pallas_call(
        functools.partial(front_kernel, per, nz),
        in_specs=[vmem] * 10 + [anywhere] * 3,
        out_specs=[anywhere] * (4 + 5 * nz + nz - 1) + [vmem] * (nz + len(KEPT)),
        out_shape=out_shapes,
        scratch_shapes=[
            *[held(wide_part)] * nz, *[held(part)] * nz, *[held(wide_part)] * nz,
            *[held(part)] * nz, *[held(part)] * nz, pltpu.VMEM((2, channels, model), BF),
            pltpu.VMEM((rows, half), BF), pltpu.VMEM((HALO, model), BF),
            pltpu.VMEM((rows, model), BF),
            held(message_shape), pltpu.VMEM((rows + HALO, gc), F32),
            pltpu.VMEM((rows + HALO, 2 * STATE), F32), pltpu.VMEM((gc, STATE), F32),
            pltpu.SemaphoreType.DMA((remotes,)), pltpu.SemaphoreType.DMA((remotes,)),
            pltpu.SemaphoreType.DMA((7 + 5 * nz,)),
        ],
        compiler_params=pltpu.CompilerParams(
            vmem_limit_bytes=VMEM, collective_id=1, has_side_effects=True
        ),
        cost_estimate=cost(90),
        name="front",
    )(
        hidden, first, first2, rest, rest2, bcdt_t, table, taps_bc, sel, ex, out_mine, out_mine2,
        cotangent,
    )
    weights, wout, cot_o, xn, out = out[0], out[1], out[2], out[3], out[4:]
    z, xr, u, xdt, y_in, messages, xrh, out = take(out, *[nz] * 5, nz - 1, nz)
    o = Named(KEPT, out)
    xnh, r, braw, brawh, ubc, bs, cs = o.xnh, o.r, o.raw, o.rawh, o.ubc, o.b, o.c
    dt, sig, cl, clt, rate, wdt, totals, table = o.dt, o.sig, o.cl, o.clt, o.rate, o.wdt, o.tot, o.table
    dt2, e12, tl2, dttl2, ec2, edt2 = o.dt2, o.e12, o.tl2, o.dttl2, o.ec2, o.edt2
    limit = (lengths[0] - zi * rows).reshape(1, 1)

    smem = pl.BlockSpec(memory_space=pltpu.SMEM)
    tile = 2 * Q if rows % (2 * Q) == 0 else Q
    tiles = rows // tile
    now = lambda columns: pl.BlockSpec((tile, columns), lambda i: (jnp.minimum(i, tiles - 1), 0))
    then = lambda columns: pl.BlockSpec((tile, columns), lambda i: (jnp.maximum(i - 1, 0), 0))
    out = pl.pallas_call(
        functools.partial(mid_kernel, groups, per),
        grid=(tiles + 1,),
        in_specs=[
            *[now(gc)] * (3 * nz), now(half), now(half), now(STATE), now(STATE),
            pl.BlockSpec((heads, tile), lambda i: (0, jnp.minimum(i, tiles - 1))),
            now(2 * heads), now(2 * heads), *[then(gc)] * (2 * nz), then(2 * heads), then(STATE),
            then(half), *[whole(v) for v in messages], whole(totals), whole(table),
            whole(ex), whole(wout), smem,
        ],
        out_specs=[
            *[
                pl.BlockSpec((tile // Q, gc, STATE), lambda i: (jnp.minimum(i, tiles - 1), 0, 0))
            ] * nz,
            now(model), *[then(gc)] * nz, then(channels), then(channels), then(half),
            pl.BlockSpec((channels + HALO, STATE), fix), pl.BlockSpec((1, channels), fix),
            pl.BlockSpec((1, channels), fix),
        ],
        out_shape=[
            *[shape((blocks, gc, STATE), BF)] * nz, shape((rows, model), BF), *[part] * nz,
            shape((rows, channels), BF), shape((rows, channels), BF), shape((rows, half), BF),
            message_shape, shape((1, channels)), shape((1, channels)),
        ],
        scratch_shapes=[
            pltpu.VMEM((channels, STATE), F32), pltpu.VMEM((channels, STATE), F32),
            pltpu.VMEM((2, tile, channels), F32), pltpu.VMEM((2, tile, channels), F32),
            pltpu.VMEM((2, tile, half), F32), pltpu.VMEM((tiles, tile, half), BF),
            pltpu.VMEM((tiles, tile, half), BF), pltpu.VMEM((tiles, tile, Q), F32),
            pltpu.VMEM((tiles, tile, Q), F32), pltpu.VMEM((tile, channels), BF),
            pltpu.SemaphoreType.DMA((2 * tiles,)), pltpu.SemaphoreType.DMA((2 * tiles,)),
        ],
        compiler_params=pltpu.CompilerParams(
            vmem_limit_bytes=VMEM, collective_id=3, has_side_effects=True
        ),
        cost_estimate=cost(30),
        name="mid",
    )(
        *y_in, *u, *z, cotangent, cot_o, bs, cs, clt, e12, dttl2, *u, *z, ec2, cs, hidden,
        *messages, totals, table, ex, wout, limit,
    )
    states, masked, dys, out = take(out, nz, 0, nz)
    dz, yn, out_hidden, message, g_gain, g_skip = out

    begin = lambda i: jnp.maximum(i - nz, 0)
    first_pass = lambda i: jnp.minimum(begin(i), blocks - 1)
    second_pass = lambda i: jnp.minimum(blocks - 1, 2 * blocks - 1 - begin(i))
    either = lambda i: jnp.minimum(begin(i), 2 * blocks - 1 - begin(i))
    one = lambda i: (first_pass(i), 0)
    two = lambda i: (second_pass(i), 0)
    both = lambda i: (either(i), 0)
    gcol = pl.BlockSpec((rows, gc), lambda i: (0, lax.rem(jnp.minimum(i, nz - 1) + 1, nz)))
    head_columns = lambda v: pl.BlockSpec((Q, v), two)
    early_shape = (nz, 2 * HEADDIM, model)
    exchange = 2 * (nz - 1) + nz * (per - 1)
    out = pl.pallas_call(
        functools.partial(scan_back_kernel, groups, per),
        grid=(nz + 2 * blocks,),
        in_specs=[
            *[pl.BlockSpec((Q, gc), one)] * nz, *[pl.BlockSpec((Q, gc), both)] * nz,
            *[pl.BlockSpec((Q, gc), two)] * (2 * nz),
            *[
                pl.BlockSpec(
                    (1, gc, STATE), lambda i: (second_pass(i), 0, 0)
                )
            ] * nz,
            *[pl.BlockSpec((HALO, gc), fix)] * nz,
            pl.BlockSpec((Q, STATE), both), pl.BlockSpec((Q, STATE), both),
            pl.BlockSpec((Q, heads), one),
            pl.BlockSpec((heads, Q), lambda i: (0, either(i))),
            head_columns(heads), head_columns(heads), head_columns(2 * heads),
            head_columns(2 * heads), head_columns(2 * heads), head_columns(2 * STATE),
            head_columns(2 * STATE), whole(brawh), whole(table), whole(taps_bc), whole(rate),
            whole(ex), whole(er), anywhere, gcol, whole(masked), gcol, whole(xn),
        ],
        out_specs=[
            *[pl.BlockSpec((Q, gc), two)] * nz, *[pl.BlockSpec((HALO, gc), fix)] * nz,
            *[pl.BlockSpec((4, gc), fix)] * nz, head_columns(heads),
            pl.BlockSpec((1, heads), fix), pl.BlockSpec((1, heads), fix),
            head_columns(2 * STATE), pl.BlockSpec((HALO, 2 * STATE), fix),
            pl.BlockSpec((4, 2 * STATE), fix),
            pl.BlockSpec((2 * HEADDIM, model), fix),
        ],
        out_shape=[
            *[shape((rows, gc), BF)] * nz, *[shape((HALO, gc), BF)] * nz, *[shape((4, gc))] * nz,
            shape((rows, heads), BF), shape((1, heads)), shape((1, heads)),
            shape((rows, 2 * STATE), BF), shape((HALO, 2 * STATE), BF), shape((4, 2 * STATE)),
            shape((2 * HEADDIM, model), BF),
        ],
        scratch_shapes=[
            *[pltpu.VMEM(message.shape, BF)] * (nz - 1), *[pltpu.VMEM(early_shape, BF)] * (per - 1),
            *[pltpu.VMEM(early_shape[1:], BF)] * (nz - 1), *[pltpu.VMEM((8, gc), F32)] * nz,
            pltpu.VMEM((8, 2 * STATE), F32), pltpu.VMEM((per, *early_shape), BF),
            pltpu.VMEM(early_shape, BF),
            pltpu.VMEM((rows, channels), F32),
            pltpu.VMEM((rows, STATE), F32), pltpu.VMEM((rows, STATE), F32),
            pltpu.VMEM((rows, heads), F32), pltpu.VMEM((heads, Q), F32),
            pltpu.VMEM((channels, STATE), F32), pltpu.VMEM((heads, STATE), F32),
            pltpu.SemaphoreType.DMA((exchange,)), pltpu.SemaphoreType.DMA((exchange,)),
        ],
        compiler_params=pltpu.CompilerParams(
            vmem_limit_bytes=VMEM, collective_id=0, has_side_effects=True
        ),
        cost_estimate=cost(50),
        name="scan_back",
    )(
        *xdt, *dys, *u, *xr, *states, *xrh, bs, cs, cl, clt, dt, sig, dt2, e12, tl2, ubc, braw,
        brawh, table, taps_bc, rate, ex, er, message, yn, masked,
        dz, xn,
    )
    dx, dxh, g_taps = list(out[:nz]), list(out[nz : 2 * nz]), out[2 * nz : 3 * nz]
    dti, g_rate, g_bias, dbc, dbch, g_taps_bc, early_total = out[3 * nz :]
    quarter = 2 * STATE // per
    share = quarter + HALO
    late_rows = 2 * HEADDIM + share + 2 * HALO
    swap_rows = HEADDIM + share + 2 * HALO
    tail_copies = 4 + nz + (per - 1) * (4 + nz) + 3 * (nz - 1) + 1
    operands = [
        *dx, *dxh, *g_taps, dz, dbc, dbch, dti, xn, xnh, weights, o.bcdt, wdt, early_total, hidden,
        cotangent, r, norm_gain[None].astype(F32), g_taps_bc, g_rate, g_bias, g_skip, g_gain, rate,
        ex,
    ]
    line16 = pltpu.VMEM((HALO, half), F32)
    line8 = pltpu.VMEM((8, half), F32)
    early_all, late_all, grad_hidden, g_norm, g_taps_bc = pl.pallas_call(
        functools.partial(tail_kernel, per, nz),
        in_specs=[vmem] * len(operands),
        out_specs=[vmem] * 5,
        out_shape=[
            shape((per, 2, 2 * HEADDIM, half), BF), shape((per, late_rows, half), BF),
            shape((rows, half), BF), shape((1, half)), shape((4, 2 * STATE)),
        ],
        scratch_shapes=[
            pltpu.VMEM((nz, per, HEADDIM, model), BF), pltpu.VMEM((per, share, model), BF),
            pltpu.VMEM((HEADS, model), F32), pltpu.VMEM((nz, HEADDIM, model), BF),
            pltpu.VMEM((share, model), BF), pltpu.VMEM((swap_rows, half), BF),
            pltpu.VMEM((swap_rows, half), BF), pltpu.VMEM((rows, half), F32),
            pltpu.VMEM((rows, half), BF), pltpu.VMEM((rows, half), BF), line16, line16, line16,
            line16, pltpu.VMEM((8, rows), F32), pltpu.VMEM((8, rows), F32), line8, line8,
            pltpu.VMEM((share, model), F32),
            *[pltpu.VMEM((nz, HEADDIM, model), BF)] * (per - 1),
            *[pltpu.VMEM((share, model), BF)] * (per - 1),
            *[pltpu.VMEM((HEADDIM, model), BF)] * (nz - 1),
            *[pltpu.VMEM((share, model), BF)] * (nz - 1), *[line8] * (per - 1),
            *[line8] * (nz - 1),
            pltpu.VMEM((2 * STATE, model), F32),
            pltpu.SemaphoreType.DMA((tail_copies,)), pltpu.SemaphoreType.DMA((tail_copies,)),
        ],
        compiler_params=pltpu.CompilerParams(
            vmem_limit_bytes=VMEM, collective_id=2, has_side_effects=True
        ),
        cost_estimate=cost(60),
        name="tail",
    )(*operands)
    inner = own_heads * HEADDIM
    each_head = jnp.asarray(np.kron(np.eye(own_heads), np.ones((HEADDIM, 1))), F32)
    row_heads = shape((1, own_heads))
    g_zx, g_out, g_bcdt, g_cx, g_gain, g_skip, g_bias, g_rate = pl.pallas_call(
        functools.partial(finish_kernel, per),
        grid=(half // Q,),
        in_specs=[
            pl.BlockSpec((per, 2, 2 * HEADDIM, Q), lambda i: (0, 0, 0, i)),
            pl.BlockSpec((per, late_rows, Q), lambda i: (0, 0, i)),
            pl.BlockSpec((per, late_rows, Q), lambda i: (0, 0, 0)), whole(each_head),
        ],
        out_specs=[
            pl.BlockSpec((Q, own_heads, 2 * HEADDIM), lambda i: (i, 0, 0)),
            pl.BlockSpec((inner, Q), lambda i: (0, i)),
            pl.BlockSpec((2 * STATE + HEADS, Q), lambda i: (0, i)), pl.BlockSpec((4, inner), fix),
            pl.BlockSpec((1, inner), fix), *[pl.BlockSpec((1, own_heads), fix)] * 3,
        ],
        out_shape=[
            shape((half, own_heads, 2 * HEADDIM)), shape((inner, half)),
            shape((2 * STATE + HEADS, half)), shape((4, inner)), shape((1, inner)), row_heads,
            row_heads, row_heads,
        ],
        compiler_params=params(),
        cost_estimate=cost(5),
        name="finish",
    )(early_all, late_all, late_all, each_head)
    return (
        out_hidden,
        grad_hidden,
        g_norm.reshape(-1),
        g_zx,
        jnp.transpose(g_bcdt),
        g_cx,
        g_taps_bc,
        g_bias.reshape(-1),
        g_rate.reshape(-1),
        g_skip.reshape(-1),
        g_gain.reshape(-1),
        g_out,
    )


def fits(mesh):
    ndp, nz, nw = mesh.shape["dp"], mesh.shape["head"], mesh.shape["width"]
    return (
        nw == 2
        and ndp in (2, 4, 8)
        and nz & (nz - 1) == 0
        and HEADS == nz * nw * ndp
        and LEN % (nz * Q) == 0
        and SEQS == ndp
        and HEADS // nw * HEADDIM % Q == 0
        and HEADS // ndp == 8
    )


def solution(mesh):
    placed = (
        P(("dp", "head"), "width"),
        P("dp"),
        P(("dp", "head"), "width"),
        P("width"),
        P("width", "head", None),
        P("width", None),
        P(None, "head"),
        P(),
        P("head"),
        P("head"),
        P("head"),
        P("head"),
        P("head", "width"),
    )
    return jax.shard_map(
        sequence_device if fits(mesh) else per_device,
        mesh=mesh,
        in_specs=placed,
        out_specs=(
            P(("dp", "head"), "width"),
            P(("dp", "head"), "width"),
            P("width"),
            P("width", "head", None),
            P("width", None),
            P(None, "head"),
            P(),
            P("head"),
            P("head"),
            P("head"),
            P("head"),
            P("head", "width"),
        ),
        check_vma=False,
    )
```

```python
import functools

import jax
import jax.numpy as jnp
import numpy as np
from jax import lax
from jax.experimental import pallas as pl
from jax.experimental.pallas import tpu as pltpu
from jax.sharding import PartitionSpec as P

D = 1024
HEADS = 32
HEADDIM = 64
STATE = 128
SCAN_BLOCK = 256
LEN = 4096
INNER = 2048
SEQS = 4


EPS = 1e-05
HIGH = lax.Precision.HIGHEST


def conv_causal(values, kernel):
    taps = kernel.shape[0]
    padded = jnp.pad(values, ((taps - 1, 0), (0, 0)))
    total = jnp.zeros_like(values)
    for offset in range(taps):
        total = total + kernel[offset] * padded[offset : offset + values.shape[0]]
    return total


def block_scan(inputs, steps, rates, bmat, cmat, block):
    length, heads, hsize = inputs.shape
    count = length // block
    in_blocks = inputs.reshape(count, block, heads, hsize)
    step_blocks = steps.reshape(count, block, heads)
    b_blocks = bmat.reshape(count, block, bmat.shape[1])
    c_blocks = cmat.reshape(count, block, cmat.shape[1])
    places = jnp.arange(block)
    lower = (places[:, None] >= places[None, :])[:, :, None]

    def advance(state, pieces):
        x_part, dt_part, b_part, c_part = pieces
        cums = jnp.cumsum(dt_part * rates, axis=0)
        spread = cums[:, None, :] - cums[None, :, :]
        decay = jnp.where(lower, jnp.exp(jnp.where(lower, spread, 0.0)), 0.0)
        scores = jnp.dot(c_part, b_part.T, precision=HIGH)
        weights = scores[:, :, None] * decay * dt_part[None, :, :]
        inside = jnp.einsum("ijh,jhp->ihp", weights, x_part, precision=HIGH)
        carried = (
            jnp.einsum("in,hpn->ihp", c_part, state, precision=HIGH) * jnp.exp(cums)[:, :, None]
        )
        tails = jnp.exp(cums[-1][None, :] - cums) * dt_part
        state = jnp.exp(cums[-1])[:, None, None] * state + jnp.einsum(
            "jh,jhp,jn->hpn", tails, x_part, b_part, precision=HIGH
        )
        return (state, inside + carried)

    start_state = jnp.zeros((heads, hsize, bmat.shape[1]), jnp.float32)
    _, result = lax.scan(
        jax.checkpoint(advance), start_state, (in_blocks, step_blocks, b_blocks, c_blocks)
    )
    return result.reshape(length, heads, hsize)


def mixer(zx, bc_raw, dt_raw, kernel_x, kernel_bc, bias_dt, log_rate, skip):
    length, heads, double = zx.shape
    hsize = double // 2
    gate = zx[:, :, :hsize]
    x_raw = zx[:, :, hsize:].reshape(length, heads * hsize)
    xs_conv = jax.nn.silu(conv_causal(x_raw, kernel_x)).reshape(length, heads, hsize)
    bc_conv = jax.nn.silu(conv_causal(bc_raw, kernel_bc))
    half = bc_conv.shape[1] // 2
    steps = jax.nn.softplus(dt_raw + bias_dt)
    rates = -jnp.exp(log_rate)
    result = (
        block_scan(xs_conv, steps, rates, bc_conv[:, :half], bc_conv[:, half:], SCAN_BLOCK)
        + skip[:, None] * xs_conv
    )
    return (result * jax.nn.silu(gate)).reshape(length, heads * hsize)


def per_device(
    hidden,
    lengths,
    cotangent,
    norm_gain,
    in_zx,
    in_bcdt,
    conv_x,
    conv_bc,
    dt_bias,
    a_log,
    d_skip,
    gnorm_gain,
    out_w,
):
    slice_rows, half_width = hidden.shape
    local_heads = in_zx.shape[1]
    head_count = lax.axis_size("head")
    head_index = lax.axis_index("head")
    total_rows = slice_rows * head_count
    seq_local = lengths.shape[0]
    inner_local = local_heads * HEADDIM
    row_ids = head_index * slice_rows + jnp.arange(slice_rows, dtype=jnp.int32)
    owner = (row_ids // LEN)[:, None] == jnp.arange(seq_local, dtype=jnp.int32)[None, :]
    limits = jnp.sum(jnp.where(owner, lengths[None, :], 0), axis=1)
    keeper = (row_ids % LEN < limits).astype(jnp.float32)[:, None]
    source = hidden.astype(jnp.float32)
    squares = lax.psum(jnp.sum(source * source, axis=1), "width")
    scale = lax.rsqrt(squares / D + EPS)[:, None]
    gain_in = norm_gain.astype(jnp.float32)
    normed = (source * scale * gain_in).astype(jnp.bfloat16)
    gathered = lax.all_gather(normed, "head", axis=0, tiled=True)
    w_zx = in_zx.reshape(half_width, local_heads * 2 * HEADDIM)
    zx_part = jnp.dot(gathered, w_zx, preferred_element_type=jnp.float32)
    bcdt_part = jnp.dot(gathered, in_bcdt, preferred_element_type=jnp.float32)
    zx_full, bcdt_full = lax.psum((zx_part, bcdt_part), "width")
    zx_seq = zx_full.reshape(seq_local, LEN, local_heads, 2 * HEADDIM)
    bc_seq = bcdt_full[:, : 2 * STATE].reshape(seq_local, LEN, 2 * STATE)
    dt_seq = lax.dynamic_slice_in_dim(
        bcdt_full, 2 * STATE + head_index * local_heads, local_heads, 1
    ).reshape(seq_local, LEN, local_heads)

    def local_mix(zx_in, bc_in, dt_in, kernel_x, kernel_bc, bias_in, log_in, skip_in):
        per_sequence = jax.vmap(mixer, in_axes=(0, 0, 0, None, None, None, None, None))
        return per_sequence(
            zx_in, bc_in, dt_in, kernel_x, kernel_bc, bias_in, log_in, skip_in
        ).reshape(total_rows, inner_local)

    gated, mix_pull = jax.vjp(
        local_mix,
        zx_seq,
        bc_seq,
        dt_seq,
        conv_x.astype(jnp.float32),
        conv_bc.astype(jnp.float32),
        dt_bias,
        a_log,
        d_skip,
    )
    total_sq = lax.psum(jnp.sum(gated * gated, axis=1), "head")
    scale_out = lax.rsqrt(total_sq / INNER + EPS)[:, None]
    gain_out = gnorm_gain.astype(jnp.float32)
    mixed = (gated * scale_out * gain_out).astype(jnp.bfloat16)
    picked = mixed
    branch = lax.psum_scatter(
        jnp.dot(picked, out_w, preferred_element_type=jnp.float32),
        "head",
        scatter_dimension=0,
        tiled=True,
    )
    out_hidden = (source + keeper * branch).astype(jnp.bfloat16)
    grad_out = cotangent.astype(jnp.float32)
    masked = (grad_out * keeper).astype(jnp.bfloat16)
    piece = lax.all_gather(masked, "head", axis=0, tiled=True)
    picked = mixed
    acc_weight = jnp.einsum("tc,td->cd", picked, piece, preferred_element_type=jnp.float32)
    product = jnp.einsum("td,cd->tc", piece, out_w, preferred_element_type=jnp.float32)
    grad_mixed = lax.psum(product, "width")
    gain_out_grad = jnp.sum(grad_mixed * gated * scale_out, axis=0)
    inner_total = lax.psum(jnp.sum(grad_mixed * gain_out * gated, axis=1), "head")
    cubed = scale_out * scale_out * scale_out
    grad_gated = scale_out * gain_out * grad_mixed - gated * cubed / INNER * inner_total[:, None]
    (
        grad_zx_seq,
        grad_bc_seq,
        grad_dt_seq,
        kernel_x_grad,
        kernel_bc_grad,
        bias_grad,
        rate_grad,
        skip_grad,
    ) = mix_pull(grad_gated)
    grad_zx = grad_zx_seq.reshape(total_rows, local_heads * 2 * HEADDIM).astype(jnp.bfloat16)
    dt_columns = jnp.zeros((total_rows, HEADS), jnp.float32)
    dt_columns = lax.dynamic_update_slice_in_dim(
        dt_columns, grad_dt_seq.reshape(total_rows, local_heads), head_index * local_heads, 1
    )
    grad_bcdt_head = jnp.concatenate(
        [grad_bc_seq.reshape(total_rows, 2 * STATE), dt_columns], axis=1
    )
    weight_zx = jnp.einsum(
        "td,tc->dc", gathered, grad_zx, preferred_element_type=jnp.float32
    ).reshape(half_width, local_heads, 2 * HEADDIM)
    normed_part = jnp.einsum("tc,dc->td", grad_zx, w_zx, preferred_element_type=jnp.float32)
    grad_normed, bcdt_summed = (
        lax.psum_scatter(normed_part, "head", scatter_dimension=0, tiled=True),
        lax.psum_scatter(grad_bcdt_head, "head", scatter_dimension=0, tiled=True),
    )
    bcdt_low = bcdt_summed.astype(jnp.bfloat16)
    grad_normed = grad_normed + jnp.einsum(
        "tk,dk->td", bcdt_low, in_bcdt, preferred_element_type=jnp.float32
    )
    weight_bcdt = jnp.einsum("td,tk->dk", normed, bcdt_low, preferred_element_type=jnp.float32)
    gain_in_grad = jnp.sum(grad_normed * source * scale, axis=0)
    across = lax.psum(jnp.sum(grad_normed * gain_in * source, axis=1), "width")
    scale_cubed = scale * scale * scale
    grad_hidden = (
        grad_out + scale * gain_in * grad_normed - source * scale_cubed / D * across[:, None]
    ).astype(jnp.bfloat16)
    summed_dp = lax.psum(
        (weight_zx, acc_weight, kernel_x_grad, bias_grad, rate_grad, skip_grad, gain_out_grad), "dp"
    )
    summed_all = lax.psum((weight_bcdt, gain_in_grad, kernel_bc_grad), ("dp", "head"))
    return (
        out_hidden,
        grad_hidden,
        summed_all[1],
        summed_dp[0],
        summed_all[0],
        summed_dp[2],
        summed_all[2],
        summed_dp[3],
        summed_dp[4],
        summed_dp[5],
        summed_dp[6],
        summed_dp[1],
    )


BF = jnp.bfloat16
F32 = jnp.float32
Q = 128
HALO = 16
NEG = -1e30
MESH = pl.DeviceIdType.MESH
VMEM = 60 * 1024 * 1024


def dot(a, b, prec=None):
    return lax.dot_general(a, b, (((1,), (0,)), ((), ())), precision=prec, preferred_element_type=F32)


def dot_t(a, b, prec=None):
    return lax.dot_general(a, b, (((1,), (1,)), ((), ())), precision=prec, preferred_element_type=F32)


def t_dot(a, b, prec=None):
    return lax.dot_general(a, b, (((0,), (0,)), ((), ())), precision=prec, preferred_element_type=F32)


def split2(v, axis=1):
    hi = v.astype(BF)
    lo = (v - hi.astype(F32)).astype(BF)
    return jnp.concatenate([hi, lo], axis=axis)


def dot_split(v, m):
    hi = v.astype(BF)
    lo = (v - hi.astype(F32)).astype(BF)
    return dot(hi, m) + dot(lo, m)


def split_dot(m, v):
    hi = v.astype(BF)
    lo = (v - hi.astype(F32)).astype(BF)
    return dot(m, hi) + dot(m, lo)


def sigmoid(v):
    return 1.0 / (1.0 + jnp.exp(-v))


def tri(kind):
    row = lax.broadcasted_iota(jnp.int32, (Q, Q), 0)
    col = lax.broadcasted_iota(jnp.int32, (Q, Q), 1)
    return {"ge": row >= col, "le": row <= col, "gt": row > col}[kind]


def slot_heads(heads, per):
    nz = heads // per
    own = HEADS // nz
    bits = per.bit_length() - 1
    slot = lax.broadcasted_iota(jnp.int32, (heads, HEADS), 0)
    head = lax.broadcasted_iota(jnp.int32, (heads, HEADS), 1)
    z = (lax.axis_index("head") - (slot >> bits)) & (nz - 1)
    m = (slot & (per - 1)) ^ lax.axis_index("dp")
    return (head == z * own + lax.axis_index("width") * per + m).astype(F32)


def prep_kernel(
    per, zx, ow, bcdt, rows_in,
    first_o, first2_o, rest_o, rest2_o, out_o, out2_o, bcdt_o, table_o,
):
    di = lax.axis_index("dp")
    wi = lax.axis_index("width")
    wide = 2 * HEADDIM
    for m in range(per):
        for w, whole_o, some_o, o_o in (
            (wi, first_o, rest_o, out_o), (1 - wi, first2_o, rest2_o, out2_o)
        ):
            head = w * per + jnp.bitwise_xor(di, m)
            v = jnp.transpose(zx[:, pl.ds(pl.multiple_of(head * wide, wide), wide)])
            for i in range(2):
                part = v[i * HEADDIM : (i + 1) * HEADDIM, :]
                if m == 0:
                    whole_o[i] = part
                else:
                    some_o[i, (m - 1) * HEADDIM : m * HEADDIM, :] = part
            o_o[m * HEADDIM : (m + 1) * HEADDIM, :] = ow[
                pl.ds(pl.multiple_of(head * HEADDIM, HEADDIM), HEADDIM), :
            ]
    n = bcdt.shape[0]
    bcdt_o[0:n, :] = bcdt[...]
    bcdt_o[n:, :] = jnp.broadcast_to(rows_in[8:9, :], (HALO, bcdt.shape[1])).astype(BF)
    rows = rows_in[0:8, :]
    half = rows.shape[1] // 2
    rows = jnp.where(wi == 0, rows[:, :half], rows[:, half:])
    step = 1
    while step < per:
        size = HEADDIM * step
        parts = [rows[:, i * size : (i + 1) * size] for i in range(half // size)]
        swapped = jnp.concatenate([parts[i ^ 1] for i in range(len(parts))], axis=1)
        rows = jnp.where(jnp.bitwise_and(di, step) != 0, swapped, rows)
        step *= 2
    table_o[...] = rows


def entry_first(per, hm, ho, hh, bcdt, table, sel, o, xn_o, buf, between, edges):
    xnh_o, r_o, raw_o, rawh_o, dt_o, sig_o = o.xnh, o.r, o.raw, o.rawh, o.dt, o.sig
    cl_o, clt_o, rate_o, wdt_o, b_o = o.cl, o.clt, o.rate, o.wdt, o.b
    rows = hm.shape[0]
    state = b_o.shape[1]
    per_head = dot(table[...], sel[...], HIGH)
    bias = per_head[5:6, :]
    rate = -jnp.exp(per_head[6:7, :])
    rate_o[...] = rate
    wbc = bcdt.at[0 : 2 * state, :]
    wdt_o[...] = dot(
        slot_heads(rate.shape[1], per).astype(BF), bcdt[2 * state : 2 * state + HEADS, :]
    ).astype(BF)
    wdt = wdt_o
    gain = bcdt[2 * state + HEADS : 2 * state + HEADS + 1, :].astype(F32)
    blocks = rows // Q
    lower = tri("ge").astype(F32)

    def norm(left, right):
        h = jnp.concatenate([left, right], axis=1).astype(F32)
        r = lax.rsqrt(jnp.mean(h * h, axis=1, keepdims=True) + EPS)
        return (h * r * gain).astype(BF), r

    def first(i, carry):
        here = pl.ds(pl.multiple_of(i * Q, Q), Q)
        xn, r = norm(hm[here, :], ho[here, :])
        xn_o[here, :] = xn
        r_o[here, :] = r
        raw = dot_t(xn, wbc[...])
        raw_o[here, :] = raw
        buf[pl.ds(pl.multiple_of(HALO + i * Q, HALO), Q), :] = raw
        steps = dot_t(xn, wdt[...]) + bias
        dt = jax.nn.softplus(steps)
        dt_o[here, :] = dt
        sig_o[here, :] = sigmoid(steps)
        da = dt * rate
        cl_o[here, :] = dot(lower, da, HIGH)
        clt_o[:, here] = lax.dot_general(
            da, lower, (((0,), (1,)), ((), ())), precision=HIGH, preferred_element_type=F32
        )
        return carry

    lax.fori_loop(0, blocks // 2, first, 0, unroll=2)
    between()
    lax.fori_loop(blocks // 2, blocks, first, 0, unroll=2)
    edges()
    half = hm.shape[1]
    xnh, _ = norm(hh[:, :half], hh[:, half:])
    xnh = jnp.where(lax.axis_index("head") > 0, xnh.astype(F32), 0.0).astype(BF)
    xnh_o[...] = xnh
    buf[0:HALO, :] = dot_t(xnh, wbc[...])
    rawh_o[...] = buf[0:HALO, :]


def entry_second(cbc, o, tot_o, buf):
    u_o, b_o, c_o, dt_o, cl_o, clt_o = o.ubc, o.b, o.c, o.dt, o.cl, o.clt
    dt2_o, e12_o, tl2_o, dttl2_o, ec2_o, edt2_o = o.dt2, o.e12, o.tl2, o.dttl2, o.ec2, o.edt2
    state = b_o.shape[1]
    blocks = b_o.shape[0] // Q

    def second(i, carry):
        here = pl.ds(pl.multiple_of(i * Q, Q), Q)
        win = buf[pl.ds(pl.multiple_of(i * Q, Q), Q + HALO), :]
        u = jnp.zeros((Q, win.shape[1]), F32)
        for k in range(4):
            u = u + cbc[k : k + 1, :] * win[HALO - 3 + k : HALO - 3 + k + Q, :]
        u_o[here, :] = u
        v = u * sigmoid(u)
        b_o[here, :] = v[:, :state].astype(BF)
        c_o[here, :] = v[:, state:].astype(BF)
        return carry

    lax.fori_loop(0, blocks, second, 0, unroll=2)
    tots = [cl_o[i * Q + Q - 1 : i * Q + Q, :] for i in range(blocks)]
    ctot = functools.reduce(lambda x, y: x + y, tots)
    heads = clt_o.shape[0]
    column = functools.reduce(
        lambda x, y: x + y, [clt_o[:, i * Q + Q - 1 : i * Q + Q] for i in range(blocks)]
    )
    hi = column.astype(BF)
    mid = (column - hi.astype(F32)).astype(BF)
    low = (column - hi.astype(F32) - mid.astype(F32)).astype(BF)
    lane = lax.broadcasted_iota(jnp.int32, (heads, tot_o.shape[1]), 1)
    tot_o[...] = jnp.where(
        lane == 0,
        hi.astype(F32),
        jnp.where(lane == 1, mid.astype(F32), jnp.where(lane == 2, low.astype(F32), 0.0)),
    ).astype(BF)
    off = jnp.zeros_like(ctot)
    for i in range(blocks):
        here = slice(i * Q, i * Q + Q)
        cl = cl_o[here, :]
        dt = dt_o[here, :]
        tail = jnp.exp(tots[i] - cl)
        dt2_o[here, :] = split2(dt)
        e12_o[here, :] = split2(jnp.exp(cl))
        tl2_o[here, :] = split2(tail)
        dttl2_o[here, :] = split2(dt * tail)
        ec2_o[here, :] = split2(jnp.exp(cl + off))
        edt2_o[here, :] = split2(dt * jnp.exp(ctot - cl - off))
        off = off + tots[i]


def decay(cl, clt, h, mask):
    return jnp.exp(jnp.where(mask, cl[:, h : h + 1] - clt[h : h + 1, :], NEG))


def lane_masks():
    lane = lax.broadcasted_iota(jnp.int32, (1, Q), 1)
    low = (lane < HEADDIM).astype(F32)
    return low.astype(BF), (1.0 - low).astype(BF)


def project(s, per, xn, o, w, cw, ex, z_o, xr_o, xrh_o, u_o, xdt_o, msg, buf, acc):
    rows = z_o.shape[0]
    gc = per * HEADDIM
    cols = slice(s * gc, s * gc + gc)
    xh = dot_t(o.xnh[...], w[1, cols, :])
    buf[0:HALO, :] = xh
    xrh_o[...] = xh
    acc[...] = jnp.zeros_like(acc)
    cut = rows // 2 if rows // 2 % Q == 0 else rows

    def part(j, carry):
        base = j * cut
        here = pl.ds(pl.multiple_of(base, Q), cut)
        buf[pl.ds(pl.multiple_of(base + HALO, HALO), cut), :] = dot_t(xn[here, :], w[1, cols, :])
        z_o[here, :] = dot_t(xn[here, :], w[0, cols, :])
        for i in range(cut // Q):
            here = pl.ds(pl.multiple_of(base + i * Q, Q), Q)
            win = buf[pl.ds(pl.multiple_of(base + i * Q, Q), Q + HALO), :]
            u = jnp.zeros((Q, gc), F32)
            for k in range(4):
                u = u + cw[k : k + 1, cols] * win[HALO - 3 + k : HALO - 3 + k + Q, :]
            xr_o[here, :] = win[HALO:, :].astype(BF)
            u_o[here, :] = u
            xs = u * sigmoid(u)
            xdt_o[here, :] = (xs * dot(o.dt2[here, :], ex[:, cols])).astype(BF)
            acc[...] += t_dot((xs * dot(o.edt2[here, :], ex[:, cols])).astype(BF), o.b[here, :])
        return carry

    lax.fori_loop(0, rows // cut, part, 0)
    msg[cols, :] = acc[...].astype(BF)


def inside(s, per, xdt, o, y_o):
    mask = tri("ge")
    low, high = lane_masks()
    rows = xdt.shape[0]
    some = 4 if rows % (4 * Q) == 0 else 1

    def part(j, carry):
        for i in range(some):
            here = pl.ds(pl.multiple_of((j * some + i) * Q, Q), Q)
            g = dot_t(o.c[here, :], o.b[here, :])
            clv, cltv = o.cl[here, :], o.clt[:, here]
            for p in range(xdt.shape[1] // Q):
                lanes = slice(p * Q, p * Q + Q)
                h = s * per + 2 * p
                ws = [(g * decay(clv, cltv, k, mask)).astype(BF) for k in (h, h + 1)]
                x = xdt[here, lanes]
                y_o[here, lanes] = dot(
                    jnp.concatenate(ws, axis=1), jnp.concatenate([x * low, x * high], axis=0)
                ).astype(BF)
        return carry

    lax.fori_loop(0, rows // (some * Q), part, 0)


class Named:
    def __init__(self, names, refs):
        for name, ref in zip(names, refs):
            setattr(self, name, ref)


KEPT = (
    "xnh", "r", "raw", "rawh", "ubc", "b", "c", "dt", "sig", "cl", "clt", "dt2", "e12", "tl2",
    "dttl2", "ec2", "edt2", "rate", "wdt", "tot", "table", "bcdt",
)


def front_kernel(per, nz, *refs):
    hidden, first, first2, rest, rest2, bcdt, table, cbc, sel, ex, refs = take(refs, *[0] * 10)
    out_mine, out2, cot, refs = take(refs, 0, 0, 0)
    w_o, wo_o, cot_o, xn_o, refs = take(refs, 0, 0, 0, 0)
    z_o, xr_o, u_o, xdt_o, y_o, messages_o, xrh_o, refs = take(refs, *[nz] * 5, nz - 1, nz)
    kept, refs = refs[: len(KEPT)], refs[len(KEPT) :]
    o = Named(KEPT, kept)
    z_v, xr_v, u_v, xdt_v, y_v, refs = take(refs, *[nz] * 5)
    w, ho, eh, xn, msg, buf, bcbuf, acc, sends, receives, locals_ = refs
    bc = o.bcdt
    rows, half = hidden.shape
    gc = per * HEADDIM
    top = nz * gc
    sibling = {"width": 1 - lax.axis_index("width")}
    z_peers = line_peers(nz, 1)
    d_peers = plane_peers(per)
    used = [0]

    def copy(source, target, peer):
        i = used[0]
        used[0] += 1
        return remote(source, target, sends, receives, i, peer)

    left, right = pl.ds(0, half), pl.ds(half, half)
    swap_first = copy(first2, w.at[:, pl.ds(0, HEADDIM), right], sibling)
    swap_rest = copy(rest2, w.at[:, pl.ds(HEADDIM, gc - HEADDIM), right], sibling)
    swap_hidden = copy(hidden, ho, sibling)
    swap_bc = copy(bcdt, bc.at[:, right], sibling)
    swap_out = copy(out2, wo_o.at[pl.ds(0, gc), right], sibling)
    swap_cot = copy(cot, cot_o, sibling)
    z_table, z_w, z_out, z_state = [], [], [], {s: [] for s in range(nz)}
    for k, peer in enumerate(z_peers):
        s = k + 1
        z_table.append(copy(table, o.table.at[:, pl.ds(s * gc, gc)], peer))
        own = w.at[:, pl.ds(0, HEADDIM), :]
        z_w.append(copy(own, w.at[:, pl.ds(s * gc, HEADDIM), :], peer))
        z_out.append(
            copy(wo_o.at[pl.ds(0, HEADDIM), :], wo_o.at[pl.ds(s * gc, HEADDIM), :], peer)
        )
        for j in range(nz):
            some = pl.ds(j * gc, gc + HALO if j == nz - 1 else gc)
            z_state[j].append(copy(msg.at[some, :], messages_o[k].at[some, :], peer))
    last = pl.ds(rows - HALO, HALO)
    edge1 = copy(hidden.at[last, :], eh.at[:, left], z_peers[0])
    edge2 = copy(ho.at[last, :], eh.at[:, right], z_peers[0])
    p_w = {s: [] for s in range(1, nz)}
    p_out = {s: [] for s in range(1, nz)}
    for s in range(1, nz):
        for k, peer in enumerate(d_peers):
            mine = pl.ds(s * gc, HEADDIM)
            there = pl.ds(s * gc + (k + 1) * HEADDIM, HEADDIM)
            via, to = k, peer
            if k + 1 == per - 1:
                first_hop = s % 2
                mine = pl.ds(s * gc + (first_hop + 1) * HEADDIM, HEADDIM)
                to = d_peers[1 - first_hop]
            p_w[s].append(copy(w.at[:, mine, :], w.at[:, there, :], to))
            p_out[s].append(copy(wo_o.at[mine, :], wo_o.at[there, :], to))

    places = [0]

    def local(source, target):
        i = places[0]
        places[0] += 1
        found = pltpu.make_async_copy(source, target, locals_.at[i])
        found.start()
        return found

    ready = [
        local(first, w.at[:, pl.ds(0, HEADDIM), left]),
        local(rest, w.at[:, pl.ds(HEADDIM, gc - HEADDIM), left]),
        local(bcdt, bc.at[:, left]),
        local(table, o.table.at[:, pl.ds(0, gc)]),
        local(out_mine, wo_o.at[pl.ds(0, gc), left]),
    ]
    meet([sibling, *z_peers, *line_peers(nz, -1), *d_peers])
    start([swap_first, *z_table, swap_hidden, swap_bc, edge1])
    ready[0].wait()
    arrive([swap_first])
    start([z_w[0], swap_rest, swap_out, swap_cot])
    for c in ready[1:]:
        c.wait()
    arrive([swap_hidden])
    start([edge2])
    arrive([swap_bc, *z_table])
    pending = []

    def pass_on(copies, s):
        arrive([copies[s % 2]])
        start([copies[2]])

    def between():
        arrive([z_w[0]])
        start([*p_w[1][:2], *z_w[1:]])

    def edges():
        arrive([edge1, edge2])

    entry_first(per, hidden, ho, eh, bc, o.table, sel, o, xn, bcbuf, between, edges)
    pass_on(p_w[1], 1)
    arrive([z_w[1], swap_rest])
    start(p_w[2][:2])
    entry_second(cbc, o, o.tot, bcbuf)
    msg[top:, :] = o.tot[...]
    pending.append(local(xn, xn_o))
    for k in range(3, nz):
        arrive([z_w[k - 1]])
        start(p_w[k][:2])
    arrive([swap_out])
    start(z_out)
    taps = o.table

    def project_group(s):
        project(
            s, per, xn, o, w, taps, ex, z_v[s], xr_v[s], xrh_o[s], u_v[s], xdt_v[s], msg, buf, acc
        )
        start(z_state[s])
        for a, b in ((z_v, z_o), (xr_v, xr_o), (u_v, u_o), (xdt_v, xdt_o)):
            pending.append(local(a[s], b[s]))

    def inside_group(s):
        inside(s, per, xdt_v[s], o, y_v[s])
        pending.append(local(y_v[s], y_o[s]))

    project_group(0)
    for k in range(2, nz):
        pass_on(p_w[k], k)
    inside_group(0)
    for k in range(1, nz):
        arrive([z_out[k - 1]])
        start(p_out[k][:2])
    for s in range(1, nz):
        arrive([p_w[s][1 - s % 2], p_w[s][2]])
        project_group(s)
        if s == nz - 2:
            for k in range(1, nz):
                pass_on(p_out[k], k)
    pending.append(local(w, w_o))
    for s in range(1, nz):
        inside_group(s)
    everything = [swap_first, swap_rest, swap_hidden, swap_bc, swap_out, swap_cot, edge1, edge2]
    everything += [*z_table, *z_w, *z_out]
    states = [c for s in range(nz) for c in z_state[s]]
    everything += states
    for s in range(1, nz):
        everything += p_w[s] + p_out[s]
        arrive([p_out[s][1 - s % 2], p_out[s][2]])
    arrive([swap_cot, *states])
    for c in everything:
        c.wait_send()
    for c in pending:
        c.wait()


def head_scale(clt, first, per, state):
    return jnp.concatenate(
        [
            jnp.broadcast_to(jnp.exp(clt[h : h + 1, Q - 1 : Q]), (HEADDIM, state))
            for h in range(first, first + per)
        ],
        axis=0,
    )


def from_messages(messages, sign, groups, per, state, store, valid=None):
    nz = len(messages) + 1
    gc = per * HEADDIM
    top = nz * gc
    totals = [
        sum(m[top:, i : i + 1].astype(F32) for i in range(3)) for m in messages
    ]
    for at, j in enumerate(groups):
        total = jnp.zeros((gc, state), F32)
        faded = jnp.zeros((per, 1), F32)
        for k in range(1, nz):
            there = (j - sign * k) % nz
            scale = jnp.exp(faded)
            scale = jnp.concatenate(
                [jnp.broadcast_to(scale[h : h + 1, :], (HEADDIM, state)) for h in range(per)],
                axis=0,
            )
            part = scale * messages[k - 1][there * gc : there * gc + gc, :].astype(F32)
            if valid is not None:
                part = jnp.where(valid(k), part, 0.0)
            total = total + part
            faded = faded + totals[k - 1][there * per : there * per + per, :]
        store[at * gc : at * gc + gc, :] = total


def mid_kernel(groups, per, *refs):
    nz = len(groups)
    y_in, u, z, cot, cot2, b, c, clt, e12, dttl2, refs = take(refs, nz, nz, nz, *[0] * 7)
    u2, z2, ec2, c2, hidden, refs = take(refs, nz, nz, 0, 0, 0)
    messages, tot, table, ex, wout, limit, refs = take(refs, nz - 1, *[0] * 5)
    gain, dsk = table.at[4:5, :], table.at[7:8, :]
    st_o, mask_o, dys_o, dz_o, yn_o, out_o, msg_o, gn_o, sk_o, refs = take(
        refs, nz, 0, nz, *[0] * 6
    )
    s, acc, yv, dv, br, br_out, br_in, sm_out, sm_in, gg, sends, receives = refs
    step = pl.program_id(0)
    tiles = pl.num_programs(0) - 1
    rows, half = cot.shape
    gc = per * HEADDIM
    state = s.shape[1]
    sibling = {"width": 1 - lax.axis_index("width")}

    def copies(k):
        return [
            remote(sm_out.at[k], sm_in.at[k], sends, receives, 2 * k, sibling),
            remote(br_out.at[k], br_in.at[k], sends, receives, 2 * k + 1, sibling),
        ]

    @pl.when(step == 0)
    def _():
        meet([sibling])
        z_index = lax.axis_index("head")
        from_messages(messages, 1, groups, per, state, s, lambda k: z_index - k >= 0)
        acc[...] = jnp.zeros_like(acc)
        gn_o[...] = jnp.zeros_like(gn_o)
        sk_o[...] = jnp.zeros_like(sk_o)

    @pl.when(step < tiles)
    def _():
        slot = lax.rem(step, 2)
        row = lax.broadcasted_iota(jnp.int32, (rows, 1), 0) + step * rows
        keep = row < limit[0, 0]
        for i, v in enumerate((cot, cot2)):
            mask_o[:, i * half : i * half + half] = jnp.where(keep, v[...].astype(F32), 0.0).astype(
                BF
            )
        dv[slot] = dot_t(mask_o[...], wout[...])
        lane = lax.broadcasted_iota(jnp.int32, (Q, Q), 1)
        for i in range(rows // Q):
            part = slice(i * Q, i * Q + Q)
            cc, bb = c[part, :], b[part, :]
            square = jnp.zeros((Q, gc), F32)
            inner = jnp.zeros((Q, gc), F32)
            for j in groups:
                here = slice(j * gc, j * gc + gc)
                sv = s[here, :]
                sb = sv.astype(BF)
                st_o[j][i] = sb
                x = u[j][part, :]
                x = x * sigmoid(x)
                e1 = dot(e12[part, :], ex[:, here])
                y = y_in[j][part, :].astype(F32) + e1 * dot_t(cc, sb) + dsk[:, here] * x
                yv[slot, part, here] = y
                xt = (x * dot(dttl2[part, :], ex[:, here])).astype(BF)
                s[here, :] = head_scale(clt.at[:, part], j * per, per, state) * sv + t_dot(xt, bb)
                zz = z[j][part, :]
                gz = y * (zz * sigmoid(zz))
                g = gz * gain[:, here]
                gg[part, here] = g.astype(BF)
                square = square + gz * gz
                inner = inner + g * dv[slot, part, here]
            sm_out[step, part, :] = jnp.where(
                lane == 0,
                jnp.sum(square, axis=1, keepdims=True),
                jnp.sum(inner, axis=1, keepdims=True),
            )
        branch = dot(gg[...], wout[...])
        br[slot] = branch[:, :half]
        br_out[step] = branch[:, half:].astype(BF)
        for copy in copies(step):
            copy.start()

    @pl.when(step > 0)
    def _():
        k = step - 1
        slot = lax.rem(k, 2)
        for copy in copies(k):
            copy.wait()
        count = nz * gc * 2
        for i in range(rows // Q):
            part = slice(i * Q, i * Q + Q)
            both = sm_out[k, part, :] + sm_in[k, part, :]
            r2 = lax.rsqrt(both[:, 0:1] / count + EPS)
            pull = both[:, 1:2] * (r2 * r2 * r2) / count
            row = lax.broadcasted_iota(jnp.int32, (Q, 1), 0) + k * rows + i * Q
            keep = jnp.where(row < limit[0, 0], r2, 0.0)
            out_o[part, :] = (
                hidden[part, :].astype(F32)
                + keep * (br[slot, part, :] + br_in[k, part, :].astype(F32))
            ).astype(BF)
            for j in groups:
                here = slice(j * gc, j * gc + gc)
                gn = gain[:, here]
                zz = z2[j][part, :]
                sz = sigmoid(zz)
                silu = zz * sz
                y = yv[slot, part, here]
                gz = y * silu
                dy_n = dv[slot, part, here]
                gr = gz * r2
                yn_o[part, here] = (gr * gn).astype(BF)
                gn_o[:, here] += jnp.sum(dy_n * gr, axis=0, keepdims=True)
                dgz = r2 * gn * dy_n - gz * pull
                dys = dgz * silu
                dys_o[j][part, :] = dys.astype(BF)
                dz_o[part, here] = (dgz * y * (sz + silu * (1.0 - sz))).astype(BF)
                x = u2[j][part, :]
                x = x * sigmoid(x)
                sk_o[:, here] += jnp.sum(dys * x, axis=0, keepdims=True)
                acc[here, :] += t_dot(
                    (dys * dot(ec2[part, :], ex[:, here])).astype(BF), c2[part, :]
                )

    @pl.when(step == tiles)
    def _():
        top = nz * gc
        msg_o[0:top, :] = acc[...].astype(BF)
        msg_o[top:, :] = tot[...]


def line_peers(count, sign):
    z = lax.axis_index("head")
    return [{"head": lax.rem(z + sign * k + count, count)} for k in range(1, count)]


def plane_peers(count):
    d = lax.axis_index("dp")
    return [{"dp": jnp.bitwise_xor(d, m)} for m in range(1, count)]


def meet(peers):
    barrier = pltpu.get_barrier_semaphore()
    for peer in peers:
        pl.semaphore_signal(barrier, inc=1, device_id=peer, device_id_type=MESH)
    pl.semaphore_wait(barrier, len(peers))


def remote(source, target, sends, receives, i, peer):
    return pltpu.make_async_remote_copy(
        src_ref=source,
        dst_ref=target,
        send_sem=sends.at[i],
        recv_sem=receives.at[i],
        device_id=peer,
        device_id_type=MESH,
    )


def conv_back(d, nxt, taps, raw, grad_o, out_o):
    win = jnp.concatenate([d, nxt[...]], axis=0)
    back = jnp.zeros_like(d)
    sums = []
    for k in range(4):
        part = win[3 - k : 3 - k + Q, :]
        back = back + taps[k : k + 1, :] * part
        sums.append(jnp.sum(raw * part, axis=0, keepdims=True))
    grad_o[...] += jnp.concatenate(sums, axis=0)
    out_o[...] = back.astype(BF)
    nxt[...] = d[0:8, :]


def conv_edge(first, taps, rawh, grad_o, outh_o):
    first = first[...]
    win = jnp.concatenate([jnp.zeros((HALO, first.shape[1]), F32), first], axis=0)
    back = jnp.zeros((HALO, first.shape[1]), F32)
    sums = []
    for k in range(4):
        part = win[3 - k : 3 - k + HALO, :]
        back = back + taps[k : k + 1, :] * part
        sums.append(jnp.sum(rawh[...] * part, axis=0, keepdims=True))
    grad_o[...] += jnp.concatenate(sums, axis=0)
    outh_o[...] = back.astype(BF)


def scan_back_kernel(groups, per, *refs):
    n = len(groups)
    nz = n
    xdt, dys, u, xr, st, xrh, rest = take(refs, n, n, n, n, n, n)
    (b, c, cl, clt, dt, sig, dt2, e12, tl2), rest = rest[:9], rest[9:]
    (ubc, braw, brawh, table, cbc, rate, ex, er), rest = rest[:8], rest[8:]
    cw, dsk = table.at[0:4, :], table.at[7:8, :]
    message, yn, masked, dz, xn, rest = take(rest, *[0] * 5)
    dx_o, dxh_o, gcx_o, rest = take(rest, n, n, n)
    dt_o, ga_o, gbias_o, bc_o, bch_o, gcb_o, etot = rest[:7]
    messages, got, line, rest = take(rest[7:], nz - 1, per - 1, nz - 1)
    du_next, rest = take(rest, n)
    db_next, early, low, dxi, dbi, dci, dai, kt, ds, vs, sends, receives = rest
    turn = pl.program_id(0)
    step = turn - nz
    blocks = (pl.num_programs(0) - nz) // 2
    heads = dt.shape[1]
    state = b.shape[1]
    gc = per * HEADDIM
    line_at, plane_at = 0, nz - 1
    back_at = plane_at + nz * (per - 1)

    def state_copies():
        return [
            remote(message, messages[i], sends, receives, line_at + i, peer)
            for i, peer in enumerate(line_peers(nz, -1))
        ]

    def plane_copies(s):
        return [
            remote(
                early.at[i + 1, s], got[i].at[s], sends, receives, plane_at + s * (per - 1) + i, peer
            )
            for i, peer in enumerate(plane_peers(per))
        ]

    def line_copy(s):
        return remote(
            low.at[s], line[s - 1], sends, receives, back_at + s - 1, line_peers(nz, -1)[s - 1]
        )

    order = [*range(1, nz), 0]
    leave = [0, nz + blocks // 4, nz + blocks - 1, nz + blocks + blocks // 4]
    added = [nz + blocks // 2, nz + blocks, nz + blocks + 3 * blocks // 8, nz + 2 * blocks - 1]

    @pl.when(turn == 0)
    def _():
        meet([*line_peers(nz, -1), *line_peers(nz, 1), *plane_peers(per)])
        for copy in state_copies():
            copy.start()

    @pl.when(turn < nz)
    def _():
        s = lax.rem(turn + 1, nz)
        g = t_dot(yn[...], masked[...]).astype(BF)
        for m in range(per):
            early[m, s, :HEADDIM, :] = g[m * HEADDIM : (m + 1) * HEADDIM, :]
        g = t_dot(dz[...], xn[...]).astype(BF)
        for m in range(per):
            early[m, s, HEADDIM:, :] = g[m * HEADDIM : (m + 1) * HEADDIM, :]

    for s, when in zip(order, leave):

        @pl.when(turn == when)
        def _(s=s):
            for copy in plane_copies(s):
                copy.start()

    @pl.when(jnp.logical_and(step >= 0, step < blocks))
    def _():
        rows = pl.ds(pl.multiple_of(step * Q, Q), Q)
        mask = tri("ge")
        lower, upper_lanes = lane_masks()
        g = dot_t(c[...], b[...])
        clv, cltv = cl[...], clt[...]
        lane = lax.broadcasted_iota(jnp.int32, (Q, heads), 1)
        dg = jnp.zeros((Q, Q), F32)
        rsum = jnp.zeros((Q, heads), F32)
        for s in groups:
            for p in range(per // 2):
                here = slice(p * Q, p * Q + Q)
                x = xdt[s][:, here]
                dy = dys[s][:, here]
                pp = dot_t(dy, jnp.concatenate([x * lower, x * upper_lanes], axis=0))
                ws = []
                for j in range(2):
                    h = s * per + 2 * p + j
                    ell = decay(clv, cltv, h, mask)
                    ws.append((g * ell).astype(BF))
                    pe = pp[:, j * Q : j * Q + Q] * ell
                    dg = dg + pe
                    m = pe * g
                    rsum = jnp.where(lane == h, jnp.sum(m, axis=1, keepdims=True), rsum)
                    kt[h : h + 1, :] = jnp.sum(m, axis=0, keepdims=True)
                dxi[rows, s * gc + p * Q : s * gc + p * Q + Q] = t_dot(
                    jnp.concatenate(ws, axis=0),
                    jnp.concatenate([dy * lower, dy * upper_lanes], axis=0),
                )
        dgb = dg.astype(BF)
        dci[rows, :] = dot(dgb, b[...])
        dbi[rows, :] = t_dot(dgb, c[...])
        upper = tri("le").astype(F32)
        dai[rows, :] = dot(upper, rsum, HIGH) - dot_t(upper, kt[...], HIGH)

    @pl.when(step == blocks)
    def _():
        for copy in state_copies():
            copy.wait()
        z = lax.axis_index("head")
        from_messages(messages, -1, groups, per, state, ds, lambda k: z + k < nz)
        for i in range(n):
            du_next[i][...] = jnp.zeros_like(du_next[i])
            gcx_o[i][...] = jnp.zeros_like(gcx_o[i])
        db_next[...] = jnp.zeros_like(db_next)
        gcb_o[...] = jnp.zeros_like(gcb_o)
        ga_o[...] = jnp.zeros_like(ga_o)
        gbias_o[...] = jnp.zeros_like(gbias_o)

    @pl.when(step >= blocks)
    def _():
        rows = pl.ds(pl.multiple_of((2 * blocks - 1 - step) * Q, Q), Q)
        rsum = jnp.zeros((Q, heads), F32)
        gsum = jnp.zeros((Q, heads), F32)
        ddt = jnp.zeros((Q, heads), F32)
        dbs = dbi[rows, :]
        dcs = dci[rows, :]
        for s in groups:
            here = slice(s * gc, s * gc + gc)
            ehere = er[here, :]
            sb = st[s][0]
            dsv = ds[here, :]
            dsb = dsv.astype(BF)
            dy = dys[s][...].astype(F32)
            dye = dy * dot(e12[...], ex[:, here])
            dyb = dye.astype(BF)
            rsum = rsum + dot((dye * dot_t(c[...], sb)).astype(BF), ehere)
            dcs = dcs + dot(dyb, sb)
            bds = dot_t(b[...], dsb)
            tail = dot(tl2[...], ex[:, here])
            dtx = dot(dt2[...], ex[:, here])
            uu = u[s][...]
            su = sigmoid(uu)
            xs = uu * su
            xt = xs * dtx * tail
            gsum = gsum + dot((xt * bds).astype(BF), ehere)
            dbs = dbs + dot(xt.astype(BF), dsb)
            dxdt = dxi[rows, here] + tail * bds
            ddt = ddt + dot((dxdt * xs).astype(BF), ehere)
            eds = head_scale(clt, s * per, per, state) * dsv
            ev = eds * sb.astype(F32)
            for j in range(per):
                h = s * per + j
                vs[h : h + 1, :] = jnp.sum(
                    ev[j * HEADDIM : (j + 1) * HEADDIM, :], axis=0, keepdims=True
                )
            ds[here, :] = eds + t_dot(dyb, c[...])
            du = (dxdt * dtx + dsk[:, here] * dy) * (su + xs * (1.0 - su))
            conv_back(
                du, du_next[s], cw.at[:, here], xr[s][...].astype(F32), gcx_o[s], dx_o[s]
            )
        vrow = dot_t(jnp.ones((8, state), F32), vs[...], HIGH)
        da = (
            dai[rows, :]
            + split_dot(tri("le").astype(BF), rsum)
            + split_dot(tri("gt").astype(BF), gsum)
            + vrow[0:1, :]
        )
        draw = (rate[...] * da + ddt) * sig[...]
        dt_o[...] = draw.astype(BF)
        ga_o[...] += jnp.sum(da * dt[...], axis=0, keepdims=True)
        gbias_o[...] += jnp.sum(draw, axis=0, keepdims=True)
        d = jnp.concatenate([dbs, dcs], axis=1)
        v = ubc[...]
        sv = sigmoid(v)
        conv_back(d * (sv + v * sv * (1.0 - sv)), db_next, cbc, braw[...], gcb_o, bc_o)

    @pl.when(step == 2 * blocks - 1)
    def _():
        for s in groups:
            here = slice(s * gc, s * gc + gc)
            conv_edge(du_next[s], cw.at[:, here], xrh[s], gcx_o[s], dxh_o[s])
        conv_edge(db_next, cbc, brawh, gcb_o, bch_o)

    def add(s):
        for copy in plane_copies(s):
            copy.wait()

        def piece(i, carry):
            part = pl.ds(pl.multiple_of(i * HALO, HALO), HALO)
            total = early[0, s, part, :].astype(F32)
            for v in got:
                total = total + v[s, part, :].astype(F32)
            low[s, part, :] = total.astype(BF)
            return carry

        lax.fori_loop(0, low.shape[1] // HALO, piece, 0, unroll=2)

    for s, when in zip(order, added):

        @pl.when(turn == when)
        def _(s=s):
            add(s)
            if s > 0:
                line_copy(s).start()

    @pl.when(step == 2 * blocks - 1)
    def _():
        for s in range(1, nz):
            line_copy(s).wait()
        for i in range(low.shape[1] // HALO):
            part = slice(i * HALO, i * HALO + HALO)
            total = low[0, part, :].astype(F32)
            for v in line:
                total = total + v[part, :].astype(F32)
            etot[part, :] = total.astype(BF)


class Copies:
    def __init__(self, sends, receives):
        self.sends, self.receives, self.all = sends, receives, []

    def __call__(self, source, target, peer):
        copy = remote(source, target, self.sends, self.receives, len(self.all), peer)
        self.all.append(copy)
        return copy


def start(copies):
    for c in copies:
        c.start()


def arrive(copies):
    for c in copies:
        c.wait_recv()


def tail_kernel(per, nz, *refs):
    dx, dxh, taps, refs = take(refs, nz, nz, nz)
    (dz, dbc, dbch, dti, xn, xnh, w, bc, wdt, early, hidden, cot, r), refs = refs[:13], refs[13:]
    (gain, gbc, grate, gbias, gskip, ggain, rate, ex), refs = refs[:8], refs[8:]
    ea, la, hid_o, norm_o, tbc_o, refs = take(refs, *[0] * 5)
    gx, gs, gdt, lx, ls, sw_out, sw_in, dxn, dxn_out, dxn_in, refs = take(refs, *[0] * 10)
    edge_out, edge_in, edge_sum, edge_next, across, across_in, nrm, nrm2, sums, refs = take(
        refs, *[0] * 9
    )
    rx, rs, zx, zs, nr, nz_r, refs = take(refs, per - 1, per - 1, nz - 1, nz - 1, per - 1, nz - 1)
    stage, sends, receives = refs
    copy = Copies(sends, receives)
    rows, half = hidden.shape
    gc = per * HEADDIM
    channels = nz * gc
    state2 = dbc.shape[1]
    quarter = state2 // per
    share = quarter + HALO
    some_dt = HEADS // per
    wi, di, zi = lax.axis_index("width"), lax.axis_index("dp"), lax.axis_index("head")
    sibling = {"width": 1 - wi}
    d_peers, z_back = plane_peers(per), line_peers(nz, -1)
    left, right = pl.ds(0, half), pl.ds(half, half)
    block = rows // nz

    early_swap = copy(early.at[:, right], ea.at[0, wi], sibling)
    late_swap = copy(sw_out, sw_in, sibling)
    dxn_swap = [
        copy(dxn_out.at[pl.ds(i * block, block), :], dxn_in.at[pl.ds(i * block, block), :], sibling)
        for i in range(nz)
    ]
    edge_swap = copy(edge_out, edge_in, sibling)
    across_swap = copy(across, across_in, sibling)
    p_share, p_x, p_early, p_norm, p_late = [], {s: [] for s in range(nz)}, [], [], []
    for k, peer in enumerate(d_peers):
        m = k + 1
        p_share.append(copy(gs.at[m], rs[k], peer))
        for s in range(nz):
            p_x[s].append(copy(gx.at[s, m], rx[k].at[s], peer))
        p_early.append(copy(ea.at[0], ea.at[m], peer))
        p_norm.append(copy(nrm, nr[k], peer))
        p_late.append(copy(la.at[0], la.at[m], peer))
    z_x, z_share, z_norm = [], [], []
    for k, peer in enumerate(z_back):
        z_x.append(copy(lx.at[k + 1], zx[k], peer))
        z_share.append(copy(ls, zs[k], peer))
        z_norm.append(copy(nrm2, nz_r[k], peer))
    z_edge = copy(edge_sum, edge_next, z_back[0])

    meet([sibling, *z_back, *line_peers(nz, 1), *d_peers])

    start([early_swap])
    ea[0, wi] = early[:, :half]

    g = t_dot(dbc[...], xn[...]) + t_dot(dbch[...], xnh[...])
    stage[0:state2, :] = g
    gdt[...] = split_dot_tr(slot_heads(dti.shape[1], per), t_dot(dti[...], xn[...]))
    per_head = jnp.concatenate([gbias[...], grate[...] * rate[...]], axis=0)
    small = jnp.concatenate(
        [
            jnp.concatenate([v[...] for v in taps], axis=1),
            ggain[...],
            gskip[...],
            dot(split2(per_head), ex[...]),
        ],
        axis=0,
    )
    both = split2(gbc[...])
    both = jnp.concatenate([both, jnp.zeros((4, 2 * state2), BF)], axis=0)
    for m in range(per):
        at = jnp.bitwise_xor(di, m)
        gs[m, 0:quarter, :] = stage[pl.ds(pl.multiple_of(at * quarter, quarter), quarter), :].astype(
            BF
        )
        lanes = jnp.concatenate(
            [
                small[:, (s * per + m) * HEADDIM : (s * per + m + 1) * HEADDIM]
                for s in range(nz)
            ],
            axis=1,
        )
        lower = jnp.concatenate([split2(lanes), both], axis=1)
        upper = gdt[pl.ds(pl.multiple_of(at * some_dt, some_dt), some_dt), :].astype(BF)
        gs[m, quarter:, :] = jnp.concatenate(
            [upper.astype(F32), lower.astype(F32)], axis=0
        ).astype(BF)
    start(p_share)
    arrive([early_swap])
    order = [*range(1, nz), 0]
    for s in order:
        g = t_dot(dx[s][...], xn[...]) + t_dot(dxh[s][...], xnh[...])
        for m in range(per):
            gx[s, m] = g[m * HEADDIM : (m + 1) * HEADDIM, :].astype(BF)
        start(p_x[s])
    start(p_early)

    def add_share():
        arrive(p_share)
        for i in range(share // HALO):
            here = slice(i * HALO, i * HALO + HALO)
            total = gs[0, here, :].astype(F32)
            for v in rs:
                total = total + v[here, :].astype(F32)
            sums[here, :] = total
        pack(sums)
        start(z_share)

    def pack(v):
        ls[0:quarter, :] = v[0:quarter, :].astype(BF)
        n = nz * HEADDIM
        rest = v[quarter:, :]
        a = rest[:, 0:n] + rest[:, n : 2 * n]
        b = rest[:, 2 * n : 2 * n + state2] + rest[:, 2 * n + state2 :]
        low_rows = jnp.concatenate([split2(a), split2(b)], axis=1)
        row = lax.broadcasted_iota(jnp.int32, (HALO, 1), 0)
        ls[quarter:, :] = jnp.where(row < some_dt, rest, low_rows.astype(F32)).astype(BF)

    def add_x(s):
        arrive(p_x[s])
        for i in range(HEADDIM // HALO):
            here = slice(i * HALO, i * HALO + HALO)
            total = gx[s, 0, here, :].astype(F32)
            for v in rx:
                total = total + v[s, here, :].astype(F32)
            lx[s, here, :] = total.astype(BF)
        if s > 0:
            start([z_x[s - 1]])

    for i in range(nz):
        here = slice(i * block, i * block + block)
        total = dot(dz[here, :], w[0])
        for s in range(nz):
            total = total + dot(dx[s][here, :], w[1, s * gc : (s + 1) * gc, :])
        total = total + dot(dbc[here, :], bc[0:state2, :]) + dot(dti[here, :], wdt[...])
        dxn[here, :] = total[:, :half]
        dxn_out[here, :] = total[:, half:].astype(BF)
        start([dxn_swap[i]])
        if i == 0:
            add_share()
            total = dot(dbch[...], bc[0:state2, :])
            for s in range(nz):
                total = total + dot(dxh[s][...], w[1, s * gc : (s + 1) * gc, :])
            edge_sum[...] = total[:, :half]
            edge_out[...] = total[:, half:]
            start([edge_swap])
        if i == 1:
            add_x(order[0])
            arrive([edge_swap])
            edge_sum[...] = edge_sum[...] + edge_in[...]
            start([z_edge])
    if nz > 2:
        add_x(order[1])

    arrive([*dxn_swap, z_edge])
    late_edge = jnp.where(zi < nz - 1, edge_next[...], 0.0)
    gain_v = gain[...]
    norm_sum = jnp.zeros((8, half), F32)
    ones = jnp.ones((8, half), BF)
    for i in range(rows // Q):
        here = slice(i * Q, i * Q + Q)
        v = dxn[here, :] + dxn_in[here, :].astype(F32)
        if i == rows // Q - 1:
            v = v + jnp.concatenate([jnp.zeros((Q - HALO, half), F32), late_edge], axis=0)
        dxn[here, :] = v
        h = hidden[here, :].astype(F32)
        vh = v * h
        norm_sum = norm_sum + jnp.sum(
            (vh * r[here, :]).reshape(Q // 8, 8, half), axis=0
        )
        across[:, here] = split_dot_t(ones, vh * gain_v)
    start([across_swap])
    nrm[...] = norm_sum
    start(p_norm)
    for s in order[2:]:
        add_x(s)
    arrive([across_swap])
    eighth = jnp.full((8, Q), 0.125, F32)
    for i in range(rows // Q):
        here = slice(i * Q, i * Q + Q)
        total = across[:, here] + across_in[:, here]
        total = t_dot(total, eighth, HIGH)
        rr = r[here, :]
        scale = rr * rr * rr / (2 * half)
        rg = rr * gain_v
        for j in range(half // Q):
            lanes = slice(j * Q, j * Q + Q)
            hid_o[here, lanes] = (
                cot[here, lanes].astype(F32)
                + rg[:, lanes] * dxn[here, lanes]
                - hidden[here, lanes].astype(F32) * (scale * total)
            ).astype(BF)
    arrive(p_norm)
    total = nrm[...]
    for v in nr:
        total = total + v[...]
    nrm2[...] = total
    start(z_norm)

    arrive([*z_x, *z_share])
    total = lx[0].astype(F32)
    for v in zx:
        total = total + v[...].astype(F32)
    mine = total.astype(BF)
    la[0, pl.ds(pl.multiple_of(wi * HEADDIM, HEADDIM), HEADDIM), :] = mine[:, :half]
    sw_out[0:HEADDIM, :] = mine[:, half:]
    n = nz * HEADDIM
    total = ls[0:quarter, :].astype(F32)
    for v in zs:
        total = total + v[0:quarter, :].astype(F32)
    sums[0:quarter, :] = total
    sw_out[HEADDIM : HEADDIM + quarter, :] = total[:, half:].astype(BF)
    total = ls[quarter:, :].astype(F32)
    own_small = total[:, 0:HEADDIM] + total[:, n : n + HEADDIM]
    for k, v in enumerate(zs):
        part = v[quarter:, :].astype(F32)
        total = total + part
        at = (k + 1) * HEADDIM
        own_small = own_small + (
            part[:, at : at + HEADDIM] + part[:, n + at : n + at + HEADDIM]
        )
    sums[quarter:, :] = total
    taps_bc = total[:, 2 * n : 2 * n + state2] + total[:, 2 * n + state2 :]
    at = HEADDIM + quarter
    sw_out[at : at + HALO, :] = total[:, half:].astype(BF)
    own_small = split2(own_small)
    own_small = jnp.concatenate(
        [own_small, jnp.zeros((HALO, half - 2 * HEADDIM), BF)], axis=1
    )
    taps_bc2 = split2(taps_bc)
    sw_out[at + HALO : at + 2 * HALO, :] = own_small
    sw_out[at + 2 * HALO : at + 3 * HALO, :] = taps_bc2
    start([late_swap])
    arrive([late_swap])
    there = pl.ds(pl.multiple_of((1 - wi) * HEADDIM, HEADDIM), HEADDIM)
    la[0, there, :] = sw_in[0:HEADDIM, :]
    base = 2 * HEADDIM
    la[0, base : base + share, :] = (
        sums[:, :half] + sw_in[HEADDIM : HEADDIM + share, :].astype(F32)
    ).astype(BF)
    base = base + share
    la[0, pl.ds(pl.multiple_of(base + wi * HALO, HALO), HALO), :] = own_small
    la[0, pl.ds(pl.multiple_of(base + (1 - wi) * HALO, HALO), HALO), :] = sw_in[
        at + HALO : at + 2 * HALO, :
    ]
    start(p_late)
    got = sw_in[at + 2 * HALO : at + 3 * HALO, :].astype(F32)
    taps_bc = taps_bc + got[:, :state2] + got[:, state2:]
    tbc_o[...] = taps_bc[some_dt : some_dt + 4, :]
    arrive(z_norm)
    total = nrm2[...]
    for v in nz_r:
        total = total + v[...]
    norm_o[...] = jnp.sum(total, axis=0, keepdims=True)

    arrive([*p_early, *p_late])
    for c in copy.all:
        c.wait_send()


def finish_kernel(per, ea, la, las, ones, zx_o, ow_o, bcdt_o, cx_o, gn_o, sk_o, bias_o, rate_o):
    di = lax.axis_index("dp")
    some_dt = HEADS // per
    quarter = (bcdt_o.shape[0] - HEADS) // per
    base = 2 * HEADDIM + quarter + HALO
    small = []
    for h in range(2 * per):
        k, j = h // per, h % per
        m = jnp.bitwise_xor(di, j)
        z_part = ea[m, k, HEADDIM:, :].astype(F32)
        x_part = la[m, k * HEADDIM : (k + 1) * HEADDIM, :].astype(F32)
        zx_o[:, h, :] = jnp.transpose(jnp.concatenate([z_part, x_part], axis=0))
        ow_o[h * HEADDIM : (h + 1) * HEADDIM, :] = ea[m, k, :HEADDIM, :].astype(F32)
        v = las[m, base + k * HALO : base + (k + 1) * HALO, :].astype(F32)
        small.append((v[:, :HEADDIM] + v[:, HEADDIM : 2 * HEADDIM])[some_dt:, :])
    for j in range(per):
        m = jnp.bitwise_xor(di, j)
        v = la[m, 2 * HEADDIM : base, :].astype(F32)
        bcdt_o[j * quarter : (j + 1) * quarter, :] = v[:quarter, :]
        at = per * quarter + j * some_dt
        bcdt_o[at : at + some_dt, :] = v[quarter : quarter + some_dt, :]

    @pl.when(pl.program_id(0) == 0)
    def _():
        rows = jnp.concatenate(small, axis=1)
        cx_o[...] = rows[0:4, :]
        gn_o[...] = rows[4:5, :]
        total = dot(rows, ones[...], HIGH)
        sk_o[...] = total[5:6, :]
        bias_o[...] = total[6:7, :] / HEADDIM
        rate_o[...] = total[7:8, :] / HEADDIM


def split_dot_tr(m, v):
    hi = v.astype(BF)
    lo = (v - hi.astype(F32)).astype(BF)
    m = m.astype(BF)
    return t_dot(m, hi) + t_dot(m, lo)


def split_dot_t(m, v):
    hi = v.astype(BF)
    lo = (v - hi.astype(F32)).astype(BF)
    return dot_t(m, hi) + dot_t(m, lo)


def shape(dims, dtype=F32):
    return jax.ShapeDtypeStruct(dims, dtype)


def whole(array):
    rank = len(array.shape)
    return pl.BlockSpec(array.shape, lambda *_: (0,) * rank)


def params():
    return pltpu.CompilerParams(vmem_limit_bytes=VMEM)


def cost(us):
    return pl.CostEstimate(flops=int(us * 1.0e8), bytes_accessed=int(us * 1.0e3), transcendentals=0)


def take(refs, *counts):
    out, at = [], 0
    for n in counts:
        out.append(refs[at] if n == 0 else refs[at : at + n])
        at += max(n, 1)
    return out + [refs[at:]]


def sequence_device(
    hidden, lengths, cotangent, norm_gain, in_zx, in_bcdt, conv_x, conv_bc,
    dt_bias, a_log, d_skip, gnorm_gain, out_w,
):
    rows, half = hidden.shape
    own_heads = in_zx.shape[1]
    nz = lax.axis_size("head")
    ndp = lax.axis_size("dp")
    zi = lax.axis_index("head")
    di = lax.axis_index("dp")
    wi = lax.axis_index("width")
    per = ndp
    heads = nz * per
    channels = heads * HEADDIM
    model = 2 * half
    blocks = rows // Q

    def swap(v):
        return lax.ppermute(v, "width", [(0, 1), (1, 0)])

    gc = per * HEADDIM
    groups = tuple(range(nz))

    onehot = np.kron(np.eye(heads), np.ones((1, HEADDIM)))
    ex = jnp.asarray(np.concatenate([onehot, onehot], axis=0), BF)
    er = jnp.asarray(onehot.T, BF)
    sel = jnp.asarray(onehot.T * (np.arange(channels) % HEADDIM == 0)[:, None], F32)

    each = lambda v: jnp.broadcast_to(v[:, None], (own_heads, HEADDIM)).reshape(1, -1)
    parameter_rows = jnp.concatenate(
        [
            conv_x.astype(F32), gnorm_gain[None].astype(F32), each(dt_bias), each(a_log),
            each(d_skip), jnp.broadcast_to(norm_gain[None].astype(F32), (8, half)),
        ],
        axis=0,
    )
    piece = shape((2, HEADDIM, half), BF)
    some = shape((2, gc - HEADDIM, half), BF)
    outs = shape((gc, half), BF)
    first, first2, rest, rest2, out_mine, out_mine2, bcdt_t, table = pl.pallas_call(
        functools.partial(prep_kernel, per),
        out_shape=[
            piece, piece, some, some, outs, outs,
            shape((2 * STATE + HEADS + HALO, half), BF), shape((8, gc)),
        ],
        compiler_params=params(),
        cost_estimate=cost(4),
        name="prep",
    )(
        in_zx.reshape(half, -1), out_w, jnp.transpose(in_bcdt), parameter_rows
    )
    taps_bc = conv_bc.astype(F32)

    step = lambda i: (i, 0)
    fix = lambda i: (0, 0)
    part = shape((rows, gc), BF)
    full = shape((rows, channels))
    anywhere = pl.BlockSpec(memory_space=pl.ANY)
    vmem = pl.BlockSpec(memory_space=pltpu.VMEM)
    narrow = shape((rows, 2 * heads), BF)
    kept = dict(
        xnh=shape((HALO, model), BF), r=shape((rows, 1)), raw=shape((rows, 2 * STATE)),
        rawh=shape((HALO, 2 * STATE)), ubc=shape((rows, 2 * STATE)), b=shape((rows, STATE), BF),
        c=shape((rows, STATE), BF), dt=shape((rows, heads)), sig=shape((rows, heads)),
        cl=shape((rows, heads)), clt=shape((heads, rows)), dt2=narrow, e12=narrow, tl2=narrow,
        dttl2=narrow, ec2=narrow, edt2=narrow, rate=shape((1, heads)),
        wdt=shape((heads, model), BF),
        bcdt=shape((2 * STATE + HEADS + HALO, model), BF), tot=shape((heads, STATE), BF), table=shape((8, channels)),
    )
    wide_part = shape((rows, gc))
    message_shape = shape((channels + HALO, STATE), BF)
    out_shapes = [
        shape((2, channels, model), BF), shape((channels, model), BF), shape((rows, half), BF),
        shape((rows, model), BF), *[wide_part] * nz, *[part] * nz, *[wide_part] * nz,
        *[part] * nz, *[part] * nz, *[message_shape] * (nz - 1), *[shape((HALO, gc))] * nz,
        *[kept[name] for name in KEPT],
    ]
    held = lambda v: pltpu.VMEM(v.shape, v.dtype)
    remotes = 6 + (3 + nz) * (nz - 1) + 2 + 2 * (nz - 1) * (per - 1)
    out = pl.pallas_call(
        functools.partial(front_kernel, per, nz),
        in_specs=[vmem] * 10 + [anywhere] * 3,
        out_specs=[anywhere] * (4 + 5 * nz + nz - 1) + [vmem] * (nz + len(KEPT)),
        out_shape=out_shapes,
        scratch_shapes=[
            *[held(wide_part)] * nz, *[held(part)] * nz, *[held(wide_part)] * nz,
            *[held(part)] * nz, *[held(part)] * nz, pltpu.VMEM((2, channels, model), BF),
            pltpu.VMEM((rows, half), BF), pltpu.VMEM((HALO, model), BF),
            pltpu.VMEM((rows, model), BF),
            held(message_shape), pltpu.VMEM((rows + HALO, gc), F32),
            pltpu.VMEM((rows + HALO, 2 * STATE), F32), pltpu.VMEM((gc, STATE), F32),
            pltpu.SemaphoreType.DMA((remotes,)), pltpu.SemaphoreType.DMA((remotes,)),
            pltpu.SemaphoreType.DMA((7 + 5 * nz,)),
        ],
        compiler_params=pltpu.CompilerParams(
            vmem_limit_bytes=VMEM, collective_id=1, has_side_effects=True
        ),
        cost_estimate=cost(90),
        name="front",
    )(
        hidden, first, first2, rest, rest2, bcdt_t, table, taps_bc, sel, ex, out_mine, out_mine2,
        cotangent,
    )
    weights, wout, cot_o, xn, out = out[0], out[1], out[2], out[3], out[4:]
    z, xr, u, xdt, y_in, messages, xrh, out = take(out, *[nz] * 5, nz - 1, nz)
    o = Named(KEPT, out)
    xnh, r, braw, brawh, ubc, bs, cs = o.xnh, o.r, o.raw, o.rawh, o.ubc, o.b, o.c
    dt, sig, cl, clt, rate, wdt, totals, table = o.dt, o.sig, o.cl, o.clt, o.rate, o.wdt, o.tot, o.table
    dt2, e12, tl2, dttl2, ec2, edt2 = o.dt2, o.e12, o.tl2, o.dttl2, o.ec2, o.edt2
    limit = (lengths[0] - zi * rows).reshape(1, 1)

    smem = pl.BlockSpec(memory_space=pltpu.SMEM)
    tile = 2 * Q if rows % (2 * Q) == 0 else Q
    tiles = rows // tile
    now = lambda columns: pl.BlockSpec((tile, columns), lambda i: (jnp.minimum(i, tiles - 1), 0))
    then = lambda columns: pl.BlockSpec((tile, columns), lambda i: (jnp.maximum(i - 1, 0), 0))
    out = pl.pallas_call(
        functools.partial(mid_kernel, groups, per),
        grid=(tiles + 1,),
        in_specs=[
            *[now(gc)] * (3 * nz), now(half), now(half), now(STATE), now(STATE),
            pl.BlockSpec((heads, tile), lambda i: (0, jnp.minimum(i, tiles - 1))),
            now(2 * heads), now(2 * heads), *[then(gc)] * (2 * nz), then(2 * heads), then(STATE),
            then(half), *[whole(v) for v in messages], whole(totals), whole(table),
            whole(ex), whole(wout), smem,
        ],
        out_specs=[
            *[
                pl.BlockSpec((tile // Q, gc, STATE), lambda i: (jnp.minimum(i, tiles - 1), 0, 0))
            ] * nz,
            now(model), *[then(gc)] * nz, then(channels), then(channels), then(half),
            pl.BlockSpec((channels + HALO, STATE), fix), pl.BlockSpec((1, channels), fix),
            pl.BlockSpec((1, channels), fix),
        ],
        out_shape=[
            *[shape((blocks, gc, STATE), BF)] * nz, shape((rows, model), BF), *[part] * nz,
            shape((rows, channels), BF), shape((rows, channels), BF), shape((rows, half), BF),
            message_shape, shape((1, channels)), shape((1, channels)),
        ],
        scratch_shapes=[
            pltpu.VMEM((channels, STATE), F32), pltpu.VMEM((channels, STATE), F32),
            pltpu.VMEM((2, tile, channels), F32), pltpu.VMEM((2, tile, channels), F32),
            pltpu.VMEM((2, tile, half), F32), pltpu.VMEM((tiles, tile, half), BF),
            pltpu.VMEM((tiles, tile, half), BF), pltpu.VMEM((tiles, tile, Q), F32),
            pltpu.VMEM((tiles, tile, Q), F32), pltpu.VMEM((tile, channels), BF),
            pltpu.SemaphoreType.DMA((2 * tiles,)), pltpu.SemaphoreType.DMA((2 * tiles,)),
        ],
        compiler_params=pltpu.CompilerParams(
            vmem_limit_bytes=VMEM, collective_id=3, has_side_effects=True
        ),
        cost_estimate=cost(30),
        name="mid",
    )(
        *y_in, *u, *z, cotangent, cot_o, bs, cs, clt, e12, dttl2, *u, *z, ec2, cs, hidden,
        *messages, totals, table, ex, wout, limit,
    )
    states, masked, dys, out = take(out, nz, 0, nz)
    dz, yn, out_hidden, message, g_gain, g_skip = out

    begin = lambda i: jnp.maximum(i - nz, 0)
    first_pass = lambda i: jnp.minimum(begin(i), blocks - 1)
    second_pass = lambda i: jnp.minimum(blocks - 1, 2 * blocks - 1 - begin(i))
    either = lambda i: jnp.minimum(begin(i), 2 * blocks - 1 - begin(i))
    one = lambda i: (first_pass(i), 0)
    two = lambda i: (second_pass(i), 0)
    both = lambda i: (either(i), 0)
    gcol = pl.BlockSpec((rows, gc), lambda i: (0, lax.rem(jnp.minimum(i, nz - 1) + 1, nz)))
    head_columns = lambda v: pl.BlockSpec((Q, v), two)
    early_shape = (nz, 2 * HEADDIM, model)
    exchange = 2 * (nz - 1) + nz * (per - 1)
    out = pl.pallas_call(
        functools.partial(scan_back_kernel, groups, per),
        grid=(nz + 2 * blocks,),
        in_specs=[
            *[pl.BlockSpec((Q, gc), one)] * nz, *[pl.BlockSpec((Q, gc), both)] * nz,
            *[pl.BlockSpec((Q, gc), two)] * (2 * nz),
            *[
                pl.BlockSpec(
                    (1, gc, STATE), lambda i: (second_pass(i), 0, 0)
                )
            ] * nz,
            *[pl.BlockSpec((HALO, gc), fix)] * nz,
            pl.BlockSpec((Q, STATE), both), pl.BlockSpec((Q, STATE), both),
            pl.BlockSpec((Q, heads), one),
            pl.BlockSpec((heads, Q), lambda i: (0, either(i))),
            head_columns(heads), head_columns(heads), head_columns(2 * heads),
            head_columns(2 * heads), head_columns(2 * heads), head_columns(2 * STATE),
            head_columns(2 * STATE), whole(brawh), whole(table), whole(taps_bc), whole(rate),
            whole(ex), whole(er), anywhere, gcol, whole(masked), gcol, whole(xn),
        ],
        out_specs=[
            *[pl.BlockSpec((Q, gc), two)] * nz, *[pl.BlockSpec((HALO, gc), fix)] * nz,
            *[pl.BlockSpec((4, gc), fix)] * nz, head_columns(heads),
            pl.BlockSpec((1, heads), fix), pl.BlockSpec((1, heads), fix),
            head_columns(2 * STATE), pl.BlockSpec((HALO, 2 * STATE), fix),
            pl.BlockSpec((4, 2 * STATE), fix),
            pl.BlockSpec((2 * HEADDIM, model), fix),
        ],
        out_shape=[
            *[shape((rows, gc), BF)] * nz, *[shape((HALO, gc), BF)] * nz, *[shape((4, gc))] * nz,
            shape((rows, heads), BF), shape((1, heads)), shape((1, heads)),
            shape((rows, 2 * STATE), BF), shape((HALO, 2 * STATE), BF), shape((4, 2 * STATE)),
            shape((2 * HEADDIM, model), BF),
        ],
        scratch_shapes=[
            *[pltpu.VMEM(message.shape, BF)] * (nz - 1), *[pltpu.VMEM(early_shape, BF)] * (per - 1),
            *[pltpu.VMEM(early_shape[1:], BF)] * (nz - 1), *[pltpu.VMEM((8, gc), F32)] * nz,
            pltpu.VMEM((8, 2 * STATE), F32), pltpu.VMEM((per, *early_shape), BF),
            pltpu.VMEM(early_shape, BF),
            pltpu.VMEM((rows, channels), F32),
            pltpu.VMEM((rows, STATE), F32), pltpu.VMEM((rows, STATE), F32),
            pltpu.VMEM((rows, heads), F32), pltpu.VMEM((heads, Q), F32),
            pltpu.VMEM((channels, STATE), F32), pltpu.VMEM((heads, STATE), F32),
            pltpu.SemaphoreType.DMA((exchange,)), pltpu.SemaphoreType.DMA((exchange,)),
        ],
        compiler_params=pltpu.CompilerParams(
            vmem_limit_bytes=VMEM, collective_id=0, has_side_effects=True
        ),
        cost_estimate=cost(50),
        name="scan_back",
    )(
        *xdt, *dys, *u, *xr, *states, *xrh, bs, cs, cl, clt, dt, sig, dt2, e12, tl2, ubc, braw,
        brawh, table, taps_bc, rate, ex, er, message, yn, masked,
        dz, xn,
    )
    dx, dxh, g_taps = list(out[:nz]), list(out[nz : 2 * nz]), out[2 * nz : 3 * nz]
    dti, g_rate, g_bias, dbc, dbch, g_taps_bc, early_total = out[3 * nz :]
    quarter = 2 * STATE // per
    share = quarter + HALO
    late_rows = 2 * HEADDIM + share + 2 * HALO
    swap_rows = HEADDIM + share + 2 * HALO
    tail_copies = 4 + nz + (per - 1) * (4 + nz) + 3 * (nz - 1) + 1
    operands = [
        *dx, *dxh, *g_taps, dz, dbc, dbch, dti, xn, xnh, weights, o.bcdt, wdt, early_total, hidden,
        cotangent, r, norm_gain[None].astype(F32), g_taps_bc, g_rate, g_bias, g_skip, g_gain, rate,
        ex,
    ]
    line16 = pltpu.VMEM((HALO, half), F32)
    line8 = pltpu.VMEM((8, half), F32)
    early_all, late_all, grad_hidden, g_norm, g_taps_bc = pl.pallas_call(
        functools.partial(tail_kernel, per, nz),
        in_specs=[vmem] * len(operands),
        out_specs=[vmem] * 5,
        out_shape=[
            shape((per, 2, 2 * HEADDIM, half), BF), shape((per, late_rows, half), BF),
            shape((rows, half), BF), shape((1, half)), shape((4, 2 * STATE)),
        ],
        scratch_shapes=[
            pltpu.VMEM((nz, per, HEADDIM, model), BF), pltpu.VMEM((per, share, model), BF),
            pltpu.VMEM((HEADS, model), F32), pltpu.VMEM((nz, HEADDIM, model), BF),
            pltpu.VMEM((share, model), BF), pltpu.VMEM((swap_rows, half), BF),
            pltpu.VMEM((swap_rows, half), BF), pltpu.VMEM((rows, half), F32),
            pltpu.VMEM((rows, half), BF), pltpu.VMEM((rows, half), BF), line16, line16, line16,
            line16, pltpu.VMEM((8, rows), F32), pltpu.VMEM((8, rows), F32), line8, line8,
            pltpu.VMEM((share, model), F32),
            *[pltpu.VMEM((nz, HEADDIM, model), BF)] * (per - 1),
            *[pltpu.VMEM((share, model), BF)] * (per - 1),
            *[pltpu.VMEM((HEADDIM, model), BF)] * (nz - 1),
            *[pltpu.VMEM((share, model), BF)] * (nz - 1), *[line8] * (per - 1),
            *[line8] * (nz - 1),
            pltpu.VMEM((2 * STATE, model), F32),
            pltpu.SemaphoreType.DMA((tail_copies,)), pltpu.SemaphoreType.DMA((tail_copies,)),
        ],
        compiler_params=pltpu.CompilerParams(
            vmem_limit_bytes=VMEM, collective_id=2, has_side_effects=True
        ),
        cost_estimate=cost(60),
        name="tail",
    )(*operands)
    inner = own_heads * HEADDIM
    each_head = jnp.asarray(np.kron(np.eye(own_heads), np.ones((HEADDIM, 1))), F32)
    row_heads = shape((1, own_heads))
    g_zx, g_out, g_bcdt, g_cx, g_gain, g_skip, g_bias, g_rate = pl.pallas_call(
        functools.partial(finish_kernel, per),
        grid=(half // Q,),
        in_specs=[
            pl.BlockSpec((per, 2, 2 * HEADDIM, Q), lambda i: (0, 0, 0, i)),
            pl.BlockSpec((per, late_rows, Q), lambda i: (0, 0, i)),
            pl.BlockSpec((per, late_rows, Q), lambda i: (0, 0, 0)), whole(each_head),
        ],
        out_specs=[
            pl.BlockSpec((Q, own_heads, 2 * HEADDIM), lambda i: (i, 0, 0)),
            pl.BlockSpec((inner, Q), lambda i: (0, i)),
            pl.BlockSpec((2 * STATE + HEADS, Q), lambda i: (0, i)), pl.BlockSpec((4, inner), fix),
            pl.BlockSpec((1, inner), fix), *[pl.BlockSpec((1, own_heads), fix)] * 3,
        ],
        out_shape=[
            shape((half, own_heads, 2 * HEADDIM)), shape((inner, half)),
            shape((2 * STATE + HEADS, half)), shape((4, inner)), shape((1, inner)), row_heads,
            row_heads, row_heads,
        ],
        compiler_params=params(),
        cost_estimate=cost(5),
        name="finish",
    )(early_all, late_all, late_all, each_head)
    return (
        out_hidden,
        grad_hidden,
        g_norm.reshape(-1),
        g_zx,
        jnp.transpose(g_bcdt),
        g_cx,
        g_taps_bc,
        g_bias.reshape(-1),
        g_rate.reshape(-1),
        g_skip.reshape(-1),
        g_gain.reshape(-1),
        g_out,
    )


def fits(mesh):
    ndp, nz, nw = mesh.shape["dp"], mesh.shape["head"], mesh.shape["width"]
    return (
        nw == 2
        and ndp in (2, 4, 8)
        and nz & (nz - 1) == 0
        and HEADS == nz * nw * ndp
        and LEN % (nz * Q) == 0
        and SEQS == ndp
        and HEADS // nw * HEADDIM % Q == 0
        and HEADS // ndp == 8
    )


def solution(mesh):
    placed = (
        P(("dp", "head"), "width"),
        P("dp"),
        P(("dp", "head"), "width"),
        P("width"),
        P("width", "head", None),
        P("width", None),
        P(None, "head"),
        P(),
        P("head"),
        P("head"),
        P("head"),
        P("head"),
        P("head", "width"),
    )
    return jax.shard_map(
        sequence_device if fits(mesh) else per_device,
        mesh=mesh,
        in_specs=placed,
        out_specs=(
            P(("dp", "head"), "width"),
            P(("dp", "head"), "width"),
            P("width"),
            P("width", "head", None),
            P("width", None),
            P(None, "head"),
            P(),
            P("head"),
            P("head"),
            P("head"),
            P("head"),
            P("head", "width"),
        ),
        check_vma=False,
    )
```

```python
import functools

import jax
import jax.numpy as jnp
import numpy as np
from jax import lax
from jax.experimental import pallas as pl
from jax.experimental.pallas import tpu as pltpu
from jax.sharding import PartitionSpec as P

D = 1024
HEADS = 32
HEADDIM = 64
STATE = 128
SCAN_BLOCK = 256
LEN = 4096
INNER = 2048
SEQS = 4


EPS = 1e-05
HIGH = lax.Precision.HIGHEST


def conv_causal(values, kernel):
    taps = kernel.shape[0]
    padded = jnp.pad(values, ((taps - 1, 0), (0, 0)))
    total = jnp.zeros_like(values)
    for offset in range(taps):
        total = total + kernel[offset] * padded[offset : offset + values.shape[0]]
    return total


def block_scan(inputs, steps, rates, bmat, cmat, block):
    length, heads, hsize = inputs.shape
    count = length // block
    in_blocks = inputs.reshape(count, block, heads, hsize)
    step_blocks = steps.reshape(count, block, heads)
    b_blocks = bmat.reshape(count, block, bmat.shape[1])
    c_blocks = cmat.reshape(count, block, cmat.shape[1])
    places = jnp.arange(block)
    lower = (places[:, None] >= places[None, :])[:, :, None]

    def advance(state, pieces):
        x_part, dt_part, b_part, c_part = pieces
        cums = jnp.cumsum(dt_part * rates, axis=0)
        spread = cums[:, None, :] - cums[None, :, :]
        decay = jnp.where(lower, jnp.exp(jnp.where(lower, spread, 0.0)), 0.0)
        scores = jnp.dot(c_part, b_part.T, precision=HIGH)
        weights = scores[:, :, None] * decay * dt_part[None, :, :]
        inside = jnp.einsum("ijh,jhp->ihp", weights, x_part, precision=HIGH)
        carried = (
            jnp.einsum("in,hpn->ihp", c_part, state, precision=HIGH) * jnp.exp(cums)[:, :, None]
        )
        tails = jnp.exp(cums[-1][None, :] - cums) * dt_part
        state = jnp.exp(cums[-1])[:, None, None] * state + jnp.einsum(
            "jh,jhp,jn->hpn", tails, x_part, b_part, precision=HIGH
        )
        return (state, inside + carried)

    start_state = jnp.zeros((heads, hsize, bmat.shape[1]), jnp.float32)
    _, result = lax.scan(
        jax.checkpoint(advance), start_state, (in_blocks, step_blocks, b_blocks, c_blocks)
    )
    return result.reshape(length, heads, hsize)


def mixer(zx, bc_raw, dt_raw, kernel_x, kernel_bc, bias_dt, log_rate, skip):
    length, heads, double = zx.shape
    hsize = double // 2
    gate = zx[:, :, :hsize]
    x_raw = zx[:, :, hsize:].reshape(length, heads * hsize)
    xs_conv = jax.nn.silu(conv_causal(x_raw, kernel_x)).reshape(length, heads, hsize)
    bc_conv = jax.nn.silu(conv_causal(bc_raw, kernel_bc))
    half = bc_conv.shape[1] // 2
    steps = jax.nn.softplus(dt_raw + bias_dt)
    rates = -jnp.exp(log_rate)
    result = (
        block_scan(xs_conv, steps, rates, bc_conv[:, :half], bc_conv[:, half:], SCAN_BLOCK)
        + skip[:, None] * xs_conv
    )
    return (result * jax.nn.silu(gate)).reshape(length, heads * hsize)


def per_device(
    hidden,
    lengths,
    cotangent,
    norm_gain,
    in_zx,
    in_bcdt,
    conv_x,
    conv_bc,
    dt_bias,
    a_log,
    d_skip,
    gnorm_gain,
    out_w,
):
    slice_rows, half_width = hidden.shape
    local_heads = in_zx.shape[1]
    head_count = lax.axis_size("head")
    head_index = lax.axis_index("head")
    total_rows = slice_rows * head_count
    seq_local = lengths.shape[0]
    inner_local = local_heads * HEADDIM
    row_ids = head_index * slice_rows + jnp.arange(slice_rows, dtype=jnp.int32)
    owner = (row_ids // LEN)[:, None] == jnp.arange(seq_local, dtype=jnp.int32)[None, :]
    limits = jnp.sum(jnp.where(owner, lengths[None, :], 0), axis=1)
    keeper = (row_ids % LEN < limits).astype(jnp.float32)[:, None]
    source = hidden.astype(jnp.float32)
    squares = lax.psum(jnp.sum(source * source, axis=1), "width")
    scale = lax.rsqrt(squares / D + EPS)[:, None]
    gain_in = norm_gain.astype(jnp.float32)
    normed = (source * scale * gain_in).astype(jnp.bfloat16)
    gathered = lax.all_gather(normed, "head", axis=0, tiled=True)
    w_zx = in_zx.reshape(half_width, local_heads * 2 * HEADDIM)
    zx_part = jnp.dot(gathered, w_zx, preferred_element_type=jnp.float32)
    bcdt_part = jnp.dot(gathered, in_bcdt, preferred_element_type=jnp.float32)
    zx_full, bcdt_full = lax.psum((zx_part, bcdt_part), "width")
    zx_seq = zx_full.reshape(seq_local, LEN, local_heads, 2 * HEADDIM)
    bc_seq = bcdt_full[:, : 2 * STATE].reshape(seq_local, LEN, 2 * STATE)
    dt_seq = lax.dynamic_slice_in_dim(
        bcdt_full, 2 * STATE + head_index * local_heads, local_heads, 1
    ).reshape(seq_local, LEN, local_heads)

    def local_mix(zx_in, bc_in, dt_in, kernel_x, kernel_bc, bias_in, log_in, skip_in):
        per_sequence = jax.vmap(mixer, in_axes=(0, 0, 0, None, None, None, None, None))
        return per_sequence(
            zx_in, bc_in, dt_in, kernel_x, kernel_bc, bias_in, log_in, skip_in
        ).reshape(total_rows, inner_local)

    gated, mix_pull = jax.vjp(
        local_mix,
        zx_seq,
        bc_seq,
        dt_seq,
        conv_x.astype(jnp.float32),
        conv_bc.astype(jnp.float32),
        dt_bias,
        a_log,
        d_skip,
    )
    total_sq = lax.psum(jnp.sum(gated * gated, axis=1), "head")
    scale_out = lax.rsqrt(total_sq / INNER + EPS)[:, None]
    gain_out = gnorm_gain.astype(jnp.float32)
    mixed = (gated * scale_out * gain_out).astype(jnp.bfloat16)
    picked = mixed
    branch = lax.psum_scatter(
        jnp.dot(picked, out_w, preferred_element_type=jnp.float32),
        "head",
        scatter_dimension=0,
        tiled=True,
    )
    out_hidden = (source + keeper * branch).astype(jnp.bfloat16)
    grad_out = cotangent.astype(jnp.float32)
    masked = (grad_out * keeper).astype(jnp.bfloat16)
    piece = lax.all_gather(masked, "head", axis=0, tiled=True)
    picked = mixed
    acc_weight = jnp.einsum("tc,td->cd", picked, piece, preferred_element_type=jnp.float32)
    product = jnp.einsum("td,cd->tc", piece, out_w, preferred_element_type=jnp.float32)
    grad_mixed = lax.psum(product, "width")
    gain_out_grad = jnp.sum(grad_mixed * gated * scale_out, axis=0)
    inner_total = lax.psum(jnp.sum(grad_mixed * gain_out * gated, axis=1), "head")
    cubed = scale_out * scale_out * scale_out
    grad_gated = scale_out * gain_out * grad_mixed - gated * cubed / INNER * inner_total[:, None]
    (
        grad_zx_seq,
        grad_bc_seq,
        grad_dt_seq,
        kernel_x_grad,
        kernel_bc_grad,
        bias_grad,
        rate_grad,
        skip_grad,
    ) = mix_pull(grad_gated)
    grad_zx = grad_zx_seq.reshape(total_rows, local_heads * 2 * HEADDIM).astype(jnp.bfloat16)
    dt_columns = jnp.zeros((total_rows, HEADS), jnp.float32)
    dt_columns = lax.dynamic_update_slice_in_dim(
        dt_columns, grad_dt_seq.reshape(total_rows, local_heads), head_index * local_heads, 1
    )
    grad_bcdt_head = jnp.concatenate(
        [grad_bc_seq.reshape(total_rows, 2 * STATE), dt_columns], axis=1
    )
    weight_zx = jnp.einsum(
        "td,tc->dc", gathered, grad_zx, preferred_element_type=jnp.float32
    ).reshape(half_width, local_heads, 2 * HEADDIM)
    normed_part = jnp.einsum("tc,dc->td", grad_zx, w_zx, preferred_element_type=jnp.float32)
    grad_normed, bcdt_summed = (
        lax.psum_scatter(normed_part, "head", scatter_dimension=0, tiled=True),
        lax.psum_scatter(grad_bcdt_head, "head", scatter_dimension=0, tiled=True),
    )
    bcdt_low = bcdt_summed.astype(jnp.bfloat16)
    grad_normed = grad_normed + jnp.einsum(
        "tk,dk->td", bcdt_low, in_bcdt, preferred_element_type=jnp.float32
    )
    weight_bcdt = jnp.einsum("td,tk->dk", normed, bcdt_low, preferred_element_type=jnp.float32)
    gain_in_grad = jnp.sum(grad_normed * source * scale, axis=0)
    across = lax.psum(jnp.sum(grad_normed * gain_in * source, axis=1), "width")
    scale_cubed = scale * scale * scale
    grad_hidden = (
        grad_out + scale * gain_in * grad_normed - source * scale_cubed / D * across[:, None]
    ).astype(jnp.bfloat16)
    summed_dp = lax.psum(
        (weight_zx, acc_weight, kernel_x_grad, bias_grad, rate_grad, skip_grad, gain_out_grad), "dp"
    )
    summed_all = lax.psum((weight_bcdt, gain_in_grad, kernel_bc_grad), ("dp", "head"))
    return (
        out_hidden,
        grad_hidden,
        summed_all[1],
        summed_dp[0],
        summed_all[0],
        summed_dp[2],
        summed_all[2],
        summed_dp[3],
        summed_dp[4],
        summed_dp[5],
        summed_dp[6],
        summed_dp[1],
    )


BF = jnp.bfloat16
F32 = jnp.float32
Q = 128
HALO = 16
NEG = -1e30
MESH = pl.DeviceIdType.MESH
VMEM = 60 * 1024 * 1024


def dot(a, b, prec=None):
    return lax.dot_general(a, b, (((1,), (0,)), ((), ())), precision=prec, preferred_element_type=F32)


def dot_t(a, b, prec=None):
    return lax.dot_general(a, b, (((1,), (1,)), ((), ())), precision=prec, preferred_element_type=F32)


def t_dot(a, b, prec=None):
    return lax.dot_general(a, b, (((0,), (0,)), ((), ())), precision=prec, preferred_element_type=F32)


def split2(v, axis=1):
    hi = v.astype(BF)
    lo = (v - hi.astype(F32)).astype(BF)
    return jnp.concatenate([hi, lo], axis=axis)


def dot_split(v, m):
    hi = v.astype(BF)
    lo = (v - hi.astype(F32)).astype(BF)
    return dot(hi, m) + dot(lo, m)


def split_dot(m, v):
    hi = v.astype(BF)
    lo = (v - hi.astype(F32)).astype(BF)
    return dot(m, hi) + dot(m, lo)


def sigmoid(v):
    return 1.0 / (1.0 + jnp.exp(-v))


def tri(kind):
    row = lax.broadcasted_iota(jnp.int32, (Q, Q), 0)
    col = lax.broadcasted_iota(jnp.int32, (Q, Q), 1)
    return {"ge": row >= col, "le": row <= col, "gt": row > col}[kind]


def slot_heads(heads, per):
    nz = heads // per
    own = HEADS // nz
    bits = per.bit_length() - 1
    slot = lax.broadcasted_iota(jnp.int32, (heads, HEADS), 0)
    head = lax.broadcasted_iota(jnp.int32, (heads, HEADS), 1)
    z = (lax.axis_index("head") - (slot >> bits)) & (nz - 1)
    m = (slot & (per - 1)) ^ lax.axis_index("dp")
    return (head == z * own + lax.axis_index("width") * per + m).astype(F32)


def prep_kernel(
    per, zx, ow, bcdt, rows_in,
    first_o, first2_o, rest_o, rest2_o, out_o, out2_o, bcdt_o, table_o,
):
    di = lax.axis_index("dp")
    wi = lax.axis_index("width")
    wide = 2 * HEADDIM
    for m in range(per):
        for w, whole_o, some_o, o_o in (
            (wi, first_o, rest_o, out_o), (1 - wi, first2_o, rest2_o, out2_o)
        ):
            head = w * per + jnp.bitwise_xor(di, m)
            v = jnp.transpose(zx[:, pl.ds(pl.multiple_of(head * wide, wide), wide)])
            for i in range(2):
                part = v[i * HEADDIM : (i + 1) * HEADDIM, :]
                if m == 0:
                    whole_o[i] = part
                else:
                    some_o[i, (m - 1) * HEADDIM : m * HEADDIM, :] = part
            o_o[m * HEADDIM : (m + 1) * HEADDIM, :] = ow[
                pl.ds(pl.multiple_of(head * HEADDIM, HEADDIM), HEADDIM), :
            ]
    n = bcdt.shape[0]
    bcdt_o[0:n, :] = bcdt[...]
    bcdt_o[n:, :] = jnp.broadcast_to(rows_in[8:9, :], (HALO, bcdt.shape[1])).astype(BF)
    rows = rows_in[0:8, :]
    half = rows.shape[1] // 2
    rows = jnp.where(wi == 0, rows[:, :half], rows[:, half:])
    step = 1
    while step < per:
        size = HEADDIM * step
        parts = [rows[:, i * size : (i + 1) * size] for i in range(half // size)]
        swapped = jnp.concatenate([parts[i ^ 1] for i in range(len(parts))], axis=1)
        rows = jnp.where(jnp.bitwise_and(di, step) != 0, swapped, rows)
        step *= 2
    table_o[...] = rows


def entry_first(per, hm, ho, hh, bcdt, table, sel, o, xn_o, buf, between, edges):
    xnh_o, r_o, raw_o, rawh_o, dt_o, sig_o = o.xnh, o.r, o.raw, o.rawh, o.dt, o.sig
    cl_o, clt_o, rate_o, wdt_o, b_o = o.cl, o.clt, o.rate, o.wdt, o.b
    rows = hm.shape[0]
    state = b_o.shape[1]
    per_head = dot(table[...], sel[...], HIGH)
    bias = per_head[5:6, :]
    rate = -jnp.exp(per_head[6:7, :])
    rate_o[...] = rate
    wbc = bcdt.at[0 : 2 * state, :]
    wdt_o[...] = dot(
        slot_heads(rate.shape[1], per).astype(BF), bcdt[2 * state : 2 * state + HEADS, :]
    ).astype(BF)
    wdt = wdt_o
    gain = bcdt[2 * state + HEADS : 2 * state + HEADS + 1, :].astype(F32)
    blocks = rows // Q
    lower = tri("ge").astype(F32)

    def norm(left, right):
        h = jnp.concatenate([left, right], axis=1).astype(F32)
        r = lax.rsqrt(jnp.mean(h * h, axis=1, keepdims=True) + EPS)
        return (h * r * gain).astype(BF), r

    def first(i, carry):
        here = pl.ds(pl.multiple_of(i * Q, Q), Q)
        xn, r = norm(hm[here, :], ho[here, :])
        xn_o[here, :] = xn
        r_o[here, :] = r
        raw = dot_t(xn, wbc[...])
        raw_o[here, :] = raw
        buf[pl.ds(pl.multiple_of(HALO + i * Q, HALO), Q), :] = raw
        steps = dot_t(xn, wdt[...]) + bias
        dt = jax.nn.softplus(steps)
        dt_o[here, :] = dt
        sig_o[here, :] = sigmoid(steps)
        da = dt * rate
        cl_o[here, :] = dot(lower, da, HIGH)
        clt_o[:, here] = lax.dot_general(
            da, lower, (((0,), (1,)), ((), ())), precision=HIGH, preferred_element_type=F32
        )
        return carry

    lax.fori_loop(0, blocks // 2, first, 0, unroll=2)
    between()
    lax.fori_loop(blocks // 2, blocks, first, 0, unroll=2)
    edges()
    half = hm.shape[1]
    xnh, _ = norm(hh[:, :half], hh[:, half:])
    xnh = jnp.where(lax.axis_index("head") > 0, xnh.astype(F32), 0.0).astype(BF)
    xnh_o[...] = xnh
    buf[0:HALO, :] = dot_t(xnh, wbc[...])
    rawh_o[...] = buf[0:HALO, :]


def entry_second(cbc, o, tot_o, buf):
    u_o, b_o, c_o, dt_o, cl_o, clt_o = o.ubc, o.b, o.c, o.dt, o.cl, o.clt
    dt2_o, e12_o, tl2_o, dttl2_o, ec2_o, edt2_o = o.dt2, o.e12, o.tl2, o.dttl2, o.ec2, o.edt2
    state = b_o.shape[1]
    blocks = b_o.shape[0] // Q

    def second(i, carry):
        here = pl.ds(pl.multiple_of(i * Q, Q), Q)
        win = buf[pl.ds(pl.multiple_of(i * Q, Q), Q + HALO), :]
        u = jnp.zeros((Q, win.shape[1]), F32)
        for k in range(4):
            u = u + cbc[k : k + 1, :] * win[HALO - 3 + k : HALO - 3 + k + Q, :]
        u_o[here, :] = u
        v = u * sigmoid(u)
        b_o[here, :] = v[:, :state].astype(BF)
        c_o[here, :] = v[:, state:].astype(BF)
        return carry

    lax.fori_loop(0, blocks, second, 0, unroll=2)
    tots = [cl_o[i * Q + Q - 1 : i * Q + Q, :] for i in range(blocks)]
    ctot = functools.reduce(lambda x, y: x + y, tots)
    heads = clt_o.shape[0]
    column = functools.reduce(
        lambda x, y: x + y, [clt_o[:, i * Q + Q - 1 : i * Q + Q] for i in range(blocks)]
    )
    hi = column.astype(BF)
    mid = (column - hi.astype(F32)).astype(BF)
    low = (column - hi.astype(F32) - mid.astype(F32)).astype(BF)
    lane = lax.broadcasted_iota(jnp.int32, (heads, tot_o.shape[1]), 1)
    tot_o[...] = jnp.where(
        lane == 0,
        hi.astype(F32),
        jnp.where(lane == 1, mid.astype(F32), jnp.where(lane == 2, low.astype(F32), 0.0)),
    ).astype(BF)
    off = jnp.zeros_like(ctot)
    for i in range(blocks):
        here = slice(i * Q, i * Q + Q)
        cl = cl_o[here, :]
        dt = dt_o[here, :]
        tail = jnp.exp(tots[i] - cl)
        dt2_o[here, :] = split2(dt)
        e12_o[here, :] = split2(jnp.exp(cl))
        tl2_o[here, :] = split2(tail)
        dttl2_o[here, :] = split2(dt * tail)
        ec2_o[here, :] = split2(jnp.exp(cl + off))
        edt2_o[here, :] = split2(dt * jnp.exp(ctot - cl - off))
        off = off + tots[i]


def decay(cl, clt, h, mask):
    return jnp.exp(jnp.where(mask, cl[:, h : h + 1] - clt[h : h + 1, :], NEG))


def lane_masks():
    lane = lax.broadcasted_iota(jnp.int32, (1, Q), 1)
    low = (lane < HEADDIM).astype(F32)
    return low.astype(BF), (1.0 - low).astype(BF)


def project(s, per, xn, o, w, cw, ex, z_o, xr_o, xrh_o, u_o, xdt_o, msg, buf, acc):
    rows = z_o.shape[0]
    gc = per * HEADDIM
    cols = slice(s * gc, s * gc + gc)
    xh = dot_t(o.xnh[...], w[1, cols, :])
    buf[0:HALO, :] = xh
    xrh_o[...] = xh
    acc[...] = jnp.zeros_like(acc)
    cut = rows // 2 if rows // 2 % Q == 0 else rows

    def part(j, carry):
        base = j * cut
        here = pl.ds(pl.multiple_of(base, Q), cut)
        buf[pl.ds(pl.multiple_of(base + HALO, HALO), cut), :] = dot_t(xn[here, :], w[1, cols, :])
        z_o[here, :] = dot_t(xn[here, :], w[0, cols, :])
        for i in range(cut // Q):
            here = pl.ds(pl.multiple_of(base + i * Q, Q), Q)
            win = buf[pl.ds(pl.multiple_of(base + i * Q, Q), Q + HALO), :]
            u = jnp.zeros((Q, gc), F32)
            for k in range(4):
                u = u + cw[k : k + 1, cols] * win[HALO - 3 + k : HALO - 3 + k + Q, :]
            xr_o[here, :] = win[HALO:, :].astype(BF)
            u_o[here, :] = u
            xs = u * sigmoid(u)
            xdt_o[here, :] = (xs * dot(o.dt2[here, :], ex[:, cols])).astype(BF)
            acc[...] += t_dot((xs * dot(o.edt2[here, :], ex[:, cols])).astype(BF), o.b[here, :])
        return carry

    lax.fori_loop(0, rows // cut, part, 0)
    msg[cols, :] = acc[...].astype(BF)


def inside(s, per, xdt, o, y_o):
    mask = tri("ge")
    low, high = lane_masks()
    rows = xdt.shape[0]
    some = 4 if rows % (4 * Q) == 0 else 1

    def part(j, carry):
        for i in range(some):
            here = pl.ds(pl.multiple_of((j * some + i) * Q, Q), Q)
            g = dot_t(o.c[here, :], o.b[here, :])
            clv, cltv = o.cl[here, :], o.clt[:, here]
            for p in range(xdt.shape[1] // Q):
                lanes = slice(p * Q, p * Q + Q)
                h = s * per + 2 * p
                ws = [(g * decay(clv, cltv, k, mask)).astype(BF) for k in (h, h + 1)]
                x = xdt[here, lanes]
                y_o[here, lanes] = dot(
                    jnp.concatenate(ws, axis=1), jnp.concatenate([x * low, x * high], axis=0)
                ).astype(BF)
        return carry

    lax.fori_loop(0, rows // (some * Q), part, 0)


class Named:
    def __init__(self, names, refs):
        for name, ref in zip(names, refs):
            setattr(self, name, ref)


KEPT = (
    "xnh", "r", "raw", "rawh", "ubc", "b", "c", "dt", "sig", "cl", "clt", "dt2", "e12", "tl2",
    "dttl2", "ec2", "edt2", "rate", "wdt", "tot", "table", "bcdt",
)


def front_kernel(per, nz, *refs):
    hidden, first, first2, rest, rest2, bcdt, table, cbc, sel, ex, refs = take(refs, *[0] * 10)
    out_mine, out2, cot, refs = take(refs, 0, 0, 0)
    w_o, wo_o, cot_o, xn_o, refs = take(refs, 0, 0, 0, 0)
    z_o, xr_o, u_o, xdt_o, y_o, messages_o, xrh_o, refs = take(refs, *[nz] * 5, nz - 1, nz)
    kept, refs = refs[: len(KEPT)], refs[len(KEPT) :]
    o = Named(KEPT, kept)
    z_v, xr_v, u_v, xdt_v, y_v, refs = take(refs, *[nz] * 5)
    w, ho, eh, xn, msg, buf, bcbuf, acc, sends, receives, locals_ = refs
    bc = o.bcdt
    rows, half = hidden.shape
    gc = per * HEADDIM
    top = nz * gc
    sibling = {"width": 1 - lax.axis_index("width")}
    z_peers = line_peers(nz, 1)
    d_peers = plane_peers(per)
    used = [0]

    def copy(source, target, peer):
        i = used[0]
        used[0] += 1
        return remote(source, target, sends, receives, i, peer)

    left, right = pl.ds(0, half), pl.ds(half, half)
    swap_first = copy(first2, w.at[:, pl.ds(0, HEADDIM), right], sibling)
    swap_rest = copy(rest2, w.at[:, pl.ds(HEADDIM, gc - HEADDIM), right], sibling)
    swap_hidden = copy(hidden, ho, sibling)
    swap_bc = copy(bcdt, bc.at[:, right], sibling)
    swap_out = copy(out2, wo_o.at[pl.ds(0, gc), right], sibling)
    swap_cot = copy(cot, cot_o, sibling)
    z_table, z_w, z_out, z_state = [], [], [], {s: [] for s in range(nz)}
    for k, peer in enumerate(z_peers):
        s = k + 1
        z_table.append(copy(table, o.table.at[:, pl.ds(s * gc, gc)], peer))
        own = w.at[:, pl.ds(0, HEADDIM), :]
        z_w.append(copy(own, w.at[:, pl.ds(s * gc, HEADDIM), :], peer))
        z_out.append(
            copy(wo_o.at[pl.ds(0, HEADDIM), :], wo_o.at[pl.ds(s * gc, HEADDIM), :], peer)
        )
        for j in range(nz):
            some = pl.ds(j * gc, gc + HALO if j == nz - 1 else gc)
            z_state[j].append(copy(msg.at[some, :], messages_o[k].at[some, :], peer))
    last = pl.ds(rows - HALO, HALO)
    edge1 = copy(hidden.at[last, :], eh.at[:, left], z_peers[0])
    edge2 = copy(ho.at[last, :], eh.at[:, right], z_peers[0])
    p_w = {s: [] for s in range(1, nz)}
    p_out = {s: [] for s in range(1, nz)}
    for s in range(1, nz):
        for k, peer in enumerate(d_peers):
            mine = pl.ds(s * gc, HEADDIM)
            there = pl.ds(s * gc + (k + 1) * HEADDIM, HEADDIM)
            via, to = k, peer
            if k + 1 == per - 1:
                first_hop = s % 2
                mine = pl.ds(s * gc + (first_hop + 1) * HEADDIM, HEADDIM)
                to = d_peers[1 - first_hop]
            p_w[s].append(copy(w.at[:, mine, :], w.at[:, there, :], to))
            p_out[s].append(copy(wo_o.at[mine, :], wo_o.at[there, :], to))

    places = [0]

    def local(source, target):
        i = places[0]
        places[0] += 1
        found = pltpu.make_async_copy(source, target, locals_.at[i])
        found.start()
        return found

    ready = [
        local(first, w.at[:, pl.ds(0, HEADDIM), left]),
        local(rest, w.at[:, pl.ds(HEADDIM, gc - HEADDIM), left]),
        local(bcdt, bc.at[:, left]),
        local(table, o.table.at[:, pl.ds(0, gc)]),
        local(out_mine, wo_o.at[pl.ds(0, gc), left]),
    ]
    meet([sibling, *z_peers, *line_peers(nz, -1), *d_peers])
    start([swap_first, *z_table, swap_hidden, swap_bc, edge1])
    ready[0].wait()
    arrive([swap_first])
    start([z_w[0], swap_rest, swap_out, swap_cot])
    for c in ready[1:]:
        c.wait()
    arrive([swap_hidden])
    start([edge2])
    arrive([swap_bc, *z_table])
    pending = []

    def pass_on(copies, s):
        arrive([copies[s % 2]])
        start([copies[2]])

    def between():
        arrive([z_w[0]])
        start([*p_w[1][:2], *z_w[1:]])

    def edges():
        arrive([edge1, edge2])

    entry_first(per, hidden, ho, eh, bc, o.table, sel, o, xn, bcbuf, between, edges)
    pass_on(p_w[1], 1)
    arrive([z_w[1], swap_rest])
    start(p_w[2][:2])
    entry_second(cbc, o, o.tot, bcbuf)
    msg[top:, :] = o.tot[...]
    pending.append(local(xn, xn_o))
    for k in range(3, nz):
        arrive([z_w[k - 1]])
        start(p_w[k][:2])
    arrive([swap_out])
    start(z_out)
    taps = o.table

    def project_group(s):
        project(
            s, per, xn, o, w, taps, ex, z_v[s], xr_v[s], xrh_o[s], u_v[s], xdt_v[s], msg, buf, acc
        )
        start(z_state[s])
        for a, b in ((z_v, z_o), (xr_v, xr_o), (u_v, u_o), (xdt_v, xdt_o)):
            pending.append(local(a[s], b[s]))

    def inside_group(s):
        inside(s, per, xdt_v[s], o, y_v[s])
        pending.append(local(y_v[s], y_o[s]))

    project_group(0)
    for k in range(2, nz):
        pass_on(p_w[k], k)
    inside_group(0)
    for k in range(1, nz):
        arrive([z_out[k - 1]])
        start(p_out[k][:2])
    for s in range(1, nz):
        arrive([p_w[s][1 - s % 2], p_w[s][2]])
        project_group(s)
        if s == nz - 2:
            for k in range(1, nz):
                pass_on(p_out[k], k)
    pending.append(local(w, w_o))
    for s in range(1, nz):
        inside_group(s)
    everything = [swap_first, swap_rest, swap_hidden, swap_bc, swap_out, swap_cot, edge1, edge2]
    everything += [*z_table, *z_w, *z_out]
    states = [c for s in range(nz) for c in z_state[s]]
    everything += states
    for s in range(1, nz):
        everything += p_w[s] + p_out[s]
        arrive([p_out[s][1 - s % 2], p_out[s][2]])
    arrive([swap_cot, *states])
    for c in everything:
        c.wait_send()
    for c in pending:
        c.wait()


def head_scale(clt, first, per, state):
    return jnp.concatenate(
        [
            jnp.broadcast_to(jnp.exp(clt[h : h + 1, Q - 1 : Q]), (HEADDIM, state))
            for h in range(first, first + per)
        ],
        axis=0,
    )


def from_messages(messages, sign, groups, per, state, store, valid=None):
    nz = len(messages) + 1
    gc = per * HEADDIM
    top = nz * gc
    totals = [
        sum(m[top:, i : i + 1].astype(F32) for i in range(3)) for m in messages
    ]
    for at, j in enumerate(groups):
        total = jnp.zeros((gc, state), F32)
        faded = jnp.zeros((per, 1), F32)
        for k in range(1, nz):
            there = (j - sign * k) % nz
            scale = jnp.exp(faded)
            scale = jnp.concatenate(
                [jnp.broadcast_to(scale[h : h + 1, :], (HEADDIM, state)) for h in range(per)],
                axis=0,
            )
            part = scale * messages[k - 1][there * gc : there * gc + gc, :].astype(F32)
            if valid is not None:
                part = jnp.where(valid(k), part, 0.0)
            total = total + part
            faded = faded + totals[k - 1][there * per : there * per + per, :]
        store[at * gc : at * gc + gc, :] = total


def mid_kernel(groups, per, *refs):
    nz = len(groups)
    y_in, u, z, cot, cot2, b, c, clt, e12, dttl2, refs = take(refs, nz, nz, nz, *[0] * 7)
    u2, z2, ec2, c2, hidden, refs = take(refs, nz, nz, 0, 0, 0)
    messages, tot, table, ex, wout, limit, refs = take(refs, nz - 1, *[0] * 5)
    gain, dsk = table.at[4:5, :], table.at[7:8, :]
    st_o, mask_o, dys_o, dz_o, yn_o, out_o, msg_o, gn_o, sk_o, refs = take(
        refs, nz, 0, nz, *[0] * 6
    )
    s, acc, yv, dv, br, br_out, br_in, sm_out, sm_in, gg, sends, receives = refs
    step = pl.program_id(0)
    tiles = pl.num_programs(0) - 1
    rows, half = cot.shape
    gc = per * HEADDIM
    state = s.shape[1]
    sibling = {"width": 1 - lax.axis_index("width")}

    def copies(k):
        return [
            remote(sm_out.at[k], sm_in.at[k], sends, receives, 2 * k, sibling),
            remote(br_out.at[k], br_in.at[k], sends, receives, 2 * k + 1, sibling),
        ]

    @pl.when(step == 0)
    def _():
        meet([sibling])
        z_index = lax.axis_index("head")
        from_messages(messages, 1, groups, per, state, s, lambda k: z_index - k >= 0)
        acc[...] = jnp.zeros_like(acc)
        gn_o[...] = jnp.zeros_like(gn_o)
        sk_o[...] = jnp.zeros_like(sk_o)

    @pl.when(step < tiles)
    def _():
        slot = lax.rem(step, 2)
        row = lax.broadcasted_iota(jnp.int32, (rows, 1), 0) + step * rows
        keep = row < limit[0, 0]
        for i, v in enumerate((cot, cot2)):
            mask_o[:, i * half : i * half + half] = jnp.where(keep, v[...].astype(F32), 0.0).astype(
                BF
            )
        dv[slot] = dot_t(mask_o[...], wout[...])
        lane = lax.broadcasted_iota(jnp.int32, (Q, Q), 1)
        for i in range(rows // Q):
            part = slice(i * Q, i * Q + Q)
            cc, bb = c[part, :], b[part, :]
            square = jnp.zeros((Q, gc), F32)
            inner = jnp.zeros((Q, gc), F32)
            for j in groups:
                here = slice(j * gc, j * gc + gc)
                sv = s[here, :]
                sb = sv.astype(BF)
                st_o[j][i] = sb
                x = u[j][part, :]
                x = x * sigmoid(x)
                e1 = dot(e12[part, :], ex[:, here])
                y = y_in[j][part, :].astype(F32) + e1 * dot_t(cc, sb) + dsk[:, here] * x
                yv[slot, part, here] = y
                xt = (x * dot(dttl2[part, :], ex[:, here])).astype(BF)
                s[here, :] = head_scale(clt.at[:, part], j * per, per, state) * sv + t_dot(xt, bb)
                zz = z[j][part, :]
                gz = y * (zz * sigmoid(zz))
                g = gz * gain[:, here]
                gg[part, here] = g.astype(BF)
                square = square + gz * gz
                inner = inner + g * dv[slot, part, here]
            sm_out[step, part, :] = jnp.where(
                lane == 0,
                jnp.sum(square, axis=1, keepdims=True),
                jnp.sum(inner, axis=1, keepdims=True),
            )
        branch = dot(gg[...], wout[...])
        br[slot] = branch[:, :half]
        br_out[step] = branch[:, half:].astype(BF)
        for copy in copies(step):
            copy.start()

    @pl.when(step > 0)
    def _():
        k = step - 1
        slot = lax.rem(k, 2)
        for copy in copies(k):
            copy.wait()
        count = nz * gc * 2
        for i in range(rows // Q):
            part = slice(i * Q, i * Q + Q)
            both = sm_out[k, part, :] + sm_in[k, part, :]
            r2 = lax.rsqrt(both[:, 0:1] / count + EPS)
            pull = both[:, 1:2] * (r2 * r2 * r2) / count
            row = lax.broadcasted_iota(jnp.int32, (Q, 1), 0) + k * rows + i * Q
            keep = jnp.where(row < limit[0, 0], r2, 0.0)
            out_o[part, :] = (
                hidden[part, :].astype(F32)
                + keep * (br[slot, part, :] + br_in[k, part, :].astype(F32))
            ).astype(BF)
            for j in groups:
                here = slice(j * gc, j * gc + gc)
                gn = gain[:, here]
                zz = z2[j][part, :]
                sz = sigmoid(zz)
                silu = zz * sz
                y = yv[slot, part, here]
                gz = y * silu
                dy_n = dv[slot, part, here]
                gr = gz * r2
                yn_o[part, here] = (gr * gn).astype(BF)
                gn_o[:, here] += jnp.sum(dy_n * gr, axis=0, keepdims=True)
                dgz = r2 * gn * dy_n - gz * pull
                dys = dgz * silu
                dys_o[j][part, :] = dys.astype(BF)
                dz_o[part, here] = (dgz * y * (sz + silu * (1.0 - sz))).astype(BF)
                x = u2[j][part, :]
                x = x * sigmoid(x)
                sk_o[:, here] += jnp.sum(dys * x, axis=0, keepdims=True)
                acc[here, :] += t_dot(
                    (dys * dot(ec2[part, :], ex[:, here])).astype(BF), c2[part, :]
                )

    @pl.when(step == tiles)
    def _():
        top = nz * gc
        msg_o[0:top, :] = acc[...].astype(BF)
        msg_o[top:, :] = tot[...]


def line_peers(count, sign):
    z = lax.axis_index("head")
    return [{"head": lax.rem(z + sign * k + count, count)} for k in range(1, count)]


def plane_peers(count):
    d = lax.axis_index("dp")
    return [{"dp": jnp.bitwise_xor(d, m)} for m in range(1, count)]


def meet(peers):
    barrier = pltpu.get_barrier_semaphore()
    for peer in peers:
        pl.semaphore_signal(barrier, inc=1, device_id=peer, device_id_type=MESH)
    pl.semaphore_wait(barrier, len(peers))


def remote(source, target, sends, receives, i, peer):
    return pltpu.make_async_remote_copy(
        src_ref=source,
        dst_ref=target,
        send_sem=sends.at[i],
        recv_sem=receives.at[i],
        device_id=peer,
        device_id_type=MESH,
    )


def conv_back(d, nxt, taps, raw, grad_o, out_o):
    win = jnp.concatenate([d, nxt[...]], axis=0)
    back = jnp.zeros_like(d)
    sums = []
    for k in range(4):
        part = win[3 - k : 3 - k + Q, :]
        back = back + taps[k : k + 1, :] * part
        sums.append(jnp.sum(raw * part, axis=0, keepdims=True))
    grad_o[...] += jnp.concatenate(sums, axis=0)
    out_o[...] = back.astype(BF)
    nxt[...] = d[0:8, :]


def conv_edge(first, taps, rawh, grad_o, outh_o):
    first = first[...]
    win = jnp.concatenate([jnp.zeros((HALO, first.shape[1]), F32), first], axis=0)
    back = jnp.zeros((HALO, first.shape[1]), F32)
    sums = []
    for k in range(4):
        part = win[3 - k : 3 - k + HALO, :]
        back = back + taps[k : k + 1, :] * part
        sums.append(jnp.sum(rawh[...] * part, axis=0, keepdims=True))
    grad_o[...] += jnp.concatenate(sums, axis=0)
    outh_o[...] = back.astype(BF)


def scan_back_kernel(groups, per, *refs):
    n = len(groups)
    nz = n
    xdt, dys, u, xr, st, xrh, rest = take(refs, n, n, n, n, n, n)
    (b, c, cl, clt, dt, sig, dt2, e12, tl2), rest = rest[:9], rest[9:]
    (ubc, braw, brawh, table, cbc, rate, ex, er), rest = rest[:8], rest[8:]
    cw, dsk = table.at[0:4, :], table.at[7:8, :]
    message, yn, masked, dz, xn, rest = take(rest, *[0] * 5)
    dx_o, dxh_o, gcx_o, rest = take(rest, n, n, n)
    dt_o, ga_o, gbias_o, bc_o, bch_o, gcb_o, etot = rest[:7]
    messages, got, line, rest = take(rest[7:], nz - 1, per - 1, nz - 1)
    du_next, rest = take(rest, n)
    db_next, early, low, dxi, dbi, dci, dai, kt, ds, vs, sends, receives = rest
    turn = pl.program_id(0)
    step = turn - nz
    blocks = (pl.num_programs(0) - nz) // 2
    heads = dt.shape[1]
    state = b.shape[1]
    gc = per * HEADDIM
    line_at, plane_at = 0, nz - 1
    back_at = plane_at + nz * (per - 1)

    def state_copies():
        return [
            remote(message, messages[i], sends, receives, line_at + i, peer)
            for i, peer in enumerate(line_peers(nz, -1))
        ]

    def plane_copies(s):
        return [
            remote(
                early.at[i + 1, s], got[i].at[s], sends, receives, plane_at + s * (per - 1) + i, peer
            )
            for i, peer in enumerate(plane_peers(per))
        ]

    def line_copy(s):
        return remote(
            low.at[s], line[s - 1], sends, receives, back_at + s - 1, line_peers(nz, -1)[s - 1]
        )

    order = [*range(1, nz), 0]
    leave = [0, nz + blocks // 4, nz + blocks - 1, nz + blocks + blocks // 4]
    added = [nz + blocks // 2, nz + blocks, nz + blocks + 3 * blocks // 8, nz + 2 * blocks - 1]

    @pl.when(turn == 0)
    def _():
        meet([*line_peers(nz, -1), *line_peers(nz, 1), *plane_peers(per)])
        for copy in state_copies():
            copy.start()

    @pl.when(turn < nz)
    def _():
        s = lax.rem(turn + 1, nz)
        g = t_dot(yn[...], masked[...]).astype(BF)
        for m in range(per):
            early[m, s, :HEADDIM, :] = g[m * HEADDIM : (m + 1) * HEADDIM, :]
        g = t_dot(dz[...], xn[...]).astype(BF)
        for m in range(per):
            early[m, s, HEADDIM:, :] = g[m * HEADDIM : (m + 1) * HEADDIM, :]

    for s, when in zip(order, leave):

        @pl.when(turn == when)
        def _(s=s):
            for copy in plane_copies(s):
                copy.start()

    @pl.when(jnp.logical_and(step >= 0, step < blocks))
    def _():
        rows = pl.ds(pl.multiple_of(step * Q, Q), Q)
        mask = tri("ge")
        lower, upper_lanes = lane_masks()
        g = dot_t(c[...], b[...])
        clv, cltv = cl[...], clt[...]
        lane = lax.broadcasted_iota(jnp.int32, (Q, heads), 1)
        dg = jnp.zeros((Q, Q), F32)
        rsum = jnp.zeros((Q, heads), F32)
        for s in groups:
            for p in range(per // 2):
                here = slice(p * Q, p * Q + Q)
                x = xdt[s][:, here]
                dy = dys[s][:, here]
                pp = dot_t(dy, jnp.concatenate([x * lower, x * upper_lanes], axis=0))
                ws = []
                for j in range(2):
                    h = s * per + 2 * p + j
                    ell = decay(clv, cltv, h, mask)
                    ws.append((g * ell).astype(BF))
                    pe = pp[:, j * Q : j * Q + Q] * ell
                    dg = dg + pe
                    m = pe * g
                    rsum = jnp.where(lane == h, jnp.sum(m, axis=1, keepdims=True), rsum)
                    kt[h : h + 1, :] = jnp.sum(m, axis=0, keepdims=True)
                dxi[rows, s * gc + p * Q : s * gc + p * Q + Q] = t_dot(
                    jnp.concatenate(ws, axis=0),
                    jnp.concatenate([dy * lower, dy * upper_lanes], axis=0),
                )
        dgb = dg.astype(BF)
        dci[rows, :] = dot(dgb, b[...])
        dbi[rows, :] = t_dot(dgb, c[...])
        upper = tri("le").astype(F32)
        dai[rows, :] = dot(upper, rsum, HIGH) - dot_t(upper, kt[...], HIGH)

    @pl.when(step == blocks)
    def _():
        for copy in state_copies():
            copy.wait()
        z = lax.axis_index("head")
        from_messages(messages, -1, groups, per, state, ds, lambda k: z + k < nz)
        for i in range(n):
            du_next[i][...] = jnp.zeros_like(du_next[i])
            gcx_o[i][...] = jnp.zeros_like(gcx_o[i])
        db_next[...] = jnp.zeros_like(db_next)
        gcb_o[...] = jnp.zeros_like(gcb_o)
        ga_o[...] = jnp.zeros_like(ga_o)
        gbias_o[...] = jnp.zeros_like(gbias_o)

    @pl.when(step >= blocks)
    def _():
        rows = pl.ds(pl.multiple_of((2 * blocks - 1 - step) * Q, Q), Q)
        rsum = jnp.zeros((Q, heads), F32)
        gsum = jnp.zeros((Q, heads), F32)
        ddt = jnp.zeros((Q, heads), F32)
        dbs = dbi[rows, :]
        dcs = dci[rows, :]
        for s in groups:
            here = slice(s * gc, s * gc + gc)
            ehere = er[here, :]
            sb = st[s][0]
            dsv = ds[here, :]
            dsb = dsv.astype(BF)
            dy = dys[s][...].astype(F32)
            dye = dy * dot(e12[...], ex[:, here])
            dyb = dye.astype(BF)
            rsum = rsum + dot((dye * dot_t(c[...], sb)).astype(BF), ehere)
            dcs = dcs + dot(dyb, sb)
            bds = dot_t(b[...], dsb)
            tail = dot(tl2[...], ex[:, here])
            dtx = dot(dt2[...], ex[:, here])
            uu = u[s][...]
            su = sigmoid(uu)
            xs = uu * su
            xt = xs * dtx * tail
            gsum = gsum + dot((xt * bds).astype(BF), ehere)
            dbs = dbs + dot(xt.astype(BF), dsb)
            dxdt = dxi[rows, here] + tail * bds
            ddt = ddt + dot((dxdt * xs).astype(BF), ehere)
            eds = head_scale(clt, s * per, per, state) * dsv
            ev = eds * sb.astype(F32)
            for j in range(per):
                h = s * per + j
                vs[h : h + 1, :] = jnp.sum(
                    ev[j * HEADDIM : (j + 1) * HEADDIM, :], axis=0, keepdims=True
                )
            ds[here, :] = eds + t_dot(dyb, c[...])
            du = (dxdt * dtx + dsk[:, here] * dy) * (su + xs * (1.0 - su))
            conv_back(
                du, du_next[s], cw.at[:, here], xr[s][...].astype(F32), gcx_o[s], dx_o[s]
            )
        vrow = dot_t(jnp.ones((8, state), F32), vs[...], HIGH)
        da = (
            dai[rows, :]
            + split_dot(tri("le").astype(BF), rsum)
            + split_dot(tri("gt").astype(BF), gsum)
            + vrow[0:1, :]
        )
        draw = (rate[...] * da + ddt) * sig[...]
        dt_o[...] = draw.astype(BF)
        ga_o[...] += jnp.sum(da * dt[...], axis=0, keepdims=True)
        gbias_o[...] += jnp.sum(draw, axis=0, keepdims=True)
        d = jnp.concatenate([dbs, dcs], axis=1)
        v = ubc[...]
        sv = sigmoid(v)
        conv_back(d * (sv + v * sv * (1.0 - sv)), db_next, cbc, braw[...], gcb_o, bc_o)

    @pl.when(step == 2 * blocks - 1)
    def _():
        for s in groups:
            here = slice(s * gc, s * gc + gc)
            conv_edge(du_next[s], cw.at[:, here], xrh[s], gcx_o[s], dxh_o[s])
        conv_edge(db_next, cbc, brawh, gcb_o, bch_o)

    def add(s):
        for copy in plane_copies(s):
            copy.wait()

        def piece(i, carry):
            part = pl.ds(pl.multiple_of(i * HALO, HALO), HALO)
            total = early[0, s, part, :].astype(F32)
            for v in got:
                total = total + v[s, part, :].astype(F32)
            low[s, part, :] = total.astype(BF)
            return carry

        lax.fori_loop(0, low.shape[1] // HALO, piece, 0, unroll=2)

    for s, when in zip(order, added):

        @pl.when(turn == when)
        def _(s=s):
            add(s)
            if s > 0:
                line_copy(s).start()

    @pl.when(step == 2 * blocks - 1)
    def _():
        for s in range(1, nz):
            line_copy(s).wait()
        for i in range(low.shape[1] // HALO):
            part = slice(i * HALO, i * HALO + HALO)
            total = low[0, part, :].astype(F32)
            for v in line:
                total = total + v[part, :].astype(F32)
            etot[part, :] = total.astype(BF)


class Copies:
    def __init__(self, sends, receives):
        self.sends, self.receives, self.all = sends, receives, []

    def __call__(self, source, target, peer):
        copy = remote(source, target, self.sends, self.receives, len(self.all), peer)
        self.all.append(copy)
        return copy


def start(copies):
    for c in copies:
        c.start()


def arrive(copies):
    for c in copies:
        c.wait_recv()


def tail_kernel(per, nz, *refs):
    dx, dxh, taps, refs = take(refs, nz, nz, nz)
    (dz, dbc, dbch, dti, xn, xnh, w, bc, wdt, early, hidden, cot, r), refs = refs[:13], refs[13:]
    (gain, gbc, grate, gbias, gskip, ggain, rate, ex), refs = refs[:8], refs[8:]
    ea, la, hid_o, norm_o, tbc_o, refs = take(refs, *[0] * 5)
    gx, gs, gdt, lx, ls, sw_out, sw_in, dxn, dxn_out, dxn_in, refs = take(refs, *[0] * 10)
    edge_out, edge_in, edge_sum, edge_next, across, across_in, nrm, nrm2, sums, refs = take(
        refs, *[0] * 9
    )
    rx, rs, zx, zs, nr, nz_r, refs = take(refs, per - 1, per - 1, nz - 1, nz - 1, per - 1, nz - 1)
    stage, sends, receives = refs
    copy = Copies(sends, receives)
    rows, half = hidden.shape
    gc = per * HEADDIM
    channels = nz * gc
    state2 = dbc.shape[1]
    quarter = state2 // per
    share = quarter + HALO
    some_dt = HEADS // per
    wi, di, zi = lax.axis_index("width"), lax.axis_index("dp"), lax.axis_index("head")
    sibling = {"width": 1 - wi}
    d_peers, z_back = plane_peers(per), line_peers(nz, -1)
    left, right = pl.ds(0, half), pl.ds(half, half)
    block = rows // nz

    early_swap = copy(early.at[:, right], ea.at[0, wi], sibling)
    late_swap = copy(sw_out, sw_in, sibling)
    dxn_swap = [
        copy(dxn_out.at[pl.ds(i * block, block), :], dxn_in.at[pl.ds(i * block, block), :], sibling)
        for i in range(nz)
    ]
    edge_swap = copy(edge_out, edge_in, sibling)
    across_swap = copy(across, across_in, sibling)
    p_share, p_x, p_early, p_norm, p_late = [], {s: [] for s in range(nz)}, [], [], []
    for k, peer in enumerate(d_peers):
        m = k + 1
        p_share.append(copy(gs.at[m], rs[k], peer))
        for s in range(nz):
            p_x[s].append(copy(gx.at[s, m], rx[k].at[s], peer))
        if m < per - 1:
            p_early.append(copy(ea.at[0], ea.at[m], peer))
        p_norm.append(copy(nrm, nr[k], peer))
        p_late.append(copy(la.at[0], la.at[m], peer))
    z_x, z_share, z_norm = [], [], []
    for k, peer in enumerate(z_back):
        z_x.append(copy(lx.at[k + 1], zx[k], peer))
        z_share.append(copy(ls, zs[k], peer))
        z_norm.append(copy(nrm2, nz_r[k], peer))
    p_relay = [
        copy(ea.at[1, 0], ea.at[per - 1, 0], d_peers[1]),
        copy(ea.at[2, 1], ea.at[per - 1, 1], d_peers[0]),
    ]
    z_edge = copy(edge_sum, edge_next, z_back[0])

    meet([sibling, *z_back, *line_peers(nz, 1), *d_peers])

    start([early_swap])
    ea[0, wi] = early[:, :half]

    g = t_dot(dbc[...], xn[...]) + t_dot(dbch[...], xnh[...])
    stage[0:state2, :] = g
    gdt[...] = split_dot_tr(slot_heads(dti.shape[1], per), t_dot(dti[...], xn[...]))
    per_head = jnp.concatenate([gbias[...], grate[...] * rate[...]], axis=0)
    small = jnp.concatenate(
        [
            jnp.concatenate([v[...] for v in taps], axis=1),
            ggain[...],
            gskip[...],
            dot(split2(per_head), ex[...]),
        ],
        axis=0,
    )
    both = split2(gbc[...])
    both = jnp.concatenate([both, jnp.zeros((4, 2 * state2), BF)], axis=0)
    for m in range(per):
        at = jnp.bitwise_xor(di, m)
        gs[m, 0:quarter, :] = stage[pl.ds(pl.multiple_of(at * quarter, quarter), quarter), :].astype(
            BF
        )
        lanes = jnp.concatenate(
            [
                small[:, (s * per + m) * HEADDIM : (s * per + m + 1) * HEADDIM]
                for s in range(nz)
            ],
            axis=1,
        )
        lower = jnp.concatenate([split2(lanes), both], axis=1)
        upper = gdt[pl.ds(pl.multiple_of(at * some_dt, some_dt), some_dt), :].astype(BF)
        gs[m, quarter:, :] = jnp.concatenate(
            [upper.astype(F32), lower.astype(F32)], axis=0
        ).astype(BF)
    start(p_share)
    arrive([early_swap])
    order = [*range(1, nz), 0]
    for s in order:
        g = t_dot(dx[s][...], xn[...]) + t_dot(dxh[s][...], xnh[...])
        for m in range(per):
            gx[s, m] = g[m * HEADDIM : (m + 1) * HEADDIM, :].astype(BF)
        start(p_x[s])
    start(p_early)

    def add_share():
        arrive(p_share)
        for i in range(share // HALO):
            here = slice(i * HALO, i * HALO + HALO)
            total = gs[0, here, :].astype(F32)
            for v in rs:
                total = total + v[here, :].astype(F32)
            sums[here, :] = total
        pack(sums)
        start(z_share)

    def pack(v):
        ls[0:quarter, :] = v[0:quarter, :].astype(BF)
        n = nz * HEADDIM
        rest = v[quarter:, :]
        a = rest[:, 0:n] + rest[:, n : 2 * n]
        b = rest[:, 2 * n : 2 * n + state2] + rest[:, 2 * n + state2 :]
        low_rows = jnp.concatenate([split2(a), split2(b)], axis=1)
        row = lax.broadcasted_iota(jnp.int32, (HALO, 1), 0)
        ls[quarter:, :] = jnp.where(row < some_dt, rest, low_rows.astype(F32)).astype(BF)

    def add_x(s):
        arrive(p_x[s])
        for i in range(HEADDIM // HALO):
            here = slice(i * HALO, i * HALO + HALO)
            total = gx[s, 0, here, :].astype(F32)
            for v in rx:
                total = total + v[s, here, :].astype(F32)
            lx[s, here, :] = total.astype(BF)
        if s > 0:
            start([z_x[s - 1]])

    for i in range(nz):
        here = slice(i * block, i * block + block)
        total = dot(dz[here, :], w[0])
        for s in range(nz):
            total = total + dot(dx[s][here, :], w[1, s * gc : (s + 1) * gc, :])
        total = total + dot(dbc[here, :], bc[0:state2, :]) + dot(dti[here, :], wdt[...])
        dxn[here, :] = total[:, :half]
        dxn_out[here, :] = total[:, half:].astype(BF)
        start([dxn_swap[i]])
        if i == 0:
            add_share()
            total = dot(dbch[...], bc[0:state2, :])
            for s in range(nz):
                total = total + dot(dxh[s][...], w[1, s * gc : (s + 1) * gc, :])
            edge_sum[...] = total[:, :half]
            edge_out[...] = total[:, half:]
            start([edge_swap])
        if i == 1:
            add_x(order[0])
            arrive([edge_swap])
            edge_sum[...] = edge_sum[...] + edge_in[...]
            start([z_edge])
    if nz > 2:
        add_x(order[1])

    arrive([*dxn_swap, z_edge])
    late_edge = jnp.where(zi < nz - 1, edge_next[...], 0.0)
    gain_v = gain[...]
    norm_sum = jnp.zeros((8, half), F32)
    ones = jnp.ones((8, half), BF)
    for i in range(rows // Q):
        here = slice(i * Q, i * Q + Q)
        v = dxn[here, :] + dxn_in[here, :].astype(F32)
        if i == rows // Q - 1:
            v = v + jnp.concatenate([jnp.zeros((Q - HALO, half), F32), late_edge], axis=0)
        dxn[here, :] = v
        h = hidden[here, :].astype(F32)
        vh = v * h
        norm_sum = norm_sum + jnp.sum(
            (vh * r[here, :]).reshape(Q // 8, 8, half), axis=0
        )
        across[:, here] = split_dot_t(ones, vh * gain_v)
    start([across_swap])
    nrm[...] = norm_sum
    start(p_norm)
    for s in order[2:]:
        add_x(s)
    arrive(p_early)
    start(p_relay)
    arrive([across_swap])
    eighth = jnp.full((8, Q), 0.125, F32)
    for i in range(rows // Q):
        here = slice(i * Q, i * Q + Q)
        total = across[:, here] + across_in[:, here]
        total = t_dot(total, eighth, HIGH)
        rr = r[here, :]
        scale = rr * rr * rr / (2 * half)
        rg = rr * gain_v
        for j in range(half // Q):
            lanes = slice(j * Q, j * Q + Q)
            hid_o[here, lanes] = (
                cot[here, lanes].astype(F32)
                + rg[:, lanes] * dxn[here, lanes]
                - hidden[here, lanes].astype(F32) * (scale * total)
            ).astype(BF)
    arrive(p_norm)
    total = nrm[...]
    for v in nr:
        total = total + v[...]
    nrm2[...] = total
    start(z_norm)

    arrive([*z_x, *z_share])
    total = lx[0].astype(F32)
    for v in zx:
        total = total + v[...].astype(F32)
    mine = total.astype(BF)
    la[0, pl.ds(pl.multiple_of(wi * HEADDIM, HEADDIM), HEADDIM), :] = mine[:, :half]
    sw_out[0:HEADDIM, :] = mine[:, half:]
    n = nz * HEADDIM
    total = ls[0:quarter, :].astype(F32)
    for v in zs:
        total = total + v[0:quarter, :].astype(F32)
    sums[0:quarter, :] = total
    sw_out[HEADDIM : HEADDIM + quarter, :] = total[:, half:].astype(BF)
    total = ls[quarter:, :].astype(F32)
    own_small = total[:, 0:HEADDIM] + total[:, n : n + HEADDIM]
    for k, v in enumerate(zs):
        part = v[quarter:, :].astype(F32)
        total = total + part
        at = (k + 1) * HEADDIM
        own_small = own_small + (
            part[:, at : at + HEADDIM] + part[:, n + at : n + at + HEADDIM]
        )
    sums[quarter:, :] = total
    taps_bc = total[:, 2 * n : 2 * n + state2] + total[:, 2 * n + state2 :]
    at = HEADDIM + quarter
    sw_out[at : at + HALO, :] = total[:, half:].astype(BF)
    own_small = split2(own_small)
    own_small = jnp.concatenate(
        [own_small, jnp.zeros((HALO, half - 2 * HEADDIM), BF)], axis=1
    )
    taps_bc2 = split2(taps_bc)
    sw_out[at + HALO : at + 2 * HALO, :] = own_small
    sw_out[at + 2 * HALO : at + 3 * HALO, :] = taps_bc2
    start([late_swap])
    arrive([late_swap])
    there = pl.ds(pl.multiple_of((1 - wi) * HEADDIM, HEADDIM), HEADDIM)
    la[0, there, :] = sw_in[0:HEADDIM, :]
    base = 2 * HEADDIM
    la[0, base : base + share, :] = (
        sums[:, :half] + sw_in[HEADDIM : HEADDIM + share, :].astype(F32)
    ).astype(BF)
    base = base + share
    la[0, pl.ds(pl.multiple_of(base + wi * HALO, HALO), HALO), :] = own_small
    la[0, pl.ds(pl.multiple_of(base + (1 - wi) * HALO, HALO), HALO), :] = sw_in[
        at + HALO : at + 2 * HALO, :
    ]
    start(p_late)
    got = sw_in[at + 2 * HALO : at + 3 * HALO, :].astype(F32)
    taps_bc = taps_bc + got[:, :state2] + got[:, state2:]
    tbc_o[...] = taps_bc[some_dt : some_dt + 4, :]
    arrive(z_norm)
    total = nrm2[...]
    for v in nz_r:
        total = total + v[...]
    norm_o[...] = jnp.sum(total, axis=0, keepdims=True)

    arrive([*p_relay, *p_late])
    for c in copy.all:
        c.wait_send()


def finish_kernel(per, ea, la, las, ones, zx_o, ow_o, bcdt_o, cx_o, gn_o, sk_o, bias_o, rate_o):
    di = lax.axis_index("dp")
    some_dt = HEADS // per
    quarter = (bcdt_o.shape[0] - HEADS) // per
    base = 2 * HEADDIM + quarter + HALO
    small = []
    for h in range(2 * per):
        k, j = h // per, h % per
        m = jnp.bitwise_xor(di, j)
        z_part = ea[m, k, HEADDIM:, :].astype(F32)
        x_part = la[m, k * HEADDIM : (k + 1) * HEADDIM, :].astype(F32)
        zx_o[:, h, :] = jnp.transpose(jnp.concatenate([z_part, x_part], axis=0))
        ow_o[h * HEADDIM : (h + 1) * HEADDIM, :] = ea[m, k, :HEADDIM, :].astype(F32)
        v = las[m, base + k * HALO : base + (k + 1) * HALO, :].astype(F32)
        small.append((v[:, :HEADDIM] + v[:, HEADDIM : 2 * HEADDIM])[some_dt:, :])
    for j in range(per):
        m = jnp.bitwise_xor(di, j)
        v = la[m, 2 * HEADDIM : base, :].astype(F32)
        bcdt_o[j * quarter : (j + 1) * quarter, :] = v[:quarter, :]
        at = per * quarter + j * some_dt
        bcdt_o[at : at + some_dt, :] = v[quarter : quarter + some_dt, :]

    @pl.when(pl.program_id(0) == 0)
    def _():
        rows = jnp.concatenate(small, axis=1)
        cx_o[...] = rows[0:4, :]
        gn_o[...] = rows[4:5, :]
        total = dot(rows, ones[...], HIGH)
        sk_o[...] = total[5:6, :]
        bias_o[...] = total[6:7, :] / HEADDIM
        rate_o[...] = total[7:8, :] / HEADDIM


def split_dot_tr(m, v):
    hi = v.astype(BF)
    lo = (v - hi.astype(F32)).astype(BF)
    m = m.astype(BF)
    return t_dot(m, hi) + t_dot(m, lo)


def split_dot_t(m, v):
    hi = v.astype(BF)
    lo = (v - hi.astype(F32)).astype(BF)
    return dot_t(m, hi) + dot_t(m, lo)


def shape(dims, dtype=F32):
    return jax.ShapeDtypeStruct(dims, dtype)


def whole(array):
    rank = len(array.shape)
    return pl.BlockSpec(array.shape, lambda *_: (0,) * rank)


def params():
    return pltpu.CompilerParams(vmem_limit_bytes=VMEM)


def cost(us):
    return pl.CostEstimate(flops=int(us * 1.0e8), bytes_accessed=int(us * 1.0e3), transcendentals=0)


def take(refs, *counts):
    out, at = [], 0
    for n in counts:
        out.append(refs[at] if n == 0 else refs[at : at + n])
        at += max(n, 1)
    return out + [refs[at:]]


def sequence_device(
    hidden, lengths, cotangent, norm_gain, in_zx, in_bcdt, conv_x, conv_bc,
    dt_bias, a_log, d_skip, gnorm_gain, out_w,
):
    rows, half = hidden.shape
    own_heads = in_zx.shape[1]
    nz = lax.axis_size("head")
    ndp = lax.axis_size("dp")
    zi = lax.axis_index("head")
    di = lax.axis_index("dp")
    wi = lax.axis_index("width")
    per = ndp
    heads = nz * per
    channels = heads * HEADDIM
    model = 2 * half
    blocks = rows // Q

    def swap(v):
        return lax.ppermute(v, "width", [(0, 1), (1, 0)])

    gc = per * HEADDIM
    groups = tuple(range(nz))

    onehot = np.kron(np.eye(heads), np.ones((1, HEADDIM)))
    ex = jnp.asarray(np.concatenate([onehot, onehot], axis=0), BF)
    er = jnp.asarray(onehot.T, BF)
    sel = jnp.asarray(onehot.T * (np.arange(channels) % HEADDIM == 0)[:, None], F32)

    each = lambda v: jnp.broadcast_to(v[:, None], (own_heads, HEADDIM)).reshape(1, -1)
    parameter_rows = jnp.concatenate(
        [
            conv_x.astype(F32), gnorm_gain[None].astype(F32), each(dt_bias), each(a_log),
            each(d_skip), jnp.broadcast_to(norm_gain[None].astype(F32), (8, half)),
        ],
        axis=0,
    )
    piece = shape((2, HEADDIM, half), BF)
    some = shape((2, gc - HEADDIM, half), BF)
    outs = shape((gc, half), BF)
    first, first2, rest, rest2, out_mine, out_mine2, bcdt_t, table = pl.pallas_call(
        functools.partial(prep_kernel, per),
        out_shape=[
            piece, piece, some, some, outs, outs,
            shape((2 * STATE + HEADS + HALO, half), BF), shape((8, gc)),
        ],
        compiler_params=params(),
        cost_estimate=cost(4),
        name="prep",
    )(
        in_zx.reshape(half, -1), out_w, jnp.transpose(in_bcdt), parameter_rows
    )
    taps_bc = conv_bc.astype(F32)

    step = lambda i: (i, 0)
    fix = lambda i: (0, 0)
    part = shape((rows, gc), BF)
    full = shape((rows, channels))
    anywhere = pl.BlockSpec(memory_space=pl.ANY)
    vmem = pl.BlockSpec(memory_space=pltpu.VMEM)
    narrow = shape((rows, 2 * heads), BF)
    kept = dict(
        xnh=shape((HALO, model), BF), r=shape((rows, 1)), raw=shape((rows, 2 * STATE)),
        rawh=shape((HALO, 2 * STATE)), ubc=shape((rows, 2 * STATE)), b=shape((rows, STATE), BF),
        c=shape((rows, STATE), BF), dt=shape((rows, heads)), sig=shape((rows, heads)),
        cl=shape((rows, heads)), clt=shape((heads, rows)), dt2=narrow, e12=narrow, tl2=narrow,
        dttl2=narrow, ec2=narrow, edt2=narrow, rate=shape((1, heads)),
        wdt=shape((heads, model), BF),
        bcdt=shape((2 * STATE + HEADS + HALO, model), BF), tot=shape((heads, STATE), BF), table=shape((8, channels)),
    )
    wide_part = shape((rows, gc))
    message_shape = shape((channels + HALO, STATE), BF)
    out_shapes = [
        shape((2, channels, model), BF), shape((channels, model), BF), shape((rows, half), BF),
        shape((rows, model), BF), *[wide_part] * nz, *[part] * nz, *[wide_part] * nz,
        *[part] * nz, *[part] * nz, *[message_shape] * (nz - 1), *[shape((HALO, gc))] * nz,
        *[kept[name] for name in KEPT],
    ]
    held = lambda v: pltpu.VMEM(v.shape, v.dtype)
    remotes = 6 + (3 + nz) * (nz - 1) + 2 + 2 * (nz - 1) * (per - 1)
    out = pl.pallas_call(
        functools.partial(front_kernel, per, nz),
        in_specs=[vmem] * 10 + [anywhere] * 3,
        out_specs=[anywhere] * (4 + 5 * nz + nz - 1) + [vmem] * (nz + len(KEPT)),
        out_shape=out_shapes,
        scratch_shapes=[
            *[held(wide_part)] * nz, *[held(part)] * nz, *[held(wide_part)] * nz,
            *[held(part)] * nz, *[held(part)] * nz, pltpu.VMEM((2, channels, model), BF),
            pltpu.VMEM((rows, half), BF), pltpu.VMEM((HALO, model), BF),
            pltpu.VMEM((rows, model), BF),
            held(message_shape), pltpu.VMEM((rows + HALO, gc), F32),
            pltpu.VMEM((rows + HALO, 2 * STATE), F32), pltpu.VMEM((gc, STATE), F32),
            pltpu.SemaphoreType.DMA((remotes,)), pltpu.SemaphoreType.DMA((remotes,)),
            pltpu.SemaphoreType.DMA((7 + 5 * nz,)),
        ],
        compiler_params=pltpu.CompilerParams(
            vmem_limit_bytes=VMEM, collective_id=1, has_side_effects=True
        ),
        cost_estimate=cost(90),
        name="front",
    )(
        hidden, first, first2, rest, rest2, bcdt_t, table, taps_bc, sel, ex, out_mine, out_mine2,
        cotangent,
    )
    weights, wout, cot_o, xn, out = out[0], out[1], out[2], out[3], out[4:]
    z, xr, u, xdt, y_in, messages, xrh, out = take(out, *[nz] * 5, nz - 1, nz)
    o = Named(KEPT, out)
    xnh, r, braw, brawh, ubc, bs, cs = o.xnh, o.r, o.raw, o.rawh, o.ubc, o.b, o.c
    dt, sig, cl, clt, rate, wdt, totals, table = o.dt, o.sig, o.cl, o.clt, o.rate, o.wdt, o.tot, o.table
    dt2, e12, tl2, dttl2, ec2, edt2 = o.dt2, o.e12, o.tl2, o.dttl2, o.ec2, o.edt2
    limit = (lengths[0] - zi * rows).reshape(1, 1)

    smem = pl.BlockSpec(memory_space=pltpu.SMEM)
    tile = 2 * Q if rows % (2 * Q) == 0 else Q
    tiles = rows // tile
    now = lambda columns: pl.BlockSpec((tile, columns), lambda i: (jnp.minimum(i, tiles - 1), 0))
    then = lambda columns: pl.BlockSpec((tile, columns), lambda i: (jnp.maximum(i - 1, 0), 0))
    out = pl.pallas_call(
        functools.partial(mid_kernel, groups, per),
        grid=(tiles + 1,),
        in_specs=[
            *[now(gc)] * (3 * nz), now(half), now(half), now(STATE), now(STATE),
            pl.BlockSpec((heads, tile), lambda i: (0, jnp.minimum(i, tiles - 1))),
            now(2 * heads), now(2 * heads), *[then(gc)] * (2 * nz), then(2 * heads), then(STATE),
            then(half), *[whole(v) for v in messages], whole(totals), whole(table),
            whole(ex), whole(wout), smem,
        ],
        out_specs=[
            *[
                pl.BlockSpec((tile // Q, gc, STATE), lambda i: (jnp.minimum(i, tiles - 1), 0, 0))
            ] * nz,
            now(model), *[then(gc)] * nz, then(channels), then(channels), then(half),
            pl.BlockSpec((channels + HALO, STATE), fix), pl.BlockSpec((1, channels), fix),
            pl.BlockSpec((1, channels), fix),
        ],
        out_shape=[
            *[shape((blocks, gc, STATE), BF)] * nz, shape((rows, model), BF), *[part] * nz,
            shape((rows, channels), BF), shape((rows, channels), BF), shape((rows, half), BF),
            message_shape, shape((1, channels)), shape((1, channels)),
        ],
        scratch_shapes=[
            pltpu.VMEM((channels, STATE), F32), pltpu.VMEM((channels, STATE), F32),
            pltpu.VMEM((2, tile, channels), F32), pltpu.VMEM((2, tile, channels), F32),
            pltpu.VMEM((2, tile, half), F32), pltpu.VMEM((tiles, tile, half), BF),
            pltpu.VMEM((tiles, tile, half), BF), pltpu.VMEM((tiles, tile, Q), F32),
            pltpu.VMEM((tiles, tile, Q), F32), pltpu.VMEM((tile, channels), BF),
            pltpu.SemaphoreType.DMA((2 * tiles,)), pltpu.SemaphoreType.DMA((2 * tiles,)),
        ],
        compiler_params=pltpu.CompilerParams(
            vmem_limit_bytes=VMEM, collective_id=3, has_side_effects=True
        ),
        cost_estimate=cost(30),
        name="mid",
    )(
        *y_in, *u, *z, cotangent, cot_o, bs, cs, clt, e12, dttl2, *u, *z, ec2, cs, hidden,
        *messages, totals, table, ex, wout, limit,
    )
    states, masked, dys, out = take(out, nz, 0, nz)
    dz, yn, out_hidden, message, g_gain, g_skip = out

    begin = lambda i: jnp.maximum(i - nz, 0)
    first_pass = lambda i: jnp.minimum(begin(i), blocks - 1)
    second_pass = lambda i: jnp.minimum(blocks - 1, 2 * blocks - 1 - begin(i))
    either = lambda i: jnp.minimum(begin(i), 2 * blocks - 1 - begin(i))
    one = lambda i: (first_pass(i), 0)
    two = lambda i: (second_pass(i), 0)
    both = lambda i: (either(i), 0)
    gcol = pl.BlockSpec((rows, gc), lambda i: (0, lax.rem(jnp.minimum(i, nz - 1) + 1, nz)))
    head_columns = lambda v: pl.BlockSpec((Q, v), two)
    early_shape = (nz, 2 * HEADDIM, model)
    exchange = 2 * (nz - 1) + nz * (per - 1)
    out = pl.pallas_call(
        functools.partial(scan_back_kernel, groups, per),
        grid=(nz + 2 * blocks,),
        in_specs=[
            *[pl.BlockSpec((Q, gc), one)] * nz, *[pl.BlockSpec((Q, gc), both)] * nz,
            *[pl.BlockSpec((Q, gc), two)] * (2 * nz),
            *[
                pl.BlockSpec(
                    (1, gc, STATE), lambda i: (second_pass(i), 0, 0)
                )
            ] * nz,
            *[pl.BlockSpec((HALO, gc), fix)] * nz,
            pl.BlockSpec((Q, STATE), both), pl.BlockSpec((Q, STATE), both),
            pl.BlockSpec((Q, heads), one),
            pl.BlockSpec((heads, Q), lambda i: (0, either(i))),
            head_columns(heads), head_columns(heads), head_columns(2 * heads),
            head_columns(2 * heads), head_columns(2 * heads), head_columns(2 * STATE),
            head_columns(2 * STATE), whole(brawh), whole(table), whole(taps_bc), whole(rate),
            whole(ex), whole(er), anywhere, gcol, whole(masked), gcol, whole(xn),
        ],
        out_specs=[
            *[pl.BlockSpec((Q, gc), two)] * nz, *[pl.BlockSpec((HALO, gc), fix)] * nz,
            *[pl.BlockSpec((4, gc), fix)] * nz, head_columns(heads),
            pl.BlockSpec((1, heads), fix), pl.BlockSpec((1, heads), fix),
            head_columns(2 * STATE), pl.BlockSpec((HALO, 2 * STATE), fix),
            pl.BlockSpec((4, 2 * STATE), fix),
            pl.BlockSpec((2 * HEADDIM, model), fix),
        ],
        out_shape=[
            *[shape((rows, gc), BF)] * nz, *[shape((HALO, gc), BF)] * nz, *[shape((4, gc))] * nz,
            shape((rows, heads), BF), shape((1, heads)), shape((1, heads)),
            shape((rows, 2 * STATE), BF), shape((HALO, 2 * STATE), BF), shape((4, 2 * STATE)),
            shape((2 * HEADDIM, model), BF),
        ],
        scratch_shapes=[
            *[pltpu.VMEM(message.shape, BF)] * (nz - 1), *[pltpu.VMEM(early_shape, BF)] * (per - 1),
            *[pltpu.VMEM(early_shape[1:], BF)] * (nz - 1), *[pltpu.VMEM((8, gc), F32)] * nz,
            pltpu.VMEM((8, 2 * STATE), F32), pltpu.VMEM((per, *early_shape), BF),
            pltpu.VMEM(early_shape, BF),
            pltpu.VMEM((rows, channels), F32),
            pltpu.VMEM((rows, STATE), F32), pltpu.VMEM((rows, STATE), F32),
            pltpu.VMEM((rows, heads), F32), pltpu.VMEM((heads, Q), F32),
            pltpu.VMEM((channels, STATE), F32), pltpu.VMEM((heads, STATE), F32),
            pltpu.SemaphoreType.DMA((exchange,)), pltpu.SemaphoreType.DMA((exchange,)),
        ],
        compiler_params=pltpu.CompilerParams(
            vmem_limit_bytes=VMEM, collective_id=0, has_side_effects=True
        ),
        cost_estimate=cost(50),
        name="scan_back",
    )(
        *xdt, *dys, *u, *xr, *states, *xrh, bs, cs, cl, clt, dt, sig, dt2, e12, tl2, ubc, braw,
        brawh, table, taps_bc, rate, ex, er, message, yn, masked,
        dz, xn,
    )
    dx, dxh, g_taps = list(out[:nz]), list(out[nz : 2 * nz]), out[2 * nz : 3 * nz]
    dti, g_rate, g_bias, dbc, dbch, g_taps_bc, early_total = out[3 * nz :]
    quarter = 2 * STATE // per
    share = quarter + HALO
    late_rows = 2 * HEADDIM + share + 2 * HALO
    swap_rows = HEADDIM + share + 2 * HALO
    tail_copies = 5 + nz + (per - 1) * (4 + nz) + 3 * (nz - 1) + 1
    operands = [
        *dx, *dxh, *g_taps, dz, dbc, dbch, dti, xn, xnh, weights, o.bcdt, wdt, early_total, hidden,
        cotangent, r, norm_gain[None].astype(F32), g_taps_bc, g_rate, g_bias, g_skip, g_gain, rate,
        ex,
    ]
    line16 = pltpu.VMEM((HALO, half), F32)
    line8 = pltpu.VMEM((8, half), F32)
    early_all, late_all, grad_hidden, g_norm, g_taps_bc = pl.pallas_call(
        functools.partial(tail_kernel, per, nz),
        in_specs=[vmem] * len(operands),
        out_specs=[vmem] * 5,
        out_shape=[
            shape((per, 2, 2 * HEADDIM, half), BF), shape((per, late_rows, half), BF),
            shape((rows, half), BF), shape((1, half)), shape((4, 2 * STATE)),
        ],
        scratch_shapes=[
            pltpu.VMEM((nz, per, HEADDIM, model), BF), pltpu.VMEM((per, share, model), BF),
            pltpu.VMEM((HEADS, model), F32), pltpu.VMEM((nz, HEADDIM, model), BF),
            pltpu.VMEM((share, model), BF), pltpu.VMEM((swap_rows, half), BF),
            pltpu.VMEM((swap_rows, half), BF), pltpu.VMEM((rows, half), F32),
            pltpu.VMEM((rows, half), BF), pltpu.VMEM((rows, half), BF), line16, line16, line16,
            line16, pltpu.VMEM((8, rows), F32), pltpu.VMEM((8, rows), F32), line8, line8,
            pltpu.VMEM((share, model), F32),
            *[pltpu.VMEM((nz, HEADDIM, model), BF)] * (per - 1),
            *[pltpu.VMEM((share, model), BF)] * (per - 1),
            *[pltpu.VMEM((HEADDIM, model), BF)] * (nz - 1),
            *[pltpu.VMEM((share, model), BF)] * (nz - 1), *[line8] * (per - 1),
            *[line8] * (nz - 1),
            pltpu.VMEM((2 * STATE, model), F32),
            pltpu.SemaphoreType.DMA((tail_copies,)), pltpu.SemaphoreType.DMA((tail_copies,)),
        ],
        compiler_params=pltpu.CompilerParams(
            vmem_limit_bytes=VMEM, collective_id=2, has_side_effects=True
        ),
        cost_estimate=cost(60),
        name="tail",
    )(*operands)
    inner = own_heads * HEADDIM
    each_head = jnp.asarray(np.kron(np.eye(own_heads), np.ones((HEADDIM, 1))), F32)
    row_heads = shape((1, own_heads))
    g_zx, g_out, g_bcdt, g_cx, g_gain, g_skip, g_bias, g_rate = pl.pallas_call(
        functools.partial(finish_kernel, per),
        grid=(half // Q,),
        in_specs=[
            pl.BlockSpec((per, 2, 2 * HEADDIM, Q), lambda i: (0, 0, 0, i)),
            pl.BlockSpec((per, late_rows, Q), lambda i: (0, 0, i)),
            pl.BlockSpec((per, late_rows, Q), lambda i: (0, 0, 0)), whole(each_head),
        ],
        out_specs=[
            pl.BlockSpec((Q, own_heads, 2 * HEADDIM), lambda i: (i, 0, 0)),
            pl.BlockSpec((inner, Q), lambda i: (0, i)),
            pl.BlockSpec((2 * STATE + HEADS, Q), lambda i: (0, i)), pl.BlockSpec((4, inner), fix),
            pl.BlockSpec((1, inner), fix), *[pl.BlockSpec((1, own_heads), fix)] * 3,
        ],
        out_shape=[
            shape((half, own_heads, 2 * HEADDIM)), shape((inner, half)),
            shape((2 * STATE + HEADS, half)), shape((4, inner)), shape((1, inner)), row_heads,
            row_heads, row_heads,
        ],
        compiler_params=params(),
        cost_estimate=cost(5),
        name="finish",
    )(early_all, late_all, late_all, each_head)
    return (
        out_hidden,
        grad_hidden,
        g_norm.reshape(-1),
        g_zx,
        jnp.transpose(g_bcdt),
        g_cx,
        g_taps_bc,
        g_bias.reshape(-1),
        g_rate.reshape(-1),
        g_skip.reshape(-1),
        g_gain.reshape(-1),
        g_out,
    )


def fits(mesh):
    ndp, nz, nw = mesh.shape["dp"], mesh.shape["head"], mesh.shape["width"]
    return (
        nw == 2
        and ndp in (2, 4, 8)
        and nz & (nz - 1) == 0
        and HEADS == nz * nw * ndp
        and LEN % (nz * Q) == 0
        and SEQS == ndp
        and HEADS // nw * HEADDIM % Q == 0
        and HEADS // ndp == 8
    )


def solution(mesh):
    placed = (
        P(("dp", "head"), "width"),
        P("dp"),
        P(("dp", "head"), "width"),
        P("width"),
        P("width", "head", None),
        P("width", None),
        P(None, "head"),
        P(),
        P("head"),
        P("head"),
        P("head"),
        P("head"),
        P("head", "width"),
    )
    return jax.shard_map(
        sequence_device if fits(mesh) else per_device,
        mesh=mesh,
        in_specs=placed,
        out_specs=(
            P(("dp", "head"), "width"),
            P(("dp", "head"), "width"),
            P("width"),
            P("width", "head", None),
            P("width", None),
            P(None, "head"),
            P(),
            P("head"),
            P("head"),
            P("head"),
            P("head"),
            P("head", "width"),
        ),
        check_vma=False,
    )
```
